32 devices in a mesh: dp: 8 (over z, x), tensor: 4 (over y, core).
Axes of the slice: x: 2, y: 2, z: 4, core: 2. Of those that a mesh axis runs over, the one named last changes fastest.
Arguments:
- resid_in: bfloat16 [4, 1024, 1024], P(None, ('dp', 'tensor')), may hold values from -6 to 6
- segment_ids: int32 [4, 1024], replicated, may hold values from 0 to 64, as said below
- out_grad: bfloat16 [4, 1024, 1024], P(None, ('dp', 'tensor')), may hold values from -6 to 6
- input_gain: float32 [1024], replicated, may hold values from 0.5 to 1.5
- ffn_gain: float32 [1024], replicated, may hold values from 0.5 to 1.5
- query_weight: bfloat16 [1024, 512], P('dp', 'tensor'), may hold values from -0.1875 to 0.1875
- keyvalue_weight: bfloat16 [1024, 2, 128], P('dp'), may hold values from -0.1875 to 0.1875
- attention_output_weight: bfloat16 [512, 1024], P('tensor', 'dp'), may hold values from -1 to 1
- mixer_input_weight: bfloat16 [1024, 2, 1536], P('dp', None, 'tensor'), may hold values from -0.1875 to 0.1875
- state_input_weight: bfloat16 [1024, 256], P('dp'), may hold values from -0.1875 to 0.1875
- step_weight: bfloat16 [1024, 24], P('dp', 'tensor'), may hold values from -0.1875 to 0.1875
- conv_mixer: float32 [4, 1536], P(None, 'tensor'), may hold values from -3 to 3
- conv_mixer_bias: float32 [1536], P('tensor'), may hold values from -2 to 2
- conv_state: float32 [4, 256], replicated, may hold values from -3 to 3
- conv_state_bias: float32 [256], replicated, may hold values from -2 to 2
- step_bias: float32 [24], P('tensor'), may hold values from -1.5 to 0.5
- decay_log: float32 [24], P('tensor'), may hold values from -12 to -2
- skip_gain: float32 [24], P('tensor'), may hold values from 0.5 to 1.5
- mixer_gain: float32 [1536], P('tensor'), may hold values from 0.5 to 1.5
- mixer_output_weight: bfloat16 [1536, 1024], P('tensor', 'dp'), may hold values from -0.15625 to 0.15625
- gate_up_weight: bfloat16 [1024, 2, 2048], P('dp', None, 'tensor'), may hold values from -0.1875 to 0.1875
- down_weight: bfloat16 [2048, 1024], P('tensor', 'dp'), may hold values from -0.125 to 0.125
Outputs:
- block_out: bfloat16 [4, 1024, 1024], P(None, ('dp', 'tensor'))
- resid_grad: float32 [4, 1024, 1024], P(None, ('dp', 'tensor'))
- input_gain_grad: float32 [1024], replicated
- ffn_gain_grad: float32 [1024], replicated
- w_query_grad: float32 [1024, 512], P('dp', 'tensor')
- w_keyval_grad: float32 [1024, 2, 128], P('dp')
- w_attn_out_grad: float32 [512, 1024], P('tensor', 'dp')
- w_mixer_in_grad: float32 [1024, 2, 1536], P('dp', None, 'tensor')
- w_state_in_grad: float32 [1024, 256], P('dp')
- w_step_grad: float32 [1024, 24], P('dp', 'tensor')
- conv_mixer_grad: float32 [4, 1536], P(None, 'tensor')
- conv_mixer_bias_grad: float32 [1536], P('tensor')
- conv_state_grad: float32 [4, 256], replicated
- conv_state_bias_grad: float32 [256], replicated
- step_bias_grad: float32 [24], P('tensor')
- decay_log_grad: float32 [24], P('tensor')
- skip_gain_grad: float32 [24], P('tensor')
- mixer_gain_grad: float32 [1536], P('tensor')
- w_mixer_out_grad: float32 [1536, 1024], P('tensor', 'dp')
- w_gate_up_grad: float32 [1024, 2, 2048], P('dp', None, 'tensor')
- w_down_grad: float32 [2048, 1024], P('tensor', 'dp')
The draws below stay inside these ranges and needn't reach their ends.
Inputs may be any that keep to these rules, and one draw needn't show every extreme that they name: `segment_ids`: in each sequence the numbers start at 0 and rise by 0 or 1 from one token to the next; equal numbers mark one document. Some sequence is one document from its first token into its last 128 tokens, where 128 // 2 of those tokens each start a new document.
All inputs are finite; a program needn't handle non-finite values.
Results may differ from the reference program's by a relative error of at most 0.035.
Values may be sent and summed in bfloat16 or wider, within the bound.
A program may use at most 320 MiB of HBM per device.

```python
import math
import jax
import jax.numpy as jnp
from jax import lax

D = 1024
HEADS = 8
KVH = 2
HEAD_DIM = 64
MIXER_HEADS = 24
MIXER_DIM = 64
STATE = 128
FF = 2048
CONV = 4
D_SSM = 1536
SPAN = 128
SEQS = 4
SEQ_LEN = 1024
N_TENSOR = 4


def draw_segment_ids(key, part):
    key = jax.random.fold_in(key, 11)
    level_key, roll_key, whole_key, tail_key = jax.random.split(key, 4)
    reach = SPAN // 2
    scale_level = jax.random.randint(level_key, (SEQS, 1), 0, 4)
    mean_length = jnp.maximum(jnp.right_shift(jnp.int32(SEQ_LEN), 2 * (3 - scale_level)), 2)
    threshold = jnp.int32(1 << 20) // mean_length
    rolled = jax.random.randint(roll_key, (SEQS, SEQ_LEN), 0, 1 << 20)
    starts = (rolled < threshold).astype(jnp.int32)
    column = jnp.arange(SEQ_LEN)[None, :]
    starts = jnp.where(column == 0, 0, starts)
    drawn = jnp.minimum(jnp.cumsum(starts, axis=1), reach)
    tail_order = jax.random.permutation(tail_key, SPAN - 1)
    tail_starts = (tail_order < reach).astype(jnp.int32)
    forced_starts = jnp.concatenate([jnp.zeros((SEQ_LEN - SPAN + 1,), jnp.int32), tail_starts])
    forced = jnp.cumsum(forced_starts)[None, :]
    single = jax.random.randint(whole_key, (), 0, SEQS)
    row_index = jnp.arange(SEQS)[:, None]
    return jnp.where(row_index == single, forced, drawn).astype(jnp.int32)


def draw_decay_log(key, part):
    key = jax.random.fold_in(key, 23)
    uniform_draw = jax.random.uniform(key, (MIXER_HEADS,), jnp.float32)
    lowest = jnp.log(0.3 / SEQ_LEN)
    highest = jnp.log(0.05)
    return (lowest + uniform_draw * (highest - lowest)).astype(jnp.float32)


def shard_levels(rng, shape, cuts, least, high):
    factor_of = 1.0
    for dim, parts in cuts:
        heights = jax.random.uniform(jax.random.fold_in(jax.random.fold_in(rng, 6), dim), (parts,), jnp.float32, least / len(cuts), high / len(cuts))
        factor_of = factor_of * jnp.repeat(jnp.exp(heights), shape[dim] // parts).reshape((-1,) + (1,) * (len(shape) - 1 - dim))
    return factor_of


def bell_draw(stream_key, extent, spread, limit, cuts=(), kind=jnp.bfloat16):
    loudness = shard_levels(stream_key, extent, cuts, -0.22, 0.18) if cuts else 1.0
    values = jax.random.normal(stream_key, extent, jnp.float32) * spread * loudness
    return jnp.minimum(jnp.maximum(values, -limit), limit).astype(kind)


def setup_inputs(seed: int = 0) -> dict:
    key_of = jax.random.split(jax.random.key(seed), 23)
    resid_in = bell_draw(key_of[0], (SEQS, SEQ_LEN, D), 1.0, 6.0, ((1, 32),))
    segment_ids = draw_segment_ids(jax.random.fold_in(key_of[22], 71), 0)
    out_grad = bell_draw(key_of[2], (SEQS, SEQ_LEN, D), 1.0, 6.0, ((1, 32),))
    input_gain = jnp.clip(1.0 + 0.1 * jax.random.normal(key_of[3], (D,), jnp.float32), 0.5, 1.5)
    ffn_gain = jnp.clip(1.0 + 0.1 * jax.random.normal(key_of[4], (D,), jnp.float32), 0.5, 1.5)
    query_weight = bell_draw(key_of[5], (D, HEADS * HEAD_DIM), D ** -0.5, 0.1875, ((0, 8), (1, 4)))
    keyvalue_weight = bell_draw(key_of[6], (D, KVH, 2 * HEAD_DIM), D ** -0.5, 0.1875, ((0, 8),))
    attention_output_weight = bell_draw(key_of[7], (HEADS * HEAD_DIM, D), (HEADS * HEAD_DIM // 16) ** -0.5, 1.0, ((0, 4), (1, 8)))
    mixer_input_weight = bell_draw(key_of[8], (D, 2, D_SSM), D ** -0.5, 0.1875, ((0, 8), (2, 4)))
    state_input_weight = bell_draw(key_of[9], (D, 2 * STATE), D ** -0.5, 0.1875, ((0, 8),))
    step_weight = bell_draw(key_of[10], (D, MIXER_HEADS), D ** -0.5, 0.1875, ((0, 8), (1, 4)))
    conv_mixer = bell_draw(key_of[11], (CONV, D_SSM), 0.5, 3.0, ((1, 4),), jnp.float32)
    conv_mixer_bias = bell_draw(key_of[12], (D_SSM,), 0.3, 2.0, ((0, 4),), jnp.float32)
    conv_state = bell_draw(key_of[13], (CONV, 2 * STATE), 0.5, 3.0, (), jnp.float32)
    conv_state_bias = bell_draw(key_of[14], (2 * STATE,), 0.3, 2.0, (), jnp.float32)
    step_bias = jnp.clip(-1.5 + 2.0 * jax.random.uniform(key_of[15], (MIXER_HEADS,), jnp.float32) ** shard_levels(key_of[15], (MIXER_HEADS,), ((0, 4),), -0.2, 0.2), -1.5, 0.5)
    decay_log = draw_decay_log(jax.random.fold_in(key_of[22], 71), 0)
    skip_gain = jnp.clip(0.5 + 1.0 * jax.random.uniform(key_of[17], (MIXER_HEADS,), jnp.float32) ** shard_levels(key_of[17], (MIXER_HEADS,), ((0, 4),), -0.2, 0.2), 0.5, 1.5)
    mixer_gain = jnp.clip(1.0 + 0.1 * jax.random.normal(key_of[18], (D_SSM,), jnp.float32), 0.5, 1.5)
    mixer_output_weight = bell_draw(key_of[19], (D_SSM, D), D_SSM ** -0.5, 0.15625, ((0, 4), (1, 8)))
    gate_up_weight = bell_draw(key_of[20], (D, 2, FF), D ** -0.5, 0.1875, ((0, 8), (2, 4)))
    down_weight = bell_draw(key_of[21], (FF, D), FF ** -0.5, 0.125, ((0, 4), (1, 8)))
    return {"resid_in": resid_in, "segment_ids": segment_ids, "out_grad": out_grad, "input_gain": input_gain, "ffn_gain": ffn_gain, "query_weight": query_weight, "keyvalue_weight": keyvalue_weight, "attention_output_weight": attention_output_weight, "mixer_input_weight": mixer_input_weight, "state_input_weight": state_input_weight, "step_weight": step_weight, "conv_mixer": conv_mixer, "conv_mixer_bias": conv_mixer_bias, "conv_state": conv_state, "conv_state_bias": conv_state_bias, "step_bias": step_bias, "decay_log": decay_log, "skip_gain": skip_gain, "mixer_gain": mixer_gain, "mixer_output_weight": mixer_output_weight, "gate_up_weight": gate_up_weight, "down_weight": down_weight}


@jax.custom_vjp
def reduced_rows(v):
    return lax.optimization_barrier(v.astype(jnp.bfloat16)).astype(jnp.float32)

@jax.custom_vjp
def reduced_backward(v):
    return v

def low_keep(v):
    return (reduced_rows(v), None)

def low_pass(kept, grad):
    return (grad,)

def back_keep(v):
    return (v, None)

def back_low(kept, grad):
    return (reduced_rows(grad),)
reduced_rows.defvjp(low_keep, low_pass)
reduced_backward.defvjp(back_keep, back_low)
EPSILON = 1e-05
ROTARY_BASE = 100000000000.0
MASKED = -1e+30
MATMUL_EXACTNESS = lax.Precision.HIGHEST

def rotate(tensor, positions, sign):
    half_dim = tensor.shape[-1] // 2
    frequency = jnp.exp(-math.log(ROTARY_BASE) * 2.0 * jnp.arange(half_dim, dtype=jnp.float32) / tensor.shape[-1])
    angle = positions[:, None] * frequency[None, :]
    cosine = jnp.cos(angle)[None, :, None, :]
    sine = sign * jnp.sin(angle)[None, :, None, :]
    first_half = tensor[..., :half_dim]
    second_half = tensor[..., half_dim:]
    return jnp.concatenate([first_half * cosine - second_half * sine, second_half * cosine + first_half * sine], -1)

def rms_norm(values, gain):
    return values * lax.rsqrt(lax.optimization_barrier(jnp.mean(values * values, -1, keepdims=True)) + EPSILON) * gain

def gate_norm(values, gate, gain):
    gated = values * jax.nn.silu(gate)
    return gated * lax.rsqrt(lax.optimization_barrier(jnp.mean(gated * gated, -1, keepdims=True)) + EPSILON) * gain

def conv_apply(extended, weight, bias, seg_ext, seg_span):
    length = seg_span.shape[1]
    summed = bias
    for tap_index in range(weight.shape[0]):
        same_doc = (seg_ext[:, tap_index:tap_index + length] == seg_span).astype(extended.dtype)
        summed = summed + weight[tap_index] * extended[:, tap_index:tap_index + length] * same_doc[..., None]
    return jax.nn.silu(summed)

def state_inner(x_heads, step_size, input_heads, output_heads, decay_rate, seg_span, seg_prev):
    cumulative = jnp.cumsum(step_size * decay_rate, axis=1)
    position = jnp.arange(seg_span.shape[1])
    same_doc = (seg_span[:, :, None] == seg_span[:, None, :]) & (position[:, None] >= position[None, :])[None]
    allowed = same_doc[..., None]
    gap_log = cumulative[:, :, None, :] - cumulative[:, None, :, :]
    decay_weight = jnp.where(allowed, jnp.exp(jnp.where(allowed, gap_log, 0.0)), 0.0)
    intersection = jnp.einsum('sthn,sjhn->stjh', output_heads, input_heads, precision=MATMUL_EXACTNESS)
    inner_y = jnp.einsum('stjh,sjh,sjhe->sthe', intersection * decay_weight, step_size, x_heads, precision=MATMUL_EXACTNESS)
    last_seg = seg_span[:, -1]
    tail_weight = jnp.where((seg_span == last_seg[:, None])[..., None], jnp.exp(cumulative[:, -1:, :] - cumulative), 0.0)
    state_local = jnp.einsum('sjh,sjhe,sjhn->shen', tail_weight * step_size, x_heads, input_heads, precision=MATMUL_EXACTNESS)
    carried = jnp.exp(cumulative[:, -1, :]) * (last_seg == seg_prev).astype(cumulative.dtype)[:, None]
    return (inner_y, carried, state_local)

def state_cross(output_heads, step_size, decay_rate, seg_span, seg_prev, state_in):
    cumulative = jnp.cumsum(step_size * decay_rate, axis=1)
    keep_prior = (seg_span == seg_prev[:, None]).astype(cumulative.dtype)[..., None]
    return jnp.einsum('sthn,shen->sthe', output_heads, state_in, precision=MATMUL_EXACTNESS) * (jnp.exp(cumulative) * keep_prior)[..., None]

def forward_layer(resid, segment_ids, input_gain, ffn_gain, query_weight, keyvalue_weight, attention_output_weight, mixer_input_weight, state_input_weight, step_weight, conv_mixer, conv_mixer_bias, conv_state, conv_state_bias, step_bias, decay_log, skip_gain, mixer_gain, mixer_output_weight, gate_up_weight, down_weight):
    sequences = resid.shape[0]
    length = resid.shape[1]
    local_heads = HEADS // N_TENSOR
    local_mixer = MIXER_HEADS // N_TENSOR
    normed_input = reduced_rows(rms_norm(resid, input_gain))
    positions = jnp.arange(length).astype(jnp.float32)
    query_projected = reduced_backward(jnp.einsum('mbn,nf->mbf', normed_input, query_weight, precision=MATMUL_EXACTNESS))
    keyvalue_projected = jnp.einsum('zou,umn->zomn', normed_input, keyvalue_weight, precision=MATMUL_EXACTNESS)
    copy_heads = jnp.array([copy_index * KVH // N_TENSOR for copy_index in range(N_TENSOR)], dtype=jnp.int32)
    keyval_copies = reduced_backward(jnp.take(keyvalue_projected, copy_heads, axis=2))
    queries = reduced_rows(rotate(query_projected.reshape(sequences, length, HEADS, HEAD_DIM), positions, 1.0))
    keys = reduced_rows(rotate(keyval_copies[..., :HEAD_DIM], positions, 1.0))
    values = reduced_rows(keyval_copies[..., HEAD_DIM:])
    keys_heads = jnp.repeat(keys, local_heads, axis=2)
    values_heads = jnp.repeat(values, local_heads, axis=2)
    block_rows = min(512, length)
    scale = 1.0 / math.sqrt(HEAD_DIM)
    key_positions = jnp.arange(length)

    def attend(first_row):
        query_block = lax.dynamic_slice_in_dim(queries, first_row, block_rows, 1)
        seg_block = lax.dynamic_slice_in_dim(segment_ids, first_row, block_rows, 1)
        query_positions = first_row + jnp.arange(block_rows)
        scores = reduced_backward(jnp.einsum('sqhe,skhe->shqk', query_block, keys_heads, precision=MATMUL_EXACTNESS) * scale)
        allowed = (key_positions[None, :] <= query_positions[:, None])[None, None] & (seg_block[:, None, :, None] == segment_ids[:, None, None, :])
        limited = jnp.where(allowed, scores, MASKED)
        largest = lax.optimization_barrier(jnp.max(limited, -1, keepdims=True))
        exponent = jnp.where(allowed, jnp.exp(limited - largest), 0.0)
        probability = exponent / lax.optimization_barrier(jnp.sum(exponent, -1, keepdims=True))
        return reduced_backward(jnp.einsum('shqk,skhe->sqhe', reduced_rows(probability), values_heads, precision=MATMUL_EXACTNESS))
    blocks = lax.map(jax.checkpoint(attend), jnp.arange(length // block_rows, dtype=jnp.int32) * block_rows)
    attention_core = jnp.moveaxis(blocks, 0, 1).reshape(sequences, length, HEADS * HEAD_DIM)
    attention_projected = jnp.einsum('uqn,nh->uqh', reduced_rows(attention_core), attention_output_weight, precision=MATMUL_EXACTNESS)
    mixed_rows = reduced_rows(reduced_backward(jnp.einsum('uxo,ofw->uxfw', normed_input, mixer_input_weight, precision=MATMUL_EXACTNESS)))
    gate_z = mixed_rows[:, :, 0]
    mixer_x = mixed_rows[:, :, 1]
    state_projected = jnp.einsum('mbn,nf->mbf', normed_input, state_input_weight, precision=MATMUL_EXACTNESS)
    state_copies = reduced_rows(reduced_backward(jnp.broadcast_to(state_projected[:, :, None, :], (sequences, length, N_TENSOR, 2 * STATE))))
    step_unactivated = reduced_backward(jnp.einsum('qji,ig->qjg', normed_input, step_weight, precision=MATMUL_EXACTNESS))
    seg_ext = jnp.pad(segment_ids, ((0, 0), (CONV - 1, 0)), constant_values=-1)
    conv_x = conv_apply(jnp.pad(mixer_x, ((0, 0), (CONV - 1, 0), (0, 0))), conv_mixer, conv_mixer_bias, seg_ext, segment_ids)
    flat_copies = state_copies.reshape(sequences, length, N_TENSOR * 2 * STATE)
    conv_bc = conv_apply(jnp.pad(flat_copies, ((0, 0), (CONV - 1, 0), (0, 0))), jnp.tile(conv_state, (1, N_TENSOR)), jnp.tile(conv_state_bias, N_TENSOR), seg_ext, segment_ids)
    conv_bc = conv_bc.reshape(sequences, length, N_TENSOR, 2 * STATE)
    input_heads = jnp.repeat(conv_bc[..., :STATE], local_mixer, axis=2)
    output_heads = jnp.repeat(conv_bc[..., STATE:], local_mixer, axis=2)
    step_size = jax.nn.softplus(step_unactivated + step_bias)
    decay_rate = -jnp.exp(decay_log)
    x_heads = conv_x.reshape(sequences, length, MIXER_HEADS, MIXER_DIM)
    block_count = length // SPAN

    def to_blocks(array):
        return jnp.moveaxis(array.reshape((sequences, block_count, SPAN) + array.shape[2:]), 1, 0)
    previous = jnp.concatenate([jnp.full((sequences, 1), -1, jnp.int32), segment_ids[:, SPAN - 1::SPAN][:, :-1]], 1)

    def scan_step(state_value, inputs):
        x_block, step_block, in_block, out_block, seg_block, prev_block = inputs
        inner_y, carried, state_local = state_inner(x_block, step_block, in_block, out_block, decay_rate, seg_block, prev_block)
        cross_y = state_cross(out_block, step_block, decay_rate, seg_block, prev_block, state_value)
        return (carried[:, :, None, None] * state_value + state_local, inner_y + cross_y)
    start_state = jnp.zeros((sequences, MIXER_HEADS, MIXER_DIM, STATE), jnp.float32)
    _, outputs = lax.scan(jax.checkpoint(scan_step), start_state, (to_blocks(x_heads), to_blocks(step_size), to_blocks(input_heads), to_blocks(output_heads), to_blocks(segment_ids), jnp.moveaxis(previous, 1, 0)))
    mixer_y = jnp.moveaxis(outputs, 0, 1).reshape(sequences, length, MIXER_HEADS, MIXER_DIM) + skip_gain[:, None] * x_heads
    mixer_normed_input = reduced_rows(gate_norm(mixer_y.reshape(sequences, length, D_SSM), gate_z, mixer_gain))
    branch_output = reduced_backward(attention_projected + jnp.einsum('uqn,nh->uqh', mixer_normed_input, mixer_output_weight, precision=MATMUL_EXACTNESS))
    hidden_rows = resid + branch_output
    normed_feedforward = reduced_rows(rms_norm(hidden_rows, ffn_gain))
    gate_up_rows = reduced_backward(jnp.einsum('pjn,nrt->pjrt', normed_feedforward, gate_up_weight, precision=MATMUL_EXACTNESS))
    swiglu_activated = reduced_rows(jax.nn.silu(gate_up_rows[:, :, 0]) * gate_up_rows[:, :, 1])
    return hidden_rows + reduced_backward(jnp.einsum('axt,tz->axz', swiglu_activated, down_weight, precision=MATMUL_EXACTNESS))

def reference(resid_in, segment_ids, out_grad, input_gain, ffn_gain, query_weight, keyvalue_weight, attention_output_weight, mixer_input_weight, state_input_weight, step_weight, conv_mixer, conv_mixer_bias, conv_state, conv_state_bias, step_bias, decay_log, skip_gain, mixer_gain, mixer_output_weight, gate_up_weight, down_weight):
    floats = tuple((array.astype(jnp.float32) for array in (resid_in, input_gain, ffn_gain, query_weight, keyvalue_weight, attention_output_weight, mixer_input_weight, state_input_weight, step_weight, conv_mixer, conv_mixer_bias, conv_state, conv_state_bias, step_bias, decay_log, skip_gain, mixer_gain, mixer_output_weight, gate_up_weight, down_weight)))

    def whole_layer(*arrays):
        return forward_layer(arrays[0], segment_ids, *arrays[1:])
    block_out, pullback = jax.vjp(whole_layer, *floats)
    gradients = pullback(out_grad.astype(jnp.float32))
    return (block_out.astype(jnp.bfloat16), gradients[0], gradients[1], gradients[2], gradients[3], gradients[4], gradients[5], gradients[6], gradients[7], gradients[8], gradients[9], gradients[10], gradients[11], gradients[12], gradients[13], gradients[14], gradients[15], gradients[16], gradients[17], gradients[18], gradients[19])
```

```python
from functools import partial
import math

import jax
import jax.numpy as jnp
from jax import lax
from jax.experimental import pallas as pl
from jax.experimental.pallas import tpu as pltpu
from jax.sharding import PartitionSpec as P

KVH = 2
EPSILON = 1e-05
ROTARY_BASE = 100000000000.0
MASKED = -1e30
MATMUL_EXACTNESS = lax.Precision.HIGHEST
LANES = 128
F32 = jnp.float32
BF16 = jnp.bfloat16
VMEM_BYTES = 60 * 2**20


def dot_nn(a, b):
    return lax.dot_general(a, b, (((1,), (0,)), ((), ())), preferred_element_type=F32)


def dot_nt(a, b):
    return lax.dot_general(a, b, (((1,), (1,)), ((), ())), preferred_element_type=F32)


def dot_tn(a, b):
    return lax.dot_general(a, b, (((0,), (0,)), ((), ())), preferred_element_type=F32)


def remote(src, dst, send_sem, recv_sem, where):
    return pltpu.make_async_remote_copy(
        src_ref=src,
        dst_ref=dst,
        send_sem=send_sem,
        recv_sem=recv_sem,
        device_id=where,
        device_id_type=pl.DeviceIdType.MESH,
    )


class Place:
    def __init__(self, devices):
        self.devices = devices
        self.lines = devices // 2
        self.dp = lax.axis_index("dp")
        self.t = lax.axis_index("tensor")
        self.z = lax.div(self.dp, 2)
        self.p = lax.rem(self.dp, 2)
        self.pair = self.dp + 1 - 2 * self.p
        self.t_near = self.t + 1 - 2 * lax.rem(self.t, 2)
        self.t_far = lax.rem(self.t + 2, 4)
        self.t_both = lax.rem(self.t_near + 2, 4)
        self.first = self.z == 0
        self.last = self.z == self.lines - 1

    def flips(self):
        bit = 1
        while bit < self.devices:
            yield self.dp + bit - 2 * bit * lax.rem(lax.div(self.dp, bit), 2)
            bit *= 2

    def greet(self, line=False, tensor=False, flips=False):
        barrier = pltpu.get_barrier_semaphore()
        count = 0

        def signal(**where):
            pl.semaphore_signal(
                barrier, inc=1, device_id=where, device_id_type=pl.DeviceIdType.MESH
            )

        if tensor:
            signal(tensor=self.t_near)
            signal(tensor=self.t_far)
            count = count + 2
        if line:
            signal(dp=self.pair)
            count = count + 1

            @pl.when(jnp.logical_not(self.first))
            def _():
                signal(dp=self.dp - 2)

            @pl.when(jnp.logical_not(self.last))
            def _():
                signal(dp=self.dp + 2)

        if flips:
            for other in self.flips():
                signal(dp=other)
                count = count + 1
        if line:
            count = count + 2
            count = count - self.first.astype(jnp.int32) - self.last.astype(jnp.int32)
        pl.semaphore_wait(barrier, count)


class LineGather:
    def __init__(self, place, view, recv, right, left, pair):
        self.at, self.view = place, view
        self.recv, self.right, self.left, self.side = recv, right, left, pair

    def copy(self, block, sem, where):
        ref = self.view(block)
        return remote(ref, ref, sem, self.recv.at[block], where)

    def send_right(self, zz):
        return self.copy(zz * 2 + self.at.p, self.right.at[zz], {"dp": self.at.dp + 2})

    def send_left(self, zz):
        return self.copy(zz * 2 + self.at.p, self.left.at[zz], {"dp": self.at.dp - 2})

    def send_pair(self, zz):
        return self.copy(zz * 2 + self.at.p, self.side.at[zz], {"dp": self.at.pair})

    def arrived(self, block):
        self.copy(block, self.side.at[0], {"dp": self.at.pair}).wait_recv()

    def start(self):
        at = self.at
        pl.when(jnp.logical_not(at.last))(lambda: self.send_right(at.z).start())
        pl.when(jnp.logical_not(at.first))(lambda: self.send_left(at.z).start())
        self.send_pair(at.z).start()

    def step(self, s):
        at = self.at
        low, high = at.z - 1 - s, at.z + 1 + s

        @pl.when(low >= 0)
        def _():
            self.arrived(low * 2 + at.p)
            pl.when(jnp.logical_not(at.last))(lambda: self.send_right(low).start())
            self.send_pair(low).start()

        @pl.when(high < at.lines)
        def _():
            self.arrived(high * 2 + at.p)
            pl.when(jnp.logical_not(at.first))(lambda: self.send_left(high).start())
            self.send_pair(high).start()

    def finish(self):
        at = self.at

        @pl.loop(0, at.lines)
        def _(zz):
            self.arrived(zz * 2 + 1 - at.p)

    def drain(self):
        at = self.at

        @pl.loop(0, at.lines)
        def _(zz):
            self.send_pair(zz).wait_send()

            @pl.when(jnp.logical_and(zz <= at.z, jnp.logical_not(at.last)))
            def _():
                self.send_right(zz).wait_send()

            @pl.when(jnp.logical_and(zz >= at.z, jnp.logical_not(at.first)))
            def _():
                self.send_left(zz).wait_send()


class LineScatter:
    def __init__(self, place, part, got, right, left, sems):
        self.at, self.part = place, part
        self.got, self.right, self.left = got, right, left
        (
            self.pair_send,
            self.pair_recv,
            self.right_send,
            self.right_recv,
            self.left_send,
            self.left_recv,
        ) = sems

    def pair_copy(self, zz):
        src = self.part(zz * 2 + 1 - self.at.p)
        return remote(
            src, self.got(zz), self.pair_send.at[zz], self.pair_recv.at[zz], {"dp": self.at.pair}
        )

    def right_copy(self, zz):
        src = self.part(zz * 2 + self.at.p)
        return remote(
            src,
            self.right(zz),
            self.right_send.at[zz],
            self.right_recv.at[zz],
            {"dp": self.at.dp + 2},
        )

    def left_copy(self, zz):
        src = self.part(zz * 2 + self.at.p)
        return remote(
            src, self.left(zz), self.left_send.at[zz], self.left_recv.at[zz], {"dp": self.at.dp - 2}
        )

    def start(self):
        at = self.at

        @pl.loop(0, at.lines)
        def _(i):
            self.pair_copy(at.lines - 1 - i).start()

    def add_into(self, ref, *others):
        total = ref[...].astype(F32)
        for other in others:
            total = total + other[...].astype(F32)
        ref[...] = total.astype(BF16)

    def step(self, i):
        at = self.at
        high, low = at.lines - 1 - i, i

        @pl.when(high > at.z)
        def _():
            self.pair_copy(high).wait_recv()
            ref = self.part(high * 2 + at.p)

            @pl.when(at.first)
            def _():
                self.add_into(ref, self.got(high))

            @pl.when(jnp.logical_not(at.first))
            def _():
                self.right_copy(high).wait_recv()
                self.add_into(ref, self.got(high), self.right(high))

            self.right_copy(high).start()

        @pl.when(low < at.z)
        def _():
            self.pair_copy(low).wait_recv()
            ref = self.part(low * 2 + at.p)

            @pl.when(at.last)
            def _():
                self.add_into(ref, self.got(low))

            @pl.when(jnp.logical_not(at.last))
            def _():
                self.left_copy(low).wait_recv()
                self.add_into(ref, self.got(low), self.left(low))

            self.left_copy(low).start()

    def finish(self, out):
        at = self.at
        self.pair_copy(at.z).wait_recv()
        out[...] = self.part(at.dp)[...].astype(F32) + self.got(at.z)[...].astype(F32)

        @pl.when(jnp.logical_not(at.first))
        def _():
            self.right_copy(at.z).wait_recv()
            out[...] += self.right(at.z)[...].astype(F32)

        @pl.when(jnp.logical_not(at.last))
        def _():
            self.left_copy(at.z).wait_recv()
            out[...] += self.left(at.z)[...].astype(F32)

    def drain(self):
        at = self.at

        @pl.loop(0, at.lines)
        def _(zz):
            self.pair_copy(zz).wait_send()
            pl.when(zz > at.z)(lambda: self.right_copy(zz).wait_send())
            pl.when(zz < at.z)(lambda: self.left_copy(zz).wait_send())


class RowGather:
    def __init__(self, place, view, send, recv):
        self.at, self.view, self.send, self.recv = place, view, send, recv

    def copy(self, rank, chunk, sem, near):
        ref = self.view(rank, chunk)
        where = {"tensor": self.at.t_near if near else self.at.t_far}
        return remote(ref, ref, self.send.at[chunk, sem], self.recv.at[chunk, rank], where)

    def start(self, chunk):
        self.copy(self.at.t, chunk, 0, False).start()
        self.copy(self.at.t, chunk, 1, True).start()

    def forward(self, chunk):
        self.copy(self.at.t_far, chunk, 2, False).wait_recv()
        self.copy(self.at.t_far, chunk, 2, True).start()

    def finish(self, chunk):
        self.copy(self.at.t_near, chunk, 1, True).wait_recv()
        self.copy(self.at.t_both, chunk, 2, True).wait_recv()

    def drain(self, chunk):
        self.copy(self.at.t, chunk, 0, False).wait_send()
        self.copy(self.at.t, chunk, 1, True).wait_send()
        self.copy(self.at.t_far, chunk, 2, True).wait_send()


class RowScatter:
    def __init__(self, place, view, near_buf, far_buf, send, recv):
        self.at, self.view = place, view
        self.near_buf, self.far_buf = near_buf, far_buf
        self.send, self.recv = send, recv

    def near_copy(self, chunk, which):
        rank = self.at.t_both if which else self.at.t_near
        return remote(
            self.view(rank, chunk),
            self.near_buf(which, chunk),
            self.send.at[chunk, which],
            self.recv.at[chunk, which],
            {"tensor": self.at.t_near},
        )

    def far_copy(self, chunk):
        return remote(
            self.view(self.at.t_far, chunk),
            self.far_buf(chunk),
            self.send.at[chunk, 2],
            self.recv.at[chunk, 2],
            {"tensor": self.at.t_far},
        )

    def start(self, chunk):
        self.near_copy(chunk, 1).start()
        self.near_copy(chunk, 0).start()

    def middle(self, chunk):
        self.near_copy(chunk, 1).wait_recv()
        ref = self.view(self.at.t_far, chunk)
        ref[...] = (ref[...].astype(F32) + self.near_buf(1, chunk)[...].astype(F32)).astype(BF16)
        self.far_copy(chunk).start()

    def finish(self, chunk):
        self.near_copy(chunk, 0).wait_recv()
        total = self.view(self.at.t, chunk)[...].astype(F32) + self.near_buf(0, chunk)[
            ...
        ].astype(F32)
        self.far_copy(chunk).wait_recv()
        return total + self.far_buf(chunk)[...].astype(F32)

    def drain(self, chunk):
        self.near_copy(chunk, 0).wait_send()
        self.near_copy(chunk, 1).wait_send()
        self.far_copy(chunk).wait_send()


def line_gather_sems(devices):
    dma = pltpu.SemaphoreType.DMA
    return [dma((devices,)), dma((devices // 2,)), dma((devices // 2,)), dma((devices // 2,))]


def line_scatter_sems(devices):
    return [pltpu.SemaphoreType.DMA((devices // 2,)) for _ in range(6)]


def rms_rows(values, gain):
    return values * lax.rsqrt(jnp.mean(values * values, -1, keepdims=True) + EPSILON) * gain


def rms_rows_grad(values, gain, grad):
    scale = lax.rsqrt(jnp.mean(values * values, -1, keepdims=True) + EPSILON)
    term = grad * gain
    inner = jnp.mean(values * term, -1, keepdims=True)
    return scale * (term - values * (scale * scale * inner)), grad * values * scale


def enter_kernel(devices, pieces, in_width, *refs):
    (x_ref, og_in, gain_ref, w_in, w_all, nx, og, proj, row_send, row_recv), sems = (
        refs[:10],
        refs[10:],
    )
    at = Place(devices)
    seqs, sub, width = x_ref.shape
    depth = w_in.shape[0]
    at.greet(line=True, tensor=True)
    w_all[pl.ds(pl.multiple_of(at.dp * depth, depth), depth), :] = w_in[...]
    gathers = []
    for i, (first, size) in enumerate(pieces):

        def view(block, first=first, size=size):
            return w_all.at[
                pl.ds(pl.multiple_of(block * depth, depth), depth), pl.ds(first, size)
            ]

        gathers.append(LineGather(at, view, *sems[4 * i : 4 * i + 4]))
    gathers[0].start()
    gain = gain_ref[...]
    mine = pl.ds(pl.multiple_of(at.t * sub, sub), sub)
    for s in range(seqs):
        nx[s, mine, :] = rms_rows(x_ref[s].astype(F32), gain).astype(BF16)
        og[s, mine, :] = og_in[s]
    half = seqs // 2

    def rows_of(buf):
        def view(rank, chunk):
            return buf.at[pl.ds(chunk * half, half), pl.ds(pl.multiple_of(rank * sub, sub), sub), :]

        return view

    row_nx = RowGather(at, rows_of(nx), row_send.at[0], row_recv.at[0])
    row_og = RowGather(at, rows_of(og), row_send.at[1], row_recv.at[1])
    for chunk in range(2):
        row_nx.start(chunk)
    for chunk in range(2):
        row_nx.forward(chunk)
    for chunk in range(2):
        row_nx.finish(chunk)
    for i, gather in enumerate(gathers):
        if i + 1 < len(gathers):
            gathers[i + 1].start()

        @pl.loop(0, at.lines - 1)
        def _(s):
            gather.step(s)

        gather.finish()
        if i == 0:
            for chunk in range(2):
                row_og.start(chunk)
        if i == 1:
            rows = nx[...].reshape(seqs * nx.shape[1], width)
            tile = LANES

            @pl.loop(0, in_width // tile)
            def _(j):
                cols = pl.ds(pl.multiple_of(j * tile, tile), tile)
                proj[:, cols] = dot_nn(rows, w_all[:, cols])

            for chunk in range(2):
                row_og.forward(chunk)
            for chunk in range(2):
                row_og.finish(chunk)
    for gather in gathers:
        gather.drain()
    for row in (row_nx, row_og):
        for chunk in range(2):
            row.drain(chunk)


def enter(devices, tensor, pieces, in_width, x, out_grad, gain, w_in):
    seqs, sub, width = x.shape
    depth, columns = w_in.shape
    span = sub * tensor
    shape = jax.ShapeDtypeStruct
    vmem = pl.BlockSpec(memory_space=pltpu.VMEM)
    dma = pltpu.SemaphoreType.DMA
    return pl.pallas_call(
        partial(enter_kernel, devices, pieces, in_width),
        out_shape=(
            shape((width, columns), BF16),
            shape((seqs, span, width), BF16),
            shape((seqs, span, width), BF16),
            shape((seqs * span, in_width), F32),
        ),
        in_specs=[vmem] * 4,
        out_specs=(vmem,) * 4,
        scratch_shapes=[dma((2, 2, 3)), dma((2, 2, 4))] + line_gather_sems(devices) * len(pieces),
        compiler_params=pltpu.CompilerParams(
            collective_id=0, has_side_effects=True, vmem_limit_bytes=VMEM_BYTES
        ),
        name="enter",
    )(x, out_grad, gain, w_in)


def ffn_kernel(devices, layout, *refs):
    (
        x_ref, a_ref, og_ref, ogl_ref, gain_ref, w_ref,
        out_ref, gh_ref, gb, nf, act, dgu, gain_grad,
        part, part2, near1, far1, near2, far2, near3, far3, hid,
        send, recv,
    ) = refs
    at = Place(devices)
    seqs, sub, width = x_ref.shape
    span = sub * 4
    half = seqs // 2
    rows = half * span
    out_w, gu_w, dn_w = (pl.ds(*layout[k]) for k in ("out", "gu", "down"))
    ff = layout["down"][1]
    at.greet(tensor=True)

    def rows_of(buf):
        def view(rank, chunk):
            return buf.at[pl.ds(chunk * half, half), pl.ds(pl.multiple_of(rank * sub, sub), sub), :]

        return view

    def parts_of(buf):
        return lambda which, chunk: buf.at[which, pl.ds(chunk * half, half)]

    def part_of(buf):
        return lambda chunk: buf.at[pl.ds(chunk * half, half)]

    branch = RowScatter(at, rows_of(part), parts_of(near1), part_of(far1), send.at[0], recv.at[0])
    ffn = RowScatter(at, rows_of(part2), parts_of(near2), part_of(far2), send.at[1], recv.at[1])
    back = RowScatter(at, rows_of(part), parts_of(near3), part_of(far3), send.at[2], recv.at[2])
    row_nf = RowGather(at, rows_of(nf), send.at[3], recv.at[3])
    row_gb = RowGather(at, rows_of(gb), send.at[4], recv.at[4])
    mine = pl.ds(pl.multiple_of(at.t * sub, sub), sub)
    gain = gain_ref[...]

    def seq_rows(chunk):
        return pl.ds(chunk * half, half)

    def tok_rows(chunk):
        return pl.ds(chunk * rows, rows)

    for c in range(2):
        value = dot_nt(a_ref[tok_rows(c), :], w_ref[:, out_w])
        part[seq_rows(c)] = value.astype(BF16).reshape(half, span, width)
        branch.start(c)
    for c in range(2):
        branch.middle(c)
    for c in range(2):
        hidden = x_ref[seq_rows(c)].astype(F32) + branch.finish(c)
        hid[seq_rows(c)] = hidden
        nf[seq_rows(c), mine, :] = rms_rows(hidden, gain).astype(BF16)
        row_nf.start(c)
    for c in range(2):
        row_nf.forward(c)
    for c in range(2):
        row_nf.finish(c)
        branch.drain(c)
        flat = nf[seq_rows(c)].reshape(rows, width)
        flat_og = og_ref[seq_rows(c)].reshape(rows, width)
        gate_up = dot_nn(flat, w_ref[:, gu_w])
        gate, up = gate_up[:, :ff], gate_up[:, ff:]
        sigmoid = jax.nn.sigmoid(gate)
        grad_act = dot_nn(flat_og, w_ref[:, dn_w])
        act[tok_rows(c), :] = (gate * sigmoid * up).astype(BF16)
        dgu[tok_rows(c), :ff] = (
            grad_act * up * sigmoid * (1.0 + gate * (1.0 - sigmoid))
        ).astype(BF16)
        dgu[tok_rows(c), ff:] = (grad_act * gate * sigmoid).astype(BF16)
        value = dot_nt(dgu[tok_rows(c), :], w_ref[:, gu_w])
        part[seq_rows(c)] = value.astype(BF16).reshape(half, span, width)
        back.start(c)
    for c in range(2):
        back.middle(c)
        value = dot_nt(act[tok_rows(c), :], w_ref[:, dn_w])
        part2[seq_rows(c)] = value.astype(BF16).reshape(half, span, width)
    total = jnp.zeros((1, width), F32)
    for c in range(2):
        grad_hidden, terms = rms_rows_grad(hid[seq_rows(c)], gain, back.finish(c))
        total = total + jnp.sum(terms.reshape(half * sub, width), 0, keepdims=True)
        grad_hidden = grad_hidden + ogl_ref[seq_rows(c)].astype(F32)
        gh_ref[seq_rows(c)] = grad_hidden
        gb[seq_rows(c), mine, :] = grad_hidden.astype(BF16)
        row_gb.start(c)
        ffn.start(c)
    gain_grad[...] = total
    for c in range(2):
        row_gb.forward(c)
        ffn.middle(c)
    for c in range(2):
        out_ref[seq_rows(c)] = (hid[seq_rows(c)] + ffn.finish(c)).astype(BF16)
        row_gb.finish(c)
    for c in range(2):
        row_nf.drain(c)
        row_gb.drain(c)
        back.drain(c)
        ffn.drain(c)


def feed_forward(devices, tensor, layout, x, a, og, out_grad, gain, w_all):
    seqs, sub, width = x.shape
    span = sub * tensor
    tokens = seqs * span
    ff = layout["down"][1]
    shape = jax.ShapeDtypeStruct
    vmem = pl.BlockSpec(memory_space=pltpu.VMEM)
    dma = pltpu.SemaphoreType.DMA
    whole, own = (seqs, span, width), (seqs, sub, width)
    return pl.pallas_call(
        partial(ffn_kernel, devices, layout),
        out_shape=(
            shape(own, BF16),
            shape(own, F32),
            shape(whole, BF16),
            shape(whole, BF16),
            shape((tokens, ff), BF16),
            shape((tokens, 2 * ff), BF16),
            shape((1, width), F32),
        ),
        in_specs=[vmem] * 6,
        out_specs=(vmem,) * 7,
        scratch_shapes=[
            pltpu.VMEM(whole, BF16),
            pltpu.VMEM(whole, BF16),
        ]
        + [pltpu.VMEM((2,) + own, BF16), pltpu.VMEM(own, BF16)] * 3
        + [
            pltpu.VMEM(own, F32),
            dma((5, 2, 3)),
            dma((5, 2, 4)),
        ],
        compiler_params=pltpu.CompilerParams(
            collective_id=1, has_side_effects=True, vmem_limit_bytes=VMEM_BYTES
        ),
        name="feed_forward",
    )(x, a, og, out_grad, gain, w_all)


def leave_kernel(devices, layout, pieces, *refs):
    (
        x_ref, gh_ref, gain_ref, w_ref, nx_ref, dp_ref, gb_ref, a_ref, nf_ref, dgu_ref, og_ref,
        act_ref, small_ref,
        rg_ref, dw_ref, sums, kvs,
        part, near, far, grads, got, right, left, small_near, small_far, small_dp, kv_near, kv_far,
        send, recv, small_send, small_recv, dp_send, dp_recv, kv_send, kv_recv, *sems,
    ) = refs
    at = Place(devices)
    seqs, sub, width = x_ref.shape
    span = sub * 4
    half = seqs // 2
    rows = half * span
    depth = width // devices
    in_w = layout["in"]
    at.greet(line=True, tensor=True, flips=True)

    def rows_of(buf):
        def view(rank, chunk):
            return buf.at[pl.ds(chunk * half, half), pl.ds(pl.multiple_of(rank * sub, sub), sub), :]

        return view

    back = RowScatter(
        at,
        rows_of(part),
        lambda which, chunk: near.at[which, pl.ds(chunk * half, half)],
        lambda chunk: far.at[pl.ds(chunk * half, half)],
        send,
        recv,
    )
    for c in range(2):
        value = dot_nt(dp_ref[pl.ds(c * rows, rows), :], w_ref[:, pl.ds(*in_w)])
        part[pl.ds(c * half, half)] = value.astype(BF16).reshape(half, span, width)
        back.start(c)
    scatters = []
    for i, (first, size) in enumerate(pieces):

        def block(buf, k, first=first, size=size):
            return buf.at[pl.ds(pl.multiple_of(k * depth, depth), depth), pl.ds(first, size)]

        scatters.append(
            LineScatter(
                at,
                partial(block, grads),
                partial(block, got),
                partial(block, right),
                partial(block, left),
                sems[6 * i : 6 * i + 6],
            )
        )

    flat_nx = nx_ref[...].reshape(2 * rows, width)

    def product(lhs, rhs_ref, first):
        size = rhs_ref.shape[-1]

        @pl.loop(0, size // LANES)
        def _(j):
            cols = pl.ds(pl.multiple_of(j * LANES, LANES), LANES)
            dst = pl.ds(pl.multiple_of(first + j * LANES, LANES), LANES)
            grads[:, dst] = dot_tn(lhs, rhs_ref[:, cols]).astype(BF16)

    product(flat_nx, dp_ref, in_w[0])
    scatters[0].start()
    for c in range(2):
        back.middle(c)
    product(gb_ref[...].reshape(2 * rows, width), a_ref, layout["out"][0])
    scatters[1].start()
    product(nf_ref[...].reshape(2 * rows, width), dgu_ref, layout["gu"][0])
    scatters[2].start()
    product(og_ref[...].reshape(2 * rows, width), act_ref, layout["down"][0])
    scatters[3].start()
    total = jnp.zeros((1, width), F32)
    gain = gain_ref[...]
    for c in range(2):
        seq = pl.ds(c * half, half)
        grad, terms = rms_rows_grad(x_ref[seq].astype(F32), gain, back.finish(c))
        rg_ref[seq] = gh_ref[seq] + grad
        total = total + jnp.sum(terms.reshape(half * sub, width), 0, keepdims=True)
    sums[...] = small_ref[...]
    sums[0:1, :] = total
    for i, (buf, where) in enumerate(
        ((small_near, {"tensor": at.t_near}), (small_far, {"tensor": at.t_far}))
    ):
        buf[0] = sums[0:8, :]
        copy = remote(buf.at[0], buf.at[1], small_send.at[i], small_recv.at[i], where)
        copy.start()
        copy.wait()
        sums[0:8, :] += buf[1]
    for i, other in enumerate(at.flips()):
        small_dp[i, 0] = sums[...]
        copy = remote(
            small_dp.at[i, 0], small_dp.at[i, 1], dp_send.at[i], dp_recv.at[i], {"dp": other}
        )
        copy.start()
        copy.wait()
        sums[...] += small_dp[i, 1]
    for i, (first, size) in enumerate(pieces):

        @pl.loop(0, at.lines - 1)
        def _(s):
            scatters[i].step(s)

        scatters[i].finish(dw_ref.at[:, pl.ds(first, size)])
        if i == 0:
            state = layout["state"]
            kvw = layout["kv"][1]
            kv_near[0, :, pl.ds(0, kvw)] = dw_ref[:, pl.ds(*layout["kv"])]
            kv_near[0, :, pl.ds(kvw, state[1])] = dw_ref[:, pl.ds(*state)]
            copy = remote(
                kv_near.at[0], kv_near.at[1], kv_send.at[0], kv_recv.at[0], {"tensor": at.t_near}
            )
            copy.start()
            copy.wait()
            kv_far[0] = kv_near[0] + kv_near[1]
            copy = remote(
                kv_far.at[0], kv_far.at[1], kv_send.at[1], kv_recv.at[1], {"tensor": at.t_far}
            )
            copy.start()
            copy.wait()
            kvs[:, pl.ds(0, kvw)] = kv_far[0, :, pl.ds(0, kvw)]
            kvs[:, pl.ds(kvw, kvw)] = kv_far[1, :, pl.ds(0, kvw)]

            @pl.when(at.t >= 2)
            def _():
                kvs[:, pl.ds(0, kvw)] = kv_far[1, :, pl.ds(0, kvw)]
                kvs[:, pl.ds(kvw, kvw)] = kv_far[0, :, pl.ds(0, kvw)]

            kvs[:, pl.ds(2 * kvw, state[1])] = (
                kv_far[0, :, pl.ds(kvw, state[1])] + kv_far[1, :, pl.ds(kvw, state[1])]
            )
    for scatter in scatters:
        scatter.drain()
    for c in range(2):
        back.drain(c)


def leave(
    devices, tensor, layout, pieces, x, gh, gain, w_all, nx, d_in, gb, a, nf, dgu, og, act, small
):
    seqs, sub, width = x.shape
    span = sub * tensor
    depth = width // devices
    columns = w_all.shape[1]
    kvw, state = layout["kv"][1], layout["state"][1]
    shape = jax.ShapeDtypeStruct
    vmem = pl.BlockSpec(memory_space=pltpu.VMEM)
    dma = pltpu.SemaphoreType.DMA
    own = (seqs, sub, width)
    rounds = devices.bit_length() - 1
    block = (devices // 2 * depth, columns)
    return pl.pallas_call(
        partial(leave_kernel, devices, layout, pieces),
        out_shape=(
            shape(own, F32),
            shape((depth, columns), F32),
            shape(small.shape, F32),
            shape((depth, 2 * kvw + state), F32),
        ),
        in_specs=[vmem] * 13,
        out_specs=(vmem,) * 4,
        scratch_shapes=[
            pltpu.VMEM((seqs, span, width), BF16),
            pltpu.VMEM((2,) + own, BF16),
            pltpu.VMEM(own, BF16),
            pltpu.VMEM((width, columns), BF16),
            pltpu.VMEM(block, BF16),
            pltpu.VMEM(block, BF16),
            pltpu.VMEM(block, BF16),
            pltpu.VMEM((2, 8, width), F32),
            pltpu.VMEM((2, 8, width), F32),
            pltpu.VMEM((rounds, 2) + small.shape, F32),
            pltpu.VMEM((2, depth, kvw + state), F32),
            pltpu.VMEM((2, depth, kvw + state), F32),
            dma((2, 3)),
            dma((2, 4)),
            dma((2,)),
            dma((2,)),
            dma((rounds,)),
            dma((rounds,)),
            dma((2,)),
            dma((2,)),
        ]
        + line_scatter_sems(devices) * len(pieces),
        compiler_params=pltpu.CompilerParams(
            collective_id=2, has_side_effects=True, vmem_limit_bytes=VMEM_BYTES
        ),
        name="leave",
    )(x, gh, gain, w_all, nx, d_in, gb, a, nf, dgu, og, act, small)


def as_sent(array):

    def short(part):
        return part.astype(jnp.bfloat16) if part.dtype == jnp.float32 else part

    return jax.tree.map(short, array)


def from_behind(array, axis, by):
    devices = lax.axis_size(axis)
    pairs = [(i, i + by) for i in range(devices) if 0 <= i + by < devices]
    return lax.ppermute(array, axis, pairs)


def prefix(array, axis, combine, identity):
    devices, mine = (lax.axis_size(axis), lax.axis_index(axis))
    everything = jax.tree.map(
        lambda part, kind: lax.all_gather(part.astype(kind), axis),
        array,
        (jnp.bfloat16, jnp.bfloat16),
    )
    start = jax.tree.map(
        lambda part, zero: jnp.broadcast_to(jnp.asarray(zero, part.dtype), part.shape),
        array,
        identity,
    )

    def turn(k, before):
        reached = k < mine
        new = combine(
            before, jax.tree.map(lambda part, own: part[k].astype(own.dtype), everything, array)
        )
        return jax.tree.map(lambda a, b: jnp.where(reached, a, b), new, before)

    return lax.fori_loop(0, devices, turn, start)


def carried_in(array, axis, join, neutral):
    count = lax.axis_size(axis)
    place = lax.axis_index(axis)
    ahead = count - 1 - place
    gathered = jax.tree.map(
        lambda a, kind: lax.all_gather(a.astype(kind), axis),
        array,
        jax.tree.map(lambda a: jnp.bfloat16 if a.dtype == jnp.float32 else a.dtype, array),
    )
    state = jax.tree.map(lambda a, e: jnp.zeros_like(a) + jnp.asarray(e, a.dtype), array, neutral)

    def one(turn, state):
        source = count - 1 - turn
        return join(
            state,
            jax.tree.map(
                lambda a, own: lax.dynamic_index_in_dim(a, source, 0, False).astype(own.dtype),
                gathered,
                array,
            ),
        )

    return lax.fori_loop(0, ahead, one, state)


def rotate(tensor, positions, sign):
    half_dim = tensor.shape[-1] // 2
    frequency = jnp.exp(
        -math.log(ROTARY_BASE) * 2.0 * jnp.arange(half_dim, dtype=jnp.float32) / tensor.shape[-1]
    )
    angle = positions[:, None] * frequency[None, :]
    cosine = jnp.cos(angle)[None, :, None, :]
    sine = sign * jnp.sin(angle)[None, :, None, :]
    first_half = tensor[..., :half_dim]
    second_half = tensor[..., half_dim:]
    return jnp.concatenate(
        [first_half * cosine - second_half * sine, second_half * cosine + first_half * sine], -1
    )


def conv_apply(extended, weight, bias, seg_ext, seg_span):
    length = seg_span.shape[1]
    summed = bias
    for tap_index in range(weight.shape[0]):
        same_doc = (seg_ext[:, tap_index : tap_index + length] == seg_span).astype(extended.dtype)
        summed = (
            summed
            + weight[tap_index] * extended[:, tap_index : tap_index + length] * same_doc[..., None]
        )
    return jax.nn.silu(summed)


def state_inner(x_heads, step_size, input_heads, output_heads, decay_rate, seg_span, seg_prev):
    cumulative = jnp.cumsum(step_size * decay_rate, axis=1)
    position = jnp.arange(seg_span.shape[1])
    same_doc = (seg_span[:, :, None] == seg_span[:, None, :]) & (
        position[:, None] >= position[None, :]
    )[None]
    allowed = same_doc[..., None]
    gap_log = cumulative[:, :, None, :] - cumulative[:, None, :, :]
    decay_weight = jnp.where(allowed, jnp.exp(jnp.where(allowed, gap_log, 0.0)), 0.0)
    intersection = jnp.einsum(
        "sthn,sjhn->stjh", output_heads, input_heads, precision=MATMUL_EXACTNESS
    )
    inner_y = jnp.einsum(
        "stjh,sjh,sjhe->sthe",
        intersection * decay_weight,
        step_size,
        x_heads,
        precision=MATMUL_EXACTNESS,
    )
    last_seg = seg_span[:, -1]
    tail_weight = jnp.where(
        (seg_span == last_seg[:, None])[..., None], jnp.exp(cumulative[:, -1:, :] - cumulative), 0.0
    )
    state_local = jnp.einsum(
        "sjh,sjhe,sjhn->shen",
        tail_weight * step_size,
        x_heads,
        input_heads,
        precision=MATMUL_EXACTNESS,
    )
    carried = (
        jnp.exp(cumulative[:, -1, :]) * (last_seg == seg_prev).astype(cumulative.dtype)[:, None]
    )
    return (inner_y, carried, state_local)


def state_cross(output_heads, step_size, decay_rate, seg_span, seg_prev, state_in):
    cumulative = jnp.cumsum(step_size * decay_rate, axis=1)
    keep_prior = (seg_span == seg_prev[:, None]).astype(cumulative.dtype)[..., None]
    return (
        jnp.einsum("sthn,shen->sthe", output_heads, state_in, precision=MATMUL_EXACTNESS)
        * (jnp.exp(cumulative) * keep_prior)[..., None]
    )


def combine_states(earlier, later):
    return (earlier[0] * later[0], later[0][:, :, None, None] * earlier[1] + later[1])


def body(
    resid_in,
    segment_ids,
    out_grad,
    input_gain,
    ffn_gain,
    query_weight,
    keyvalue_weight,
    attention_output_weight,
    mixer_input_weight,
    state_input_weight,
    step_weight,
    conv_mixer,
    conv_mixer_bias,
    conv_state,
    conv_state_bias,
    step_bias,
    decay_log,
    skip_gain,
    mixer_gain,
    mixer_output_weight,
    gate_up_weight,
    down_weight,
):
    tensor_count = lax.axis_size("tensor")
    shard_count = lax.axis_size("dp")
    tensor_rank = lax.axis_index("tensor")
    shard_rank = lax.axis_index("dp")
    sequences, sub_rows, model_width = resid_in.shape
    span_rows = sub_rows * tensor_count
    head_dim = keyvalue_weight.shape[2] // 2
    query_width = query_weight.shape[1]
    local_heads = query_width // head_dim
    mixer_local = step_weight.shape[1]
    mixer_width = conv_mixer.shape[1]
    mixer_total = mixer_width * tensor_count
    mixer_dim = mixer_width // mixer_local
    state_dim = state_input_weight.shape[1] // 2
    edge_rows = conv_mixer.shape[0] - 1
    scale = 1.0 / math.sqrt(head_dim)
    keyval_index = tensor_rank * KVH // tensor_count
    keyvalue_local = lax.dynamic_index_in_dim(keyvalue_weight, keyval_index, 1, keepdims=False)
    ff = down_weight.shape[0]
    depth = query_weight.shape[0]
    layout = {}
    columns = 0
    for name, size in (
        ("q", query_width),
        ("kv", 2 * head_dim),
        ("step", LANES),
        ("x", mixer_width),
        ("state", 2 * state_dim),
        ("z", mixer_width),
        ("out", query_width + mixer_width),
        ("gu", 2 * ff),
        ("down", ff),
    ):
        layout[name] = (columns, size)
        columns += size
    layout["in"] = (0, layout["out"][0])
    w_packed = jnp.concatenate(
        [
            query_weight,
            keyvalue_local,
            jnp.pad(step_weight, ((0, 0), (0, LANES - mixer_local))),
            mixer_input_weight[:, 1],
            state_input_weight,
            mixer_input_weight[:, 0],
            jnp.concatenate([attention_output_weight, mixer_output_weight], 0).T,
            gate_up_weight.reshape(depth, 2 * ff),
            down_weight.T,
        ],
        1,
    )
    early = (0, layout["z"][0])
    w_all, span_normed_input, span_gradient, projected = enter(
        shard_count,
        tensor_count,
        (early, layout["z"], layout["out"], layout["gu"], layout["down"]),
        layout["out"][0],
        resid_in,
        out_grad,
        input_gain[None, :],
        w_packed,
    )

    def columns_of(array, name):
        first, size = layout[name]
        return array[..., first : first + size]

    projected = projected.reshape(sequences, span_rows, -1)
    first_row = shard_rank * span_rows
    query_pos = first_row + jnp.arange(span_rows, dtype=jnp.int32)
    positions = query_pos.astype(jnp.float32)
    seg_span = lax.dynamic_slice_in_dim(segment_ids, first_row, span_rows, 1)
    seg_padded = jnp.pad(segment_ids, ((0, 0), (edge_rows, 0)), constant_values=-1)
    seg_ext = lax.dynamic_slice_in_dim(seg_padded, first_row, span_rows + edge_rows, 1)
    seg_prev = seg_ext[:, edge_rows - 1]

    def tensor_total(partial_value):
        return jax.tree.map(
            lambda part: part.astype(jnp.float32), lax.psum(as_sent(partial_value), "tensor")
        )

    def over_keys(packed_keys, fold_step, initial):
        return fold_step(
            initial, lax.all_gather(packed_keys, "dp", axis=1, tiled=True), jnp.int32(0)
        )

    def key_allowed(key_count):
        key_pos = jnp.arange(key_count, dtype=jnp.int32)
        causal = (key_pos[None, :] <= query_pos[:, None])[None, None]
        return causal & (seg_span[:, None, :, None] == segment_ids[:, None, None, :])

    query_projected = columns_of(projected, "q")
    keyvalue_projected = columns_of(projected, "kv")
    queries = rotate(
        query_projected.reshape(sequences, span_rows, local_heads, head_dim), positions, 1.0
    ).astype(jnp.bfloat16)
    keys_own = rotate(keyvalue_projected[:, :, None, :head_dim], positions, 1.0)[:, :, 0].astype(
        jnp.bfloat16
    )
    values_own = keyvalue_projected[:, :, head_dim:].astype(jnp.bfloat16)
    packed = jnp.concatenate([keys_own, values_own], -1)

    def forward_fold(state_carry, shard_piece, key_first):
        running_max, running_sum, accumulated = state_carry
        key_count = shard_piece.shape[1]
        scores = (
            jnp.einsum(
                "sqhe,ske->shqk",
                queries,
                shard_piece[:, :, :head_dim],
                preferred_element_type=jnp.float32,
            )
            * scale
        )
        allowed = key_allowed(key_count)
        new_max = jnp.maximum(running_max, jnp.max(jnp.where(allowed, scores, MASKED), -1))
        exp_scores = jnp.where(allowed, jnp.exp(scores - new_max[..., None]), 0.0)
        running_sum = jnp.sum(exp_scores, -1)
        accumulated = jnp.einsum(
            "shqk,ske->shqe",
            exp_scores.astype(jnp.bfloat16),
            shard_piece[:, :, head_dim:],
            preferred_element_type=jnp.float32,
        )
        return (new_max, running_sum, accumulated)

    start_fold = (
        jnp.full((sequences, local_heads, span_rows), MASKED, jnp.float32),
        jnp.zeros((sequences, local_heads, span_rows), jnp.float32),
        jnp.zeros((sequences, local_heads, span_rows, head_dim), jnp.float32),
    )
    final_max, final_sum, final_acc = over_keys(packed, forward_fold, start_fold)
    log_total = final_max + jnp.log(final_sum)
    attention_out = final_acc / final_sum[..., None]
    attention_rows = jnp.transpose(attention_out, (0, 2, 1, 3))
    attention_reduced = attention_rows.reshape(sequences, span_rows, query_width).astype(
        jnp.bfloat16
    )
    gate_z = columns_of(projected, "z").astype(jnp.bfloat16)
    mixer_x = columns_of(projected, "x").astype(jnp.bfloat16)
    state_projected = columns_of(projected, "state").astype(jnp.bfloat16)
    step_unactivated = columns_of(projected, "step")[..., :mixer_local]
    edge_x, edge_state = from_behind(
        (mixer_x[:, span_rows - edge_rows :], state_projected[:, span_rows - edge_rows :]), "dp", 1
    )
    ext_x = jnp.concatenate([edge_x, mixer_x], 1).astype(jnp.float32)
    ext_state = jnp.concatenate([edge_state, state_projected], 1).astype(jnp.float32)
    conv_x_fn = partial(conv_apply, seg_ext=seg_ext, seg_span=seg_span)
    conv_x = conv_x_fn(ext_x, conv_mixer, conv_mixer_bias)
    conv_bc = conv_x_fn(ext_state, conv_state, conv_state_bias)
    step_pre = step_unactivated + step_bias
    step_size = jax.nn.softplus(step_pre)
    decay_rate = -jnp.exp(decay_log)
    x_heads = conv_x.reshape(sequences, span_rows, mixer_local, mixer_dim)
    head_shape = (sequences, span_rows, mixer_local, state_dim)

    def intra_fn(x_value, step_value, bc_value, decay_value):
        input_heads = jnp.broadcast_to(bc_value[:, :, None, :state_dim], head_shape)
        output_heads = jnp.broadcast_to(bc_value[:, :, None, state_dim:], head_shape)
        return state_inner(
            x_value, step_value, input_heads, output_heads, decay_value, seg_span, seg_prev
        )

    def cross_fn(bc_value, step_value, decay_value, prior_value):
        output_heads = jnp.broadcast_to(bc_value[:, :, None, state_dim:], head_shape)
        return state_cross(output_heads, step_value, decay_value, seg_span, seg_prev, prior_value)

    inner_y, carry_local, state_local = intra_fn(x_heads, step_size, conv_bc, decay_rate)
    scan_identity = (jnp.ones_like(carry_local), jnp.zeros_like(state_local))
    prior_carry, state_prior = prefix(
        (carry_local, state_local), "dp", combine_states, scan_identity
    )
    cross_y = cross_fn(conv_bc, step_size, decay_rate, state_prior)
    mixer_y = (inner_y + cross_y + skip_gain[:, None] * x_heads).reshape(
        sequences, span_rows, mixer_width
    )
    gate_float = gate_z.astype(jnp.float32)
    gate_sigmoid = jax.nn.sigmoid(gate_float)
    gated = mixer_y * (gate_float * gate_sigmoid)
    square_total = tensor_total(jnp.sum(gated * gated, -1, keepdims=True))
    norm_scale = lax.rsqrt(square_total / mixer_total + EPSILON)
    mixer_normed_input = (gated * norm_scale * mixer_gain).astype(jnp.bfloat16)
    tokens = sequences * span_rows
    branch_low = jnp.concatenate([attention_reduced, mixer_normed_input], -1).reshape(tokens, -1)
    block_out, grad_hidden, grad_branch, span_feedforward, activated, grad_gate_up, ffn_gain_part = (
        feed_forward(
            shard_count,
            tensor_count,
            layout,
            resid_in,
            branch_low,
            span_gradient,
            out_grad,
            ffn_gain[None, :],
            w_all,
        )
    )
    grad_low = jnp.einsum(
        "irh,hy->iry", grad_branch, columns_of(w_all, "out"), preferred_element_type=jnp.float32
    )
    grad_attention = grad_low[..., :query_width]
    grad_mixer_norm = grad_low[..., query_width:]
    grad_attn_low = grad_attention.reshape(sequences, span_rows, local_heads, head_dim).astype(
        jnp.bfloat16
    )
    delta = jnp.transpose(
        jnp.sum(grad_attn_low.astype(jnp.float32) * attention_rows, -1), (0, 2, 1)
    )
    query_zero = jnp.zeros((sequences, local_heads, span_rows, head_dim), jnp.float32)

    def backward_fold(state_carry, shard_piece, key_first):
        key_count = shard_piece.shape[1]
        keys_piece = shard_piece[:, :, :head_dim]
        scores = (
            jnp.einsum("sqhe,ske->shqk", queries, keys_piece, preferred_element_type=jnp.float32)
            * scale
        )
        allowed = key_allowed(key_count)
        exp_scores = jnp.where(allowed, jnp.exp(scores - log_total[..., None]), 0.0)
        grad_probs = jnp.einsum(
            "sqhe,ske->shqk",
            grad_attn_low,
            shard_piece[:, :, head_dim:],
            preferred_element_type=jnp.float32,
        )
        grad_scores = (exp_scores * (grad_probs - delta[..., None])).astype(jnp.bfloat16)
        grad_query = (
            jnp.einsum(
                "shqk,ske->shqe", grad_scores, keys_piece, preferred_element_type=jnp.float32
            )
            * scale
        )
        grad_key_piece = (
            jnp.einsum("shqk,sqhe->ske", grad_scores, queries, preferred_element_type=jnp.float32)
            * scale
        )
        grad_value_piece = jnp.einsum(
            "shqk,sqhe->ske",
            exp_scores.astype(jnp.bfloat16),
            grad_attn_low,
            preferred_element_type=jnp.float32,
        )
        updated = jnp.concatenate([grad_key_piece, grad_value_piece], -1)
        return (grad_query, updated)

    keys_zero = jnp.zeros((sequences, span_rows * shard_count, 2 * head_dim), jnp.float32)
    grad_query, grad_keys_all = over_keys(packed, backward_fold, (query_zero, keys_zero))
    grad_keyval = lax.psum_scatter(grad_keys_all, "dp", scatter_dimension=1, tiled=True)
    query_projected_gradient = (
        rotate(jnp.transpose(grad_query, (0, 2, 1, 3)), positions, -1.0)
        .reshape(sequences, span_rows, query_width)
        .astype(jnp.bfloat16)
    )
    grad_key_pre = rotate(grad_keyval[:, :, None, :head_dim], positions, -1.0)[:, :, 0]
    keyvalue_reduced_gradient = jnp.concatenate(
        [grad_key_pre, grad_keyval[:, :, head_dim:]], -1
    ).astype(jnp.bfloat16)
    gain_term = grad_mixer_norm * mixer_gain
    grad_mixer_gain = jnp.sum(grad_mixer_norm * gated * norm_scale, (0, 1))
    inner_total = tensor_total(jnp.sum(gated * gain_term, -1, keepdims=True))
    grad_gated = norm_scale * (
        gain_term - gated * norm_scale * norm_scale * inner_total / mixer_total
    )
    grad_mixer_y = grad_gated * (gate_float * gate_sigmoid)
    grad_gate_z = grad_gated * mixer_y * gate_sigmoid * (1.0 + gate_float * (1.0 - gate_sigmoid))
    grad_y_heads = grad_mixer_y.reshape(sequences, span_rows, mixer_local, mixer_dim)
    grad_skip = jnp.sum(grad_y_heads * x_heads, (0, 1, 3))
    _, cross_pull = jax.vjp(cross_fn, conv_bc, step_size, decay_rate, state_prior)
    grad_bc_cross, grad_step_cross, grad_decay_cross, grad_prior = cross_pull(grad_y_heads)
    later_carry, grad_after = carried_in(
        (carry_local, grad_prior), "dp", combine_states, scan_identity
    )
    grad_carry = jnp.sum(grad_after * state_prior, (2, 3))
    _, intra_pull = jax.vjp(intra_fn, x_heads, step_size, conv_bc, decay_rate)
    grad_x_intra, grad_step_intra, grad_bc_intra, grad_decay_intra = intra_pull(
        (grad_y_heads, grad_carry, grad_after)
    )
    grad_conv_x = (grad_x_intra + skip_gain[:, None] * grad_y_heads).reshape(
        sequences, span_rows, mixer_width
    )
    grad_conv_bc = grad_bc_intra + grad_bc_cross
    grad_step_pre = (grad_step_intra + grad_step_cross) * jax.nn.sigmoid(step_pre)
    grad_step_bias = jnp.sum(grad_step_pre, (0, 1))
    grad_decay_log = (grad_decay_intra + grad_decay_cross) * decay_rate
    step_reduced_gradient = grad_step_pre.astype(jnp.bfloat16)
    _, conv_x_pull = jax.vjp(conv_x_fn, ext_x, conv_mixer, conv_mixer_bias)
    grad_ext_x, grad_conv_w, grad_conv_b = conv_x_pull(grad_conv_x)
    _, conv_bc_pull = jax.vjp(conv_x_fn, ext_state, conv_state, conv_state_bias)
    grad_ext_state, grad_state_w, grad_state_b = conv_bc_pull(grad_conv_bc)
    back_x, back_state = (
        from_behind(grad_ext_x[:, :edge_rows].astype(jnp.bfloat16), "dp", -1).astype(jnp.float32),
        from_behind(grad_ext_state[:, :edge_rows].astype(jnp.bfloat16), "dp", -1).astype(
            jnp.float32
        ),
    )
    tail_pad = ((0, 0), (span_rows - edge_rows, 0), (0, 0))
    grad_mixer_x = grad_ext_x[:, edge_rows:] + jnp.pad(back_x, tail_pad)
    grad_state_pre = grad_ext_state[:, edge_rows:] + jnp.pad(back_state, tail_pad)
    mixed_gradient = jnp.stack([grad_gate_z, grad_mixer_x], 2).astype(jnp.bfloat16)
    state_reduced_gradient = grad_state_pre.astype(jnp.bfloat16)
    grad_in = jnp.concatenate(
        [
            query_projected_gradient,
            keyvalue_reduced_gradient,
            jnp.pad(step_reduced_gradient, ((0, 0), (0, 0), (0, LANES - mixer_local))),
            grad_mixer_x.astype(jnp.bfloat16),
            state_reduced_gradient,
            grad_gate_z.astype(jnp.bfloat16),
        ],
        -1,
    ).reshape(tokens, -1)

    def row(array):
        return jnp.pad(array, ((0, 0), (0, model_width - array.shape[1])))

    def lanes(array):
        return jnp.pad(array[None, :], ((0, 0), (0, LANES - array.shape[0])))

    small = jnp.concatenate(
        [
            jnp.zeros((1, model_width), jnp.float32),
            ffn_gain_part,
            row(grad_state_w),
            row(grad_state_b[None, :]),
            jnp.zeros((1, model_width), jnp.float32),
            row(grad_conv_w),
            row(grad_conv_b[None, :]),
            row(grad_mixer_gain[None, :]),
            row(jnp.concatenate([lanes(grad_step_bias), lanes(grad_decay_log), lanes(grad_skip)], 1)),
            jnp.zeros((1, model_width), jnp.float32),
        ],
        0,
    )
    resid_grad, weight_grads, sums, replicated = leave(
        shard_count,
        tensor_count,
        layout,
        (layout["in"], layout["out"], layout["gu"], layout["down"]),
        resid_in,
        grad_hidden,
        input_gain[None, :],
        w_all,
        span_normed_input,
        grad_in,
        grad_branch,
        branch_low,
        span_feedforward,
        grad_gate_up,
        span_gradient,
        activated,
        small,
    )
    out_grads = columns_of(weight_grads, "out").T
    kv_width = 2 * head_dim
    return (
        block_out,
        resid_grad,
        sums[0],
        sums[1],
        columns_of(weight_grads, "q"),
        replicated[:, : 2 * kv_width].reshape(depth, 2, kv_width),
        out_grads[:query_width],
        jnp.stack([columns_of(weight_grads, "z"), columns_of(weight_grads, "x")], 1),
        replicated[:, 2 * kv_width :],
        columns_of(weight_grads, "step")[:, :mixer_local],
        sums[8:12, :mixer_width],
        sums[12, :mixer_width],
        sums[2:6, : 2 * state_dim],
        sums[6, : 2 * state_dim],
        sums[14, :mixer_local],
        sums[14, LANES : LANES + mixer_local],
        sums[14, 2 * LANES : 2 * LANES + mixer_local],
        sums[13, :mixer_width],
        out_grads[query_width:],
        columns_of(weight_grads, "gu").reshape(depth, 2, ff),
        columns_of(weight_grads, "down").T,
    )


def solution(mesh):
    placed = (
        P(None, ("dp", "tensor"), None),
        P(),
        P(None, ("dp", "tensor"), None),
        P(),
        P(),
        P("dp", "tensor"),
        P("dp", None, None),
        P("tensor", "dp"),
        P("dp", None, "tensor"),
        P("dp", None),
        P("dp", "tensor"),
        P(None, "tensor"),
        P("tensor"),
        P(),
        P(),
        P("tensor"),
        P("tensor"),
        P("tensor"),
        P("tensor"),
        P("tensor", "dp"),
        P("dp", None, "tensor"),
        P("tensor", "dp"),
    )
    return jax.shard_map(
        body,
        mesh=mesh,
        in_specs=placed,
        out_specs=(
            P(None, ("dp", "tensor"), None),
            P(None, ("dp", "tensor"), None),
            P(),
            P(),
            P("dp", "tensor"),
            P("dp", None, None),
            P("tensor", "dp"),
            P("dp", None, "tensor"),
            P("dp", None),
            P("dp", "tensor"),
            P(None, "tensor"),
            P("tensor"),
            P(),
            P(),
            P("tensor"),
            P("tensor"),
            P("tensor"),
            P("tensor"),
            P("tensor", "dp"),
            P("dp", None, "tensor"),
            P("tensor", "dp"),
        ),
        check_vma=False,
    )
```

```python
from functools import partial
import math

import jax
import jax.numpy as jnp
import numpy as np
from jax import lax
from jax.experimental import pallas as pl
from jax.experimental.pallas import tpu as pltpu
from jax.sharding import PartitionSpec as P

KVH = 2
EPSILON = 1e-05
ROTARY_BASE = 100000000000.0
MASKED = -1e30
MATMUL_EXACTNESS = lax.Precision.HIGHEST
LANES = 128
F32 = jnp.float32
BF16 = jnp.bfloat16
VMEM_BYTES = 62 * 2**20


def dot_nn(a, b):
    return lax.dot_general(a, b, (((1,), (0,)), ((), ())), preferred_element_type=F32)


def dot_nt(a, b):
    return lax.dot_general(a, b, (((1,), (1,)), ((), ())), preferred_element_type=F32)


def dot_tn(a, b):
    return lax.dot_general(a, b, (((0,), (0,)), ((), ())), preferred_element_type=F32)


def remote(src, dst, send_sem, recv_sem, where):
    return pltpu.make_async_remote_copy(
        src_ref=src,
        dst_ref=dst,
        send_sem=send_sem,
        recv_sem=recv_sem,
        device_id=where,
        device_id_type=pl.DeviceIdType.MESH,
    )


class Place:
    def __init__(self, devices):
        self.devices = devices
        self.lines = devices // 2
        self.dp = lax.axis_index("dp")
        self.t = lax.axis_index("tensor")
        self.z = lax.div(self.dp, 2)
        self.p = lax.rem(self.dp, 2)
        self.pair = self.dp + 1 - 2 * self.p
        self.t_near = self.t + 1 - 2 * lax.rem(self.t, 2)
        self.t_far = lax.rem(self.t + 2, 4)
        self.t_both = lax.rem(self.t_near + 2, 4)
        self.first = self.z == 0
        self.last = self.z == self.lines - 1

    def flips(self):
        bit = 1
        while bit < self.devices:
            yield self.dp + bit - 2 * bit * lax.rem(lax.div(self.dp, bit), 2)
            bit *= 2

    def greet(self, line=False, tensor=False, flips=False):
        barrier = pltpu.get_barrier_semaphore()
        count = 0

        def signal(**where):
            pl.semaphore_signal(
                barrier, inc=1, device_id=where, device_id_type=pl.DeviceIdType.MESH
            )

        if tensor:
            signal(tensor=self.t_near)
            signal(tensor=self.t_far)
            count = count + 2
        if line:
            signal(dp=self.pair)
            count = count + 1

            @pl.when(jnp.logical_not(self.first))
            def _():
                signal(dp=self.dp - 2)

            @pl.when(jnp.logical_not(self.last))
            def _():
                signal(dp=self.dp + 2)

        if flips:
            for other in self.flips():
                signal(dp=other)
                count = count + 1
        if line:
            count = count + 2
            count = count - self.first.astype(jnp.int32) - self.last.astype(jnp.int32)
        pl.semaphore_wait(barrier, count)


class LineGather:
    def __init__(self, place, view, recv, right, left, pair):
        self.at, self.view = place, view
        self.recv, self.right, self.left, self.side = recv, right, left, pair

    def copy(self, block, sem, where):
        ref = self.view(block)
        return remote(ref, ref, sem, self.recv.at[block], where)

    def send_right(self, zz):
        return self.copy(zz * 2 + self.at.p, self.right.at[zz], {"dp": self.at.dp + 2})

    def send_left(self, zz):
        return self.copy(zz * 2 + self.at.p, self.left.at[zz], {"dp": self.at.dp - 2})

    def send_pair(self, zz):
        return self.copy(zz * 2 + self.at.p, self.side.at[zz], {"dp": self.at.pair})

    def arrived(self, block):
        self.copy(block, self.side.at[0], {"dp": self.at.pair}).wait_recv()

    def start(self):
        at = self.at
        pl.when(jnp.logical_not(at.last))(lambda: self.send_right(at.z).start())
        pl.when(jnp.logical_not(at.first))(lambda: self.send_left(at.z).start())
        self.send_pair(at.z).start()

    def step(self, s):
        at = self.at
        low, high = at.z - 1 - s, at.z + 1 + s

        @pl.when(low >= 0)
        def _():
            self.arrived(low * 2 + at.p)
            pl.when(jnp.logical_not(at.last))(lambda: self.send_right(low).start())
            self.send_pair(low).start()

        @pl.when(high < at.lines)
        def _():
            self.arrived(high * 2 + at.p)
            pl.when(jnp.logical_not(at.first))(lambda: self.send_left(high).start())
            self.send_pair(high).start()

    def finish(self):
        at = self.at

        @pl.loop(0, at.lines)
        def _(zz):
            self.arrived(zz * 2 + 1 - at.p)

    def drain(self):
        at = self.at

        @pl.loop(0, at.lines)
        def _(zz):
            self.send_pair(zz).wait_send()

            @pl.when(jnp.logical_and(zz <= at.z, jnp.logical_not(at.last)))
            def _():
                self.send_right(zz).wait_send()

            @pl.when(jnp.logical_and(zz >= at.z, jnp.logical_not(at.first)))
            def _():
                self.send_left(zz).wait_send()


class LineScatter:
    def __init__(self, place, part, got, right, left, sems, causal=False):
        self.at, self.part = place, part
        self.got, self.right, self.left = got, right, left
        self.causal = causal
        (
            self.pair_send,
            self.pair_recv,
            self.right_send,
            self.right_recv,
            self.left_send,
            self.left_recv,
        ) = sems

    def pair_copy(self, zz):
        src = self.part(zz * 2 + 1 - self.at.p)
        return remote(
            src, self.got(zz), self.pair_send.at[zz], self.pair_recv.at[zz], {"dp": self.at.pair}
        )

    def right_copy(self, zz):
        src = self.part(zz * 2 + self.at.p)
        return remote(
            src,
            self.right(zz),
            self.right_send.at[zz],
            self.right_recv.at[zz],
            {"dp": self.at.dp + 2},
        )

    def left_copy(self, zz):
        src = self.part(zz * 2 + self.at.p)
        return remote(
            src, self.left(zz), self.left_send.at[zz], self.left_recv.at[zz], {"dp": self.at.dp - 2}
        )

    def start(self):
        at = self.at

        @pl.loop(0, at.z + 1 if self.causal else at.lines)
        def _(i):
            self.pair_copy(i if self.causal else at.lines - 1 - i).start()

    def add_into(self, ref, *others):
        total = ref[...].astype(F32)
        for other in others:
            total = total + other[...].astype(F32)
        ref[...] = total.astype(BF16)

    def step(self, i):
        at = self.at
        high, low = at.lines - 1 - i, i
        if self.causal:
            self.step_low(low)
            return

        @pl.when(at.z < at.lines // 2)
        def _():
            self.step_high(high)
            self.step_low(low)

        @pl.when(at.z >= at.lines // 2)
        def _():
            self.step_low(low)
            self.step_high(high)

    def step_high(self, high):
        at = self.at

        @pl.when(high > at.z)
        def _():
            self.pair_copy(high).wait_recv()
            ref = self.part(high * 2 + at.p)

            @pl.when(at.first)
            def _():
                self.add_into(ref, self.got(high))

            @pl.when(jnp.logical_not(at.first))
            def _():
                self.right_copy(high).wait_recv()
                self.add_into(ref, self.got(high), self.right(high))

            self.right_copy(high).start()

    def step_low(self, low):
        at = self.at

        @pl.when(low < at.z)
        def _():
            self.pair_copy(low).wait_recv()
            ref = self.part(low * 2 + at.p)

            @pl.when(at.last)
            def _():
                self.add_into(ref, self.got(low))

            @pl.when(jnp.logical_not(at.last))
            def _():
                self.left_copy(low).wait_recv()
                self.add_into(ref, self.got(low), self.left(low))

            self.left_copy(low).start()

    def finish(self, out):
        at = self.at
        self.pair_copy(at.z).wait_recv()
        out[...] = self.part(at.dp)[...].astype(F32) + self.got(at.z)[...].astype(F32)

        if not self.causal:

            @pl.when(jnp.logical_not(at.first))
            def _():
                self.right_copy(at.z).wait_recv()
                out[...] += self.right(at.z)[...].astype(F32)

        @pl.when(jnp.logical_not(at.last))
        def _():
            self.left_copy(at.z).wait_recv()
            out[...] += self.left(at.z)[...].astype(F32)

    def drain(self):
        at = self.at

        @pl.loop(0, at.z + 1 if self.causal else at.lines)
        def _(zz):
            self.pair_copy(zz).wait_send()
            if not self.causal:
                pl.when(zz > at.z)(lambda: self.right_copy(zz).wait_send())
            pl.when(zz < at.z)(lambda: self.left_copy(zz).wait_send())

    def run_causal(self, out):
        @pl.loop(0, self.at.lines - 1)
        def _(s):
            self.step(s)

        self.finish(out)


class RowGather:
    def __init__(self, place, view, send, recv):
        self.at, self.view, self.send, self.recv = place, view, send, recv

    def copy(self, rank, chunk, sem, near):
        ref = self.view(rank, chunk)
        where = {"tensor": self.at.t_near if near else self.at.t_far}
        return remote(ref, ref, self.send.at[chunk, sem], self.recv.at[chunk, rank], where)

    def start(self, chunk):
        self.copy(self.at.t, chunk, 0, False).start()
        self.copy(self.at.t, chunk, 1, True).start()

    def forward(self, chunk):
        self.copy(self.at.t_far, chunk, 2, False).wait_recv()
        self.copy(self.at.t_far, chunk, 2, True).start()

    def finish(self, chunk):
        self.copy(self.at.t_near, chunk, 1, True).wait_recv()
        self.copy(self.at.t_both, chunk, 2, True).wait_recv()

    def drain(self, chunk):
        self.copy(self.at.t, chunk, 0, False).wait_send()
        self.copy(self.at.t, chunk, 1, True).wait_send()
        self.copy(self.at.t_far, chunk, 2, True).wait_send()


class RowScatter:
    def __init__(self, place, view, near_buf, far_buf, send, recv):
        self.at, self.view = place, view
        self.near_buf, self.far_buf = near_buf, far_buf
        self.send, self.recv = send, recv

    def near_copy(self, chunk, which):
        rank = self.at.t_both if which else self.at.t_near
        return remote(
            self.view(rank, chunk),
            self.near_buf(which, chunk),
            self.send.at[chunk, which],
            self.recv.at[chunk, which],
            {"tensor": self.at.t_near},
        )

    def far_copy(self, chunk):
        return remote(
            self.view(self.at.t_far, chunk),
            self.far_buf(chunk),
            self.send.at[chunk, 2],
            self.recv.at[chunk, 2],
            {"tensor": self.at.t_far},
        )

    def start(self, chunk):
        self.near_copy(chunk, 1).start()
        self.near_copy(chunk, 0).start()

    def middle(self, chunk):
        self.near_copy(chunk, 1).wait_recv()
        ref = self.view(self.at.t_far, chunk)
        ref[...] = (ref[...].astype(F32) + self.near_buf(1, chunk)[...].astype(F32)).astype(BF16)
        self.far_copy(chunk).start()

    def finish(self, chunk):
        self.near_copy(chunk, 0).wait_recv()
        total = self.view(self.at.t, chunk)[...].astype(F32) + self.near_buf(0, chunk)[
            ...
        ].astype(F32)
        self.far_copy(chunk).wait_recv()
        return total + self.far_buf(chunk)[...].astype(F32)

    def drain(self, chunk):
        self.near_copy(chunk, 0).wait_send()
        self.near_copy(chunk, 1).wait_send()
        self.far_copy(chunk).wait_send()


def line_gather_sems(devices):
    dma = pltpu.SemaphoreType.DMA
    return [dma((devices,)), dma((devices // 2,)), dma((devices // 2,)), dma((devices // 2,))]


def line_scatter_sems(devices):
    return [pltpu.SemaphoreType.DMA((devices // 2,)) for _ in range(6)]


def rms_rows(values, gain):
    return values * lax.rsqrt(jnp.mean(values * values, -1, keepdims=True) + EPSILON) * gain


def rms_rows_grad(values, gain, grad):
    scale = lax.rsqrt(jnp.mean(values * values, -1, keepdims=True) + EPSILON)
    term = grad * gain
    inner = jnp.mean(values * term, -1, keepdims=True)
    return scale * (term - values * (scale * scale * inner)), grad * values * scale


def ffn_kernel(devices, layout, *refs):
    (
        x_ref, a_ref, og_ref, ogl_ref, gain_ref, w_ref,
        out_ref, gh_ref, gb, nf, act, dgu, gain_grad,
        part, part2, near1, far1, near2, far2, near3, far3, hid,
        send, recv,
    ) = refs
    at = Place(devices)
    seqs, sub, width = x_ref.shape
    span = sub * 4
    half = seqs // 2
    rows = half * span
    out_w, gu_w, dn_w = (pl.ds(*layout[k]) for k in ("out", "gu", "down"))
    ff = layout["down"][1]
    at.greet(tensor=True)

    def rows_of(buf):
        def view(rank, chunk):
            return buf.at[pl.ds(chunk * half, half), pl.ds(pl.multiple_of(rank * sub, sub), sub), :]

        return view

    def parts_of(buf):
        return lambda which, chunk: buf.at[which, pl.ds(chunk * half, half)]

    def part_of(buf):
        return lambda chunk: buf.at[pl.ds(chunk * half, half)]

    branch = RowScatter(at, rows_of(part), parts_of(near1), part_of(far1), send.at[0], recv.at[0])
    ffn = RowScatter(at, rows_of(part2), parts_of(near2), part_of(far2), send.at[1], recv.at[1])
    back = RowScatter(at, rows_of(part), parts_of(near3), part_of(far3), send.at[2], recv.at[2])
    row_nf = RowGather(at, rows_of(nf), send.at[3], recv.at[3])
    row_gb = RowGather(at, rows_of(gb), send.at[4], recv.at[4])
    mine = pl.ds(pl.multiple_of(at.t * sub, sub), sub)
    gain = gain_ref[...]

    def seq_rows(chunk):
        return pl.ds(chunk * half, half)

    def tok_rows(chunk):
        return pl.ds(chunk * rows, rows)

    for c in range(2):
        value = dot_nt(a_ref[tok_rows(c), :], w_ref[:, out_w])
        part[seq_rows(c)] = value.astype(BF16).reshape(half, span, width)
        branch.start(c)
    for c in range(2):
        branch.middle(c)
    for c in range(2):
        hidden = x_ref[seq_rows(c)].astype(F32) + branch.finish(c)
        hid[seq_rows(c)] = hidden
        nf[seq_rows(c), mine, :] = rms_rows(hidden, gain).astype(BF16)
        row_nf.start(c)
    for c in range(2):
        row_nf.forward(c)
    for c in range(2):
        row_nf.finish(c)
        branch.drain(c)
        flat = nf[seq_rows(c)].reshape(rows, width)
        flat_og = og_ref[seq_rows(c)].reshape(rows, width)
        gate_up = dot_nn(flat, w_ref[:, gu_w])
        gate, up = gate_up[:, :ff], gate_up[:, ff:]
        sigmoid = jax.nn.sigmoid(gate)
        grad_act = dot_nn(flat_og, w_ref[:, dn_w])
        act[tok_rows(c), :] = (gate * sigmoid * up).astype(BF16)
        dgu[tok_rows(c), :ff] = (
            grad_act * up * sigmoid * (1.0 + gate * (1.0 - sigmoid))
        ).astype(BF16)
        dgu[tok_rows(c), ff:] = (grad_act * gate * sigmoid).astype(BF16)
        value = dot_nt(dgu[tok_rows(c), :], w_ref[:, gu_w])
        part[seq_rows(c)] = value.astype(BF16).reshape(half, span, width)
        back.start(c)
    for c in range(2):
        back.middle(c)
        value = dot_nt(act[tok_rows(c), :], w_ref[:, dn_w])
        part2[seq_rows(c)] = value.astype(BF16).reshape(half, span, width)
    total = jnp.zeros((1, width), F32)
    for c in range(2):
        grad_hidden, terms = rms_rows_grad(hid[seq_rows(c)], gain, back.finish(c))
        total = total + jnp.sum(terms.reshape(half * sub, width), 0, keepdims=True)
        grad_hidden = grad_hidden + ogl_ref[seq_rows(c)].astype(F32)
        gh_ref[seq_rows(c)] = grad_hidden
        gb[seq_rows(c), mine, :] = grad_hidden.astype(BF16)
        row_gb.start(c)
        ffn.start(c)
    gain_grad[...] = total
    for c in range(2):
        row_gb.forward(c)
        ffn.middle(c)
    for c in range(2):
        out_ref[seq_rows(c)] = (hid[seq_rows(c)] + ffn.finish(c)).astype(BF16)
        row_gb.finish(c)
    for c in range(2):
        row_nf.drain(c)
        row_gb.drain(c)
        back.drain(c)
        ffn.drain(c)


def feed_forward(devices, tensor, layout, x, a, og, out_grad, gain, w_all):
    seqs, sub, width = x.shape
    span = sub * tensor
    tokens = seqs * span
    ff = layout["down"][1]
    shape = jax.ShapeDtypeStruct
    vmem = pl.BlockSpec(memory_space=pltpu.VMEM)
    dma = pltpu.SemaphoreType.DMA
    whole, own = (seqs, span, width), (seqs, sub, width)
    return pl.pallas_call(
        partial(ffn_kernel, devices, layout),
        out_shape=(
            shape(own, BF16),
            shape(own, F32),
            shape(whole, BF16),
            shape(whole, BF16),
            shape((tokens, ff), BF16),
            shape((tokens, 2 * ff), BF16),
            shape((1, width), F32),
        ),
        in_specs=[vmem] * 6,
        out_specs=(vmem,) * 7,
        scratch_shapes=[
            pltpu.VMEM(whole, BF16),
            pltpu.VMEM(whole, BF16),
        ]
        + [pltpu.VMEM((2,) + own, BF16), pltpu.VMEM(own, BF16)] * 3
        + [
            pltpu.VMEM(own, F32),
            dma((5, 2, 3)),
            dma((5, 2, 4)),
        ],
        compiler_params=pltpu.CompilerParams(
            collective_id=1, has_side_effects=True, vmem_limit_bytes=VMEM_BYTES
        ),
        name="feed_forward",
    )(x, a, og, out_grad, gain, w_all)


def to_row(column):
    size = column.shape[0]
    eye = iota((size, size), 0) == iota((size, size), 1)
    return jnp.sum(jnp.where(eye, column, 0.0), 0, keepdims=True)


def to_column(row):
    size = row.shape[1]
    eye = iota((size, size), 0) == iota((size, size), 1)
    return jnp.sum(jnp.where(eye, row, 0.0), 1, keepdims=True)


def iota(shape, dim):
    return lax.broadcasted_iota(jnp.int32, shape, dim)


def spread(columns, heads, head_dim):
    rows = columns.shape[0]
    lane = iota((rows, LANES), 1)
    blocks = []
    for first in range(0, heads, LANES // head_dim):
        block = jnp.broadcast_to(columns[:, first : first + 1], (rows, LANES))
        for k in range(1, LANES // head_dim):
            block = jnp.where(lane >= k * head_dim, columns[:, first + k : first + k + 1], block)
        blocks.append(block)
    return jnp.concatenate(blocks, 1)


def head_sums(values, heads, head_dim):
    rows = values.shape[0]
    lane = iota((rows, LANES), 1)
    out = jnp.zeros((rows, LANES), F32)
    per = LANES // head_dim
    for h in range(heads):
        block = values[:, h // per * LANES : (h // per + 1) * LANES]
        inside = jnp.logical_and(lane >= h % per * head_dim, lane < (h % per + 1) * head_dim)
        total = jnp.sum(jnp.where(inside, block, 0.0), 1, keepdims=True)
        out = jnp.where(lane == h, total, out)
    return out


def pick_halves(blocks, head_dim):
    lane = iota(blocks[0].shape, 1)
    per = LANES // head_dim
    out = []
    for first in range(0, len(blocks), per):
        block = blocks[first]
        for k in range(1, per):
            block = jnp.where(lane >= k * head_dim, blocks[first + k], block)
        out.append(block)
    return jnp.concatenate(out, 1)


def softplus(value):
    return jnp.maximum(value, 0.0) + jnp.log1p(jnp.exp(-jnp.abs(value)))


def running_sum(values, backward=False):
    rows = values.shape[0]
    row = iota(values.shape, 0)
    step = 1
    while step < rows:
        if backward:
            moved = jnp.where(row < rows - step, pltpu.roll(values, rows - step, 0), 0.0)
        else:
            moved = jnp.where(row >= step, pltpu.roll(values, step, 0), 0.0)
        values = values + moved
        step *= 2
    return values


def turn(values, cosine, sine, half):
    lane = iota(values.shape, 1)
    first = lax.rem(lane, 2 * half) < half
    swapped = jnp.where(
        first, pltpu.roll(values, LANES - half, 1), pltpu.roll(values, half, 1)
    )
    return values * cosine + swapped * sine


def decay_parts(step_pre, decay_log, bias):
    step = softplus(step_pre + bias)
    rate = -jnp.exp(decay_log)
    return step, rate, running_sum(step * rate)


def same_document(aux, row):
    span = aux.shape[0]
    same = aux[:, 5:6] == row
    causal = iota((span, span), 0) >= iota((span, span), 1)
    return jnp.where(jnp.logical_and(same, causal), 0.0, MASKED)


class Neighbours:
    def __init__(self, at):
        self.at = at

    def greet(self, flips=False):
        at = self.at
        barrier = pltpu.get_barrier_semaphore()
        end = at.devices - 1

        def signal(**where):
            pl.semaphore_signal(
                barrier, inc=1, device_id=where, device_id_type=pl.DeviceIdType.MESH
            )

        for other in (at.t_near, at.t_far, at.t_both):
            signal(tensor=other)
        signal(dp=at.pair)
        count = 4
        for step in (1, 2):
            low, high = at.dp >= step, at.dp + step <= end
            pl.when(low)(partial(signal, dp=at.dp - step))
            pl.when(high)(partial(signal, dp=at.dp + step))
            count = count + low.astype(jnp.int32) + high.astype(jnp.int32)
        if flips:
            for other in at.flips():
                signal(dp=other)
                count = count + 1
        pl.semaphore_wait(barrier, count)


class TensorTotal:
    def __init__(self, at, own, got, send, recv):
        self.at, self.own, self.got, self.send, self.recv = at, own, got, send, recv

    def copies(self):
        others = (self.at.t_near, self.at.t_far, self.at.t_both)
        return [
            remote(
                self.own, self.got.at[i], self.send.at[i], self.recv.at[i], {"tensor": other}
            )
            for i, other in enumerate(others)
        ]

    def start(self):
        for copy in self.copies():
            copy.start()

    def finish(self):
        for copy in self.copies():
            copy.wait()
        return self.own[...] + self.got[0] + self.got[1] + self.got[2]


class StatePass:
    def __init__(self, at, local, pair_in, chain_in, chain_out, share, result, sems, backward):
        self.at, self.local, self.pair_in = at, local, pair_in
        self.chain_in, self.chain_out, self.share, self.result = chain_in, chain_out, share, result
        self.backward = backward
        self.pair_send, self.pair_recv, self.chain_send, self.chain_recv = sems[:4]
        self.share_send, self.share_recv = sems[4:]
        self.half = local.shape[0] // 2
        self.size = result.shape[1]
        self.head = at.last if backward else at.first
        self.tail = at.first if backward else at.last
        self.onward = at.dp - 2 if backward else at.dp + 2

    def pair_copy(self):
        src = self.local.at[pl.ds((1 - self.at.p) * self.half, self.half)]
        return remote(
            src, self.pair_in, self.pair_send.at[0], self.pair_recv.at[0], {"dp": self.at.pair}
        )

    def chain_copy(self, i):
        return remote(
            self.chain_out.at[i],
            self.chain_in.at[i],
            self.chain_send.at[i],
            self.chain_recv.at[i],
            {"dp": self.onward},
        )

    def share_copy(self, i):
        return remote(
            self.share.at[i],
            self.result.at[self.at.p * self.half + i],
            self.share_send.at[i],
            self.share_recv.at[i],
            {"dp": self.at.pair},
        )

    def start(self):
        self.pair_copy().start()

    def run(self):
        at, size = self.at, self.size
        sooner = at.p == (1 if self.backward else 0)
        self.pair_copy().wait_recv()
        for i in range(self.half):
            mine = self.local[at.p * self.half + i].astype(F32)
            other = self.pair_in[i].astype(F32)
            one = jnp.where(sooner, mine, other)
            two = jnp.where(sooner, other, mine)
            state1, keep1 = one[:size], one[size : size + 1]
            state2, keep2 = two[:size], two[size : size + 1]

            @pl.when(self.head)
            def _():
                self.chain_in[i] = jnp.zeros(self.chain_in.shape[1:], BF16)

            @pl.when(jnp.logical_not(self.head))
            def _():
                self.chain_copy(i).wait_recv()

            before = self.chain_in[i].astype(F32)
            middle = keep1 * before + state1

            @pl.when(jnp.logical_not(self.tail))
            def _():
                self.chain_out[i] = (keep2 * middle + state2).astype(BF16)
                self.chain_copy(i).start()

            self.result[at.p * self.half + i] = jnp.where(sooner, before, middle).astype(BF16)
            self.share[i] = jnp.where(sooner, middle, before).astype(BF16)
            self.share_copy(i).start()

    def finish(self):
        at = self.at
        for i in range(self.half):
            remote(
                self.share.at[i],
                self.result.at[(1 - at.p) * self.half + i],
                self.share_send.at[i],
                self.share_recv.at[i],
                {"dp": at.pair},
            ).wait_recv()
            self.share_copy(i).wait_send()
            pl.when(jnp.logical_not(self.tail))(lambda: self.chain_copy(i).wait_send())
        self.pair_copy().wait_send()


def state_pass_scratch(half, size, width):
    dma = pltpu.SemaphoreType.DMA
    return [
        pltpu.VMEM((half, size + 16, width), BF16),
        pltpu.VMEM((half, size, width), BF16),
        pltpu.VMEM((half, size, width), BF16),
        pltpu.VMEM((half, size, width), BF16),
        dma((1,)),
        dma((1,)),
        dma((half,)),
        dma((half,)),
        dma((half,)),
        dma((half,)),
    ]


def mixer_kernel(cfg, *refs):
    (
        x_ref, og_in, gain_ref, w_in, ao_in, mo_in, dn_in, aux_ref, seg_ref, all_ref, rope_ref, taps_ref,
        tap_bias, step_bias, decay_log, skip_ref, mgain_ref,
        w_all, nx, og, low, kv, q2, probs, att, ext, pre, step_buf, entering, carry, y_buf, z_buf,
        squares,
        local, xs_buf, row_send, row_recv, kv_sems, halo_sems, sq_own, sq_got, sq_send, sq_recv,
        *rest,
    ) = refs
    devices, layout, pieces, heads = (cfg[k] for k in ("devices", "layout", "pieces", "heads"))
    at = Place(devices)
    seqs, sub, width = x_ref.shape
    span = sub * 4
    tokens = seqs * span
    depth = w_in.shape[0]
    xw = layout["x"][1]
    head_dim = xw // heads
    sw = layout["state"][1]
    size = sw // 2
    mixed = xw + sw
    qw = layout["q"][1]
    at_dim = qw // 2
    pass_refs, sems = rest[:10], rest[10:]
    own_rows = pl.ds(pl.multiple_of(at.dp * depth, depth), depth)
    Neighbours(at).greet()
    first_w = w_in.shape[1] - layout["gu"][1]
    w_all[own_rows, pl.ds(0, first_w)] = w_in[:, :first_w]
    w_all[own_rows, pl.ds(*layout["gu"])] = w_in[:, first_w:]
    gathers = []
    for i, (first, count) in enumerate(pieces):

        def view(block, first=first, count=count):
            return w_all.at[
                pl.ds(pl.multiple_of(block * depth, depth), depth), pl.ds(first, count)
            ]

        gathers.append(LineGather(at, view, *sems[4 * i : 4 * i + 4]))

    def steps(i, *which):
        for s in which:
            if s < at.lines - 1:
                gathers[i].step(s)
        if which[-1] == 2:
            pl.loop(3, max(at.lines - 1, 3))(lambda s: gathers[i].step(s))
            gathers[i].finish()

    gathers[0].start()
    gain = gain_ref[...]
    mine = pl.ds(pl.multiple_of(at.t * sub, sub), sub)
    for s in range(seqs):
        nx[s, mine, :] = rms_rows(x_ref[s].astype(F32), gain).astype(BF16)
        og[s, mine, :] = og_in[s]
    half = seqs // 2

    def rows_of(buf):
        def view(rank, chunk):
            return buf.at[pl.ds(chunk * half, half), pl.ds(pl.multiple_of(rank * sub, sub), sub), :]

        return view

    row_nx = RowGather(at, rows_of(nx), row_send.at[0], row_recv.at[0])
    row_og = RowGather(at, rows_of(og), row_send.at[1], row_recv.at[1])
    for chunk in range(2):
        row_nx.start(chunk)
    gathers[1].start()
    out_at, dn_at = layout["out"][0], layout["down"][0]
    w_all[own_rows, pl.ds(out_at, qw)] = ao_in[...].T
    w_all[own_rows, pl.ds(out_at + qw, xw)] = mo_in[...].T
    w_all[own_rows, pl.ds(*layout["down"])] = dn_in[...].T
    for chunk in range(2):
        row_nx.forward(chunk)
    for chunk in range(2):
        row_nx.finish(chunk)
    steps(0, 0, 1, 2)
    rows = nx[...].reshape(tokens, width)

    def project(name):
        first, count = layout[name]
        return dot_nn(rows, w_all[:, pl.ds(first, count)])

    value = project("x").astype(BF16).astype(F32)
    ext[:, pl.ds(8, span), pl.ds(0, xw)] = value.reshape(seqs, span, xw)
    value = project("state").astype(BF16).astype(F32)
    ext[:, pl.ds(8, span), pl.ds(xw, sw)] = value.reshape(seqs, span, sw)
    before, after = at.dp > 0, at.dp < devices - 1

    def halo():
        return remote(
            ext.at[:, pl.ds(span, 8), :],
            ext.at[:, pl.ds(0, 8), :],
            halo_sems.at[0],
            halo_sems.at[1],
            {"dp": at.dp + 1},
        )

    pl.when(after)(lambda: halo().start())
    step_buf[...] = project("step").reshape(seqs, span, LANES)
    steps(1, 0)
    for chunk in range(2):
        row_og.start(chunk)
    pl.when(before)(lambda: halo().wait_recv())

    @pl.when(jnp.logical_not(before))
    def _():
        ext[:, pl.ds(0, 8), :] = jnp.zeros((seqs, 8, mixed), F32)

    def scan_parts(s):
        return decay_parts(step_buf[s], decay_log[...], step_bias[...])

    @pl.loop(0, seqs)
    def _(s):
        aux = aux_ref[s]
        total = tap_bias[...] + taps_ref[3:4, :] * ext[s, pl.ds(8, span), :]
        for back in (1, 2, 3):
            moved = ext[s, pl.ds(8 - back, span), :] * aux[:, back - 1 : back]
            total = total + taps_ref[3 - back : 4 - back, :] * moved
        pre[s] = total
        active = total * jax.nn.sigmoid(total)
        step, _, running = scan_parts(s)
        scaled = active[:, :xw] * spread(step, heads, head_dim)
        xs_buf[s] = scaled.astype(BF16)
        end = running[span - 1 : span, :]
        tail = spread(jnp.exp(end - running) * aux[:, 4:5], heads, head_dim)
        state_in = active[:, xw : xw + size].astype(BF16)
        local[s, :size, :] = dot_tn(state_in, (scaled * tail).astype(BF16)).astype(BF16)
        keep = jnp.broadcast_to(jnp.exp(end) * aux[span - 1 : span, 3:4], (16, LANES))
        keep = spread(keep, heads, head_dim).astype(BF16)
        local[s, size : size + 16, :] = keep
        carry[s] = keep

    passing = StatePass(
        at, local, pass_refs[0], pass_refs[1], pass_refs[2], pass_refs[3], entering,
        pass_refs[4:], False,
    )
    passing.start()
    gathers[2].start()
    steps(1, 1, 2)
    lane = iota((span, LANES), 1)
    cosine, sine = rope_ref[:, :LANES], rope_ref[:, LANES:]
    queries = project("q").reshape(seqs, span, qw)
    pairs = project("kv").reshape(seqs, span, qw)
    key_cosine = jnp.where(lane < at_dim, cosine, 1.0)
    key_sine = jnp.where(lane < at_dim, sine, 0.0)
    scale = 1.0 / math.sqrt(at_dim)
    for s in range(seqs):
        kv[at.dp, s] = turn(pairs[s], key_cosine, key_sine, at_dim // 2).astype(BF16)
    kv_gather = LineGather(
        at, lambda block: kv.at[block], *(kv_sems.at[i] for i in range(3)), kv_sems.at[3]
    )
    kv_gather.start()
    for s in range(seqs):
        turned = turn(queries[s], cosine, sine, at_dim // 2) * scale
        q2[s, :span, :] = jnp.where(lane < at_dim, turned, 0.0).astype(BF16)
        turned = pltpu.roll(turned, at_dim, 1)
        q2[s, span:, :] = jnp.where(lane < at_dim, turned, 0.0).astype(BF16)
    z_buf[...] = project("z").astype(BF16).reshape(seqs, span, xw)
    passing.run()
    for s in range(2):
        if s < at.lines - 1:
            kv_gather.step(s)

    @pl.loop(0, seqs)
    def _(s):
        aux = aux_ref[s]
        active = pre[s] * jax.nn.sigmoid(pre[s])
        _, _, running = scan_parts(s)
        running_rows = running.T
        allowed = same_document(aux, seg_ref[s])
        state_in = active[:, xw : xw + size].astype(BF16)
        state_out = active[:, xw + size :].astype(BF16)
        joined = dot_nt(state_out, state_in)
        blocks = []
        for h in range(heads):
            gap = running[:, h : h + 1] - running_rows[h : h + 1, :]
            weight = (joined * jnp.exp(gap + allowed)).astype(BF16)
            cols = pl.ds(h * head_dim // LANES * LANES, LANES)
            blocks.append(dot_nn(weight, xs_buf[s, :, cols]))
        y_buf[s] = pick_halves(blocks, head_dim) + skip_ref[...] * active[:, :xw]

    pl.loop(2, max(at.lines - 1, 2))(lambda s: kv_gather.step(s))
    kv_gather.finish()
    steps(2, 0, 1, 2)
    gathers[3].start()
    for chunk in range(2):
        row_og.forward(chunk)
    count = devices * span
    key_at = iota((span, count), 1)
    query_at = iota((span, count), 0) + at.dp * span

    @pl.loop(0, seqs)
    def _(s):
        keys = kv[:, s].reshape(count, qw)
        allowed = jnp.logical_and(aux_ref[s][:, 5:6] == all_ref[s], key_at <= query_at)
        bias = jnp.where(allowed, 0.0, MASKED)
        outs = []
        for h in range(2):
            part = pl.ds(h * span, span)
            scores = dot_nt(q2[s, part, :], keys) + bias
            power = jnp.exp(scores - jnp.max(scores, 1, keepdims=True))
            weight = power * (1.0 / jnp.sum(power, 1, keepdims=True))
            weight = weight.astype(BF16)
            probs[s, part, :] = weight
            outs.append(dot_nn(weight, keys))
        att[s] = jnp.where(lane < at_dim, pltpu.roll(outs[0], at_dim, 1), outs[1])

    low[:, pl.ds(0, qw)] = att[...].reshape(tokens, qw).astype(BF16)
    passing.finish()
    sq_own[...] = jnp.zeros(sq_own.shape, F32)
    for s in range(seqs):
        aux = aux_ref[s]
        state_out = (pre[s, :, pl.ds(xw + size, size)])
        state_out = (state_out * jax.nn.sigmoid(state_out)).astype(BF16)
        _, _, running = scan_parts(s)
        factor = spread(jnp.exp(running) * aux[:, 3:4], heads, head_dim)
        y = y_buf[s] + dot_nn(state_out, entering[s]) * factor
        y_buf[s] = y
        gate = z_buf[s].astype(F32)
        gated = y * gate * jax.nn.sigmoid(gate)
        sq_own[s : s + 1, :] = to_row(jnp.sum(gated * gated, 1, keepdims=True))
    total = TensorTotal(at, sq_own, sq_got, sq_send, sq_recv)
    total.start()
    steps(3, 0, 1)
    gathers[4].start()
    squares[...] = total.finish()
    for s in range(seqs):
        gate = z_buf[s].astype(F32)
        gated = y_buf[s] * gate * jax.nn.sigmoid(gate)
        norm = lax.rsqrt(to_column(squares[s : s + 1, :]) / (4 * xw) + EPSILON)
        low[pl.ds(s * span, span), pl.ds(qw, xw)] = (gated * norm * mgain_ref[...]).astype(BF16)
    for chunk in range(2):
        row_og.finish(chunk)
    steps(3, 2)
    steps(4, 0, 1, 2)
    for gather in [*gathers, kv_gather]:
        gather.drain()
    for row in (row_nx, row_og):
        for chunk in range(2):
            row.drain(chunk)
    pl.when(after)(lambda: halo().wait_send())


def mixer(cfg, x, *args):
    devices, layout, pieces, heads = (cfg[k] for k in ("devices", "layout", "pieces", "heads"))
    seqs, sub, width = x.shape
    span = sub * 4
    tokens = seqs * span
    columns = layout["down"][0] + layout["down"][1]
    xw, sw, qw = (layout[k][1] for k in ("x", "state", "q"))
    size = sw // 2
    count = devices * span
    shape = jax.ShapeDtypeStruct
    vmem = pl.BlockSpec(memory_space=pltpu.VMEM)
    dma = pltpu.SemaphoreType.DMA
    outs = (
        shape((width, columns), BF16),
        shape((seqs, span, width), BF16),
        shape((seqs, span, width), BF16),
        shape((tokens, qw + xw), BF16),
        shape((devices, seqs, span, qw), BF16),
        shape((seqs, 2 * span, qw), BF16),
        shape((seqs, 2 * span, count), BF16),
        shape((seqs, span, qw), F32),
        shape((seqs, span + 8, xw + sw), F32),
        shape((seqs, span, xw + sw), F32),
        shape((seqs, span, LANES), F32),
        shape((seqs, size, xw), BF16),
        shape((seqs, 16, xw), BF16),
        shape((seqs, span, xw), F32),
        shape((seqs, span, xw), BF16),
        shape((8, span), F32),
    )
    return pl.pallas_call(
        partial(mixer_kernel, cfg),
        out_shape=outs,
        in_specs=[vmem] * (1 + len(args)),
        out_specs=(vmem,) * len(outs),
        scratch_shapes=[
            pltpu.VMEM((seqs, size + 16, xw), BF16),
            pltpu.VMEM((seqs, span, xw), BF16),
            dma((2, 2, 3)),
            dma((2, 2, 4)),
            dma((4, devices)),
            dma((2,)),
            pltpu.VMEM((8, span), F32),
            pltpu.VMEM((3, 8, span), F32),
            dma((3,)),
            dma((3,)),
        ]
        + state_pass_scratch(seqs // 2, size, xw)
        + line_gather_sems(devices) * len(pieces),
        compiler_params=pltpu.CompilerParams(
            collective_id=0, has_side_effects=True, vmem_limit_bytes=VMEM_BYTES
        ),
        name="mixer",
    )(x, *args)


def back_kernel(cfg, *refs):
    (
        x_ref, gh_ref, gain_ref, w_any, nx_ref, og_ref, gb_ref, low_ref, nf_any, dgu_any, act_ref,
        kv_any, q2_ref, probs_any, att_ref, ext_ref, pre_ref, step_ref, entering, carry, y_ref,
        z_ref, squares, aux_ref, seg_ref, rope_ref, taps_ref, step_bias, decay_log, skip_ref,
        mgain_ref, fgain_ref,
        rg_ref, dw_ref, sums, kvs,
        w_ref, d_in, dlow, dy, dbc, dcum, ext_grad, halo_got, local2, after_state, keys_buf,
        prob_buf, dkv, dkv_got, dkv_line, dkv_own,
        part, near, far, grads, got, line, small_near, small_far, small_dp, kv_near, kv_far,
        sq_own, sq_got,
        w_sem, early_sems, load_sems, halo_sems, sq_send, sq_recv, send, recv, small_send, small_recv,
        dp_send, dp_recv, kv_send, kv_recv,
        *rest,
    ) = refs
    devices, layout, pieces, heads = (cfg[k] for k in ("devices", "layout", "scatters", "heads"))
    at = Place(devices)
    seqs, sub, width = x_ref.shape
    span = sub * 4
    tokens = seqs * span
    half = seqs // 2
    rows = half * span
    depth = width // devices
    xw, sw, qw = (layout[k][1] for k in ("x", "state", "q"))
    size = sw // 2
    head_dim = xw // heads
    at_dim = qw // 2
    mixed = xw + sw
    count = devices * span
    in_w = layout["in"][1]
    pass_refs, kv_sems, sems = rest[:10], rest[10:16], rest[16:]
    load = pltpu.make_async_copy(w_any.at[:, pl.ds(0, w_ref.shape[1])], w_ref, w_sem)
    load.start()
    early = (
        pltpu.make_async_copy(nf_any, part, early_sems.at[0]),
        pltpu.make_async_copy(dgu_any, d_in.at[:, pl.ds(0, dgu_any.shape[1])], early_sems.at[1]),
    )
    for copy in early:
        copy.start()

    slots = keys_buf.shape[0]

    def loads(s):
        slot = s % slots
        return (
            pltpu.make_async_copy(kv_any.at[:, s], keys_buf.at[slot], load_sems.at[0, slot]),
            pltpu.make_async_copy(probs_any.at[s], prob_buf.at[slot], load_sems.at[1, slot]),
        )

    for copy in loads(0):
        copy.start()
    Neighbours(at).greet(flips=True)

    def rows_of(buf):
        def view(rank, chunk):
            return buf.at[pl.ds(chunk * half, half), pl.ds(pl.multiple_of(rank * sub, sub), sub), :]

        return view

    scatters = []
    for i, (first, columns) in enumerate(pieces):

        def block(buf, k, first=first, columns=columns):
            return buf.at[pl.ds(pl.multiple_of(k * depth, depth), depth), pl.ds(first, columns)]

        scatters.append(
            LineScatter(
                at,
                partial(block, grads),
                partial(block, got),
                lambda zz, block=block: block(line, zz + 1),
                partial(block, line),
                sems[6 * i : 6 * i + 6],
            )
        )

    def steps(i):
        @pl.loop(0, at.lines - 1)
        def _(s):
            scatters[i].step(s)

    def finish(i):
        first, columns = pieces[i]
        scatters[i].finish(dw_ref.at[:, pl.ds(first, columns)])

    def product(lhs, rhs_ref, first, columns, into):
        tile = 2 * LANES if columns % (2 * LANES) == 0 else LANES

        @pl.loop(0, columns // tile)
        def _(j):
            src = pl.ds(pl.multiple_of(first + j * tile, LANES), tile)
            dst = pl.ds(pl.multiple_of(into + j * tile, LANES), tile)
            grads[:, dst] = dot_tn(lhs, rhs_ref[:, src]).astype(BF16)

    def weights(name_or_piece, lhs_ref, rhs_ref, first):
        into, columns = name_or_piece
        product(lhs_ref[...].reshape(tokens, width), rhs_ref, first, columns, into)

    dn, gu, out = layout["down"], layout["gu"], layout["out"]
    weights(dn, og_ref, act_ref, 0)
    scatters[0].start()
    load.wait()
    dlow[...] = dot_nn(
        gb_ref[...].reshape(tokens, width), w_ref[:, pl.ds(*layout["out"])]
    )
    mixer_gain = jnp.zeros((1, xw), F32)
    sq_own[...] = jnp.zeros(sq_own.shape, F32)
    for s in range(seqs):
        gate = z_ref[s].astype(F32)
        gated = y_ref[s] * gate * jax.nn.sigmoid(gate)
        norm = lax.rsqrt(to_column(squares[s : s + 1, :]) / (4 * xw) + EPSILON)
        grad = dlow[pl.ds(s * span, span), pl.ds(qw, xw)]
        mixer_gain = mixer_gain + jnp.sum(grad * gated * norm, 0, keepdims=True)
        inner = jnp.sum(gated * grad * mgain_ref[...], 1, keepdims=True)
        sq_own[s : s + 1, :] = to_row(inner)
    total = TensorTotal(at, sq_own, sq_got, sq_send, sq_recv)
    total.start()
    for copy in early:
        copy.wait()
    weights(gu, part, d_in, 0)
    inner_rows = total.finish()
    for s in range(seqs):
        gate = z_ref[s].astype(F32)
        sigmoid = jax.nn.sigmoid(gate)
        gated = y_ref[s] * gate * sigmoid
        norm = lax.rsqrt(to_column(squares[s : s + 1, :]) / (4 * xw) + EPSILON)
        inner = to_column(inner_rows[s : s + 1, :])
        term = dlow[pl.ds(s * span, span), pl.ds(qw, xw)] * mgain_ref[...]
        grad = norm * (term - gated * (norm * norm * inner / (4 * xw)))
        dy[s] = grad * gate * sigmoid
        grad = grad * y_ref[s] * sigmoid * (1.0 + gate * (1.0 - sigmoid))
        d_in[pl.ds(s * span, span), pl.ds(*layout["z"])] = grad.astype(BF16)

    def parts(s):
        active = pre_ref[s] * jax.nn.sigmoid(pre_ref[s])
        step, rate, running = decay_parts(step_ref[s], decay_log[...], step_bias[...])
        state_in = active[:, xw : xw + size].astype(BF16)
        state_out = active[:, xw + size :].astype(BF16)
        return active[:, :xw], state_in, state_out, step, rate, running

    @pl.loop(0, seqs)
    def _(s):
        _, _, state_out, _, _, running = parts(s)
        factor = spread(jnp.exp(running) * aux_ref[s][:, 3:4], heads, head_dim)
        low = (dy[s] * factor).astype(BF16)
        local2[s, :size, :] = dot_tn(state_out, low).astype(BF16)
        local2[s, size:, :] = carry[s]

    passing = StatePass(
        at, local2, pass_refs[0], pass_refs[1], pass_refs[2], pass_refs[3], after_state,
        pass_refs[4:], True,
    )
    passing.start()
    scatters[1].start()
    weights(out, gb_ref, low_ref, 0)

    @pl.loop(0, seqs)
    def _(s):
        x, state_in, state_out, step, _, running = parts(s)
        running_rows = running.T
        allowed = same_document(aux_ref[s], seg_ref[s])
        xs = (x * spread(step, heads, head_dim)).astype(BF16)
        joined = dot_nt(state_out, state_in)
        lane = iota((span, LANES), 1)
        d_joined = jnp.zeros((span, span), F32)
        d_running = jnp.zeros((span, LANES), F32)
        blocks = []
        for h in range(heads):
            cols = slice(h * head_dim // LANES * LANES, h * head_dim // LANES * LANES + LANES)
            begin = h * head_dim % LANES
            inside = jnp.logical_and(lane >= begin, lane < begin + head_dim)
            grad = dy[s, :, pl.ds(cols.start, LANES)]
            decay = jnp.exp(running[:, h : h + 1] - running_rows[h : h + 1, :] + allowed)
            weight = joined * decay
            d_weight = dot_nt(jnp.where(inside, grad, 0.0).astype(BF16), xs[:, cols])
            d_joined = d_joined + d_weight * decay
            product_ = (d_weight * weight).astype(BF16)
            one = (lane == h).astype(BF16)
            d_running = d_running + dot_nn(product_, one) - dot_tn(product_, one)
            blocks.append(dot_tn(weight.astype(BF16), grad.astype(BF16)))
        dlow[pl.ds(pl.multiple_of(s * span, span), span), pl.ds(qw, xw)] = pick_halves(blocks, head_dim)
        d_joined = d_joined.astype(BF16)
        factor = spread(jnp.exp(running) * aux_ref[s][:, 3:4], heads, head_dim)
        crossed = dot_nn(state_out, entering[s]) * factor
        dcum[s] = d_running + head_sums(dy[s] * crossed, heads, head_dim)
        low = (dy[s] * factor).astype(BF16)
        dbc[s, :, :size] = dot_tn(d_joined, state_out)
        dbc[s, :, size:] = dot_nn(d_joined, state_in) + dot_nt(low, entering[s])

    steps(0)
    passing.run()
    scatters[2].start()
    lane = iota((span, LANES), 1)
    upper = lane >= at_dim
    cosine, sine = rope_ref[:, :LANES], rope_ref[:, LANES:]
    scale = 1.0 / math.sqrt(at_dim)
    for s in range(seqs):
        slot = s % slots
        for copy in loads(s):
            copy.wait()
        if slots > 1 and s + 1 < seqs:
            for copy in loads(s + 1):
                copy.start()
        keys = keys_buf[slot].reshape(count, qw)
        grad = dlow[pl.ds(s * span, span), pl.ds(0, qw)].astype(BF16).astype(F32)
        inner = grad * att_ref[s]
        d_keys = jnp.zeros((count, qw), F32)
        d_query = []
        for h in range(2):
            mine = upper if h else jnp.logical_not(upper)
            delta = jnp.sum(jnp.where(mine, inner, 0.0), 1, keepdims=True)
            moved = grad if h else pltpu.roll(grad, at_dim, 1)
            moved = jnp.where(upper, moved, 0.0).astype(BF16)
            weight = prob_buf[slot, pl.ds(h * span, span), :]
            d_weight = dot_nt(moved, keys)
            d_score = (weight.astype(F32) * (d_weight - delta)).astype(BF16)
            query = q2_ref[s, pl.ds(h * span, span), :]
            d_keys = d_keys + dot_tn(d_score, query) + dot_tn(weight, moved)
            d_query.append(dot_nn(d_score, keys))
        dkv[:, s] = d_keys.astype(BF16).reshape(devices, span, qw)
        if slots == 1 and s + 1 < seqs:
            for copy in loads(s + 1):
                copy.start()
        d_query = jnp.where(upper, pltpu.roll(d_query[1], at_dim, 1), d_query[0]) * scale
        d_in[pl.ds(s * span, span), pl.ds(*layout["q"])] = turn(
            d_query, cosine, -sine, at_dim // 2
        ).astype(BF16)
    kv_scatter = LineScatter(
        at,
        lambda k: dkv.at[k],
        lambda zz: dkv_got.at[zz],
        None,
        lambda zz: dkv_line.at[zz],
        kv_sems,
        causal=True,
    )
    kv_scatter.start()
    passing.finish()
    tap_grads = [jnp.zeros((1, mixed), F32) for _ in range(4)]
    bias_grad = jnp.zeros((1, mixed), F32)
    step_grad = jnp.zeros((1, LANES), F32)
    decay_grad = jnp.zeros((1, LANES), F32)
    skip_grad = jnp.zeros((1, xw), F32)
    ext_grad[:, pl.ds(0, 8), :] = jnp.zeros((seqs, 8, mixed), F32)
    for s in range(seqs):
        aux = aux_ref[s]
        x, state_in, state_out, step, rate, running = parts(s)
        step_wide = spread(step, heads, head_dim)
        xs = x * step_wide
        end = running[span - 1 : span, :]
        tail = spread(jnp.exp(end - running) * aux[:, 4:5], heads, head_dim)
        later = after_state[s]
        found = dot_nn(state_in, later)
        weighted = xs * tail
        d_xs = dlow[pl.ds(s * span, span), pl.ds(qw, xw)] + found * tail
        d_in_state = dbc[s, :, :size] + dot_nt(weighted.astype(BF16), later)
        moved = head_sums(found * weighted, heads, head_dim)
        carried = jnp.sum(later.astype(F32) * entering[s].astype(F32), 0, keepdims=True)
        carried = head_sums(carried, heads, head_dim) * jnp.exp(end) * aux[span - 1 : span, 3:4]
        final = jnp.sum(moved, 0, keepdims=True) + carried
        d_running = dcum[s] - moved
        d_running = d_running + jnp.where(iota((span, LANES), 0) == span - 1, final, 0.0)
        d_decay = running_sum(d_running, backward=True)
        d_step = head_sums(d_xs * x, heads, head_dim) + d_decay * rate
        d_step = d_step * jax.nn.sigmoid(step_ref[s] + step_bias[...])
        d_in[pl.ds(s * span, span), pl.ds(*layout["step"])] = d_step.astype(BF16)
        step_grad = step_grad + jnp.sum(d_step, 0, keepdims=True)
        decay_grad = decay_grad + jnp.sum(d_decay * step, 0, keepdims=True) * rate
        skip_grad = skip_grad + jnp.sum(dy[s] * x, 0, keepdims=True)
        d_x = d_xs * step_wide + skip_ref[...] * dy[s]
        value = pre_ref[s]
        sigmoid = jax.nn.sigmoid(value)
        slope = sigmoid * (1.0 + value * (1.0 - sigmoid))
        outer = jnp.concatenate([d_x, d_in_state, dbc[s, :, size:]], 1) * slope
        bias_grad = bias_grad + jnp.sum(outer, 0, keepdims=True)
        ext_grad[s, pl.ds(8, span), :] = taps_ref[3:4, :] * outer
        tap_grads[3] = tap_grads[3] + jnp.sum(
            outer * ext_ref[s, pl.ds(8, span), :], 0, keepdims=True
        )
        for back in (1, 2, 3):
            valid = outer * aux[:, back - 1 : back]
            tap_grads[3 - back] = tap_grads[3 - back] + jnp.sum(
                valid * ext_ref[s, pl.ds(8 - back, span), :], 0, keepdims=True
            )
            ext_grad[s, pl.ds(8 - back, span), :] += taps_ref[3 - back : 4 - back, :] * valid
    before, after = at.dp > 0, at.dp < devices - 1

    def halo():
        return remote(
            ext_grad.at[:, pl.ds(0, 8), :],
            halo_got,
            halo_sems.at[0],
            halo_sems.at[1],
            {"dp": at.dp - 1},
        )

    pl.when(before)(lambda: halo().start())
    sums[...] = jnp.zeros(sums.shape, F32)
    sums[1:2, :] = fgain_ref[...]
    for k in range(4):
        sums[2 + k : 3 + k, pl.ds(0, sw)] = tap_grads[k][:, xw:]
        sums[8 + k : 9 + k, pl.ds(0, xw)] = tap_grads[k][:, :xw]
    sums[6:7, pl.ds(0, sw)] = bias_grad[:, xw:]
    sums[12:13, pl.ds(0, xw)] = bias_grad[:, :xw]
    sums[13:14, pl.ds(0, xw)] = mixer_gain
    sums[14:15, pl.ds(0, LANES)] = step_grad
    sums[14:15, pl.ds(LANES, LANES)] = decay_grad
    sums[14:15, pl.ds(2 * LANES, LANES)] = head_sums(
        jnp.broadcast_to(skip_grad, (8, xw)), heads, head_dim
    )[:1]
    steps(1)
    finish(0)
    kv_scatter.run_causal(dkv_own)
    for s in range(seqs):
        key_cosine = jnp.where(upper, 1.0, cosine)
        key_sine = jnp.where(upper, 0.0, -sine)
        d_in[pl.ds(s * span, span), pl.ds(*layout["kv"])] = turn(
            dkv_own[s], key_cosine, key_sine, at_dim // 2
        ).astype(BF16)
    q_piece, x_piece = pieces[3], pieces[4]
    weights(q_piece, nx_ref, d_in, q_piece[0])
    scatters[3].start()
    pl.when(after)(lambda: halo().wait_recv())
    ends = pl.ds(span, 8)

    @pl.when(after)
    def _():
        ext_grad[:, ends, :] += halo_got[...]

    value = ext_grad[:, pl.ds(8, span), :].reshape(tokens, mixed).astype(BF16)
    d_in[:, pl.ds(layout["x"][0], mixed)] = value
    back = RowScatter(
        at,
        rows_of(part),
        lambda which, chunk: near.at[which, pl.ds(chunk * half, half)],
        lambda chunk: far.at[pl.ds(chunk * half, half)],
        send,
        recv,
    )
    for c in range(2):
        value = dot_nt(d_in[pl.ds(c * rows, rows), :], w_ref[:, pl.ds(0, in_w)])
        part[pl.ds(c * half, half)] = value.astype(BF16).reshape(half, span, width)
        back.start(c)
    weights(x_piece, nx_ref, d_in, x_piece[0])
    scatters[4].start()
    steps(2)
    finish(1)
    for c in range(2):
        back.middle(c)
    steps(3)
    finish(2)
    total = jnp.zeros((1, width), F32)
    gain = gain_ref[...]
    for c in range(2):
        seq = pl.ds(c * half, half)
        grad, terms = rms_rows_grad(x_ref[seq].astype(F32), gain, back.finish(c))
        rg_ref[seq] = gh_ref[seq] + grad
        total = total + jnp.sum(terms.reshape(half * sub, width), 0, keepdims=True)
    sums[0:1, :] = total
    for i, (buf, where) in enumerate(
        ((small_near, {"tensor": at.t_near}), (small_far, {"tensor": at.t_far}))
    ):
        copy = remote(sums.at[pl.ds(0, 8)], buf, small_send.at[i], small_recv.at[i], where)
        copy.start()
        copy.wait()
        sums[0:8, :] += buf[...]
    for i, other in enumerate(at.flips()):
        copy = remote(sums, small_dp.at[i], dp_send.at[i], dp_recv.at[i], {"dp": other})
        copy.start()
        copy.wait()
        sums[...] += small_dp[i]
    steps(4)
    finish(3)
    finish(4)
    kvw = layout["kv"][1]
    kv_near[0, :, pl.ds(0, kvw)] = dw_ref[:, pl.ds(*layout["kv"])]
    kv_near[0, :, pl.ds(kvw, sw)] = dw_ref[:, pl.ds(*layout["state"])]
    copy = remote(kv_near.at[0], kv_near.at[1], kv_send.at[0], kv_recv.at[0], {"tensor": at.t_near})
    copy.start()
    copy.wait()
    kv_far[0] = kv_near[0] + kv_near[1]
    copy = remote(kv_far.at[0], kv_far.at[1], kv_send.at[1], kv_recv.at[1], {"tensor": at.t_far})
    copy.start()
    copy.wait()
    kvs[:, pl.ds(0, kvw)] = kv_far[0, :, pl.ds(0, kvw)]
    kvs[:, pl.ds(kvw, kvw)] = kv_far[1, :, pl.ds(0, kvw)]

    @pl.when(at.t >= 2)
    def _():
        kvs[:, pl.ds(0, kvw)] = kv_far[1, :, pl.ds(0, kvw)]
        kvs[:, pl.ds(kvw, kvw)] = kv_far[0, :, pl.ds(0, kvw)]

    kvs[:, pl.ds(2 * kvw, sw)] = kv_far[0, :, pl.ds(kvw, sw)] + kv_far[1, :, pl.ds(kvw, sw)]
    for scatter in [*scatters, kv_scatter]:
        scatter.drain()
    for c in range(2):
        back.drain(c)
    pl.when(before)(lambda: halo().wait_send())


def backward(cfg, x, *args):
    devices, layout, pieces, heads = (cfg[k] for k in ("devices", "layout", "scatters", "heads"))
    seqs, sub, width = x.shape
    span = sub * 4
    tokens = seqs * span
    half = seqs // 2
    depth = width // devices
    lines = devices // 2
    columns = layout["down"][0] + layout["down"][1]
    xw, sw, qw, kvw = (layout[k][1] for k in ("x", "state", "q", "kv"))
    size = sw // 2
    mixed = xw + sw
    in_w = layout["in"][1]
    own = (seqs, sub, width)
    rounds = devices.bit_length() - 1
    slots = 2 if devices * span <= 2048 else 1
    shape = jax.ShapeDtypeStruct
    vmem = pl.BlockSpec(memory_space=pltpu.VMEM)
    hbm = pl.BlockSpec(memory_space=pl.ANY)
    dma = pltpu.SemaphoreType.DMA
    in_specs = [vmem] * (1 + len(args))
    for i in (3, 8, 9, 11, 13):
        in_specs[i] = hbm
    return pl.pallas_call(
        partial(back_kernel, cfg),
        out_shape=(
            shape(own, F32),
            shape((depth, columns), F32),
            shape((16, width), F32),
            shape((depth, 2 * kvw + sw), F32),
        ),
        in_specs=in_specs,
        out_specs=(vmem,) * 4,
        scratch_shapes=[
            pltpu.VMEM((width, in_w + qw + xw), BF16),
            pltpu.VMEM((tokens, in_w), BF16),
            pltpu.VMEM((tokens, qw + xw), F32),
            pltpu.VMEM((seqs, span, xw), F32),
            pltpu.VMEM((seqs, span, sw), F32),
            pltpu.VMEM((seqs, span, LANES), F32),
            pltpu.VMEM((seqs, span + 8, mixed), F32),
            pltpu.VMEM((seqs, 8, mixed), F32),
            pltpu.VMEM((seqs, size + 16, xw), BF16),
            pltpu.VMEM((seqs, size, xw), BF16),
            pltpu.VMEM((slots, devices, span, qw), BF16),
            pltpu.VMEM((slots, 2 * span, devices * span), BF16),
            pltpu.VMEM((devices, seqs, span, qw), BF16),
            pltpu.VMEM((lines, seqs, span, qw), BF16),
            pltpu.VMEM((lines, seqs, span, qw), BF16),
            pltpu.VMEM((seqs, span, qw), F32),
            pltpu.VMEM((seqs, span, width), BF16),
            pltpu.VMEM((2,) + own, BF16),
            pltpu.VMEM(own, BF16),
            pltpu.VMEM((width, columns), BF16),
            pltpu.VMEM((lines * depth, columns), BF16),
            pltpu.VMEM(((lines + 1) * depth, columns), BF16),
            pltpu.VMEM((8, width), F32),
            pltpu.VMEM((8, width), F32),
            pltpu.VMEM((rounds, 16, width), F32),
            pltpu.VMEM((2, depth, kvw + sw), F32),
            pltpu.VMEM((2, depth, kvw + sw), F32),
            pltpu.VMEM((8, span), F32),
            pltpu.VMEM((3, 8, span), F32),
            dma,
            dma((2,)),
            dma((2, 2)),
            dma((2,)),
            dma((3,)),
            dma((3,)),
            dma((2, 3)),
            dma((2, 4)),
            dma((2,)),
            dma((2,)),
            dma((rounds,)),
            dma((rounds,)),
            dma((2,)),
            dma((2,)),
        ]
        + state_pass_scratch(half, size, xw)
        + line_scatter_sems(devices) * (1 + len(pieces)),
        compiler_params=pltpu.CompilerParams(
            collective_id=2, has_side_effects=True, vmem_limit_bytes=VMEM_BYTES
        ),
        name="backward",
    )(x, *args)


def rope_table(length, head_dim):
    half = head_dim // 2
    frequency = np.exp(-math.log(ROTARY_BASE) * 2.0 * np.arange(half) / head_dim)
    angle = np.arange(length)[:, None] * frequency[None, :]
    cosine, sine = np.cos(angle), np.sin(angle)
    copies = LANES // head_dim
    table = [cosine, cosine] * copies + [-sine, sine] * copies
    return np.concatenate(table, 1).astype(np.float32)


def body(
    resid_in,
    segment_ids,
    out_grad,
    input_gain,
    ffn_gain,
    query_weight,
    keyvalue_weight,
    attention_output_weight,
    mixer_input_weight,
    state_input_weight,
    step_weight,
    conv_mixer,
    conv_mixer_bias,
    conv_state,
    conv_state_bias,
    step_bias,
    decay_log,
    skip_gain,
    mixer_gain,
    mixer_output_weight,
    gate_up_weight,
    down_weight,
):
    tensor_count = lax.axis_size("tensor")
    shard_count = lax.axis_size("dp")
    tensor_rank = lax.axis_index("tensor")
    shard_rank = lax.axis_index("dp")
    sequences, sub_rows, model_width = resid_in.shape
    span_rows = sub_rows * tensor_count
    head_dim = keyvalue_weight.shape[2] // 2
    query_width = query_weight.shape[1]
    local_heads = query_width // head_dim
    mixer_local = step_weight.shape[1]
    mixer_width = conv_mixer.shape[1]
    mixer_total = mixer_width * tensor_count
    mixer_dim = mixer_width // mixer_local
    state_dim = state_input_weight.shape[1] // 2
    edge_rows = conv_mixer.shape[0] - 1
    scale = 1.0 / math.sqrt(head_dim)
    keyval_index = tensor_rank * KVH // tensor_count
    keyvalue_local = lax.dynamic_index_in_dim(keyvalue_weight, keyval_index, 1, keepdims=False)
    ff = down_weight.shape[0]
    depth = query_weight.shape[0]
    layout = {}
    columns = 0
    for name, size in (
        ("step", LANES),
        ("x", mixer_width),
        ("state", 2 * state_dim),
        ("q", query_width),
        ("kv", 2 * head_dim),
        ("z", mixer_width),
        ("out", query_width + mixer_width),
        ("gu", 2 * ff),
        ("down", ff),
    ):
        layout[name] = (columns, size)
        columns += size
    layout["in"] = (0, layout["out"][0])
    def columns_of(array, name):
        first, size = layout[name]
        return array[..., first : first + size]

    w_packed = jnp.concatenate(
        [
            jnp.pad(step_weight, ((0, 0), (0, LANES - mixer_local))),
            mixer_input_weight[:, 1],
            state_input_weight,
            query_weight,
            keyvalue_local,
            mixer_input_weight[:, 0],
            gate_up_weight.reshape(depth, 2 * ff),
        ],
        1,
    )
    first_row = shard_rank * span_rows
    seg_span = lax.dynamic_slice_in_dim(segment_ids, first_row, span_rows, 1)
    seg_padded = jnp.pad(segment_ids, ((0, 0), (edge_rows, 0)), constant_values=-1)
    seg_ext = lax.dynamic_slice_in_dim(seg_padded, first_row, span_rows + edge_rows, 1)
    same = [seg_ext[:, edge_rows - d : edge_rows - d + span_rows] == seg_span for d in (1, 2, 3)]
    aux = jnp.stack(
        [
            *same,
            seg_span == seg_ext[:, edge_rows - 1 : edge_rows],
            seg_span == seg_span[:, -1:],
            seg_span,
        ],
        -1,
    ).astype(jnp.float32)
    rope = lax.dynamic_slice_in_dim(
        jnp.asarray(rope_table(segment_ids.shape[1], head_dim)), first_row, span_rows, 0
    )

    def lanes(array):
        return jnp.pad(array[None, :], ((0, 0), (0, LANES - array.shape[0])))

    config = {
        "devices": shard_count,
        "layout": layout,
        "heads": mixer_local,
        "pieces": (
            (layout["step"][0], layout["q"][0] - layout["step"][0]),
            (layout["q"][0], layout["out"][0] - layout["q"][0]),
            layout["out"],
            layout["gu"],
            layout["down"],
        ),
        "scatters": (
            layout["down"],
            layout["gu"],
            layout["out"],
            (layout["q"][0], layout["out"][0] - layout["q"][0]),
            (layout["step"][0], layout["q"][0] - layout["step"][0]),
        ),
    }
    (
        w_all, span_normed_input, span_gradient, branch_low, keys, queries, probs, attention, ext,
        pre, step_pre, entering, state_decay, mixer_y, gate_z, squares,
    ) = mixer(
        config,
        resid_in,
        out_grad,
        input_gain[None, :],
        w_packed,
        attention_output_weight,
        mixer_output_weight,
        down_weight,
        aux,
        seg_span.astype(jnp.float32)[:, None, :],
        segment_ids.astype(jnp.float32)[:, None, :],
        rope,
        jnp.concatenate([conv_mixer, conv_state], 1),
        jnp.concatenate([conv_mixer_bias, conv_state_bias])[None, :],
        lanes(step_bias),
        lanes(decay_log),
        jnp.repeat(skip_gain, mixer_dim)[None, :],
        mixer_gain[None, :],
    )
    block_out, grad_hidden, grad_branch, span_feedforward, activated, grad_gate_up, ffn_gain_part = (
        feed_forward(
            shard_count,
            tensor_count,
            layout,
            resid_in,
            branch_low,
            span_gradient,
            out_grad,
            ffn_gain[None, :],
            w_all,
        )
    )
    resid_grad, weight_grads, sums, replicated = backward(
        config,
        resid_in,
        grad_hidden,
        input_gain[None, :],
        w_all,
        span_normed_input,
        span_gradient,
        grad_branch,
        branch_low,
        span_feedforward,
        grad_gate_up,
        activated,
        keys,
        queries,
        probs,
        attention,
        ext,
        pre,
        step_pre,
        entering,
        state_decay,
        mixer_y,
        gate_z,
        squares,
        aux,
        seg_span.astype(jnp.float32)[:, None, :],
        rope,
        jnp.concatenate([conv_mixer, conv_state], 1),
        lanes(step_bias),
        lanes(decay_log),
        jnp.repeat(skip_gain, mixer_dim)[None, :],
        mixer_gain[None, :],
        ffn_gain_part,
    )
    out_grads = columns_of(weight_grads, "out").T
    kv_width = 2 * head_dim
    return (
        block_out,
        resid_grad,
        sums[0],
        sums[1],
        columns_of(weight_grads, "q"),
        replicated[:, : 2 * kv_width].reshape(depth, 2, kv_width),
        out_grads[:query_width],
        jnp.stack([columns_of(weight_grads, "z"), columns_of(weight_grads, "x")], 1),
        replicated[:, 2 * kv_width :],
        columns_of(weight_grads, "step")[:, :mixer_local],
        sums[8:12, :mixer_width],
        sums[12, :mixer_width],
        sums[2:6, : 2 * state_dim],
        sums[6, : 2 * state_dim],
        sums[14, :mixer_local],
        sums[14, LANES : LANES + mixer_local],
        sums[14, 2 * LANES : 2 * LANES + mixer_local],
        sums[13, :mixer_width],
        out_grads[query_width:],
        columns_of(weight_grads, "gu").reshape(depth, 2, ff),
        columns_of(weight_grads, "down").T,
    )


def solution(mesh):
    placed = (
        P(None, ("dp", "tensor"), None),
        P(),
        P(None, ("dp", "tensor"), None),
        P(),
        P(),
        P("dp", "tensor"),
        P("dp", None, None),
        P("tensor", "dp"),
        P("dp", None, "tensor"),
        P("dp", None),
        P("dp", "tensor"),
        P(None, "tensor"),
        P("tensor"),
        P(),
        P(),
        P("tensor"),
        P("tensor"),
        P("tensor"),
        P("tensor"),
        P("tensor", "dp"),
        P("dp", None, "tensor"),
        P("tensor", "dp"),
    )
    return jax.shard_map(
        body,
        mesh=mesh,
        in_specs=placed,
        out_specs=(
            P(None, ("dp", "tensor"), None),
            P(None, ("dp", "tensor"), None),
            P(),
            P(),
            P("dp", "tensor"),
            P("dp", None, None),
            P("tensor", "dp"),
            P("dp", None, "tensor"),
            P("dp", None),
            P("dp", "tensor"),
            P(None, "tensor"),
            P("tensor"),
            P(),
            P(),
            P("tensor"),
            P("tensor"),
            P("tensor"),
            P("tensor"),
            P("tensor", "dp"),
            P("dp", None, "tensor"),
            P("tensor", "dp"),
        ),
        check_vma=False,
    )
```

```python
from functools import partial
import math

import jax
import jax.numpy as jnp
import numpy as np
from jax import lax
from jax.experimental import pallas as pl
from jax.experimental.pallas import tpu as pltpu
from jax.sharding import PartitionSpec as P

KVH = 2
EPSILON = 1e-05
ROTARY_BASE = 100000000000.0
MASKED = -1e30
MATMUL_EXACTNESS = lax.Precision.HIGHEST
LANES = 128
F32 = jnp.float32
BF16 = jnp.bfloat16
VMEM_BYTES = 63 * 2**20


def dot_nn(a, b):
    return lax.dot_general(a, b, (((1,), (0,)), ((), ())), preferred_element_type=F32)


def dot_nt(a, b):
    return lax.dot_general(a, b, (((1,), (1,)), ((), ())), preferred_element_type=F32)


def dot_tn(a, b):
    return lax.dot_general(a, b, (((0,), (0,)), ((), ())), preferred_element_type=F32)


def remote(src, dst, send_sem, recv_sem, where):
    return pltpu.make_async_remote_copy(
        src_ref=src,
        dst_ref=dst,
        send_sem=send_sem,
        recv_sem=recv_sem,
        device_id=where,
        device_id_type=pl.DeviceIdType.MESH,
    )


def add_into(ref, *others):
    total = ref[...].astype(F32)
    for other in others:
        total = total + other[...].astype(F32)
    ref[...] = total.astype(BF16)


class Place:
    def __init__(self, devices):
        self.devices = devices
        self.lines = devices // 2
        self.dp = lax.axis_index("dp")
        self.t = lax.axis_index("tensor")
        self.z = lax.div(self.dp, 2)
        self.p = lax.rem(self.dp, 2)
        self.pair = self.dp + 1 - 2 * self.p
        self.t_near = self.t + 1 - 2 * lax.rem(self.t, 2)
        self.t_far = lax.rem(self.t + 2, 4)
        self.t_both = lax.rem(self.t_near + 2, 4)
        self.first = self.z == 0
        self.last = self.z == self.lines - 1

    def flips(self):
        bit = 1
        while bit < self.devices:
            yield self.dp + bit - 2 * bit * lax.rem(lax.div(self.dp, bit), 2)
            bit *= 2


class LineGather:
    def __init__(self, place, view, recv, right, left, pair, causal=False):
        self.at, self.view = place, view
        self.causal = causal
        self.recv, self.right, self.left, self.side = recv, right, left, pair

    def copy(self, block, sem, where):
        ref = self.view(block)
        return remote(ref, ref, sem, self.recv.at[block], where)

    def send_right(self, zz):
        return self.copy(zz * 2 + self.at.p, self.right.at[zz], {"dp": self.at.dp + 2})

    def send_left(self, zz):
        return self.copy(zz * 2 + self.at.p, self.left.at[zz], {"dp": self.at.dp - 2})

    def send_pair(self, zz):
        return self.copy(zz * 2 + self.at.p, self.side.at[zz], {"dp": self.at.pair})

    def arrived(self, block):
        self.copy(block, self.side.at[0], {"dp": self.at.pair}).wait_recv()

    def start(self):
        at = self.at
        pl.when(jnp.logical_not(at.last))(lambda: self.send_right(at.z).start())
        if not self.causal:
            pl.when(jnp.logical_not(at.first))(lambda: self.send_left(at.z).start())
        self.send_pair(at.z).start()

    def step(self, s):
        at = self.at
        low, high = at.z - 1 - s, at.z + 1 + s

        @pl.when(low >= 0)
        def _():
            self.arrived(low * 2 + at.p)
            pl.when(jnp.logical_not(at.last))(lambda: self.send_right(low).start())
            self.send_pair(low).start()

        if self.causal:
            return

        @pl.when(high < at.lines)
        def _():
            self.arrived(high * 2 + at.p)
            pl.when(jnp.logical_not(at.first))(lambda: self.send_left(high).start())
            self.send_pair(high).start()

    def finish(self):
        at = self.at

        @pl.loop(0, at.z + 1 if self.causal else at.lines)
        def _(zz):
            self.arrived(zz * 2 + 1 - at.p)

    def drain(self):
        at = self.at

        @pl.loop(0, at.z + 1 if self.causal else at.lines)
        def _(zz):
            self.send_pair(zz).wait_send()

            @pl.when(jnp.logical_and(zz <= at.z, jnp.logical_not(at.last)))
            def _():
                self.send_right(zz).wait_send()

            if self.causal:
                return

            @pl.when(jnp.logical_and(zz >= at.z, jnp.logical_not(at.first)))
            def _():
                self.send_left(zz).wait_send()


class CrossGather:
    def __init__(self, place, view, recv, right, left, pair):
        self.at, self.view = place, view
        self.recv, self.right, self.left, self.side = recv, right, left, pair

    def copy(self, block, sem, where):
        ref = self.view(block)
        return remote(ref, ref, sem, self.recv.at[block], where)

    def send_right(self, block):
        return self.copy(block, self.right.at[block], {"dp": self.at.dp + 2})

    def send_left(self, block):
        return self.copy(block, self.left.at[block], {"dp": self.at.dp - 2})

    def send_pair(self):
        return self.copy(self.at.dp, self.side.at[0], {"dp": self.at.pair})

    def arrived(self, block):
        self.copy(block, self.side.at[0], {"dp": self.at.pair}).wait_recv()

    def onward(self, block, right, left):
        at = self.at
        if right:
            pl.when(jnp.logical_not(at.last))(lambda: self.send_right(block).start())
        if left:
            pl.when(jnp.logical_not(at.first))(lambda: self.send_left(block).start())

    def start(self):
        self.send_pair().start()
        self.onward(self.at.dp, True, True)

    def begin(self):
        self.arrived(self.at.pair)
        self.onward(self.at.pair, True, True)

    def step(self, s):
        at = self.at
        low, high = at.z - 1 - s, at.z + 1 + s
        for q in (at.p, 1 - at.p):

            @pl.when(low >= 0)
            def _():
                self.arrived(low * 2 + q)
                self.onward(low * 2 + q, True, False)

            @pl.when(high < at.lines)
            def _():
                self.arrived(high * 2 + q)
                self.onward(high * 2 + q, False, True)

    def finish(self):
        pass

    def drain(self):
        at = self.at
        self.send_pair().wait_send()

        @pl.loop(0, at.devices)
        def _(block):
            zz = lax.div(block, 2)

            @pl.when(jnp.logical_and(zz <= at.z, jnp.logical_not(at.last)))
            def _():
                self.send_right(block).wait_send()

            @pl.when(jnp.logical_and(zz >= at.z, jnp.logical_not(at.first)))
            def _():
                self.send_left(block).wait_send()


class LineScatter:
    def __init__(self, place, part, got, right, left, sems, causal=False):
        self.at, self.part = place, part
        self.got, self.right, self.left = got, right, left
        self.causal = causal
        (
            self.pair_send,
            self.pair_recv,
            self.right_send,
            self.right_recv,
            self.left_send,
            self.left_recv,
        ) = sems

    def pair_copy(self, zz):
        src = self.part(zz * 2 + 1 - self.at.p)
        return remote(
            src, self.got(zz), self.pair_send.at[zz], self.pair_recv.at[zz], {"dp": self.at.pair}
        )

    def right_copy(self, zz):
        src = self.part(zz * 2 + self.at.p)
        return remote(
            src,
            self.right(zz),
            self.right_send.at[zz],
            self.right_recv.at[zz],
            {"dp": self.at.dp + 2},
        )

    def left_copy(self, zz):
        src = self.part(zz * 2 + self.at.p)
        return remote(
            src, self.left(zz), self.left_send.at[zz], self.left_recv.at[zz], {"dp": self.at.dp - 2}
        )

    def start(self):
        at = self.at

        @pl.loop(0, at.z + 1 if self.causal else at.lines)
        def _(i):
            self.pair_copy(i if self.causal else at.lines - 1 - i).start()

    def step(self, i):
        at = self.at
        high, low = at.lines - 1 - i, i
        if self.causal:
            self.step_low(low)
            return

        @pl.when(at.z < at.lines // 2)
        def _():
            self.step_high(high)
            self.step_low(low)

        @pl.when(at.z >= at.lines // 2)
        def _():
            self.step_low(low)
            self.step_high(high)

    def step_high(self, high):
        at = self.at

        @pl.when(high > at.z)
        def _():
            self.pair_copy(high).wait_recv()
            ref = self.part(high * 2 + at.p)

            @pl.when(at.first)
            def _():
                add_into(ref, self.got(high))

            @pl.when(jnp.logical_not(at.first))
            def _():
                self.right_copy(high).wait_recv()
                add_into(ref, self.got(high), self.right(high))

            self.right_copy(high).start()

    def step_low(self, low):
        at = self.at

        @pl.when(low < at.z)
        def _():
            self.pair_copy(low).wait_recv()
            ref = self.part(low * 2 + at.p)

            @pl.when(at.last)
            def _():
                add_into(ref, self.got(low))

            @pl.when(jnp.logical_not(at.last))
            def _():
                self.left_copy(low).wait_recv()
                add_into(ref, self.got(low), self.left(low))

            self.left_copy(low).start()

    def finish(self, out):
        at = self.at
        self.pair_copy(at.z).wait_recv()
        out[...] = self.part(at.dp)[...].astype(F32) + self.got(at.z)[...].astype(F32)

        if not self.causal:

            @pl.when(jnp.logical_not(at.first))
            def _():
                self.right_copy(at.z).wait_recv()
                out[...] += self.right(at.z)[...].astype(F32)

        @pl.when(jnp.logical_not(at.last))
        def _():
            self.left_copy(at.z).wait_recv()
            out[...] += self.left(at.z)[...].astype(F32)

    def drain(self):
        at = self.at

        @pl.loop(0, at.z + 1 if self.causal else at.lines)
        def _(zz):
            self.pair_copy(zz).wait_send()
            if not self.causal:
                pl.when(zz > at.z)(lambda: self.right_copy(zz).wait_send())
            pl.when(zz < at.z)(lambda: self.left_copy(zz).wait_send())

    def run_causal(self, out):
        @pl.loop(0, self.at.lines - 1)
        def _(s):
            self.step(s)

        self.finish(out)


class CrossScatter:
    def __init__(self, place, part, got, line, sems):
        self.at, self.part, self.got, self.line = place, part, got, line
        self.pair_send, self.pair_recv = sems[0].at[0], sems[0].at[1]
        self.right_send, self.right_recv, self.left_send, self.left_recv = sems[1:]

    def right_copy(self, zz, q):
        block = zz * 2 + q
        return remote(
            self.part(block),
            self.line(zz + 1, q),
            self.right_send.at[block],
            self.right_recv.at[block],
            {"dp": self.at.dp + 2},
        )

    def left_copy(self, zz, q):
        block = zz * 2 + q
        return remote(
            self.part(block),
            self.line(zz, q),
            self.left_send.at[block],
            self.left_recv.at[block],
            {"dp": self.at.dp - 2},
        )

    def pair_copy(self):
        return remote(
            self.part(self.at.pair), self.got, self.pair_send, self.pair_recv, {"dp": self.at.pair}
        )

    def start(self):
        pass

    def step(self, i):
        at = self.at
        high, low = at.lines - 1 - i, i

        @pl.when(at.z < at.lines // 2)
        def _():
            self.step_high(high)
            self.step_low(low)

        @pl.when(at.z >= at.lines // 2)
        def _():
            self.step_low(low)
            self.step_high(high)

    def step_high(self, high):
        at = self.at

        @pl.when(high > at.z)
        def _():
            for q in (1 - at.p, at.p):

                @pl.when(jnp.logical_not(at.first))
                def _():
                    self.right_copy(high, q).wait_recv()
                    add_into(self.part(high * 2 + q), self.line(high + 1, q))

                self.right_copy(high, q).start()

    def step_low(self, low):
        at = self.at

        @pl.when(low < at.z)
        def _():
            for q in (1 - at.p, at.p):

                @pl.when(jnp.logical_not(at.last))
                def _():
                    self.left_copy(low, q).wait_recv()
                    add_into(self.part(low * 2 + q), self.line(low, q))

                self.left_copy(low, q).start()

    def join(self):
        at = self.at
        for q in (1 - at.p, at.p):
            ref = self.part(at.z * 2 + q)

            @pl.when(jnp.logical_not(at.first))
            def _():
                self.right_copy(at.z, q).wait_recv()
                add_into(ref, self.line(at.z + 1, q))

            @pl.when(jnp.logical_not(at.last))
            def _():
                self.left_copy(at.z, q).wait_recv()
                add_into(ref, self.line(at.z, q))

            if q is not at.p:
                self.pair_copy().start()

    def finish(self, out):
        self.pair_copy().wait_recv()
        out[...] = self.part(self.at.dp)[...].astype(F32) + self.got[...].astype(F32)

    def drain(self):
        at = self.at
        self.pair_copy().wait_send()

        @pl.loop(0, at.devices)
        def _(block):
            zz, q = lax.div(block, 2), lax.rem(block, 2)
            pl.when(zz > at.z)(lambda: self.right_copy(zz, q).wait_send())
            pl.when(zz < at.z)(lambda: self.left_copy(zz, q).wait_send())


class RowGather:
    def __init__(self, place, view, send, recv):
        self.at, self.view, self.send, self.recv = place, view, send, recv

    def copy(self, rank, chunk, sem, near):
        ref = self.view(rank, chunk)
        where = {"tensor": self.at.t_near if near else self.at.t_far}
        return remote(ref, ref, self.send.at[chunk, sem], self.recv.at[chunk, rank], where)

    def start(self, chunk):
        self.copy(self.at.t, chunk, 0, False).start()
        self.copy(self.at.t, chunk, 1, True).start()

    def forward(self, chunk):
        self.copy(self.at.t_far, chunk, 2, False).wait_recv()
        self.copy(self.at.t_far, chunk, 2, True).start()

    def finish(self, chunk):
        self.copy(self.at.t_near, chunk, 1, True).wait_recv()
        self.copy(self.at.t_both, chunk, 2, True).wait_recv()

    def drain(self, chunk):
        self.copy(self.at.t, chunk, 0, False).wait_send()
        self.copy(self.at.t, chunk, 1, True).wait_send()
        self.copy(self.at.t_far, chunk, 2, True).wait_send()


class RowScatter:
    def __init__(self, place, view, near_buf, far_buf, send, recv):
        self.at, self.view = place, view
        self.near_buf, self.far_buf = near_buf, far_buf
        self.send, self.recv = send, recv

    def near_copy(self, chunk, which):
        rank = self.at.t_both if which else self.at.t_near
        return remote(
            self.view(rank, chunk),
            self.near_buf(which, chunk),
            self.send.at[chunk, which],
            self.recv.at[chunk, which],
            {"tensor": self.at.t_near},
        )

    def far_copy(self, chunk):
        return remote(
            self.view(self.at.t_far, chunk),
            self.far_buf(chunk),
            self.send.at[chunk, 2],
            self.recv.at[chunk, 2],
            {"tensor": self.at.t_far},
        )

    def start(self, chunk):
        self.near_copy(chunk, 1).start()
        self.near_copy(chunk, 0).start()

    def middle(self, chunk):
        self.near_copy(chunk, 1).wait_recv()
        ref = self.view(self.at.t_far, chunk)
        ref[...] = (ref[...].astype(F32) + self.near_buf(1, chunk)[...].astype(F32)).astype(BF16)
        self.far_copy(chunk).start()

    def finish(self, chunk):
        self.near_copy(chunk, 0).wait_recv()
        total = self.view(self.at.t, chunk)[...].astype(F32) + self.near_buf(0, chunk)[
            ...
        ].astype(F32)
        self.far_copy(chunk).wait_recv()
        return total + self.far_buf(chunk)[...].astype(F32)

    def drain(self, chunk):
        self.near_copy(chunk, 0).wait_send()
        self.near_copy(chunk, 1).wait_send()
        self.far_copy(chunk).wait_send()


def line_gather_sems(devices):
    dma = pltpu.SemaphoreType.DMA
    return [dma((devices,)), dma((devices // 2,)), dma((devices // 2,)), dma((devices // 2,))]


def line_scatter_sems(devices):
    return [pltpu.SemaphoreType.DMA((devices // 2,)) for _ in range(6)]


def rms_rows(values, gain):
    return values * lax.rsqrt(jnp.mean(values * values, -1, keepdims=True) + EPSILON) * gain


def rms_rows_grad(values, gain, grad):
    scale = lax.rsqrt(jnp.mean(values * values, -1, keepdims=True) + EPSILON)
    term = grad * gain
    inner = jnp.mean(values * term, -1, keepdims=True)
    return scale * (term - values * (scale * scale * inner)), grad * values * scale


def ffn_kernel(devices, layout, *refs):
    (
        x_ref, a_ref, og_ref, ogl_ref, gain_ref, w_any, dn_in,
        out_ref, gh_ref, gb, nf, act, dgu, gain_grad,
        part, part2, near1, far1, near2, far2, near3, far3, hid,
        w_ref, w_dn, w_sem, send, recv, *sems,
    ) = refs
    at = Place(devices)
    seqs, sub, width = x_ref.shape
    span = sub * 4
    half = seqs // 2
    rows = half * span
    first = layout["out"][0]
    out_w, gu_w = (pl.ds(layout[k][0] - first, layout[k][1]) for k in ("out", "gu"))
    ff = layout["down"][1]
    depth = dn_in.shape[1]
    load = pltpu.make_async_copy(w_any.at[:, pl.ds(first, w_ref.shape[1])], w_ref, w_sem)
    load.start()
    w_dn[pl.ds(pl.multiple_of(at.dp * depth, depth), depth), :] = dn_in[...].T
    Neighbours(at).greet()

    def rows_of(buf):
        def view(rank, chunk):
            return buf.at[pl.ds(chunk * half, half), pl.ds(pl.multiple_of(rank * sub, sub), sub), :]

        return view

    def parts_of(buf):
        return lambda which, chunk: buf.at[which, pl.ds(chunk * half, half)]

    def part_of(buf):
        return lambda chunk: buf.at[pl.ds(chunk * half, half)]

    branch = RowScatter(at, rows_of(part), parts_of(near1), part_of(far1), send.at[0], recv.at[0])
    ffn = RowScatter(at, rows_of(part2), parts_of(near2), part_of(far2), send.at[1], recv.at[1])
    back = RowScatter(at, rows_of(part), parts_of(near3), part_of(far3), send.at[2], recv.at[2])
    row_nf = RowGather(at, rows_of(nf), send.at[3], recv.at[3])
    row_gb = RowGather(at, rows_of(gb), send.at[4], recv.at[4])
    mine = pl.ds(pl.multiple_of(at.t * sub, sub), sub)
    gain = gain_ref[...].reshape(1, width)

    def seq_rows(chunk):
        return pl.ds(chunk * half, half)

    def tok_rows(chunk):
        return pl.ds(chunk * rows, rows)

    gather = LineGather(
        at, lambda block: w_dn.at[pl.ds(pl.multiple_of(block * depth, depth), depth), :], *sems
    )
    gather.start()
    load.wait()
    for c in range(2):
        value = dot_nt(a_ref[tok_rows(c), :], w_ref[:, out_w])
        part[seq_rows(c)] = value.astype(BF16).reshape(half, span, width)
        branch.start(c)
    for c in range(2):
        branch.middle(c)
    gather.step(0)
    for c in range(2):
        hidden = x_ref[seq_rows(c)].astype(F32) + branch.finish(c)
        hid[seq_rows(c)] = hidden
        nf[seq_rows(c), mine, :] = rms_rows(hidden, gain).astype(BF16)
        row_nf.start(c)
    gather.step(1)
    for c in range(2):
        row_nf.forward(c)
    pl.loop(2, at.lines - 1)(lambda s: gather.step(s))
    gather.finish()
    for c in range(2):
        row_nf.finish(c)
        branch.drain(c)
        flat = nf[seq_rows(c)].reshape(rows, width)
        flat_og = og_ref[seq_rows(c)].reshape(rows, width)
        gate_up = dot_nn(flat, w_ref[:, gu_w])
        gate, up = gate_up[:, :ff], gate_up[:, ff:]
        sigmoid = jax.nn.sigmoid(gate)
        grad_act = dot_nn(flat_og, w_dn[...])
        act[tok_rows(c), :] = (gate * sigmoid * up).astype(BF16)
        dgu[tok_rows(c), :ff] = (
            grad_act * up * sigmoid * (1.0 + gate * (1.0 - sigmoid))
        ).astype(BF16)
        dgu[tok_rows(c), ff:] = (grad_act * gate * sigmoid).astype(BF16)
        value = dot_nt(dgu[tok_rows(c), :], w_ref[:, gu_w])
        part[seq_rows(c)] = value.astype(BF16).reshape(half, span, width)
        back.start(c)
    for c in range(2):
        back.middle(c)
        value = dot_nt(act[tok_rows(c), :], w_dn[...])
        part2[seq_rows(c)] = value.astype(BF16).reshape(half, span, width)
    total = jnp.zeros((1, width), F32)
    for c in range(2):
        grad_hidden, terms = rms_rows_grad(hid[seq_rows(c)], gain, back.finish(c))
        total = total + jnp.sum(terms.reshape(half * sub, width), 0, keepdims=True)
        grad_hidden = grad_hidden + ogl_ref[seq_rows(c)].astype(F32)
        gh_ref[seq_rows(c)] = grad_hidden
        gb[seq_rows(c), mine, :] = grad_hidden.astype(BF16)
        row_gb.start(c)
        ffn.start(c)
    gain_grad[...] = total
    for c in range(2):
        row_gb.forward(c)
        ffn.middle(c)
    for c in range(2):
        out_ref[seq_rows(c)] = (hid[seq_rows(c)] + ffn.finish(c)).astype(BF16)
        row_gb.finish(c)
    for c in range(2):
        row_nf.drain(c)
        row_gb.drain(c)
        back.drain(c)
        ffn.drain(c)
    gather.drain()


def feed_forward(devices, tensor, layout, x, a, og, out_grad, gain, w_all, w_down):
    seqs, sub, width = x.shape
    span = sub * tensor
    tokens = seqs * span
    ff = layout["down"][1]
    shape = jax.ShapeDtypeStruct
    vmem = pl.BlockSpec(memory_space=pltpu.VMEM)
    dma = pltpu.SemaphoreType.DMA
    whole, own = (seqs, span, width), (seqs, sub, width)
    return pl.pallas_call(
        partial(ffn_kernel, devices, layout),
        out_shape=(
            shape(own, BF16),
            shape(own, F32),
            shape(whole, BF16),
            shape(whole, BF16),
            shape((tokens, ff), BF16),
            shape((tokens, 2 * ff), BF16),
            shape((1, width), F32),
        ),
        in_specs=[vmem] * 5 + [pl.BlockSpec(memory_space=pl.ANY), vmem],
        out_specs=(vmem,) * 7,
        scratch_shapes=[
            pltpu.VMEM(whole, BF16),
            pltpu.VMEM(whole, BF16),
        ]
        + [pltpu.VMEM((2,) + own, BF16), pltpu.VMEM(own, BF16)] * 3
        + [
            pltpu.VMEM(own, F32),
            pltpu.VMEM((width, layout["down"][0] - layout["out"][0]), BF16),
            pltpu.VMEM((width, ff), BF16),
            dma,
            dma((5, 2, 3)),
            dma((5, 2, 4)),
        ]
        + line_gather_sems(devices),
        compiler_params=pltpu.CompilerParams(
            collective_id=1, has_side_effects=True, vmem_limit_bytes=VMEM_BYTES
        ),
        name="feed_forward",
    )(x, a, og, out_grad, gain, w_all, w_down)


def to_row(column):
    size = column.shape[0]
    eye = iota((size, size), 0) == iota((size, size), 1)
    return jnp.sum(jnp.where(eye, column, 0.0), 0, keepdims=True)


def to_column(row):
    size = row.shape[1]
    eye = iota((size, size), 0) == iota((size, size), 1)
    return jnp.sum(jnp.where(eye, row, 0.0), 1, keepdims=True)


def iota(shape, dim):
    return lax.broadcasted_iota(jnp.int32, shape, dim)


def spread(columns, heads, head_dim):
    rows = columns.shape[0]
    lane = iota((rows, LANES), 1)
    blocks = []
    for first in range(0, heads, LANES // head_dim):
        block = jnp.broadcast_to(columns[:, first : first + 1], (rows, LANES))
        for k in range(1, LANES // head_dim):
            block = jnp.where(lane >= k * head_dim, columns[:, first + k : first + k + 1], block)
        blocks.append(block)
    return jnp.concatenate(blocks, 1)


def head_sums(values, heads, head_dim):
    rows = values.shape[0]
    lane = iota((rows, LANES), 1)
    out = jnp.zeros((rows, LANES), F32)
    per = LANES // head_dim
    for h in range(heads):
        block = values[:, h // per * LANES : (h // per + 1) * LANES]
        inside = jnp.logical_and(lane >= h % per * head_dim, lane < (h % per + 1) * head_dim)
        total = jnp.sum(jnp.where(inside, block, 0.0), 1, keepdims=True)
        out = jnp.where(lane == h, total, out)
    return out


def pick_halves(blocks, head_dim):
    lane = iota(blocks[0].shape, 1)
    per = LANES // head_dim
    out = []
    for first in range(0, len(blocks), per):
        block = blocks[first]
        for k in range(1, per):
            block = jnp.where(lane >= k * head_dim, blocks[first + k], block)
        out.append(block)
    return jnp.concatenate(out, 1)


def softplus(value):
    return jnp.maximum(value, 0.0) + jnp.log1p(jnp.exp(-jnp.abs(value)))


def running_sum(values, backward=False):
    rows = values.shape[0]
    row = iota(values.shape, 0)
    step = 1
    while step < rows:
        if backward:
            moved = jnp.where(row < rows - step, pltpu.roll(values, rows - step, 0), 0.0)
        else:
            moved = jnp.where(row >= step, pltpu.roll(values, step, 0), 0.0)
        values = values + moved
        step *= 2
    return values


def turn(values, cosine, sine, half):
    lane = iota(values.shape, 1)
    first = lax.rem(lane, 2 * half) < half
    swapped = jnp.where(
        first, pltpu.roll(values, LANES - half, 1), pltpu.roll(values, half, 1)
    )
    return values * cosine + swapped * sine


def decay_parts(step_pre, decay_log, bias):
    step = softplus(step_pre + bias)
    rate = -jnp.exp(decay_log)
    return step, rate, running_sum(step * rate)


def same_document(aux, row):
    span = aux.shape[0]
    same = aux[:, 5:6] == row
    causal = iota((span, span), 0) >= iota((span, span), 1)
    return jnp.where(jnp.logical_and(same, causal), 0.0, MASKED)


class Neighbours:
    def __init__(self, at):
        self.at = at

    def greet(self, flips=False):
        at = self.at
        barrier = pltpu.get_barrier_semaphore()
        end = at.devices - 1

        def signal(**where):
            pl.semaphore_signal(
                barrier, inc=1, device_id=where, device_id_type=pl.DeviceIdType.MESH
            )

        for other in (at.t_near, at.t_far, at.t_both):
            signal(tensor=other)
        signal(dp=at.pair)
        count = 4
        for step in (1, 2):
            low, high = at.dp >= step, at.dp + step <= end
            pl.when(low)(partial(signal, dp=at.dp - step))
            pl.when(high)(partial(signal, dp=at.dp + step))
            count = count + low.astype(jnp.int32) + high.astype(jnp.int32)
        if flips:
            for other in at.flips():
                signal(dp=other)
                count = count + 1
        pl.semaphore_wait(barrier, count)


class TensorTotal:
    def __init__(self, at, own, got, send, recv):
        self.at, self.own, self.got, self.send, self.recv = at, own, got, send, recv

    def copies(self):
        others = (self.at.t_near, self.at.t_far, self.at.t_both)
        return [
            remote(
                self.own, self.got.at[i], self.send.at[i], self.recv.at[i], {"tensor": other}
            )
            for i, other in enumerate(others)
        ]

    def start(self):
        for copy in self.copies():
            copy.start()

    def finish(self):
        for copy in self.copies():
            copy.wait()
        return self.own[...] + self.got[0] + self.got[1] + self.got[2]


class StatePass:
    def __init__(self, at, local, pair_in, chain_in, chain_out, share, result, sems, backward):
        self.at, self.local, self.pair_in = at, local, pair_in
        self.chain_in, self.chain_out, self.share, self.result = chain_in, chain_out, share, result
        self.backward = backward
        self.pair_send, self.pair_recv, self.chain_send, self.chain_recv = sems[:4]
        self.share_send, self.share_recv = sems[4:]
        self.half = local.shape[0] // 2
        self.size = result.shape[1]
        self.head = at.last if backward else at.first
        self.tail = at.first if backward else at.last
        self.onward = at.dp - 2 if backward else at.dp + 2

    def pair_copy(self):
        src = self.local.at[pl.ds((1 - self.at.p) * self.half, self.half)]
        return remote(
            src, self.pair_in, self.pair_send.at[0], self.pair_recv.at[0], {"dp": self.at.pair}
        )

    def chain_copy(self, i):
        return remote(
            self.chain_out.at[i],
            self.chain_in.at[i],
            self.chain_send.at[i],
            self.chain_recv.at[i],
            {"dp": self.onward},
        )

    def share_copy(self, i):
        return remote(
            self.share.at[i],
            self.result.at[self.at.p * self.half + i],
            self.share_send.at[i],
            self.share_recv.at[i],
            {"dp": self.at.pair},
        )

    def start(self):
        self.pair_copy().start()

    def run(self):
        at, size = self.at, self.size
        sooner = at.p == (1 if self.backward else 0)
        self.pair_copy().wait_recv()
        for i in range(self.half):
            mine = self.local[at.p * self.half + i].astype(F32)
            other = self.pair_in[i].astype(F32)
            one = jnp.where(sooner, mine, other)
            two = jnp.where(sooner, other, mine)
            state1, keep1 = one[:size], one[size : size + 1]
            state2, keep2 = two[:size], two[size : size + 1]

            @pl.when(self.head)
            def _():
                self.chain_in[i] = jnp.zeros(self.chain_in.shape[1:], BF16)

            @pl.when(jnp.logical_not(self.head))
            def _():
                self.chain_copy(i).wait_recv()

            before = self.chain_in[i].astype(F32)
            middle = keep1 * before + state1

            @pl.when(jnp.logical_not(self.tail))
            def _():
                self.chain_out[i] = (keep2 * middle + state2).astype(BF16)
                self.chain_copy(i).start()

            self.result[at.p * self.half + i] = jnp.where(sooner, before, middle).astype(BF16)
            self.share[i] = jnp.where(sooner, middle, before).astype(BF16)
            self.share_copy(i).start()

    def finish(self):
        at = self.at
        for i in range(self.half):
            remote(
                self.share.at[i],
                self.result.at[(1 - at.p) * self.half + i],
                self.share_send.at[i],
                self.share_recv.at[i],
                {"dp": at.pair},
            ).wait_recv()
            self.share_copy(i).wait_send()
            pl.when(jnp.logical_not(self.tail))(lambda: self.chain_copy(i).wait_send())
        self.pair_copy().wait_send()


def state_pass_scratch(half, size, width):
    dma = pltpu.SemaphoreType.DMA
    return [
        pltpu.VMEM((half, size + 16, width), BF16),
        pltpu.VMEM((half, size, width), BF16),
        pltpu.VMEM((half, size, width), BF16),
        pltpu.VMEM((half, size, width), BF16),
        dma((1,)),
        dma((1,)),
        dma((half,)),
        dma((half,)),
        dma((half,)),
        dma((half,)),
    ]


def packed_columns(layout, name):
    return pl.ds(*layout[name])


def span_row(rows, first, span):
    total = rows.shape[1]
    return pltpu.roll(rows, lax.rem(total - first, total), 1)[:, :span]


def shifted_column(row, before, back):
    span = row.shape[1]
    at, lane = iota((span, span), 0), iota((span, span), 1)
    now = jnp.where(lane == at - back, row, 0.0)
    earlier = jnp.where(lane == at - back + span, before, 0.0)
    return jnp.sum(now + earlier, 1, keepdims=True)


def mixer_kernel(cfg, *refs):
    (
        x_ref, og_in, gain_ref, q_in, kv_in, mi_in, st_in, sp_in, gu_in, ao_in, mo_in, seg_ref,
        rope_any, xt_ref, xb_ref, stt_ref, sb_ref, head_ref, mgain_ref,
        w_all, nx, og, low, kv, q2, probs, att, ext, pre, step_buf, entering, carry, y_buf, z_buf,
        squares, aux_ref, seg_rows,
        local, xs_buf, nxh, rope_ref, rope_sem, row_send, row_recv, kv_sems, halo_sems, sq_own,
        sq_got, sq_send, sq_recv,
        *rest,
    ) = refs
    devices, layout, pieces, heads = (cfg[k] for k in ("devices", "layout", "pieces", "heads"))
    at = Place(devices)
    seqs, sub, width = x_ref.shape
    span = sub * 4
    tokens = seqs * span
    depth = q_in.shape[0]
    xw = layout["x"][1]
    head_dim = xw // heads
    sw = layout["state"][1]
    size = sw // 2
    mixed = xw + sw
    qw = layout["q"][1]
    at_dim = qw // 2
    count = devices * span
    pass_refs, sems = rest[:10], rest[10:]
    own_rows = pl.ds(pl.multiple_of(at.dp * depth, depth), depth)
    rope_copy = pltpu.make_async_copy(
        rope_any.at[pl.ds(pl.multiple_of(at.dp * span, span), span), :], rope_ref, rope_sem
    )
    rope_copy.start()
    kv[...] = jnp.zeros(kv.shape, BF16)

    def own(name, value):
        w_all[own_rows, packed_columns(layout, name)] = value

    own("x", mi_in[:, 1, :])
    own("state", st_in[...])
    own("step", jnp.zeros((depth, LANES), BF16))
    w_all[own_rows, pl.ds(layout["step"][0], sp_in.shape[1])] = sp_in[...]
    Neighbours(at).greet()
    gathers = []
    for i, (first, columns, cross) in enumerate(pieces):

        def view(block, first=first, columns=columns):
            return w_all.at[
                pl.ds(pl.multiple_of(block * depth, depth), depth), pl.ds(first, columns)
            ]

        kind = CrossGather if cross else LineGather
        gathers.append(kind(at, view, *sems[4 * i : 4 * i + 4]))

    def step(i, s):
        if s < at.lines - 1:
            gathers[i].step(s)
        if s == 2:
            pl.loop(3, max(at.lines - 1, 3))(lambda k: gathers[i].step(k))

    gathers[0].start()
    gain = gain_ref[...].reshape(1, width)
    mine = pl.ds(pl.multiple_of(at.t * sub, sub), sub)
    for s in range(seqs):
        nx[s, mine, :] = rms_rows(x_ref[s].astype(F32), gain).astype(BF16)
    half = seqs // 2

    def rows_of(buf):
        def view(rank, chunk):
            return buf.at[pl.ds(chunk * half, half), pl.ds(pl.multiple_of(rank * sub, sub), sub), :]

        return view

    row_nx = RowGather(at, rows_of(nx), row_send.at[0], row_recv.at[0])
    row_og = RowGather(at, rows_of(og), row_send.at[1], row_recv.at[1])
    for chunk in range(2):
        row_nx.start(chunk)
    own("kv", jnp.where(at.t < 2, kv_in[:, 0, :], kv_in[:, 1, :]))
    own("q", q_in[...])
    own("z", mi_in[:, 0, :])
    gathers[1].start()
    out_at, gu_at = layout["out"][0], layout["gu"][0]
    w_all[own_rows, pl.ds(out_at, qw)] = ao_in[...].T
    w_all[own_rows, pl.ds(out_at + qw, xw)] = mo_in[...].T
    ff = gu_in.shape[2]
    w_all[own_rows, pl.ds(gu_at, ff)] = gu_in[:, 0, :]
    w_all[own_rows, pl.ds(gu_at + ff, ff)] = gu_in[:, 1, :]
    for s in range(seqs):
        og[s, mine, :] = og_in[s]
    before, after = at.dp > 0, at.dp < devices - 1
    seg = seg_ref[...].astype(F32)
    now = span_row(seg, at.dp * span, span)
    old = jnp.where(before, span_row(seg, jnp.maximum(at.dp - 1, 0) * span, span), -1.0)
    seg_rows[...] = jnp.zeros(seg_rows.shape, F32)
    seg_rows[0:seqs, :] = now
    for s in range(seqs):
        row, earlier = now[s : s + 1, :], old[s : s + 1, :]
        column = to_column(row)
        same = [(shifted_column(row, earlier, k) == column).astype(F32) for k in (1, 2, 3)]
        same.append((column == earlier[:, span - 1 :]).astype(F32))
        same.append((column == row[:, span - 1 :]).astype(F32))
        same.append(column)
        lane = iota((span, LANES), 1)
        total = jnp.zeros((span, LANES), F32)
        for k, value in enumerate(same):
            total = jnp.where(lane == k, value, total)
        aux_ref[s] = total
    for chunk in range(2):
        row_nx.forward(chunk)
    for chunk in range(2):
        row_nx.finish(chunk)
    for chunk in range(2):
        row_og.start(chunk)

    def halo():
        return remote(
            nx.at[:, pl.ds(span - 16, 16), :],
            nxh,
            halo_sems.at[0],
            halo_sems.at[1],
            {"dp": at.dp + 1},
        )

    pl.when(after)(lambda: halo().start())
    step(0, 0)
    step(0, 1)
    step(1, 0)
    step(0, 2)
    gathers[2].start()
    step(1, 1)
    for chunk in range(2):
        row_og.forward(chunk)
    pl.when(before)(lambda: halo().wait_recv())

    @pl.when(jnp.logical_not(before))
    def _():
        nxh[...] = jnp.zeros(nxh.shape, BF16)

    gathers[0].finish()
    rows = nx[...].reshape(tokens, width)
    rows_before = nxh[...].reshape(seqs * 16, width)

    def project(name):
        return dot_nn(rows, w_all[:, packed_columns(layout, name)])

    for name, first in (("x", 0), ("state", xw)):
        columns = layout[name][1]
        value = project(name).astype(BF16).astype(F32)
        ext[:, pl.ds(8, span), pl.ds(first, columns)] = value.reshape(seqs, span, columns)
        value = dot_nn(rows_before, w_all[:, packed_columns(layout, name)])
        value = value.astype(BF16).astype(F32).reshape(seqs, 16, columns)
        ext[:, pl.ds(0, 8), pl.ds(first, columns)] = value[:, 8:, :]
    step_buf[...] = project("step").reshape(seqs, span, LANES)
    taps = jnp.concatenate([xt_ref[...], stt_ref[...]], 1)
    tap_bias = jnp.concatenate([xb_ref[...].reshape(1, xw), sb_ref[...].reshape(1, sw)], 1)
    step_bias, decay_log, skips = head_ref[0:1, :], head_ref[1:2, :], head_ref[2:3, :]

    def scan_parts(s):
        return decay_parts(step_buf[s], decay_log, step_bias)

    @pl.loop(0, seqs)
    def _(s):
        aux = aux_ref[s]
        total = tap_bias + taps[3:4, :] * ext[s, pl.ds(8, span), :]
        for back in (1, 2, 3):
            moved = ext[s, pl.ds(8 - back, span), :] * aux[:, back - 1 : back]
            total = total + taps[3 - back : 4 - back, :] * moved
        pre[s] = total
        active = total * jax.nn.sigmoid(total)
        step, _, running = scan_parts(s)
        scaled = active[:, :xw] * spread(step, heads, head_dim)
        xs_buf[s] = scaled.astype(BF16)
        end = running[span - 1 : span, :]
        tail = spread(jnp.exp(end - running) * aux[:, 4:5], heads, head_dim)
        state_in = active[:, xw : xw + size].astype(BF16)
        local[s, :size, :] = dot_tn(state_in, (scaled * tail).astype(BF16)).astype(BF16)
        keep = jnp.broadcast_to(jnp.exp(end) * aux[span - 1 : span, 3:4], (16, LANES))
        keep = spread(keep, heads, head_dim).astype(BF16)
        local[s, size : size + 16, :] = keep
        carry[s] = keep

    passing = StatePass(
        at, local, pass_refs[0], pass_refs[1], pass_refs[2], pass_refs[3], entering,
        pass_refs[4:], False,
    )
    passing.start()
    step(1, 2)
    gathers[1].finish()
    rope_copy.wait()
    lane = iota((span, LANES), 1)
    cosine, sine = rope_ref[:, :LANES], rope_ref[:, LANES:]
    pairs = project("kv").reshape(seqs, span, qw)
    key_cosine = jnp.where(lane < at_dim, cosine, 1.0)
    key_sine = jnp.where(lane < at_dim, sine, 0.0)
    scale = 1.0 / math.sqrt(at_dim)
    for s in range(seqs):
        kv[at.dp, s] = turn(pairs[s], key_cosine, key_sine, at_dim // 2).astype(BF16)
    kv_gather = LineGather(
        at,
        lambda block: kv.at[block],
        kv_sems.at[0],
        kv_sems.at[1],
        kv_sems.at[2],
        kv_sems.at[3],
        causal=True,
    )
    kv_gather.start()
    queries = project("q").reshape(seqs, span, qw)
    for s in range(seqs):
        turned = turn(queries[s], cosine, sine, at_dim // 2) * scale
        q2[s, :span, :] = jnp.where(lane < at_dim, turned, 0.0).astype(BF16)
        turned = pltpu.roll(turned, at_dim, 1)
        q2[s, span:, :] = jnp.where(lane < at_dim, turned, 0.0).astype(BF16)
    gathers[2].begin() if pieces[2][2] else None
    step(2, 0)
    passing.run()
    gathers[3].start()
    z_buf[...] = project("z").astype(BF16).reshape(seqs, span, xw)
    kv_gather.step(0)
    step(2, 1)
    @pl.loop(0, seqs)
    def _(s):
        aux = aux_ref[s]
        active = pre[s] * jax.nn.sigmoid(pre[s])
        _, _, running = scan_parts(s)
        running_rows = running.T
        allowed = same_document(aux, seg_rows[pl.ds(s, 1), :])
        state_in = active[:, xw : xw + size].astype(BF16)
        state_out = active[:, xw + size :].astype(BF16)
        joined = dot_nt(state_out, state_in)
        blocks = []
        for h in range(heads):
            gap = running[:, h : h + 1] - running_rows[h : h + 1, :]
            weight = (joined * jnp.exp(gap + allowed)).astype(BF16)
            cols = pl.ds(h * head_dim // LANES * LANES, LANES)
            blocks.append(dot_nn(weight, xs_buf[s, :, cols]))
        y_buf[s] = pick_halves(blocks, head_dim) + spread(skips, heads, head_dim) * active[:, :xw]

    pl.loop(1, at.lines - 1)(lambda s: kv_gather.step(s))
    step(2, 2)
    step(3, 0)
    passing.finish()
    sq_own[...] = jnp.zeros(sq_own.shape, F32)
    for s in range(seqs):
        aux = aux_ref[s]
        state_out = pre[s, :, pl.ds(xw + size, size)]
        state_out = (state_out * jax.nn.sigmoid(state_out)).astype(BF16)
        _, _, running = scan_parts(s)
        factor = spread(jnp.exp(running) * aux[:, 3:4], heads, head_dim)
        y = y_buf[s] + dot_nn(state_out, entering[s]) * factor
        y_buf[s] = y
        gate = z_buf[s].astype(F32)
        gated = y * gate * jax.nn.sigmoid(gate)
        sq_own[s : s + 1, :] = to_row(jnp.sum(gated * gated, 1, keepdims=True))
    total = TensorTotal(at, sq_own, sq_got, sq_send, sq_recv)
    total.start()
    kv_gather.finish()
    step(3, 1)
    key_at = iota((span, count), 1)
    query_at = iota((span, count), 0) + at.dp * span
    causal = key_at <= query_at

    @pl.loop(0, seqs)
    def _(s):
        keys = kv[:, s].reshape(count, qw)
        row = seg_ref[pl.ds(s, 1), :].astype(F32)
        allowed = jnp.logical_and(aux_ref[s][:, 5:6] == row, causal)
        bias = jnp.where(allowed, 0.0, MASKED)
        outs = []
        for h in range(2):
            part = pl.ds(h * span, span)
            scores = dot_nt(q2[s, part, :], keys) + bias
            power = jnp.exp(scores - jnp.max(scores, 1, keepdims=True))
            weight = power * (1.0 / jnp.sum(power, 1, keepdims=True))
            weight = weight.astype(BF16)
            probs[s, part, :] = weight
            outs.append(dot_nn(weight, keys))
        att[s] = jnp.where(lane < at_dim, pltpu.roll(outs[0], at_dim, 1), outs[1])

    low[:, pl.ds(0, qw)] = att[...].reshape(tokens, qw).astype(BF16)
    squares[...] = total.finish()
    for s in range(seqs):
        gate = z_buf[s].astype(F32)
        gated = y_buf[s] * gate * jax.nn.sigmoid(gate)
        norm = lax.rsqrt(to_column(squares[s : s + 1, :]) / (4 * xw) + EPSILON)
        value = gated * norm * mgain_ref[...].reshape(1, xw)
        low[pl.ds(s * span, span), pl.ds(qw, xw)] = value.astype(BF16)
    for chunk in range(2):
        row_og.finish(chunk)
    step(3, 2)
    gathers[2].finish()
    gathers[3].finish()
    for gather in [*gathers, kv_gather]:
        gather.drain()
    for row in (row_nx, row_og):
        for chunk in range(2):
            row.drain(chunk)
    pl.when(after)(lambda: halo().wait_send())


def gather_sems(devices, pieces):
    dma = pltpu.SemaphoreType.DMA
    out = []
    for _, _, cross in pieces:
        out += [dma((devices,)) for _ in range(4)] if cross else line_gather_sems(devices)
    return out


def mixer(cfg, x, *args):
    devices, layout, pieces, heads = (cfg[k] for k in ("devices", "layout", "pieces", "heads"))
    seqs, sub, width = x.shape
    span = sub * 4
    tokens = seqs * span
    xw, sw, qw = (layout[k][1] for k in ("x", "state", "q"))
    size = sw // 2
    count = devices * span
    shape = jax.ShapeDtypeStruct
    vmem = pl.BlockSpec(memory_space=pltpu.VMEM)
    dma = pltpu.SemaphoreType.DMA
    outs = (
        shape((width, layout["down"][0]), BF16),
        shape((seqs, span, width), BF16),
        shape((seqs, span, width), BF16),
        shape((tokens, qw + xw), BF16),
        shape((devices, seqs, span, qw), BF16),
        shape((seqs, 2 * span, qw), BF16),
        shape((seqs, 2 * span, count), BF16),
        shape((seqs, span, qw), F32),
        shape((seqs, span + 8, xw + sw), F32),
        shape((seqs, span, xw + sw), F32),
        shape((seqs, span, LANES), F32),
        shape((seqs, size, xw), BF16),
        shape((seqs, 16, xw), BF16),
        shape((seqs, span, xw), F32),
        shape((seqs, span, xw), BF16),
        shape((8, span), F32),
        shape((seqs, span, LANES), F32),
        shape((8, span), F32),
    )
    in_specs = [vmem] * (1 + len(args))
    in_specs[12] = pl.BlockSpec(memory_space=pl.ANY)
    return pl.pallas_call(
        partial(mixer_kernel, cfg),
        out_shape=outs,
        in_specs=in_specs,
        out_specs=(vmem,) * len(outs),
        scratch_shapes=[
            pltpu.VMEM((seqs, size + 16, xw), BF16),
            pltpu.VMEM((seqs, span, xw), BF16),
            pltpu.VMEM((seqs, 16, width), BF16),
            pltpu.VMEM((span, 2 * LANES), F32),
            dma,
            dma((2, 2, 3)),
            dma((2, 2, 4)),
            dma((4, devices)),
            dma((2,)),
            pltpu.VMEM((8, span), F32),
            pltpu.VMEM((3, 8, span), F32),
            dma((3,)),
            dma((3,)),
        ]
        + state_pass_scratch(seqs // 2, size, xw)
        + gather_sems(devices, pieces),
        compiler_params=pltpu.CompilerParams(
            collective_id=0, has_side_effects=True, vmem_limit_bytes=VMEM_BYTES
        ),
        name="mixer",
    )(x, *args)


def back_kernel(cfg, *refs):
    (
        x_ref, gh_ref, gain_ref, w_any, nx_ref, og_ref, gb_ref, low_ref, nf_any, dgu_any, act_ref,
        kv_any, q2_ref, probs_any, att_ref, ext_ref, pre_ref, step_ref, entering, carry, y_ref,
        z_ref, squares, aux_ref, seg_ref, rope_any, xt_ref, stt_ref, head_ref, mgain_ref, fgain_ref,
        rg_ref, dw_ref, sums, kvs,
        w_ref, d_in, dlow, dy, dbc, dcum, ext_grad, halo_got, local2, after_state, keys_buf,
        prob_buf, dkv, dkv_got, dkv_line, dkv_own,
        part, near, far, grads, got, line, line2, small_near, small_far, small_dp, kv_near, kv_far,
        sq_own, sq_got,
        rope_ref, w_sem, early_sems, rope_sem, load_sems, halo_sems, sq_send, sq_recv, send, recv, small_send, small_recv,
        dp_send, dp_recv, kv_send, kv_recv,
        *rest,
    ) = refs
    devices, layout, pieces, heads = (cfg[k] for k in ("devices", "layout", "scatters", "heads"))
    at = Place(devices)
    seqs, sub, width = x_ref.shape
    span = sub * 4
    tokens = seqs * span
    half = seqs // 2
    rows = half * span
    depth = width // devices
    xw, sw, qw = (layout[k][1] for k in ("x", "state", "q"))
    size = sw // 2
    head_dim = xw // heads
    at_dim = qw // 2
    mixed = xw + sw
    count = devices * span
    in_w = layout["in"][1]
    pass_refs, kv_sems, sems = rest[:10], rest[10:16], rest[16:]
    load = pltpu.make_async_copy(w_any.at[:, pl.ds(0, w_ref.shape[1])], w_ref, w_sem)
    load.start()
    early = (
        pltpu.make_async_copy(nf_any, part, early_sems.at[0]),
        pltpu.make_async_copy(dgu_any, d_in.at[:, pl.ds(0, dgu_any.shape[1])], early_sems.at[1]),
    )
    for copy in early:
        copy.start()
    rope_copy = pltpu.make_async_copy(
        rope_any.at[pl.ds(pl.multiple_of(at.dp * span, span), span), :], rope_ref, rope_sem
    )
    rope_copy.start()

    slots = keys_buf.shape[0]

    def loads(s):
        slot = s % slots
        return (
            pltpu.make_async_copy(kv_any.at[:, s], keys_buf.at[slot], load_sems.at[0, slot]),
            pltpu.make_async_copy(probs_any.at[s], prob_buf.at[slot], load_sems.at[1, slot]),
        )

    for copy in loads(0):
        copy.start()
    Neighbours(at).greet(flips=True)
    taps = jnp.concatenate([xt_ref[...], stt_ref[...]], 1)
    step_bias, decay_log, skips = head_ref[0:1, :], head_ref[1:2, :], head_ref[2:3, :]
    mixer_scale = mgain_ref[...].reshape(1, xw)

    def rows_of(buf):
        def view(rank, chunk):
            return buf.at[pl.ds(chunk * half, half), pl.ds(pl.multiple_of(rank * sub, sub), sub), :]

        return view

    scatters = []
    used = 0
    slots_used = 0
    for first, columns, cross in pieces:

        def block(buf, k, first=first, columns=columns):
            return buf.at[pl.ds(pl.multiple_of(k * depth, depth), depth), pl.ds(first, columns)]

        if cross:
            wide = pl.ds(slots_used, columns)
            slots_used += columns
            scatters.append(
                CrossScatter(
                    at,
                    partial(block, grads),
                    block(got, 0),
                    lambda zz, q, wide=wide: line2.at[
                        pl.ds(pl.multiple_of((zz * 2 + q) * depth, depth), depth), wide
                    ],
                    sems[used : used + 5],
                )
            )
            used += 5
        else:
            scatters.append(
                LineScatter(
                    at,
                    partial(block, grads),
                    partial(block, got),
                    lambda zz, block=block: block(line, zz + 1),
                    partial(block, line),
                    sems[used : used + 6],
                )
            )
            used += 6

    def steps(i):
        @pl.loop(0, at.lines - 1)
        def _(s):
            scatters[i].step(s)

        if pieces[i][2]:
            scatters[i].join()

    def finish(i):
        first, columns, _ = pieces[i]
        scatters[i].finish(dw_ref.at[:, pl.ds(first, columns)])

    def product(lhs, rhs_ref, first, columns, into):
        tile = 2 * LANES if columns % (2 * LANES) == 0 else LANES

        @pl.loop(0, columns // tile)
        def _(j):
            src = pl.ds(pl.multiple_of(first + j * tile, LANES), tile)
            dst = pl.ds(pl.multiple_of(into + j * tile, LANES), tile)
            grads[:, dst] = dot_tn(lhs, rhs_ref[:, src]).astype(BF16)

    def weights(i, lhs_ref, rhs_ref, first):
        into, columns, _ = pieces[i]
        product(lhs_ref[...].reshape(tokens, width), rhs_ref, first, columns, into)

    ff = layout["down"][1]
    weights(0, og_ref, act_ref, 0)
    scatters[0].start()
    load.wait()
    dlow[...] = dot_nn(
        gb_ref[...].reshape(tokens, width), w_ref[:, pl.ds(*layout["out"])]
    )
    mixer_gain = jnp.zeros((1, xw), F32)
    sq_own[...] = jnp.zeros(sq_own.shape, F32)
    for s in range(seqs):
        gate = z_ref[s].astype(F32)
        gated = y_ref[s] * gate * jax.nn.sigmoid(gate)
        norm = lax.rsqrt(to_column(squares[s : s + 1, :]) / (4 * xw) + EPSILON)
        grad = dlow[pl.ds(s * span, span), pl.ds(qw, xw)]
        mixer_gain = mixer_gain + jnp.sum(grad * gated * norm, 0, keepdims=True)
        inner = jnp.sum(gated * grad * mixer_scale, 1, keepdims=True)
        sq_own[s : s + 1, :] = to_row(inner)
    total = TensorTotal(at, sq_own, sq_got, sq_send, sq_recv)
    total.start()
    for copy in early:
        copy.wait()
    weights(1, part, d_in, 0)
    weights(2, part, d_in, ff)
    inner_rows = total.finish()
    for s in range(seqs):
        gate = z_ref[s].astype(F32)
        sigmoid = jax.nn.sigmoid(gate)
        gated = y_ref[s] * gate * sigmoid
        norm = lax.rsqrt(to_column(squares[s : s + 1, :]) / (4 * xw) + EPSILON)
        inner = to_column(inner_rows[s : s + 1, :])
        term = dlow[pl.ds(s * span, span), pl.ds(qw, xw)] * mixer_scale
        grad = norm * (term - gated * (norm * norm * inner / (4 * xw)))
        dy[s] = grad * gate * sigmoid
        grad = grad * y_ref[s] * sigmoid * (1.0 + gate * (1.0 - sigmoid))
        d_in[pl.ds(s * span, span), pl.ds(*layout["z"])] = grad.astype(BF16)

    def parts(s):
        active = pre_ref[s] * jax.nn.sigmoid(pre_ref[s])
        step, rate, running = decay_parts(step_ref[s], decay_log, step_bias)
        state_in = active[:, xw : xw + size].astype(BF16)
        state_out = active[:, xw + size :].astype(BF16)
        return active[:, :xw], state_in, state_out, step, rate, running

    @pl.loop(0, seqs)
    def _(s):
        _, _, state_out, _, _, running = parts(s)
        factor = spread(jnp.exp(running) * aux_ref[s][:, 3:4], heads, head_dim)
        low = (dy[s] * factor).astype(BF16)
        local2[s, :size, :] = dot_tn(state_out, low).astype(BF16)
        local2[s, size:, :] = carry[s]

    passing = StatePass(
        at, local2, pass_refs[0], pass_refs[1], pass_refs[2], pass_refs[3], after_state,
        pass_refs[4:], True,
    )
    passing.start()
    scatters[1].start()
    weights(3, gb_ref, low_ref, 0)
    steps(0)
    @pl.loop(0, seqs)
    def _(s):
        x, state_in, state_out, step, _, running = parts(s)
        running_rows = running.T
        allowed = same_document(aux_ref[s], seg_ref[pl.ds(s, 1), :])
        xs = (x * spread(step, heads, head_dim)).astype(BF16)
        joined = dot_nt(state_out, state_in)
        lane = iota((span, LANES), 1)
        d_joined = jnp.zeros((span, span), F32)
        d_running = jnp.zeros((span, LANES), F32)
        blocks = []
        for h in range(heads):
            cols = slice(h * head_dim // LANES * LANES, h * head_dim // LANES * LANES + LANES)
            begin = h * head_dim % LANES
            inside = jnp.logical_and(lane >= begin, lane < begin + head_dim)
            grad = dy[s, :, pl.ds(cols.start, LANES)]
            decay = jnp.exp(running[:, h : h + 1] - running_rows[h : h + 1, :] + allowed)
            weight = joined * decay
            d_weight = dot_nt(jnp.where(inside, grad, 0.0).astype(BF16), xs[:, cols])
            d_joined = d_joined + d_weight * decay
            product_ = (d_weight * weight).astype(BF16)
            one = (lane == h).astype(BF16)
            d_running = d_running + dot_nn(product_, one) - dot_tn(product_, one)
            blocks.append(dot_tn(weight.astype(BF16), grad.astype(BF16)))
        dlow[pl.ds(pl.multiple_of(s * span, span), span), pl.ds(qw, xw)] = pick_halves(blocks, head_dim)
        d_joined = d_joined.astype(BF16)
        factor = spread(jnp.exp(running) * aux_ref[s][:, 3:4], heads, head_dim)
        crossed = dot_nn(state_out, entering[s]) * factor
        dcum[s] = d_running + head_sums(dy[s] * crossed, heads, head_dim)
        low = (dy[s] * factor).astype(BF16)
        dbc[s, :, :size] = dot_tn(d_joined, state_out)
        dbc[s, :, size:] = dot_nn(d_joined, state_in) + dot_nt(low, entering[s])

    passing.run()
    scatters[2].start()
    scatters[3].start()
    lane = iota((span, LANES), 1)
    upper = lane >= at_dim
    rope_copy.wait()
    cosine, sine = rope_ref[:, :LANES], rope_ref[:, LANES:]
    scale = 1.0 / math.sqrt(at_dim)
    for s in range(seqs):
        slot = s % slots
        for copy in loads(s):
            copy.wait()
        if slots > 1 and s + 1 < seqs:
            for copy in loads(s + 1):
                copy.start()
        keys = keys_buf[slot].reshape(count, qw)
        grad = dlow[pl.ds(s * span, span), pl.ds(0, qw)].astype(BF16).astype(F32)
        inner = grad * att_ref[s]
        d_keys = jnp.zeros((count, qw), F32)
        d_query = []
        for h in range(2):
            mine = upper if h else jnp.logical_not(upper)
            delta = jnp.sum(jnp.where(mine, inner, 0.0), 1, keepdims=True)
            moved = grad if h else pltpu.roll(grad, at_dim, 1)
            moved = jnp.where(upper, moved, 0.0).astype(BF16)
            weight = prob_buf[slot, pl.ds(h * span, span), :]
            d_weight = dot_nt(moved, keys)
            d_score = (weight.astype(F32) * (d_weight - delta)).astype(BF16)
            query = q2_ref[s, pl.ds(h * span, span), :]
            d_keys = d_keys + dot_tn(d_score, query) + dot_tn(weight, moved)
            d_query.append(dot_nn(d_score, keys))
        dkv[:, s] = d_keys.astype(BF16).reshape(devices, span, qw)
        if slots == 1 and s + 1 < seqs:
            for copy in loads(s + 1):
                copy.start()
        d_query = jnp.where(upper, pltpu.roll(d_query[1], at_dim, 1), d_query[0]) * scale
        d_in[pl.ds(s * span, span), pl.ds(*layout["q"])] = turn(
            d_query, cosine, -sine, at_dim // 2
        ).astype(BF16)
    kv_scatter = LineScatter(
        at,
        lambda k: dkv.at[k],
        lambda zz: dkv_got.at[zz],
        None,
        lambda zz: dkv_line.at[zz],
        kv_sems,
        causal=True,
    )
    kv_scatter.start()
    steps(1)
    finish(0)
    weights(4, nx_ref, d_in, pieces[4][0])
    scatters[4].start()
    passing.finish()
    tap_grads = [jnp.zeros((1, mixed), F32) for _ in range(4)]
    bias_grad = jnp.zeros((1, mixed), F32)
    step_grad = jnp.zeros((1, LANES), F32)
    decay_grad = jnp.zeros((1, LANES), F32)
    skip_grad = jnp.zeros((1, xw), F32)
    ext_grad[:, pl.ds(0, 8), :] = jnp.zeros((seqs, 8, mixed), F32)
    for s in range(seqs):
        aux = aux_ref[s]
        x, state_in, state_out, step, rate, running = parts(s)
        step_wide = spread(step, heads, head_dim)
        xs = x * step_wide
        end = running[span - 1 : span, :]
        tail = spread(jnp.exp(end - running) * aux[:, 4:5], heads, head_dim)
        later = after_state[s]
        found = dot_nn(state_in, later)
        weighted = xs * tail
        d_xs = dlow[pl.ds(s * span, span), pl.ds(qw, xw)] + found * tail
        d_in_state = dbc[s, :, :size] + dot_nt(weighted.astype(BF16), later)
        moved = head_sums(found * weighted, heads, head_dim)
        carried = jnp.sum(later.astype(F32) * entering[s].astype(F32), 0, keepdims=True)
        carried = head_sums(carried, heads, head_dim) * jnp.exp(end) * aux[span - 1 : span, 3:4]
        final = jnp.sum(moved, 0, keepdims=True) + carried
        d_running = dcum[s] - moved
        d_running = d_running + jnp.where(iota((span, LANES), 0) == span - 1, final, 0.0)
        d_decay = running_sum(d_running, backward=True)
        d_step = head_sums(d_xs * x, heads, head_dim) + d_decay * rate
        d_step = d_step * jax.nn.sigmoid(step_ref[s] + step_bias)
        d_in[pl.ds(s * span, span), pl.ds(*layout["step"])] = d_step.astype(BF16)
        step_grad = step_grad + jnp.sum(d_step, 0, keepdims=True)
        decay_grad = decay_grad + jnp.sum(d_decay * step, 0, keepdims=True) * rate
        skip_grad = skip_grad + jnp.sum(dy[s] * x, 0, keepdims=True)
        d_x = d_xs * step_wide + spread(skips, heads, head_dim) * dy[s]
        value = pre_ref[s]
        sigmoid = jax.nn.sigmoid(value)
        slope = sigmoid * (1.0 + value * (1.0 - sigmoid))
        outer = jnp.concatenate([d_x, d_in_state, dbc[s, :, size:]], 1) * slope
        bias_grad = bias_grad + jnp.sum(outer, 0, keepdims=True)
        ext_grad[s, pl.ds(8, span), :] = taps[3:4, :] * outer
        tap_grads[3] = tap_grads[3] + jnp.sum(
            outer * ext_ref[s, pl.ds(8, span), :], 0, keepdims=True
        )
        for back in (1, 2, 3):
            valid = outer * aux[:, back - 1 : back]
            tap_grads[3 - back] = tap_grads[3 - back] + jnp.sum(
                valid * ext_ref[s, pl.ds(8 - back, span), :], 0, keepdims=True
            )
            ext_grad[s, pl.ds(8 - back, span), :] += taps[3 - back : 4 - back, :] * valid
    before, after = at.dp > 0, at.dp < devices - 1

    def halo():
        return remote(
            ext_grad.at[:, pl.ds(0, 8), :],
            halo_got,
            halo_sems.at[0],
            halo_sems.at[1],
            {"dp": at.dp - 1},
        )

    pl.when(before)(lambda: halo().start())
    sums[...] = jnp.zeros(sums.shape, F32)
    sums[1:2, :] = fgain_ref[...]
    for k in range(4):
        sums[2 + k : 3 + k, pl.ds(0, sw)] = tap_grads[k][:, xw:]
        sums[8 + k : 9 + k, pl.ds(0, xw)] = tap_grads[k][:, :xw]
    sums[6:7, pl.ds(0, sw)] = bias_grad[:, xw:]
    sums[12:13, pl.ds(0, xw)] = bias_grad[:, :xw]
    sums[13:14, pl.ds(0, xw)] = mixer_gain
    sums[14:15, pl.ds(0, LANES)] = step_grad
    sums[14:15, pl.ds(LANES, LANES)] = decay_grad
    sums[14:15, pl.ds(2 * LANES, LANES)] = head_sums(
        jnp.broadcast_to(skip_grad, (8, xw)), heads, head_dim
    )[:1]
    steps(2)
    kv_scatter.run_causal(dkv_own)
    for s in range(seqs):
        key_cosine = jnp.where(upper, 1.0, cosine)
        key_sine = jnp.where(upper, 0.0, -sine)
        d_in[pl.ds(s * span, span), pl.ds(*layout["kv"])] = turn(
            dkv_own[s], key_cosine, key_sine, at_dim // 2
        ).astype(BF16)
    pl.when(after)(lambda: halo().wait_recv())
    ends = pl.ds(span, 8)

    @pl.when(after)
    def _():
        ext_grad[:, ends, :] += halo_got[...]

    value = ext_grad[:, pl.ds(8, span), :].reshape(tokens, mixed).astype(BF16)
    d_in[:, pl.ds(layout["x"][0], mixed)] = value
    back = RowScatter(
        at,
        rows_of(part),
        lambda which, chunk: near.at[which, pl.ds(chunk * half, half)],
        lambda chunk: far.at[pl.ds(chunk * half, half)],
        send,
        recv,
    )
    weights(5, nx_ref, d_in, pieces[5][0])
    scatters[5].start()
    back = RowScatter(
        at,
        rows_of(part),
        lambda which, chunk: near.at[which, pl.ds(chunk * half, half)],
        lambda chunk: far.at[pl.ds(chunk * half, half)],
        send,
        recv,
    )
    for c in range(2):
        value = dot_nt(d_in[pl.ds(c * rows, rows), :], w_ref[:, pl.ds(0, in_w)])
        part[pl.ds(c * half, half)] = value.astype(BF16).reshape(half, span, width)
        back.start(c)
    weights(6, nx_ref, d_in, pieces[6][0])
    scatters[6].start()
    steps(3)
    finish(1)
    for c in range(2):
        back.middle(c)
    steps(4)
    finish(2)
    total = jnp.zeros((1, width), F32)
    gain = gain_ref[...].reshape(1, width)
    for c in range(2):
        seq = pl.ds(c * half, half)
        grad, terms = rms_rows_grad(x_ref[seq].astype(F32), gain, back.finish(c))
        rg_ref[seq] = gh_ref[seq] + grad
        total = total + jnp.sum(terms.reshape(half * sub, width), 0, keepdims=True)
    sums[0:1, :] = total
    exchanges = [
        (sums.at[pl.ds(0, 8)], small_near, small_send.at[0], small_recv.at[0], {"tensor": at.t_near}),
        (sums.at[pl.ds(0, 8)], small_far, small_send.at[1], small_recv.at[1], {"tensor": at.t_far}),
    ] + [
        (sums, small_dp.at[i], dp_send.at[i], dp_recv.at[i], {"dp": other})
        for i, other in enumerate(at.flips())
    ]

    def begin(i):
        remote(*exchanges[i]).start()

    def end(i):
        remote(*exchanges[i]).wait()
        into, other = exchanges[i][:2]
        into[...] += other[...]

    begin(0)
    finish(3)
    end(0)
    begin(1)
    steps(5)
    end(1)
    begin(2)
    finish(4)
    end(2)
    begin(3)
    steps(6)
    end(3)
    finish(5)
    kvw = layout["kv"][1]
    kv_near[0, :, pl.ds(0, kvw)] = dw_ref[:, pl.ds(*layout["kv"])]
    kv_near[0, :, pl.ds(kvw, sw)] = dw_ref[:, pl.ds(*layout["state"])]
    copy = remote(kv_near.at[0], kv_near.at[1], kv_send.at[0], kv_recv.at[0], {"tensor": at.t_near})
    copy.start()
    begin(4)
    finish(6)
    copy.wait()
    kv_far[0] = kv_near[0] + kv_near[1]
    copy = remote(kv_far.at[0], kv_far.at[1], kv_send.at[1], kv_recv.at[1], {"tensor": at.t_far})
    copy.start()
    end(4)
    for i in range(5, len(exchanges)):
        begin(i)
        end(i)
    copy.wait()
    kvs[:, pl.ds(0, kvw)] = kv_far[0, :, pl.ds(0, kvw)]
    kvs[:, pl.ds(kvw, kvw)] = kv_far[1, :, pl.ds(0, kvw)]

    @pl.when(at.t >= 2)
    def _():
        kvs[:, pl.ds(0, kvw)] = kv_far[1, :, pl.ds(0, kvw)]
        kvs[:, pl.ds(kvw, kvw)] = kv_far[0, :, pl.ds(0, kvw)]

    kvs[:, pl.ds(2 * kvw, sw)] = kv_far[0, :, pl.ds(kvw, sw)] + kv_far[1, :, pl.ds(kvw, sw)]
    for scatter in [*scatters, kv_scatter]:
        scatter.drain()
    for c in range(2):
        back.drain(c)
    pl.when(before)(lambda: halo().wait_send())


def scatter_sems(devices, pieces):
    dma = pltpu.SemaphoreType.DMA
    out = []
    for _, _, cross in pieces:
        if cross:
            out += [dma((2,))] + [dma((devices,)) for _ in range(4)]
        else:
            out += line_scatter_sems(devices)
    return out


def backward(cfg, x, *args):
    devices, layout, pieces, heads = (cfg[k] for k in ("devices", "layout", "scatters", "heads"))
    seqs, sub, width = x.shape
    span = sub * 4
    tokens = seqs * span
    half = seqs // 2
    depth = width // devices
    lines = devices // 2
    columns = layout["down"][0] + layout["down"][1]
    xw, sw, qw, kvw = (layout[k][1] for k in ("x", "state", "q", "kv"))
    size = sw // 2
    mixed = xw + sw
    in_w = layout["in"][1]
    own = (seqs, sub, width)
    rounds = devices.bit_length() - 1
    crossed = max(LANES, sum(piece[1] for piece in pieces if piece[2]))
    slots = 2 if devices * span <= 2048 else 1
    shape = jax.ShapeDtypeStruct
    vmem = pl.BlockSpec(memory_space=pltpu.VMEM)
    hbm = pl.BlockSpec(memory_space=pl.ANY)
    dma = pltpu.SemaphoreType.DMA
    in_specs = [vmem] * (1 + len(args))
    for i in (3, 8, 9, 11, 13, 25):
        in_specs[i] = hbm
    return pl.pallas_call(
        partial(back_kernel, cfg),
        out_shape=(
            shape(own, F32),
            shape((depth, columns), F32),
            shape((16, width), F32),
            shape((depth, 2 * kvw + sw), F32),
        ),
        in_specs=in_specs,
        out_specs=(vmem,) * 4,
        scratch_shapes=[
            pltpu.VMEM((width, in_w + qw + xw), BF16),
            pltpu.VMEM((tokens, in_w), BF16),
            pltpu.VMEM((tokens, qw + xw), F32),
            pltpu.VMEM((seqs, span, xw), F32),
            pltpu.VMEM((seqs, span, sw), F32),
            pltpu.VMEM((seqs, span, LANES), F32),
            pltpu.VMEM((seqs, span + 8, mixed), F32),
            pltpu.VMEM((seqs, 8, mixed), F32),
            pltpu.VMEM((seqs, size + 16, xw), BF16),
            pltpu.VMEM((seqs, size, xw), BF16),
            pltpu.VMEM((slots, devices, span, qw), BF16),
            pltpu.VMEM((slots, 2 * span, devices * span), BF16),
            pltpu.VMEM((devices, seqs, span, qw), BF16),
            pltpu.VMEM((lines, seqs, span, qw), BF16),
            pltpu.VMEM((lines, seqs, span, qw), BF16),
            pltpu.VMEM((seqs, span, qw), F32),
            pltpu.VMEM((seqs, span, width), BF16),
            pltpu.VMEM((2,) + own, BF16),
            pltpu.VMEM(own, BF16),
            pltpu.VMEM((width, columns), BF16),
            pltpu.VMEM((lines * depth, columns), BF16),
            pltpu.VMEM(((lines + 1) * depth, columns), BF16),
            pltpu.VMEM(((lines + 1) * 2 * depth, crossed), BF16),
            pltpu.VMEM((8, width), F32),
            pltpu.VMEM((8, width), F32),
            pltpu.VMEM((rounds, 16, width), F32),
            pltpu.VMEM((2, depth, kvw + sw), F32),
            pltpu.VMEM((2, depth, kvw + sw), F32),
            pltpu.VMEM((8, span), F32),
            pltpu.VMEM((3, 8, span), F32),
            pltpu.VMEM((span, 2 * LANES), F32),
            dma,
            dma((2,)),
            dma,
            dma((2, 2)),
            dma((2,)),
            dma((3,)),
            dma((3,)),
            dma((2, 3)),
            dma((2, 4)),
            dma((2,)),
            dma((2,)),
            dma((rounds,)),
            dma((rounds,)),
            dma((2,)),
            dma((2,)),
        ]
        + state_pass_scratch(half, size, xw)
        + line_scatter_sems(devices)
        + scatter_sems(devices, pieces),
        compiler_params=pltpu.CompilerParams(
            collective_id=2, has_side_effects=True, vmem_limit_bytes=VMEM_BYTES
        ),
        name="backward",
    )(x, *args)


def unpack_kernel(layout, local, *refs):
    (
        dw, kvs, sums, rg, block,
        block_out, rg_out, gain1, gain2, wq, wkv, wao, wmi, wst, wsp, cw, cb, csw, csb, sbias,
        dlog, skip, mgain, wmo, wgu, wdn,
    ) = refs
    block_out[...] = block[...]
    rg_out[...] = rg[...]
    width = sums.shape[1]
    xw, sw = layout["x"][1], layout["state"][1]
    qw = layout["q"][1]
    ff = layout["down"][1]
    kvw = layout["kv"][1]

    def part(name):
        return dw[:, pl.ds(*layout[name])]

    gain1[...] = sums[0:1, :].reshape(width)
    gain2[...] = sums[1:2, :].reshape(width)
    wq[...] = part("q")
    wkv[:, 0, :] = kvs[:, :kvw]
    wkv[:, 1, :] = kvs[:, kvw : 2 * kvw]
    out = part("out")
    wao[...] = out[:, :qw].T
    wmo[...] = out[:, qw:].T
    wdn[...] = part("down").T
    wmi[:, 0, :] = part("z")
    wmi[:, 1, :] = part("x")
    wst[...] = kvs[:, 2 * kvw :]
    wsp[...] = part("step")[:, :local]
    gate_up = part("gu")
    wgu[:, 0, :] = gate_up[:, :ff]
    wgu[:, 1, :] = gate_up[:, ff:]
    cw[...] = sums[8:12, :xw]
    cb[...] = sums[12:13, :xw].reshape(xw)
    csw[...] = sums[2:6, :sw]
    csb[...] = sums[6:7, :sw].reshape(sw)
    sbias[...] = sums[14:15, :local].reshape(local)
    dlog[...] = sums[14:15, LANES : LANES + local].reshape(local)
    skip[...] = sums[14:15, 2 * LANES : 2 * LANES + local].reshape(local)
    mgain[...] = sums[13:14, :xw].reshape(xw)


def unpack(layout, local, dw, kvs, sums, rg, block):
    depth = dw.shape[0]
    width = sums.shape[1]
    xw, sw, qw, ff, kvw = (layout[k][1] for k in ("x", "state", "q", "down", "kv"))

    def shape(*dims):
        return jax.ShapeDtypeStruct(dims, F32)

    outs = (
        jax.ShapeDtypeStruct(block.shape, BF16),
        shape(*rg.shape),
        shape(width),
        shape(width),
        shape(depth, qw),
        shape(depth, 2, kvw),
        shape(qw, depth),
        shape(depth, 2, xw),
        shape(depth, sw),
        shape(depth, local),
        shape(4, xw),
        shape(xw),
        shape(4, sw),
        shape(sw),
        shape(local),
        shape(local),
        shape(local),
        shape(xw),
        shape(xw, depth),
        shape(depth, 2, ff),
        shape(ff, depth),
    )
    vmem = pl.BlockSpec(memory_space=pltpu.VMEM)
    return pl.pallas_call(
        partial(unpack_kernel, layout, local),
        out_shape=outs,
        in_specs=[vmem] * 5,
        out_specs=(vmem,) * len(outs),
        name="unpack",
    )(dw, kvs, sums, rg, block)


def rope_table(length, head_dim):
    half = head_dim // 2
    frequency = np.exp(-math.log(ROTARY_BASE) * 2.0 * np.arange(half) / head_dim)
    angle = np.arange(length)[:, None] * frequency[None, :]
    cosine, sine = np.cos(angle), np.sin(angle)
    copies = LANES // head_dim
    table = [cosine, cosine] * copies + [-sine, sine] * copies
    return np.concatenate(table, 1).astype(np.float32)


def body(
    resid_in,
    segment_ids,
    out_grad,
    input_gain,
    ffn_gain,
    query_weight,
    keyvalue_weight,
    attention_output_weight,
    mixer_input_weight,
    state_input_weight,
    step_weight,
    conv_mixer,
    conv_mixer_bias,
    conv_state,
    conv_state_bias,
    step_bias,
    decay_log,
    skip_gain,
    mixer_gain,
    mixer_output_weight,
    gate_up_weight,
    down_weight,
):
    tensor_count = lax.axis_size("tensor")
    shard_count = lax.axis_size("dp")
    head_dim = keyvalue_weight.shape[2] // 2
    query_width = query_weight.shape[1]
    mixer_local = step_weight.shape[1]
    mixer_width = conv_mixer.shape[1]
    state_width = state_input_weight.shape[1]
    ff = down_weight.shape[0]
    layout = {}
    columns = 0
    for name, size in (
        ("x", mixer_width),
        ("state", state_width),
        ("step", LANES),
        ("kv", 2 * head_dim),
        ("q", query_width),
        ("z", mixer_width),
        ("out", query_width + mixer_width),
        ("gu", 2 * ff),
        ("down", ff),
    ):
        layout[name] = (columns, size)
        columns += size
    layout["in"] = (0, layout["out"][0])
    kv_at, q_at, gu_at = (layout[k][0] for k in ("kv", "q", "gu"))
    config = {
        "devices": shard_count,
        "layout": layout,
        "heads": mixer_local,
        "pieces": (
            (0, kv_at, False),
            (kv_at, layout["out"][0] - kv_at, False),
            (*layout["out"], True),
            (*layout["gu"], False),
        ),
        "scatters": (
            (*layout["down"], False),
            (gu_at, ff, False),
            (gu_at + ff, ff, False),
            (*layout["out"], True),
            (q_at, layout["out"][0] - q_at, False),
            (layout["state"][0], q_at - layout["state"][0], False),
            (*layout["x"], False),
        ),
    }

    def lanes(array):
        return jnp.pad(array, (0, LANES - array.shape[0]))

    head_rows = jnp.stack([lanes(step_bias), lanes(decay_log), lanes(skip_gain)])
    rope = jnp.asarray(rope_table(segment_ids.shape[1], head_dim))
    (
        w_all, span_normed_input, span_gradient, branch_low, keys, queries, probs, attention, ext,
        pre, step_pre, entering, state_decay, mixer_y, gate_z, squares, aux, seg_rows,
    ) = mixer(
        config,
        resid_in,
        out_grad,
        input_gain,
        query_weight,
        keyvalue_weight,
        mixer_input_weight,
        state_input_weight,
        step_weight,
        gate_up_weight,
        attention_output_weight,
        mixer_output_weight,
        segment_ids,
        rope,
        conv_mixer,
        conv_mixer_bias,
        conv_state,
        conv_state_bias,
        head_rows,
        mixer_gain,
    )
    block_out, grad_hidden, grad_branch, span_feedforward, activated, grad_gate_up, ffn_gain_part = (
        feed_forward(
            shard_count,
            tensor_count,
            layout,
            resid_in,
            branch_low,
            span_gradient,
            out_grad,
            ffn_gain,
            w_all,
            down_weight,
        )
    )
    resid_grad, weight_grads, sums, replicated = backward(
        config,
        resid_in,
        grad_hidden,
        input_gain,
        w_all,
        span_normed_input,
        span_gradient,
        grad_branch,
        branch_low,
        span_feedforward,
        grad_gate_up,
        activated,
        keys,
        queries,
        probs,
        attention,
        ext,
        pre,
        step_pre,
        entering,
        state_decay,
        mixer_y,
        gate_z,
        squares,
        aux,
        seg_rows,
        rope,
        conv_mixer,
        conv_state,
        head_rows,
        mixer_gain,
        ffn_gain_part,
    )
    return unpack(layout, mixer_local, weight_grads, replicated, sums, resid_grad, block_out)


def solution(mesh):
    placed = (
        P(None, ("dp", "tensor"), None),
        P(),
        P(None, ("dp", "tensor"), None),
        P(),
        P(),
        P("dp", "tensor"),
        P("dp", None, None),
        P("tensor", "dp"),
        P("dp", None, "tensor"),
        P("dp", None),
        P("dp", "tensor"),
        P(None, "tensor"),
        P("tensor"),
        P(),
        P(),
        P("tensor"),
        P("tensor"),
        P("tensor"),
        P("tensor"),
        P("tensor", "dp"),
        P("dp", None, "tensor"),
        P("tensor", "dp"),
    )
    return jax.shard_map(
        body,
        mesh=mesh,
        in_specs=placed,
        out_specs=(
            P(None, ("dp", "tensor"), None),
            P(None, ("dp", "tensor"), None),
            P(),
            P(),
            P("dp", "tensor"),
            P("dp", None, None),
            P("tensor", "dp"),
            P("dp", None, "tensor"),
            P("dp", None),
            P("dp", "tensor"),
            P(None, "tensor"),
            P("tensor"),
            P(),
            P(),
            P("tensor"),
            P("tensor"),
            P("tensor"),
            P("tensor"),
            P("tensor", "dp"),
            P("dp", None, "tensor"),
            P("tensor", "dp"),
        ),
        check_vma=False,
    )
```

```python
from functools import partial
import math

import jax
import jax.numpy as jnp
import numpy as np
from jax import lax
from jax.experimental import pallas as pl
from jax.experimental.pallas import tpu as pltpu
from jax.sharding import PartitionSpec as P

KVH = 2
EPSILON = 1e-05
ROTARY_BASE = 100000000000.0
MASKED = -1e30
MATMUL_EXACTNESS = lax.Precision.HIGHEST
LANES = 128
F32 = jnp.float32
BF16 = jnp.bfloat16
VMEM_BYTES = 63 * 2**20
JOINED_TOKENS = 4096


def dot_nn(a, b):
    return lax.dot_general(a, b, (((1,), (0,)), ((), ())), preferred_element_type=F32)


def dot_nt(a, b):
    return lax.dot_general(a, b, (((1,), (1,)), ((), ())), preferred_element_type=F32)


def dot_tn(a, b):
    return lax.dot_general(a, b, (((0,), (0,)), ((), ())), preferred_element_type=F32)


def remote(src, dst, send_sem, recv_sem, where):
    return pltpu.make_async_remote_copy(
        src_ref=src,
        dst_ref=dst,
        send_sem=send_sem,
        recv_sem=recv_sem,
        device_id=where,
        device_id_type=pl.DeviceIdType.MESH,
    )


def add_into(ref, *others):
    total = ref[...].astype(F32)
    for other in others:
        total = total + other[...].astype(F32)
    ref[...] = total.astype(BF16)


class Place:
    def __init__(self, devices):
        self.devices = devices
        self.lines = devices // 2
        self.dp = lax.axis_index("dp")
        self.t = lax.axis_index("tensor")
        self.z = lax.div(self.dp, 2)
        self.p = lax.rem(self.dp, 2)
        self.pair = self.dp + 1 - 2 * self.p
        self.t_near = self.t + 1 - 2 * lax.rem(self.t, 2)
        self.t_far = lax.rem(self.t + 2, 4)
        self.t_both = lax.rem(self.t_near + 2, 4)
        self.first = self.z == 0
        self.last = self.z == self.lines - 1

    def flips(self):
        bit = 1
        while bit < self.devices:
            yield self.dp + bit - 2 * bit * lax.rem(lax.div(self.dp, bit), 2)
            bit *= 2


class LineGather:
    def __init__(self, place, view, recv, right, left, pair, causal=False):
        self.at, self.view = place, view
        self.causal = causal
        self.recv, self.right, self.left, self.side = recv, right, left, pair

    def copy(self, block, sem, where):
        ref = self.view(block)
        return remote(ref, ref, sem, self.recv.at[block], where)

    def send_right(self, zz):
        return self.copy(zz * 2 + self.at.p, self.right.at[zz], {"dp": self.at.dp + 2})

    def send_left(self, zz):
        return self.copy(zz * 2 + self.at.p, self.left.at[zz], {"dp": self.at.dp - 2})

    def send_pair(self, zz):
        return self.copy(zz * 2 + self.at.p, self.side.at[zz], {"dp": self.at.pair})

    def arrived(self, block):
        self.copy(block, self.side.at[0], {"dp": self.at.pair}).wait_recv()

    def start(self):
        at = self.at
        pl.when(jnp.logical_not(at.last))(lambda: self.send_right(at.z).start())
        if not self.causal:
            pl.when(jnp.logical_not(at.first))(lambda: self.send_left(at.z).start())
        self.send_pair(at.z).start()

    def step(self, s):
        at = self.at
        low, high = at.z - 1 - s, at.z + 1 + s

        @pl.when(low >= 0)
        def _():
            self.arrived(low * 2 + at.p)
            pl.when(jnp.logical_not(at.last))(lambda: self.send_right(low).start())
            self.send_pair(low).start()

        if self.causal:
            return

        @pl.when(high < at.lines)
        def _():
            self.arrived(high * 2 + at.p)
            pl.when(jnp.logical_not(at.first))(lambda: self.send_left(high).start())
            self.send_pair(high).start()

    def finish(self):
        at = self.at

        @pl.loop(0, at.z + 1 if self.causal else at.lines)
        def _(zz):
            self.arrived(zz * 2 + 1 - at.p)

    def drain(self):
        at = self.at

        @pl.loop(0, at.z + 1 if self.causal else at.lines)
        def _(zz):
            self.send_pair(zz).wait_send()

            @pl.when(jnp.logical_and(zz <= at.z, jnp.logical_not(at.last)))
            def _():
                self.send_right(zz).wait_send()

            if self.causal:
                return

            @pl.when(jnp.logical_and(zz >= at.z, jnp.logical_not(at.first)))
            def _():
                self.send_left(zz).wait_send()


class CrossGather:
    def __init__(self, place, view, recv, right, left, pair):
        self.at, self.view = place, view
        self.recv, self.right, self.left, self.side = recv, right, left, pair

    def copy(self, block, sem, where):
        ref = self.view(block)
        return remote(ref, ref, sem, self.recv.at[block], where)

    def send_right(self, block):
        return self.copy(block, self.right.at[block], {"dp": self.at.dp + 2})

    def send_left(self, block):
        return self.copy(block, self.left.at[block], {"dp": self.at.dp - 2})

    def send_pair(self):
        return self.copy(self.at.dp, self.side.at[0], {"dp": self.at.pair})

    def arrived(self, block):
        self.copy(block, self.side.at[0], {"dp": self.at.pair}).wait_recv()

    def onward(self, block, right, left):
        at = self.at
        if right:
            pl.when(jnp.logical_not(at.last))(lambda: self.send_right(block).start())
        if left:
            pl.when(jnp.logical_not(at.first))(lambda: self.send_left(block).start())

    def start(self):
        self.send_pair().start()
        self.onward(self.at.dp, True, True)

    def begin(self):
        self.arrived(self.at.pair)
        self.onward(self.at.pair, True, True)

    def step(self, s):
        at = self.at
        low, high = at.z - 1 - s, at.z + 1 + s
        for q in (at.p, 1 - at.p):

            @pl.when(low >= 0)
            def _():
                self.arrived(low * 2 + q)
                self.onward(low * 2 + q, True, False)

            @pl.when(high < at.lines)
            def _():
                self.arrived(high * 2 + q)
                self.onward(high * 2 + q, False, True)

    def finish(self):
        pass

    def drain(self):
        at = self.at
        self.send_pair().wait_send()

        @pl.loop(0, at.devices)
        def _(block):
            zz = lax.div(block, 2)

            @pl.when(jnp.logical_and(zz <= at.z, jnp.logical_not(at.last)))
            def _():
                self.send_right(block).wait_send()

            @pl.when(jnp.logical_and(zz >= at.z, jnp.logical_not(at.first)))
            def _():
                self.send_left(block).wait_send()


class LineScatter:
    def __init__(self, place, part, got, right, left, sems, causal=False):
        self.at, self.part = place, part
        self.got, self.right, self.left = got, right, left
        self.causal = causal
        (
            self.pair_send,
            self.pair_recv,
            self.right_send,
            self.right_recv,
            self.left_send,
            self.left_recv,
        ) = sems

    def pair_copy(self, zz):
        src = self.part(zz * 2 + 1 - self.at.p)
        return remote(
            src, self.got(zz), self.pair_send.at[zz], self.pair_recv.at[zz], {"dp": self.at.pair}
        )

    def right_copy(self, zz):
        src = self.part(zz * 2 + self.at.p)
        return remote(
            src,
            self.right(zz),
            self.right_send.at[zz],
            self.right_recv.at[zz],
            {"dp": self.at.dp + 2},
        )

    def left_copy(self, zz):
        src = self.part(zz * 2 + self.at.p)
        return remote(
            src, self.left(zz), self.left_send.at[zz], self.left_recv.at[zz], {"dp": self.at.dp - 2}
        )

    def start(self):
        at = self.at

        @pl.loop(0, at.z + 1 if self.causal else at.lines)
        def _(i):
            self.pair_copy(i if self.causal else at.lines - 1 - i).start()

    def step(self, i):
        at = self.at
        high, low = at.lines - 1 - i, i
        if self.causal:
            self.step_low(low)
            return

        @pl.when(at.z < at.lines // 2)
        def _():
            self.step_high(high)
            self.step_low(low)

        @pl.when(at.z >= at.lines // 2)
        def _():
            self.step_low(low)
            self.step_high(high)

    def step_high(self, high):
        at = self.at

        @pl.when(high > at.z)
        def _():
            self.pair_copy(high).wait_recv()
            ref = self.part(high * 2 + at.p)

            @pl.when(at.first)
            def _():
                add_into(ref, self.got(high))

            @pl.when(jnp.logical_not(at.first))
            def _():
                self.right_copy(high).wait_recv()
                add_into(ref, self.got(high), self.right(high))

            self.right_copy(high).start()

    def step_low(self, low):
        at = self.at

        @pl.when(low < at.z)
        def _():
            self.pair_copy(low).wait_recv()
            ref = self.part(low * 2 + at.p)

            @pl.when(at.last)
            def _():
                add_into(ref, self.got(low))

            @pl.when(jnp.logical_not(at.last))
            def _():
                self.left_copy(low).wait_recv()
                add_into(ref, self.got(low), self.left(low))

            self.left_copy(low).start()

    def finish(self, out):
        at = self.at
        self.pair_copy(at.z).wait_recv()
        out[...] = self.part(at.dp)[...].astype(F32) + self.got(at.z)[...].astype(F32)

        if not self.causal:

            @pl.when(jnp.logical_not(at.first))
            def _():
                self.right_copy(at.z).wait_recv()
                out[...] += self.right(at.z)[...].astype(F32)

        @pl.when(jnp.logical_not(at.last))
        def _():
            self.left_copy(at.z).wait_recv()
            out[...] += self.left(at.z)[...].astype(F32)

    def drain(self):
        at = self.at

        @pl.loop(0, at.z + 1 if self.causal else at.lines)
        def _(zz):
            self.pair_copy(zz).wait_send()
            if not self.causal:
                pl.when(zz > at.z)(lambda: self.right_copy(zz).wait_send())
            pl.when(zz < at.z)(lambda: self.left_copy(zz).wait_send())

    def run_causal(self, out):
        @pl.loop(0, self.at.lines - 1)
        def _(s):
            self.step(s)

        self.finish(out)


class CrossScatter:
    def __init__(self, place, part, got, line, sems):
        self.at, self.part, self.got, self.line = place, part, got, line
        self.pair_send, self.pair_recv = sems[0].at[0], sems[0].at[1]
        self.right_send, self.right_recv, self.left_send, self.left_recv = sems[1:]

    def right_copy(self, zz, q):
        block = zz * 2 + q
        return remote(
            self.part(block),
            self.line(zz + 1, q),
            self.right_send.at[block],
            self.right_recv.at[block],
            {"dp": self.at.dp + 2},
        )

    def left_copy(self, zz, q):
        block = zz * 2 + q
        return remote(
            self.part(block),
            self.line(zz, q),
            self.left_send.at[block],
            self.left_recv.at[block],
            {"dp": self.at.dp - 2},
        )

    def pair_copy(self):
        return remote(
            self.part(self.at.pair), self.got, self.pair_send, self.pair_recv, {"dp": self.at.pair}
        )

    def start(self):
        pass

    def step(self, i):
        at = self.at
        high, low = at.lines - 1 - i, i

        @pl.when(at.z < at.lines // 2)
        def _():
            self.step_high(high)
            self.step_low(low)

        @pl.when(at.z >= at.lines // 2)
        def _():
            self.step_low(low)
            self.step_high(high)

    def step_high(self, high):
        at = self.at

        @pl.when(high > at.z)
        def _():
            for q in (1 - at.p, at.p):

                @pl.when(jnp.logical_not(at.first))
                def _():
                    self.right_copy(high, q).wait_recv()
                    add_into(self.part(high * 2 + q), self.line(high + 1, q))

                self.right_copy(high, q).start()

    def step_low(self, low):
        at = self.at

        @pl.when(low < at.z)
        def _():
            for q in (1 - at.p, at.p):

                @pl.when(jnp.logical_not(at.last))
                def _():
                    self.left_copy(low, q).wait_recv()
                    add_into(self.part(low * 2 + q), self.line(low, q))

                self.left_copy(low, q).start()

    def join(self):
        at = self.at
        for q in (1 - at.p, at.p):
            ref = self.part(at.z * 2 + q)

            @pl.when(jnp.logical_not(at.first))
            def _():
                self.right_copy(at.z, q).wait_recv()
                add_into(ref, self.line(at.z + 1, q))

            @pl.when(jnp.logical_not(at.last))
            def _():
                self.left_copy(at.z, q).wait_recv()
                add_into(ref, self.line(at.z, q))

            if q is not at.p:
                self.pair_copy().start()

    def finish(self, out):
        self.pair_copy().wait_recv()
        out[...] = self.part(self.at.dp)[...].astype(F32) + self.got[...].astype(F32)

    def drain(self):
        at = self.at
        self.pair_copy().wait_send()

        @pl.loop(0, at.devices)
        def _(block):
            zz, q = lax.div(block, 2), lax.rem(block, 2)
            pl.when(zz > at.z)(lambda: self.right_copy(zz, q).wait_send())
            pl.when(zz < at.z)(lambda: self.left_copy(zz, q).wait_send())


class RowGather:
    def __init__(self, place, view, send, recv):
        self.at, self.view, self.send, self.recv = place, view, send, recv

    def copy(self, rank, chunk, sem, near):
        ref = self.view(rank, chunk)
        where = {"tensor": self.at.t_near if near else self.at.t_far}
        return remote(ref, ref, self.send.at[chunk, sem], self.recv.at[chunk, rank], where)

    def start(self, chunk):
        self.copy(self.at.t, chunk, 0, False).start()
        self.copy(self.at.t, chunk, 1, True).start()

    def forward(self, chunk):
        self.copy(self.at.t_far, chunk, 2, False).wait_recv()
        self.copy(self.at.t_far, chunk, 2, True).start()

    def finish(self, chunk):
        self.copy(self.at.t_near, chunk, 1, True).wait_recv()
        self.copy(self.at.t_both, chunk, 2, True).wait_recv()

    def drain(self, chunk):
        self.copy(self.at.t, chunk, 0, False).wait_send()
        self.copy(self.at.t, chunk, 1, True).wait_send()
        self.copy(self.at.t_far, chunk, 2, True).wait_send()


class RowScatter:
    def __init__(self, place, view, near_buf, far_buf, send, recv):
        self.at, self.view = place, view
        self.near_buf, self.far_buf = near_buf, far_buf
        self.send, self.recv = send, recv

    def near_copy(self, chunk, which):
        rank = self.at.t_both if which else self.at.t_near
        return remote(
            self.view(rank, chunk),
            self.near_buf(which, chunk),
            self.send.at[chunk, which],
            self.recv.at[chunk, which],
            {"tensor": self.at.t_near},
        )

    def far_copy(self, chunk):
        return remote(
            self.view(self.at.t_far, chunk),
            self.far_buf(chunk),
            self.send.at[chunk, 2],
            self.recv.at[chunk, 2],
            {"tensor": self.at.t_far},
        )

    def start(self, chunk):
        self.near_copy(chunk, 1).start()
        self.near_copy(chunk, 0).start()

    def middle(self, chunk):
        self.near_copy(chunk, 1).wait_recv()
        ref = self.view(self.at.t_far, chunk)
        ref[...] = (ref[...].astype(F32) + self.near_buf(1, chunk)[...].astype(F32)).astype(BF16)
        self.far_copy(chunk).start()

    def finish(self, chunk):
        self.near_copy(chunk, 0).wait_recv()
        total = self.view(self.at.t, chunk)[...].astype(F32) + self.near_buf(0, chunk)[
            ...
        ].astype(F32)
        self.far_copy(chunk).wait_recv()
        return total + self.far_buf(chunk)[...].astype(F32)

    def drain(self, chunk):
        self.near_copy(chunk, 0).wait_send()
        self.near_copy(chunk, 1).wait_send()
        self.far_copy(chunk).wait_send()


def line_gather_sems(devices):
    dma = pltpu.SemaphoreType.DMA
    return [dma((devices,)), dma((devices // 2,)), dma((devices // 2,)), dma((devices // 2,))]


def line_scatter_sems(devices):
    return [pltpu.SemaphoreType.DMA((devices // 2,)) for _ in range(6)]


def rms_rows(values, gain):
    return values * lax.rsqrt(jnp.mean(values * values, -1, keepdims=True) + EPSILON) * gain


def rms_rows_grad(values, gain, grad):
    scale = lax.rsqrt(jnp.mean(values * values, -1, keepdims=True) + EPSILON)
    term = grad * gain
    inner = jnp.mean(values * term, -1, keepdims=True)
    return scale * (term - values * (scale * scale * inner)), grad * values * scale


def ffn_kernel(devices, layout, *refs, joined=None):
    (
        x_ref, a_ref, og_ref, ogl_ref, gain_ref, w_any, dn_in,
        out_ref, gh_ref, gb, nf, act, dgu, gain_grad,
        part, part2, near1, far1, near2, far2, near3, far3, hid,
        w_ref, w_dn, w_sem, send, recv, *sems,
    ) = refs
    at = Place(devices)
    seqs, sub, width = x_ref.shape
    span = sub * 4
    half = seqs // 2
    rows = half * span
    first = layout["out"][0] if joined is None else 0
    out_w, gu_w = (pl.ds(layout[k][0] - first, layout[k][1]) for k in ("out", "gu"))
    ff = layout["down"][1]
    if joined is None:
        depth = dn_in.shape[1]
        load = pltpu.make_async_copy(w_any.at[:, pl.ds(first, w_ref.shape[1])], w_ref, w_sem)
        load.start()
        w_dn[pl.ds(pl.multiple_of(at.dp * depth, depth), depth), :] = dn_in[...].T
        Neighbours(at).greet()
    else:
        w_ref = w_any

    def down():
        return w_dn[...] if joined is None else w_ref[:, pl.ds(*layout["down"])]

    def rows_of(buf):
        def view(rank, chunk):
            return buf.at[pl.ds(chunk * half, half), pl.ds(pl.multiple_of(rank * sub, sub), sub), :]

        return view

    def parts_of(buf):
        return lambda which, chunk: buf.at[which, pl.ds(chunk * half, half)]

    def part_of(buf):
        return lambda chunk: buf.at[pl.ds(chunk * half, half)]

    branch = RowScatter(at, rows_of(part), parts_of(near1), part_of(far1), send.at[0], recv.at[0])
    ffn = RowScatter(at, rows_of(part2), parts_of(near2), part_of(far2), send.at[1], recv.at[1])
    back = RowScatter(at, rows_of(part), parts_of(near3), part_of(far3), send.at[2], recv.at[2])
    row_nf = RowGather(at, rows_of(nf), send.at[3], recv.at[3])
    row_gb = RowGather(at, rows_of(gb), send.at[4], recv.at[4])
    mine = pl.ds(pl.multiple_of(at.t * sub, sub), sub)
    gain = gain_ref[...].reshape(1, width)

    def seq_rows(chunk):
        return pl.ds(chunk * half, half)

    def tok_rows(chunk):
        return pl.ds(chunk * rows, rows)

    if joined is None:
        gather = LineGather(
            at, lambda block: w_dn.at[pl.ds(pl.multiple_of(block * depth, depth), depth), :], *sems
        )
        gather.start()
        load.wait()
        gather_step = gather.step
    else:
        joined.step(3, 2)
        gather_step = partial(joined.step, 4)
    for c in range(2):
        value = dot_nt(a_ref[tok_rows(c), :], w_ref[:, out_w])
        part[seq_rows(c)] = value.astype(BF16).reshape(half, span, width)
        branch.start(c)
    for c in range(2):
        branch.middle(c)
    gather_step(0)
    for c in range(2):
        hidden = x_ref[seq_rows(c)].astype(F32) + branch.finish(c)
        hid[seq_rows(c)] = hidden
        nf[seq_rows(c), mine, :] = rms_rows(hidden, gain).astype(BF16)
        row_nf.start(c)
    gather_step(1)
    if joined is not None:
        gather_step(2)
        joined.gathers[3].finish()
        joined.gathers[4].finish()
    for c in range(2):
        row_nf.forward(c)
    if joined is None:
        pl.loop(2, at.lines - 1)(lambda s: gather.step(s))
        gather.finish()
    for c in range(2):
        row_nf.finish(c)
        branch.drain(c)
        flat = nf[seq_rows(c)].reshape(rows, width)
        flat_og = og_ref[seq_rows(c)].reshape(rows, width)
        gate_up = dot_nn(flat, w_ref[:, gu_w])
        gate, up = gate_up[:, :ff], gate_up[:, ff:]
        sigmoid = jax.nn.sigmoid(gate)
        grad_act = dot_nn(flat_og, down())
        act[tok_rows(c), :] = (gate * sigmoid * up).astype(BF16)
        dgu[tok_rows(c), :ff] = (
            grad_act * up * sigmoid * (1.0 + gate * (1.0 - sigmoid))
        ).astype(BF16)
        dgu[tok_rows(c), ff:] = (grad_act * gate * sigmoid).astype(BF16)
        value = dot_nt(dgu[tok_rows(c), :], w_ref[:, gu_w])
        part[seq_rows(c)] = value.astype(BF16).reshape(half, span, width)
        back.start(c)
    for c in range(2):
        value = dot_nt(act[tok_rows(c), :], down())
        part2[seq_rows(c)] = value.astype(BF16).reshape(half, span, width)
    if joined is not None:
        joined.activations_ready()
    for c in range(2):
        back.middle(c)
    total = jnp.zeros((1, width), F32)
    for c in range(2):
        grad_hidden, terms = rms_rows_grad(hid[seq_rows(c)], gain, back.finish(c))
        total = total + jnp.sum(terms.reshape(half * sub, width), 0, keepdims=True)
        grad_hidden = grad_hidden + ogl_ref[seq_rows(c)].astype(F32)
        gh_ref[seq_rows(c)] = grad_hidden
        gb[seq_rows(c), mine, :] = grad_hidden.astype(BF16)
        row_gb.start(c)
        ffn.start(c)
    gain_grad[...] = total
    for c in range(2):
        row_gb.forward(c)
        ffn.middle(c)
    for c in range(2):
        out_ref[seq_rows(c)] = (hid[seq_rows(c)] + ffn.finish(c)).astype(BF16)
        row_gb.finish(c)
    def drain():
        for c in range(2):
            row_nf.drain(c)
            row_gb.drain(c)
            back.drain(c)
            ffn.drain(c)

    drain()
    if joined is None:
        gather.drain()


def ffn_specs(cfg):
    layout = cfg["layout"]
    seqs, sub, width = cfg["rows"]
    span = sub * 4
    tokens = seqs * span
    ff = layout["down"][1]
    dma = pltpu.SemaphoreType.DMA
    whole, own = (seqs, span, width), (seqs, sub, width)
    outs = (
        (own, BF16),
        (own, F32),
        (whole, BF16),
        (whole, BF16),
        ((tokens, ff), BF16),
        ((tokens, 2 * ff), BF16),
        ((1, width), F32),
    )
    buffers = [pltpu.VMEM(whole, BF16), pltpu.VMEM(whole, BF16)]
    buffers += [pltpu.VMEM((2,) + own, BF16), pltpu.VMEM(own, BF16)] * 3
    buffers += [pltpu.VMEM(own, F32)]
    weights = [
        pltpu.VMEM((width, layout["down"][0] - layout["out"][0]), BF16),
        pltpu.VMEM((width, ff), BF16),
        dma,
    ]
    sems = [dma((5, 2, 3)), dma((5, 2, 4))]
    return outs, buffers, weights, sems


def feed_forward(cfg, x, a, og, out_grad, gain, w_all, w_down):
    outs, buffers, weights, sems = ffn_specs(cfg)
    vmem = pl.BlockSpec(memory_space=pltpu.VMEM)
    return pl.pallas_call(
        partial(ffn_kernel, cfg["devices"], cfg["layout"]),
        out_shape=tuple(jax.ShapeDtypeStruct(*out) for out in outs),
        in_specs=[vmem] * 5 + [pl.BlockSpec(memory_space=pl.ANY), vmem],
        out_specs=(vmem,) * 7,
        scratch_shapes=buffers + weights + sems + line_gather_sems(cfg["devices"]),
        compiler_params=pltpu.CompilerParams(
            collective_id=1, has_side_effects=True, vmem_limit_bytes=VMEM_BYTES
        ),
        name="feed_forward",
    )(x, a, og, out_grad, gain, w_all, w_down)


def to_row(column):
    size = column.shape[0]
    eye = iota((size, size), 0) == iota((size, size), 1)
    return jnp.sum(jnp.where(eye, column, 0.0), 0, keepdims=True)


def to_column(row):
    size = row.shape[1]
    eye = iota((size, size), 0) == iota((size, size), 1)
    return jnp.sum(jnp.where(eye, row, 0.0), 1, keepdims=True)


def iota(shape, dim):
    return lax.broadcasted_iota(jnp.int32, shape, dim)


def spread(columns, heads, head_dim):
    rows = columns.shape[0]
    lane = iota((rows, LANES), 1)
    blocks = []
    for first in range(0, heads, LANES // head_dim):
        block = jnp.broadcast_to(columns[:, first : first + 1], (rows, LANES))
        for k in range(1, LANES // head_dim):
            block = jnp.where(lane >= k * head_dim, columns[:, first + k : first + k + 1], block)
        blocks.append(block)
    return jnp.concatenate(blocks, 1)


def head_sums(values, heads, head_dim):
    rows = values.shape[0]
    lane = iota((rows, LANES), 1)
    out = jnp.zeros((rows, LANES), F32)
    per = LANES // head_dim
    for h in range(heads):
        block = values[:, h // per * LANES : (h // per + 1) * LANES]
        inside = jnp.logical_and(lane >= h % per * head_dim, lane < (h % per + 1) * head_dim)
        total = jnp.sum(jnp.where(inside, block, 0.0), 1, keepdims=True)
        out = jnp.where(lane == h, total, out)
    return out


def pick_halves(blocks, head_dim):
    lane = iota(blocks[0].shape, 1)
    per = LANES // head_dim
    out = []
    for first in range(0, len(blocks), per):
        block = blocks[first]
        for k in range(1, per):
            block = jnp.where(lane >= k * head_dim, blocks[first + k], block)
        out.append(block)
    return jnp.concatenate(out, 1)


def softplus(value):
    return jnp.maximum(value, 0.0) + jnp.log1p(jnp.exp(-jnp.abs(value)))


def running_sum(values, backward=False):
    rows = values.shape[0]
    row = iota(values.shape, 0)
    step = 1
    while step < rows:
        if backward:
            moved = jnp.where(row < rows - step, pltpu.roll(values, rows - step, 0), 0.0)
        else:
            moved = jnp.where(row >= step, pltpu.roll(values, step, 0), 0.0)
        values = values + moved
        step *= 2
    return values


def turn(values, cosine, sine, half):
    lane = iota(values.shape, 1)
    first = lax.rem(lane, 2 * half) < half
    swapped = jnp.where(
        first, pltpu.roll(values, LANES - half, 1), pltpu.roll(values, half, 1)
    )
    return values * cosine + swapped * sine


def decay_parts(step_pre, decay_log, bias):
    step = softplus(step_pre + bias)
    rate = -jnp.exp(decay_log)
    return step, rate, running_sum(step * rate)


def same_document(aux, row):
    span = aux.shape[0]
    same = aux[:, 5:6] == row
    causal = iota((span, span), 0) >= iota((span, span), 1)
    return jnp.where(jnp.logical_and(same, causal), 0.0, MASKED)


class Neighbours:
    def __init__(self, at):
        self.at = at

    def greet(self, flips=False):
        at = self.at
        barrier = pltpu.get_barrier_semaphore()
        end = at.devices - 1

        def signal(**where):
            pl.semaphore_signal(
                barrier, inc=1, device_id=where, device_id_type=pl.DeviceIdType.MESH
            )

        for other in (at.t_near, at.t_far, at.t_both):
            signal(tensor=other)
        signal(dp=at.pair)
        count = 4
        for step in (1, 2):
            low, high = at.dp >= step, at.dp + step <= end
            pl.when(low)(partial(signal, dp=at.dp - step))
            pl.when(high)(partial(signal, dp=at.dp + step))
            count = count + low.astype(jnp.int32) + high.astype(jnp.int32)
        if flips:
            for other in at.flips():
                signal(dp=other)
                count = count + 1
        pl.semaphore_wait(barrier, count)


class TensorTotal:
    def __init__(self, at, own, got, send, recv):
        self.at, self.own, self.got, self.send, self.recv = at, own, got, send, recv

    def copies(self):
        others = (self.at.t_near, self.at.t_far, self.at.t_both)
        return [
            remote(
                self.own, self.got.at[i], self.send.at[i], self.recv.at[i], {"tensor": other}
            )
            for i, other in enumerate(others)
        ]

    def start(self):
        for copy in self.copies():
            copy.start()

    def finish(self):
        for copy in self.copies():
            copy.wait()
        return self.own[...] + self.got[0] + self.got[1] + self.got[2]


class StatePass:
    def __init__(self, at, local, pair_in, chain_in, chain_out, share, result, sems, backward):
        self.at, self.local, self.pair_in = at, local, pair_in
        self.chain_in, self.chain_out, self.share, self.result = chain_in, chain_out, share, result
        self.backward = backward
        self.pair_send, self.pair_recv, self.chain_send, self.chain_recv = sems[:4]
        self.share_send, self.share_recv = sems[4:]
        self.half = local.shape[0] // 2
        self.size = result.shape[1]
        self.head = at.last if backward else at.first
        self.tail = at.first if backward else at.last
        self.onward = at.dp - 2 if backward else at.dp + 2

    def pair_copy(self):
        src = self.local.at[pl.ds((1 - self.at.p) * self.half, self.half)]
        return remote(
            src, self.pair_in, self.pair_send.at[0], self.pair_recv.at[0], {"dp": self.at.pair}
        )

    def chain_copy(self, i):
        return remote(
            self.chain_out.at[i],
            self.chain_in.at[i],
            self.chain_send.at[i],
            self.chain_recv.at[i],
            {"dp": self.onward},
        )

    def share_copy(self, i):
        return remote(
            self.share.at[i],
            self.result.at[self.at.p * self.half + i],
            self.share_send.at[i],
            self.share_recv.at[i],
            {"dp": self.at.pair},
        )

    def start(self):
        self.pair_copy().start()

    def run(self):
        at, size = self.at, self.size
        sooner = at.p == (1 if self.backward else 0)
        self.pair_copy().wait_recv()
        for i in range(self.half):
            mine = self.local[at.p * self.half + i].astype(F32)
            other = self.pair_in[i].astype(F32)
            one = jnp.where(sooner, mine, other)
            two = jnp.where(sooner, other, mine)
            state1, keep1 = one[:size], one[size : size + 1]
            state2, keep2 = two[:size], two[size : size + 1]

            @pl.when(self.head)
            def _():
                self.chain_in[i] = jnp.zeros(self.chain_in.shape[1:], BF16)

            @pl.when(jnp.logical_not(self.head))
            def _():
                self.chain_copy(i).wait_recv()

            before = self.chain_in[i].astype(F32)
            middle = keep1 * before + state1

            @pl.when(jnp.logical_not(self.tail))
            def _():
                self.chain_out[i] = (keep2 * middle + state2).astype(BF16)
                self.chain_copy(i).start()

            self.result[at.p * self.half + i] = jnp.where(sooner, before, middle).astype(BF16)
            self.share[i] = jnp.where(sooner, middle, before).astype(BF16)
            self.share_copy(i).start()

    def finish(self):
        at = self.at
        for i in range(self.half):
            remote(
                self.share.at[i],
                self.result.at[(1 - at.p) * self.half + i],
                self.share_send.at[i],
                self.share_recv.at[i],
                {"dp": at.pair},
            ).wait_recv()
            self.share_copy(i).wait_send()
            pl.when(jnp.logical_not(self.tail))(lambda: self.chain_copy(i).wait_send())
        self.pair_copy().wait_send()


def state_pass_scratch(half, size, width):
    dma = pltpu.SemaphoreType.DMA
    return [
        pltpu.VMEM((half, size + 16, width), BF16),
        pltpu.VMEM((half, size, width), BF16),
        pltpu.VMEM((half, size, width), BF16),
        pltpu.VMEM((half, size, width), BF16),
        dma((1,)),
        dma((1,)),
        dma((half,)),
        dma((half,)),
        dma((half,)),
        dma((half,)),
    ]


def packed_columns(layout, name):
    return pl.ds(*layout[name])


def span_row(rows, first, span):
    total = rows.shape[1]
    return pltpu.roll(rows, lax.rem(total - first, total), 1)[:, :span]


def shifted_column(row, before, back):
    span = row.shape[1]
    at, lane = iota((span, span), 0), iota((span, span), 1)
    now = jnp.where(lane == at - back, row, 0.0)
    earlier = jnp.where(lane == at - back + span, before, 0.0)
    return jnp.sum(now + earlier, 1, keepdims=True)


def mixer_kernel(cfg, *refs, joined=None):
    (
        x_ref, og_in, gain_ref, q_in, kv_in, mi_in, st_in, sp_in, gu_in, ao_in, mo_in, seg_ref,
        rope_any, xt_ref, xb_ref, stt_ref, sb_ref, head_ref, mgain_ref,
        w_all, nx, og, low, kv, q2, probs, att, ext, pre, step_buf, entering, carry, y_buf, z_buf,
        squares, aux_ref, seg_rows,
        local, xs_buf, nxh, rope_ref, rope_sem, row_send, row_recv, kv_sems, halo_sems, sq_own,
        sq_got, sq_send, sq_recv,
        *rest,
    ) = refs
    devices, layout, pieces, heads = (cfg[k] for k in ("devices", "layout", "pieces", "heads"))
    at = Place(devices)
    seqs, sub, width = x_ref.shape
    span = sub * 4
    tokens = seqs * span
    depth = q_in.shape[0]
    xw = layout["x"][1]
    head_dim = xw // heads
    sw = layout["state"][1]
    size = sw // 2
    mixed = xw + sw
    qw = layout["q"][1]
    at_dim = qw // 2
    count = devices * span
    pass_refs, sems = rest[:10], rest[10:]
    own_rows = pl.ds(pl.multiple_of(at.dp * depth, depth), depth)
    rope_copy = pltpu.make_async_copy(
        rope_any.at[pl.ds(pl.multiple_of(at.dp * span, span), span), :], rope_ref, rope_sem
    )
    rope_copy.start()
    kv[...] = jnp.zeros(kv.shape, BF16)

    def own(name, value):
        w_all[own_rows, packed_columns(layout, name)] = value

    own("x", mi_in[:, 1, :])
    own("state", st_in[...])
    own("step", jnp.zeros((depth, LANES), BF16))
    w_all[own_rows, pl.ds(layout["step"][0], sp_in.shape[1])] = sp_in[...]
    Neighbours(at).greet(flips=joined is not None)
    if joined is not None:
        own("down", joined.dn_in[...].T)
    gathers = []
    for i, (first, columns, cross) in enumerate(pieces):

        def view(block, first=first, columns=columns):
            return w_all.at[
                pl.ds(pl.multiple_of(block * depth, depth), depth), pl.ds(first, columns)
            ]

        kind = CrossGather if cross else LineGather
        gathers.append(kind(at, view, *sems[4 * i : 4 * i + 4]))

    def step(i, s):
        if s < at.lines - 1:
            gathers[i].step(s)
        if s == 2:
            pl.loop(3, max(at.lines - 1, 3))(lambda k: gathers[i].step(k))

    gathers[0].start()
    gain = gain_ref[...].reshape(1, width)
    mine = pl.ds(pl.multiple_of(at.t * sub, sub), sub)
    for s in range(seqs):
        nx[s, mine, :] = rms_rows(x_ref[s].astype(F32), gain).astype(BF16)
    half = seqs // 2

    def rows_of(buf):
        def view(rank, chunk):
            return buf.at[pl.ds(chunk * half, half), pl.ds(pl.multiple_of(rank * sub, sub), sub), :]

        return view

    row_nx = RowGather(at, rows_of(nx), row_send.at[0], row_recv.at[0])
    row_og = RowGather(at, rows_of(og), row_send.at[1], row_recv.at[1])
    for chunk in range(2):
        row_nx.start(chunk)
    own("kv", jnp.where(at.t < 2, kv_in[:, 0, :], kv_in[:, 1, :]))
    own("q", q_in[...])
    own("z", mi_in[:, 0, :])
    gathers[1].start()
    out_at, gu_at = layout["out"][0], layout["gu"][0]
    w_all[own_rows, pl.ds(out_at, qw)] = ao_in[...].T
    w_all[own_rows, pl.ds(out_at + qw, xw)] = mo_in[...].T
    ff = gu_in.shape[2]
    w_all[own_rows, pl.ds(gu_at, ff)] = gu_in[:, 0, :]
    w_all[own_rows, pl.ds(gu_at + ff, ff)] = gu_in[:, 1, :]
    for s in range(seqs):
        og[s, mine, :] = og_in[s]
    before, after = at.dp > 0, at.dp < devices - 1
    seg = seg_ref[...].astype(F32)
    now = span_row(seg, at.dp * span, span)
    old = jnp.where(before, span_row(seg, jnp.maximum(at.dp - 1, 0) * span, span), -1.0)
    seg_rows[...] = jnp.zeros(seg_rows.shape, F32)
    seg_rows[0:seqs, :] = now
    for s in range(seqs):
        row, earlier = now[s : s + 1, :], old[s : s + 1, :]
        column = to_column(row)
        same = [(shifted_column(row, earlier, k) == column).astype(F32) for k in (1, 2, 3)]
        same.append((column == earlier[:, span - 1 :]).astype(F32))
        same.append((column == row[:, span - 1 :]).astype(F32))
        same.append(column)
        lane = iota((span, LANES), 1)
        total = jnp.zeros((span, LANES), F32)
        for k, value in enumerate(same):
            total = jnp.where(lane == k, value, total)
        aux_ref[s] = total
    for chunk in range(2):
        row_nx.forward(chunk)
    for chunk in range(2):
        row_nx.finish(chunk)
    for chunk in range(2):
        row_og.start(chunk)

    def halo():
        return remote(
            nx.at[:, pl.ds(span - 16, 16), :],
            nxh,
            halo_sems.at[0],
            halo_sems.at[1],
            {"dp": at.dp + 1},
        )

    pl.when(after)(lambda: halo().start())
    step(0, 0)
    step(0, 1)
    step(1, 0)
    step(0, 2)
    gathers[2].start()
    step(1, 1)
    for chunk in range(2):
        row_og.forward(chunk)
    pl.when(before)(lambda: halo().wait_recv())

    @pl.when(jnp.logical_not(before))
    def _():
        nxh[...] = jnp.zeros(nxh.shape, BF16)

    gathers[0].finish()
    rows = nx[...].reshape(tokens, width)
    rows_before = nxh[...].reshape(seqs * 16, width)

    def project(name):
        return dot_nn(rows, w_all[:, packed_columns(layout, name)])

    for name, first in (("x", 0), ("state", xw)):
        columns = layout[name][1]
        value = project(name).astype(BF16).astype(F32)
        ext[:, pl.ds(8, span), pl.ds(first, columns)] = value.reshape(seqs, span, columns)
        value = dot_nn(rows_before, w_all[:, packed_columns(layout, name)])
        value = value.astype(BF16).astype(F32).reshape(seqs, 16, columns)
        ext[:, pl.ds(0, 8), pl.ds(first, columns)] = value[:, 8:, :]
    step_buf[...] = project("step").reshape(seqs, span, LANES)
    taps = jnp.concatenate([xt_ref[...], stt_ref[...]], 1)
    tap_bias = jnp.concatenate([xb_ref[...].reshape(1, xw), sb_ref[...].reshape(1, sw)], 1)
    step_bias, decay_log, skips = head_ref[0:1, :], head_ref[1:2, :], head_ref[2:3, :]

    def scan_parts(s):
        return decay_parts(step_buf[s], decay_log, step_bias)

    @pl.loop(0, seqs)
    def _(s):
        aux = aux_ref[s]
        total = tap_bias + taps[3:4, :] * ext[s, pl.ds(8, span), :]
        for back in (1, 2, 3):
            moved = ext[s, pl.ds(8 - back, span), :] * aux[:, back - 1 : back]
            total = total + taps[3 - back : 4 - back, :] * moved
        pre[s] = total
        active = total * jax.nn.sigmoid(total)
        step, _, running = scan_parts(s)
        scaled = active[:, :xw] * spread(step, heads, head_dim)
        xs_buf[s] = scaled.astype(BF16)
        end = running[span - 1 : span, :]
        tail = spread(jnp.exp(end - running) * aux[:, 4:5], heads, head_dim)
        state_in = active[:, xw : xw + size].astype(BF16)
        local[s, :size, :] = dot_tn(state_in, (scaled * tail).astype(BF16)).astype(BF16)
        keep = jnp.broadcast_to(jnp.exp(end) * aux[span - 1 : span, 3:4], (16, LANES))
        keep = spread(keep, heads, head_dim).astype(BF16)
        local[s, size : size + 16, :] = keep
        carry[s] = keep

    passing = StatePass(
        at, local, pass_refs[0], pass_refs[1], pass_refs[2], pass_refs[3], entering,
        pass_refs[4:], False,
    )
    passing.start()
    step(1, 2)
    gathers[1].finish()
    rope_copy.wait()
    lane = iota((span, LANES), 1)
    cosine, sine = rope_ref[:, :LANES], rope_ref[:, LANES:]
    pairs = project("kv").reshape(seqs, span, qw)
    key_cosine = jnp.where(lane < at_dim, cosine, 1.0)
    key_sine = jnp.where(lane < at_dim, sine, 0.0)
    scale = 1.0 / math.sqrt(at_dim)
    for s in range(seqs):
        kv[at.dp, s] = turn(pairs[s], key_cosine, key_sine, at_dim // 2).astype(BF16)
    kv_gather = LineGather(
        at,
        lambda block: kv.at[block],
        kv_sems.at[0],
        kv_sems.at[1],
        kv_sems.at[2],
        kv_sems.at[3],
        causal=True,
    )
    kv_gather.start()
    queries = project("q").reshape(seqs, span, qw)
    for s in range(seqs):
        turned = turn(queries[s], cosine, sine, at_dim // 2) * scale
        q2[s, :span, :] = jnp.where(lane < at_dim, turned, 0.0).astype(BF16)
        turned = pltpu.roll(turned, at_dim, 1)
        q2[s, span:, :] = jnp.where(lane < at_dim, turned, 0.0).astype(BF16)
    gathers[2].begin() if pieces[2][2] else None
    step(2, 0)
    passing.run()
    gathers[3].start()
    z_buf[...] = project("z").astype(BF16).reshape(seqs, span, xw)
    kv_gather.step(0)
    step(2, 1)
    @pl.loop(0, seqs)
    def _(s):
        aux = aux_ref[s]
        active = pre[s] * jax.nn.sigmoid(pre[s])
        _, _, running = scan_parts(s)
        running_rows = running.T
        allowed = same_document(aux, seg_rows[pl.ds(s, 1), :])
        state_in = active[:, xw : xw + size].astype(BF16)
        state_out = active[:, xw + size :].astype(BF16)
        joined = dot_nt(state_out, state_in)
        blocks = []
        for h in range(heads):
            gap = running[:, h : h + 1] - running_rows[h : h + 1, :]
            weight = (joined * jnp.exp(gap + allowed)).astype(BF16)
            cols = pl.ds(h * head_dim // LANES * LANES, LANES)
            blocks.append(dot_nn(weight, xs_buf[s, :, cols]))
        y_buf[s] = pick_halves(blocks, head_dim) + spread(skips, heads, head_dim) * active[:, :xw]

    pl.loop(1, at.lines - 1)(lambda s: kv_gather.step(s))
    step(2, 2)
    step(3, 0)
    passing.finish()
    sq_own[...] = jnp.zeros(sq_own.shape, F32)
    for s in range(seqs):
        aux = aux_ref[s]
        state_out = pre[s, :, pl.ds(xw + size, size)]
        state_out = (state_out * jax.nn.sigmoid(state_out)).astype(BF16)
        _, _, running = scan_parts(s)
        factor = spread(jnp.exp(running) * aux[:, 3:4], heads, head_dim)
        y = y_buf[s] + dot_nn(state_out, entering[s]) * factor
        y_buf[s] = y
        gate = z_buf[s].astype(F32)
        gated = y * gate * jax.nn.sigmoid(gate)
        sq_own[s : s + 1, :] = to_row(jnp.sum(gated * gated, 1, keepdims=True))
    total = TensorTotal(at, sq_own, sq_got, sq_send, sq_recv)
    total.start()
    kv_gather.finish()
    step(3, 1)
    if joined is not None:
        gathers[4].start()
    key_at = iota((span, count), 1)
    query_at = iota((span, count), 0) + at.dp * span
    causal = key_at <= query_at

    @pl.loop(0, seqs)
    def _(s):
        keys = kv[:, s].reshape(count, qw)
        row = seg_ref[pl.ds(s, 1), :].astype(F32)
        allowed = jnp.logical_and(aux_ref[s][:, 5:6] == row, causal)
        bias = jnp.where(allowed, 0.0, MASKED)
        outs = []
        for h in range(2):
            part = pl.ds(h * span, span)
            scores = dot_nt(q2[s, part, :], keys) + bias
            power = jnp.exp(scores - jnp.max(scores, 1, keepdims=True))
            weight = power * (1.0 / jnp.sum(power, 1, keepdims=True))
            weight = weight.astype(BF16)
            probs[s, part, :] = weight
            outs.append(dot_nn(weight, keys))
        att[s] = jnp.where(lane < at_dim, pltpu.roll(outs[0], at_dim, 1), outs[1])

    low[:, pl.ds(0, qw)] = att[...].reshape(tokens, qw).astype(BF16)
    squares[...] = total.finish()
    for s in range(seqs):
        gate = z_buf[s].astype(F32)
        gated = y_buf[s] * gate * jax.nn.sigmoid(gate)
        norm = lax.rsqrt(to_column(squares[s : s + 1, :]) / (4 * xw) + EPSILON)
        value = gated * norm * mgain_ref[...].reshape(1, xw)
        low[pl.ds(s * span, span), pl.ds(qw, xw)] = value.astype(BF16)
    for chunk in range(2):
        row_og.finish(chunk)
    def drain():
        for gather in [*gathers[:3], kv_gather]:
            gather.drain()
        for row in (row_nx, row_og):
            for chunk in range(2):
                row.drain(chunk)
        pl.when(after)(lambda: halo().wait_send())

    if joined is not None:
        gathers[2].finish()
        joined.step, joined.gathers = step, gathers
        joined.drains.append(drain)
        return
    step(3, 2)
    gathers[2].finish()
    gathers[3].finish()
    gathers[3].drain()
    drain()


def gather_sems(devices, pieces):
    dma = pltpu.SemaphoreType.DMA
    out = []
    for _, _, cross in pieces:
        out += [dma((devices,)) for _ in range(4)] if cross else line_gather_sems(devices)
    return out


def mixer_specs(cfg, columns):
    devices, layout, pieces, heads = (cfg[k] for k in ("devices", "layout", "pieces", "heads"))
    seqs, sub, width = cfg["rows"]
    span = sub * 4
    tokens = seqs * span
    xw, sw, qw = (layout[k][1] for k in ("x", "state", "q"))
    size = sw // 2
    count = devices * span
    dma = pltpu.SemaphoreType.DMA
    outs = (
        ((width, columns), BF16),
        ((seqs, span, width), BF16),
        ((seqs, span, width), BF16),
        ((tokens, qw + xw), BF16),
        ((devices, seqs, span, qw), BF16),
        ((seqs, 2 * span, qw), BF16),
        ((seqs, 2 * span, count), BF16),
        ((seqs, span, qw), F32),
        ((seqs, span + 8, xw + sw), F32),
        ((seqs, span, xw + sw), F32),
        ((seqs, span, LANES), F32),
        ((seqs, size, xw), BF16),
        ((seqs, 16, xw), BF16),
        ((seqs, span, xw), F32),
        ((seqs, span, xw), BF16),
        ((8, span), F32),
        ((seqs, span, LANES), F32),
        ((8, span), F32),
    )
    scratch = [
        pltpu.VMEM((seqs, size + 16, xw), BF16),
        pltpu.VMEM((seqs, span, xw), BF16),
        pltpu.VMEM((seqs, 16, width), BF16),
        pltpu.VMEM((span, 2 * LANES), F32),
        dma,
        dma((2, 2, 3)),
        dma((2, 2, 4)),
        dma((4, devices)),
        dma((2,)),
        pltpu.VMEM((8, span), F32),
        pltpu.VMEM((3, 8, span), F32),
        dma((3,)),
        dma((3,)),
    ]
    scratch += state_pass_scratch(seqs // 2, size, xw) + gather_sems(devices, pieces)
    return outs, scratch


def mixer(cfg, x, *args):
    outs, scratch = mixer_specs(cfg, cfg["layout"]["down"][0])
    vmem = pl.BlockSpec(memory_space=pltpu.VMEM)
    in_specs = [vmem] * (1 + len(args))
    in_specs[12] = pl.BlockSpec(memory_space=pl.ANY)
    return pl.pallas_call(
        partial(mixer_kernel, cfg),
        out_shape=tuple(jax.ShapeDtypeStruct(*out) for out in outs),
        in_specs=in_specs,
        out_specs=(vmem,) * len(outs),
        scratch_shapes=scratch,
        compiler_params=pltpu.CompilerParams(
            collective_id=0, has_side_effects=True, vmem_limit_bytes=VMEM_BYTES
        ),
        name="mixer",
    )(x, *args)


def back_kernel(cfg, *refs, joined=None):
    (
        x_ref, gh_ref, gain_ref, w_any, nx_ref, og_ref, gb_ref, low_ref, nf_any, dgu_any, act_ref,
        kv_any, q2_ref, probs_any, att_ref, ext_ref, pre_ref, step_ref, entering, carry, y_ref,
        z_ref, squares, aux_ref, seg_ref, rope_any, xt_ref, stt_ref, head_ref, mgain_ref, fgain_ref,
        rg_ref, dw_ref, sums, kvs,
        w_ref, d_in, dlow, dy, dbc, dcum, ext_grad, halo_got, local2, after_state, keys_buf,
        prob_buf, dkv, dkv_got, dkv_line, dkv_own,
        part, near, far, grads, got, line, line2, small_near, small_far, small_dp, kv_near, kv_far,
        sq_own, sq_got,
        rope_ref, w_sem, early_sems, rope_sem, load_sems, halo_sems, sq_send, sq_recv, send, recv, small_send, small_recv,
        dp_send, dp_recv, kv_send, kv_recv,
        *rest,
    ) = refs
    devices, layout, pieces, heads = (cfg[k] for k in ("devices", "layout", "scatters", "heads"))
    at = Place(devices)
    seqs, sub, width = x_ref.shape
    span = sub * 4
    tokens = seqs * span
    half = seqs // 2
    rows = half * span
    depth = width // devices
    xw, sw, qw = (layout[k][1] for k in ("x", "state", "q"))
    size = sw // 2
    head_dim = xw // heads
    at_dim = qw // 2
    mixed = xw + sw
    count = devices * span
    in_w = layout["in"][1]
    pass_refs, kv_sems, sems = rest[:10], rest[10:16], rest[16:]
    slots = 1 if joined is not None else keys_buf.shape[0]

    def loads(s):
        slot = s % slots
        return (
            pltpu.make_async_copy(kv_any.at[:, s], keys_buf.at[slot], load_sems.at[0, slot]),
            pltpu.make_async_copy(probs_any.at[s], prob_buf.at[slot], load_sems.at[1, slot]),
        )

    if joined is None:
        load = pltpu.make_async_copy(w_any.at[:, pl.ds(0, w_ref.shape[1])], w_ref, w_sem)
        load.start()
        early = (
            pltpu.make_async_copy(nf_any, part, early_sems.at[0]),
            pltpu.make_async_copy(dgu_any, d_in.at[:, pl.ds(0, dgu_any.shape[1])], early_sems.at[1]),
        )
        for copy in early:
            copy.start()
        rope_copy = pltpu.make_async_copy(
            rope_any.at[pl.ds(pl.multiple_of(at.dp * span, span), span), :], rope_ref, rope_sem
        )
        rope_copy.start()
        for copy in loads(0):
            copy.start()
        Neighbours(at).greet(flips=True)
        nf_ref, dgu_ref = part, d_in
    else:
        w_ref, nf_ref, dgu_ref = w_any, nf_any, dgu_any
    taps = jnp.concatenate([xt_ref[...], stt_ref[...]], 1)
    step_bias, decay_log, skips = head_ref[0:1, :], head_ref[1:2, :], head_ref[2:3, :]
    mixer_scale = mgain_ref[...].reshape(1, xw)

    def rows_of(buf):
        def view(rank, chunk):
            return buf.at[pl.ds(chunk * half, half), pl.ds(pl.multiple_of(rank * sub, sub), sub), :]

        return view

    scatters = []
    used = 0
    slots_used = 0
    kept = layout["gu"][0]

    def terms(first):
        return w_any if joined is not None and first >= kept else grads

    for first, columns, cross in pieces:

        def block(buf, k, first=first, columns=columns):
            return buf.at[pl.ds(pl.multiple_of(k * depth, depth), depth), pl.ds(first, columns)]

        if cross:
            wide = pl.ds(slots_used, columns)
            slots_used += columns
            scatters.append(
                CrossScatter(
                    at,
                    partial(block, terms(first)),
                    block(got, 0),
                    lambda zz, q, wide=wide: line2.at[
                        pl.ds(pl.multiple_of((zz * 2 + q) * depth, depth), depth), wide
                    ],
                    sems[used : used + 5],
                )
            )
            used += 5
        else:
            scatters.append(
                LineScatter(
                    at,
                    partial(block, terms(first)),
                    partial(block, got),
                    lambda zz, block=block: block(line, zz + 1),
                    partial(block, line),
                    sems[used : used + 6],
                )
            )
            used += 6

    def steps(i):
        @pl.loop(0, at.lines - 1)
        def _(s):
            scatters[i].step(s)

        if pieces[i][2]:
            scatters[i].join()

    def finish(i):
        first, columns, _ = pieces[i]
        scatters[i].finish(dw_ref.at[:, pl.ds(first, columns)])

    def product(lhs, rhs_ref, first, columns, into):
        tile = 2 * LANES if columns % (2 * LANES) == 0 else LANES

        @pl.loop(0, columns // tile)
        def _(j):
            src = pl.ds(pl.multiple_of(first + j * tile, LANES), tile)
            dst = pl.ds(pl.multiple_of(into + j * tile, LANES), tile)
            terms(into)[:, dst] = dot_tn(lhs, rhs_ref[:, src]).astype(BF16)

    def weights(i, lhs_ref, rhs_ref, first):
        into, columns, _ = pieces[i]
        product(lhs_ref[...].reshape(tokens, width), rhs_ref, first, columns, into)

    ff = layout["down"][1]

    def activations_ready():
        if joined is not None:
            joined.gathers[3].drain()
            joined.gathers[4].drain()
        weights(0, og_ref, act_ref, 0)
        scatters[0].start()

    if joined is not None:
        joined.activations_ready = activations_ready
        yield
    else:
        activations_ready()
        load.wait()
    dlow[...] = dot_nn(
        gb_ref[...].reshape(tokens, width), w_ref[:, pl.ds(*layout["out"])]
    )
    mixer_gain = jnp.zeros((1, xw), F32)
    sq_own[...] = jnp.zeros(sq_own.shape, F32)
    for s in range(seqs):
        gate = z_ref[s].astype(F32)
        gated = y_ref[s] * gate * jax.nn.sigmoid(gate)
        norm = lax.rsqrt(to_column(squares[s : s + 1, :]) / (4 * xw) + EPSILON)
        grad = dlow[pl.ds(s * span, span), pl.ds(qw, xw)]
        mixer_gain = mixer_gain + jnp.sum(grad * gated * norm, 0, keepdims=True)
        inner = jnp.sum(gated * grad * mixer_scale, 1, keepdims=True)
        sq_own[s : s + 1, :] = to_row(inner)
    total = TensorTotal(at, sq_own, sq_got, sq_send, sq_recv)
    total.start()
    if joined is None:
        for copy in early:
            copy.wait()
    weights(1, nf_ref, dgu_ref, 0)
    weights(2, nf_ref, dgu_ref, ff)
    inner_rows = total.finish()
    for s in range(seqs):
        gate = z_ref[s].astype(F32)
        sigmoid = jax.nn.sigmoid(gate)
        gated = y_ref[s] * gate * sigmoid
        norm = lax.rsqrt(to_column(squares[s : s + 1, :]) / (4 * xw) + EPSILON)
        inner = to_column(inner_rows[s : s + 1, :])
        term = dlow[pl.ds(s * span, span), pl.ds(qw, xw)] * mixer_scale
        grad = norm * (term - gated * (norm * norm * inner / (4 * xw)))
        dy[s] = grad * gate * sigmoid
        grad = grad * y_ref[s] * sigmoid * (1.0 + gate * (1.0 - sigmoid))
        d_in[pl.ds(s * span, span), pl.ds(*layout["z"])] = grad.astype(BF16)

    def parts(s):
        active = pre_ref[s] * jax.nn.sigmoid(pre_ref[s])
        step, rate, running = decay_parts(step_ref[s], decay_log, step_bias)
        state_in = active[:, xw : xw + size].astype(BF16)
        state_out = active[:, xw + size :].astype(BF16)
        return active[:, :xw], state_in, state_out, step, rate, running

    @pl.loop(0, seqs)
    def _(s):
        _, _, state_out, _, _, running = parts(s)
        factor = spread(jnp.exp(running) * aux_ref[s][:, 3:4], heads, head_dim)
        low = (dy[s] * factor).astype(BF16)
        local2[s, :size, :] = dot_tn(state_out, low).astype(BF16)
        local2[s, size:, :] = carry[s]

    passing = StatePass(
        at, local2, pass_refs[0], pass_refs[1], pass_refs[2], pass_refs[3], after_state,
        pass_refs[4:], True,
    )
    passing.start()
    scatters[1].start()
    weights(3, gb_ref, low_ref, 0)
    steps(0)
    @pl.loop(0, seqs)
    def _(s):
        x, state_in, state_out, step, _, running = parts(s)
        running_rows = running.T
        allowed = same_document(aux_ref[s], seg_ref[pl.ds(s, 1), :])
        xs = (x * spread(step, heads, head_dim)).astype(BF16)
        joined = dot_nt(state_out, state_in)
        lane = iota((span, LANES), 1)
        d_joined = jnp.zeros((span, span), F32)
        d_running = jnp.zeros((span, LANES), F32)
        blocks = []
        for h in range(heads):
            cols = slice(h * head_dim // LANES * LANES, h * head_dim // LANES * LANES + LANES)
            begin = h * head_dim % LANES
            inside = jnp.logical_and(lane >= begin, lane < begin + head_dim)
            grad = dy[s, :, pl.ds(cols.start, LANES)]
            decay = jnp.exp(running[:, h : h + 1] - running_rows[h : h + 1, :] + allowed)
            weight = joined * decay
            d_weight = dot_nt(jnp.where(inside, grad, 0.0).astype(BF16), xs[:, cols])
            d_joined = d_joined + d_weight * decay
            product_ = (d_weight * weight).astype(BF16)
            one = (lane == h).astype(BF16)
            d_running = d_running + dot_nn(product_, one) - dot_tn(product_, one)
            blocks.append(dot_tn(weight.astype(BF16), grad.astype(BF16)))
        dlow[pl.ds(pl.multiple_of(s * span, span), span), pl.ds(qw, xw)] = pick_halves(blocks, head_dim)
        d_joined = d_joined.astype(BF16)
        factor = spread(jnp.exp(running) * aux_ref[s][:, 3:4], heads, head_dim)
        crossed = dot_nn(state_out, entering[s]) * factor
        dcum[s] = d_running + head_sums(dy[s] * crossed, heads, head_dim)
        low = (dy[s] * factor).astype(BF16)
        dbc[s, :, :size] = dot_tn(d_joined, state_out)
        dbc[s, :, size:] = dot_nn(d_joined, state_in) + dot_nt(low, entering[s])

    passing.run()
    scatters[2].start()
    scatters[3].start()
    lane = iota((span, LANES), 1)
    upper = lane >= at_dim
    if joined is None:
        rope_copy.wait()
    cosine, sine = rope_ref[:, :LANES], rope_ref[:, LANES:]
    scale = 1.0 / math.sqrt(at_dim)
    for s in range(seqs):
        slot = s % slots
        if joined is None:
            for copy in loads(s):
                copy.wait()
            if slots > 1 and s + 1 < seqs:
                for copy in loads(s + 1):
                    copy.start()
            keys, weights_ref = keys_buf[slot].reshape(count, qw), prob_buf.at[slot]
        else:
            keys, weights_ref = kv_any[:, s].reshape(count, qw), probs_any.at[s]
        grad = dlow[pl.ds(s * span, span), pl.ds(0, qw)].astype(BF16).astype(F32)
        inner = grad * att_ref[s]
        d_keys = jnp.zeros((count, qw), F32)
        d_query = []
        for h in range(2):
            mine = upper if h else jnp.logical_not(upper)
            delta = jnp.sum(jnp.where(mine, inner, 0.0), 1, keepdims=True)
            moved = grad if h else pltpu.roll(grad, at_dim, 1)
            moved = jnp.where(upper, moved, 0.0).astype(BF16)
            weight = weights_ref[pl.ds(h * span, span), :]
            d_weight = dot_nt(moved, keys)
            d_score = (weight.astype(F32) * (d_weight - delta)).astype(BF16)
            query = q2_ref[s, pl.ds(h * span, span), :]
            d_keys = d_keys + dot_tn(d_score, query) + dot_tn(weight, moved)
            d_query.append(dot_nn(d_score, keys))
        dkv[:, s] = d_keys.astype(BF16).reshape(devices, span, qw)
        if joined is None and slots == 1 and s + 1 < seqs:
            for copy in loads(s + 1):
                copy.start()
        d_query = jnp.where(upper, pltpu.roll(d_query[1], at_dim, 1), d_query[0]) * scale
        d_in[pl.ds(s * span, span), pl.ds(*layout["q"])] = turn(
            d_query, cosine, -sine, at_dim // 2
        ).astype(BF16)
    kv_scatter = LineScatter(
        at,
        lambda k: dkv.at[k],
        lambda zz: dkv_got.at[zz],
        None,
        lambda zz: dkv_line.at[zz],
        kv_sems,
        causal=True,
    )
    kv_scatter.start()
    steps(1)
    finish(0)
    weights(4, nx_ref, d_in, pieces[4][0])
    scatters[4].start()
    passing.finish()
    tap_grads = [jnp.zeros((1, mixed), F32) for _ in range(4)]
    bias_grad = jnp.zeros((1, mixed), F32)
    step_grad = jnp.zeros((1, LANES), F32)
    decay_grad = jnp.zeros((1, LANES), F32)
    skip_grad = jnp.zeros((1, xw), F32)
    ext_grad[:, pl.ds(0, 8), :] = jnp.zeros((seqs, 8, mixed), F32)
    for s in range(seqs):
        aux = aux_ref[s]
        x, state_in, state_out, step, rate, running = parts(s)
        step_wide = spread(step, heads, head_dim)
        xs = x * step_wide
        end = running[span - 1 : span, :]
        tail = spread(jnp.exp(end - running) * aux[:, 4:5], heads, head_dim)
        later = after_state[s]
        found = dot_nn(state_in, later)
        weighted = xs * tail
        d_xs = dlow[pl.ds(s * span, span), pl.ds(qw, xw)] + found * tail
        d_in_state = dbc[s, :, :size] + dot_nt(weighted.astype(BF16), later)
        moved = head_sums(found * weighted, heads, head_dim)
        carried = jnp.sum(later.astype(F32) * entering[s].astype(F32), 0, keepdims=True)
        carried = head_sums(carried, heads, head_dim) * jnp.exp(end) * aux[span - 1 : span, 3:4]
        final = jnp.sum(moved, 0, keepdims=True) + carried
        d_running = dcum[s] - moved
        d_running = d_running + jnp.where(iota((span, LANES), 0) == span - 1, final, 0.0)
        d_decay = running_sum(d_running, backward=True)
        d_step = head_sums(d_xs * x, heads, head_dim) + d_decay * rate
        d_step = d_step * jax.nn.sigmoid(step_ref[s] + step_bias)
        d_in[pl.ds(s * span, span), pl.ds(*layout["step"])] = d_step.astype(BF16)
        step_grad = step_grad + jnp.sum(d_step, 0, keepdims=True)
        decay_grad = decay_grad + jnp.sum(d_decay * step, 0, keepdims=True) * rate
        skip_grad = skip_grad + jnp.sum(dy[s] * x, 0, keepdims=True)
        d_x = d_xs * step_wide + spread(skips, heads, head_dim) * dy[s]
        value = pre_ref[s]
        sigmoid = jax.nn.sigmoid(value)
        slope = sigmoid * (1.0 + value * (1.0 - sigmoid))
        outer = jnp.concatenate([d_x, d_in_state, dbc[s, :, size:]], 1) * slope
        bias_grad = bias_grad + jnp.sum(outer, 0, keepdims=True)
        ext_grad[s, pl.ds(8, span), :] = taps[3:4, :] * outer
        tap_grads[3] = tap_grads[3] + jnp.sum(
            outer * ext_ref[s, pl.ds(8, span), :], 0, keepdims=True
        )
        for back in (1, 2, 3):
            valid = outer * aux[:, back - 1 : back]
            tap_grads[3 - back] = tap_grads[3 - back] + jnp.sum(
                valid * ext_ref[s, pl.ds(8 - back, span), :], 0, keepdims=True
            )
            ext_grad[s, pl.ds(8 - back, span), :] += taps[3 - back : 4 - back, :] * valid
    before, after = at.dp > 0, at.dp < devices - 1

    def halo():
        return remote(
            ext_grad.at[:, pl.ds(0, 8), :],
            halo_got,
            halo_sems.at[0],
            halo_sems.at[1],
            {"dp": at.dp - 1},
        )

    pl.when(before)(lambda: halo().start())
    sums[...] = jnp.zeros(sums.shape, F32)
    sums[1:2, :] = fgain_ref[...]
    for k in range(4):
        sums[2 + k : 3 + k, pl.ds(0, sw)] = tap_grads[k][:, xw:]
        sums[8 + k : 9 + k, pl.ds(0, xw)] = tap_grads[k][:, :xw]
    sums[6:7, pl.ds(0, sw)] = bias_grad[:, xw:]
    sums[12:13, pl.ds(0, xw)] = bias_grad[:, :xw]
    sums[13:14, pl.ds(0, xw)] = mixer_gain
    sums[14:15, pl.ds(0, LANES)] = step_grad
    sums[14:15, pl.ds(LANES, LANES)] = decay_grad
    sums[14:15, pl.ds(2 * LANES, LANES)] = head_sums(
        jnp.broadcast_to(skip_grad, (8, xw)), heads, head_dim
    )[:1]
    steps(2)
    kv_scatter.run_causal(dkv_own)
    for s in range(seqs):
        key_cosine = jnp.where(upper, 1.0, cosine)
        key_sine = jnp.where(upper, 0.0, -sine)
        d_in[pl.ds(s * span, span), pl.ds(*layout["kv"])] = turn(
            dkv_own[s], key_cosine, key_sine, at_dim // 2
        ).astype(BF16)
    pl.when(after)(lambda: halo().wait_recv())
    ends = pl.ds(span, 8)

    @pl.when(after)
    def _():
        ext_grad[:, ends, :] += halo_got[...]

    value = ext_grad[:, pl.ds(8, span), :].reshape(tokens, mixed).astype(BF16)
    d_in[:, pl.ds(layout["x"][0], mixed)] = value
    back = RowScatter(
        at,
        rows_of(part),
        lambda which, chunk: near.at[which, pl.ds(chunk * half, half)],
        lambda chunk: far.at[pl.ds(chunk * half, half)],
        send,
        recv,
    )
    weights(5, nx_ref, d_in, pieces[5][0])
    scatters[5].start()
    back = RowScatter(
        at,
        rows_of(part),
        lambda which, chunk: near.at[which, pl.ds(chunk * half, half)],
        lambda chunk: far.at[pl.ds(chunk * half, half)],
        send,
        recv,
    )
    for c in range(2):
        value = dot_nt(d_in[pl.ds(c * rows, rows), :], w_ref[:, pl.ds(0, in_w)])
        part[pl.ds(c * half, half)] = value.astype(BF16).reshape(half, span, width)
        back.start(c)
    weights(6, nx_ref, d_in, pieces[6][0])
    scatters[6].start()
    steps(3)
    finish(1)
    for c in range(2):
        back.middle(c)
    steps(4)
    finish(2)
    total = jnp.zeros((1, width), F32)
    gain = gain_ref[...].reshape(1, width)
    for c in range(2):
        seq = pl.ds(c * half, half)
        grad, terms = rms_rows_grad(x_ref[seq].astype(F32), gain, back.finish(c))
        rg_ref[seq] = gh_ref[seq] + grad
        total = total + jnp.sum(terms.reshape(half * sub, width), 0, keepdims=True)
    sums[0:1, :] = total
    exchanges = [
        (sums.at[pl.ds(0, 8)], small_near, small_send.at[0], small_recv.at[0], {"tensor": at.t_near}),
        (sums.at[pl.ds(0, 8)], small_far, small_send.at[1], small_recv.at[1], {"tensor": at.t_far}),
    ] + [
        (sums, small_dp.at[i], dp_send.at[i], dp_recv.at[i], {"dp": other})
        for i, other in enumerate(at.flips())
    ]

    def begin(i):
        remote(*exchanges[i]).start()

    def end(i):
        remote(*exchanges[i]).wait()
        into, other = exchanges[i][:2]
        into[...] += other[...]

    begin(0)
    finish(3)
    end(0)
    begin(1)
    steps(5)
    end(1)
    begin(2)
    finish(4)
    end(2)
    begin(3)
    steps(6)
    end(3)
    finish(5)
    kvw = layout["kv"][1]
    kv_near[0, :, pl.ds(0, kvw)] = dw_ref[:, pl.ds(*layout["kv"])]
    kv_near[0, :, pl.ds(kvw, sw)] = dw_ref[:, pl.ds(*layout["state"])]
    copy = remote(kv_near.at[0], kv_near.at[1], kv_send.at[0], kv_recv.at[0], {"tensor": at.t_near})
    copy.start()
    begin(4)
    finish(6)
    copy.wait()
    kv_far[0] = kv_near[0] + kv_near[1]
    copy = remote(kv_far.at[0], kv_far.at[1], kv_send.at[1], kv_recv.at[1], {"tensor": at.t_far})
    copy.start()
    end(4)
    for i in range(5, len(exchanges)):
        begin(i)
        end(i)
    copy.wait()
    kvs[:, pl.ds(0, kvw)] = kv_far[0, :, pl.ds(0, kvw)]
    kvs[:, pl.ds(kvw, kvw)] = kv_far[1, :, pl.ds(0, kvw)]

    @pl.when(at.t >= 2)
    def _():
        kvs[:, pl.ds(0, kvw)] = kv_far[1, :, pl.ds(0, kvw)]
        kvs[:, pl.ds(kvw, kvw)] = kv_far[0, :, pl.ds(0, kvw)]

    kvs[:, pl.ds(2 * kvw, sw)] = kv_far[0, :, pl.ds(kvw, sw)] + kv_far[1, :, pl.ds(kvw, sw)]
    for scatter in [*scatters, kv_scatter]:
        scatter.drain()
    for c in range(2):
        back.drain(c)
    pl.when(before)(lambda: halo().wait_send())
    yield


def scatter_sems(devices, pieces):
    dma = pltpu.SemaphoreType.DMA
    out = []
    for _, _, cross in pieces:
        if cross:
            out += [dma((2,))] + [dma((devices,)) for _ in range(4)]
        else:
            out += line_scatter_sems(devices)
    return out


def back_specs(cfg, joined=False):
    devices, layout, pieces = (cfg[k] for k in ("devices", "layout", "scatters"))
    seqs, sub, width = cfg["rows"]
    span = sub * 4
    tokens = seqs * span
    half = seqs // 2
    depth = width // devices
    lines = devices // 2
    columns = layout["down"][0] + layout["down"][1]
    xw, sw, qw, kvw = (layout[k][1] for k in ("x", "state", "q", "kv"))
    size = sw // 2
    mixed = xw + sw
    in_w = layout["in"][1]
    own = (seqs, sub, width)
    rounds = devices.bit_length() - 1
    crossed = max(LANES, sum(piece[1] for piece in pieces if piece[2]))
    slots = 2 if devices * span <= 2048 else 1
    dma = pltpu.SemaphoreType.DMA
    outs = (
        (own, F32),
        ((depth, columns), F32),
        ((16, width), F32),
        ((depth, 2 * kvw + sw), F32),
    )
    scratch = {
        "w": pltpu.VMEM((width, in_w + qw + xw), BF16),
        "d_in": pltpu.VMEM((tokens, in_w), BF16),
        "dlow": pltpu.VMEM((tokens, qw + xw), F32),
        "dy": pltpu.VMEM((seqs, span, xw), F32),
        "dbc": pltpu.VMEM((seqs, span, sw), F32),
        "dcum": pltpu.VMEM((seqs, span, LANES), F32),
        "ext_grad": pltpu.VMEM((seqs, span + 8, mixed), F32),
        "halo_got": pltpu.VMEM((seqs, 8, mixed), F32),
        "local2": pltpu.VMEM((seqs, size + 16, xw), BF16),
        "after_state": pltpu.VMEM((seqs, size, xw), BF16),
        "keys_buf": pltpu.VMEM((slots, devices, span, qw), BF16),
        "prob_buf": pltpu.VMEM((slots, 2 * span, devices * span), BF16),
        "dkv": pltpu.VMEM((devices, seqs, span, qw), BF16),
        "dkv_got": pltpu.VMEM((lines, seqs, span, qw), BF16),
        "dkv_line": pltpu.VMEM((lines, seqs, span, qw), BF16),
        "dkv_own": pltpu.VMEM((seqs, span, qw), F32),
        "part": pltpu.VMEM((seqs, span, width), BF16),
        "near": pltpu.VMEM((2,) + own, BF16),
        "far": pltpu.VMEM(own, BF16),
        "grads": pltpu.VMEM((width, layout["gu"][0] if joined else columns), BF16),
        "got": pltpu.VMEM((lines * depth, columns), BF16),
        "line": pltpu.VMEM(((lines + 1) * depth, columns), BF16),
        "line2": pltpu.VMEM(((lines + 1) * 2 * depth, crossed), BF16),
        "small_near": pltpu.VMEM((8, width), F32),
        "small_far": pltpu.VMEM((8, width), F32),
        "small_dp": pltpu.VMEM((rounds, 16, width), F32),
        "kv_near": pltpu.VMEM((2, depth, kvw + sw), F32),
        "kv_far": pltpu.VMEM((2, depth, kvw + sw), F32),
        "sq_own": pltpu.VMEM((8, span), F32),
        "sq_got": pltpu.VMEM((3, 8, span), F32),
        "rope": pltpu.VMEM((span, 2 * LANES), F32),
        "w_sem": dma,
        "early_sems": dma((2,)),
        "rope_sem": dma,
        "load_sems": dma((2, 2)),
        "halo_sems": dma((2,)),
        "sq_send": dma((3,)),
        "sq_recv": dma((3,)),
        "send": dma((2, 3)),
        "recv": dma((2, 4)),
        "small_send": dma((2,)),
        "small_recv": dma((2,)),
        "dp_send": dma((rounds,)),
        "dp_recv": dma((rounds,)),
        "kv_send": dma((2,)),
        "kv_recv": dma((2,)),
    }
    rest = (
        state_pass_scratch(half, size, xw)
        + line_scatter_sems(devices)
        + scatter_sems(devices, pieces)
    )
    return outs, scratch, rest


APART = (
    "w", "keys_buf", "prob_buf", "part", "rope", "w_sem", "early_sems", "rope_sem", "load_sems",
)


def run_back(cfg, *refs):
    for _ in back_kernel(cfg, *refs):
        pass


def backward(cfg, x, *args):
    outs, scratch, rest = back_specs(cfg)
    vmem = pl.BlockSpec(memory_space=pltpu.VMEM)
    in_specs = [vmem] * (1 + len(args))
    for i in (3, 8, 9, 11, 13, 25):
        in_specs[i] = pl.BlockSpec(memory_space=pl.ANY)
    return pl.pallas_call(
        partial(run_back, cfg),
        out_shape=tuple(jax.ShapeDtypeStruct(*out) for out in outs),
        in_specs=in_specs,
        out_specs=(vmem,) * len(outs),
        scratch_shapes=list(scratch.values()) + rest,
        compiler_params=pltpu.CompilerParams(
            collective_id=2, has_side_effects=True, vmem_limit_bytes=VMEM_BYTES
        ),
        name="backward",
    )(x, *args)


class Joined:
    def __init__(self, dn_in):
        self.dn_in = dn_in
        self.drains = []


def joined_kernel(cfg, *refs):
    devices, layout = cfg["devices"], cfg["layout"]
    inputs, refs = refs[:21], refs[21:]
    dn_in, fgain_ref = inputs[19:]
    x_ref, og_in, gain_ref = inputs[:3]
    rope_any, xt_ref, _, stt_ref, _, head_ref, mgain_ref = inputs[12:19]
    inputs = inputs[:19]
    block_out, rg, dw, sums, kvs = refs[:5]
    refs = refs[5:]

    def take(count):
        nonlocal refs
        taken, refs = refs[:count], refs[count:]
        return taken

    mix_outs, mix_scratch = mixer_specs(cfg, layout["down"][0] + layout["down"][1])
    mixed = take(len(mix_outs))
    mixed_scratch = take(len(mix_scratch))
    ffn_outs, buffers, _, sems = ffn_specs(cfg)
    fed = (block_out, *take(len(ffn_outs) - 1))
    fed_scratch = (*take(len(buffers)), None, None, None, *take(len(sems)))
    _, scratch, rest = back_specs(cfg, True)
    names = [name for name in scratch if name not in APART]
    mine = dict(zip(names, take(len(names))))
    mine["part"] = fed_scratch[0]
    mine["rope"] = mixed_scratch[3]
    back_scratch = [mine.get(name) for name in scratch] + list(take(len(rest)))
    (
        w_all, nx, og, low, kv, q2, probs, att, ext, pre, step_buf, entering, carry, y_buf, z_buf,
        squares, aux_ref, seg_rows,
    ) = mixed
    _, gh, gb, nf, act, dgu, gain_part = fed
    joined = Joined(dn_in)
    later = back_kernel(
        cfg, x_ref, gh, gain_ref, w_all, nx, og, gb, low, nf, dgu, act, kv, q2, probs, att, ext, pre,
        step_buf, entering, carry, y_buf, z_buf, squares, aux_ref, seg_rows, rope_any, xt_ref, stt_ref,
        head_ref, mgain_ref, gain_part, rg, dw, sums, kvs, *back_scratch, joined=joined,
    )
    mixer_kernel(cfg, *inputs, *mixed, *mixed_scratch, joined=joined)
    next(later)
    ffn_kernel(
        devices, layout, x_ref, low, og, og_in, fgain_ref, w_all, None, *fed, *fed_scratch,
        joined=joined,
    )
    next(later)
    for drain in joined.drains:
        drain()


def joined_layer(cfg, *args):
    layout = cfg["layout"]
    mix_outs, mix_scratch = mixer_specs(cfg, layout["down"][0] + layout["down"][1])
    ffn_outs, buffers, _, sems = ffn_specs(cfg)
    outs, scratch, rest = back_specs(cfg, True)
    vmem = pl.BlockSpec(memory_space=pltpu.VMEM)
    in_specs = [vmem] * len(args)
    in_specs[12] = pl.BlockSpec(memory_space=pl.ANY)
    return pl.pallas_call(
        partial(joined_kernel, cfg),
        out_shape=tuple(jax.ShapeDtypeStruct(*out) for out in (ffn_outs[0], *outs)),
        in_specs=in_specs,
        out_specs=(vmem,) * 5,
        scratch_shapes=[pltpu.VMEM(*out) for out in mix_outs]
        + mix_scratch
        + [pltpu.VMEM(*out) for out in ffn_outs[1:]]
        + buffers
        + sems
        + [ref for name, ref in scratch.items() if name not in APART]
        + rest,
        compiler_params=pltpu.CompilerParams(
            collective_id=0, has_side_effects=True, vmem_limit_bytes=VMEM_BYTES
        ),
        name="layer",
    )(*args)


def unpack_kernel(layout, local, *refs):
    (
        dw, kvs, sums, rg, block,
        block_out, rg_out, gain1, gain2, wq, wkv, wao, wmi, wst, wsp, cw, cb, csw, csb, sbias,
        dlog, skip, mgain, wmo, wgu, wdn,
    ) = refs
    block_out[...] = block[...]
    rg_out[...] = rg[...]
    width = sums.shape[1]
    xw, sw = layout["x"][1], layout["state"][1]
    qw = layout["q"][1]
    ff = layout["down"][1]
    kvw = layout["kv"][1]

    def part(name):
        return dw[:, pl.ds(*layout[name])]

    gain1[...] = sums[0:1, :].reshape(width)
    gain2[...] = sums[1:2, :].reshape(width)
    wq[...] = part("q")
    wkv[:, 0, :] = kvs[:, :kvw]
    wkv[:, 1, :] = kvs[:, kvw : 2 * kvw]
    out = part("out")
    wao[...] = out[:, :qw].T
    wmo[...] = out[:, qw:].T
    wdn[...] = part("down").T
    wmi[:, 0, :] = part("z")
    wmi[:, 1, :] = part("x")
    wst[...] = kvs[:, 2 * kvw :]
    wsp[...] = part("step")[:, :local]
    gate_up = part("gu")
    wgu[:, 0, :] = gate_up[:, :ff]
    wgu[:, 1, :] = gate_up[:, ff:]
    cw[...] = sums[8:12, :xw]
    cb[...] = sums[12:13, :xw].reshape(xw)
    csw[...] = sums[2:6, :sw]
    csb[...] = sums[6:7, :sw].reshape(sw)
    sbias[...] = sums[14:15, :local].reshape(local)
    dlog[...] = sums[14:15, LANES : LANES + local].reshape(local)
    skip[...] = sums[14:15, 2 * LANES : 2 * LANES + local].reshape(local)
    mgain[...] = sums[13:14, :xw].reshape(xw)


def unpack(layout, local, dw, kvs, sums, rg, block):
    depth = dw.shape[0]
    width = sums.shape[1]
    xw, sw, qw, ff, kvw = (layout[k][1] for k in ("x", "state", "q", "down", "kv"))

    def shape(*dims):
        return jax.ShapeDtypeStruct(dims, F32)

    outs = (
        jax.ShapeDtypeStruct(block.shape, BF16),
        shape(*rg.shape),
        shape(width),
        shape(width),
        shape(depth, qw),
        shape(depth, 2, kvw),
        shape(qw, depth),
        shape(depth, 2, xw),
        shape(depth, sw),
        shape(depth, local),
        shape(4, xw),
        shape(xw),
        shape(4, sw),
        shape(sw),
        shape(local),
        shape(local),
        shape(local),
        shape(xw),
        shape(xw, depth),
        shape(depth, 2, ff),
        shape(ff, depth),
    )
    vmem = pl.BlockSpec(memory_space=pltpu.VMEM)
    return pl.pallas_call(
        partial(unpack_kernel, layout, local),
        out_shape=outs,
        in_specs=[vmem] * 5,
        out_specs=(vmem,) * len(outs),
        name="unpack",
    )(dw, kvs, sums, rg, block)


def rope_table(length, head_dim):
    half = head_dim // 2
    frequency = np.exp(-math.log(ROTARY_BASE) * 2.0 * np.arange(half) / head_dim)
    angle = np.arange(length)[:, None] * frequency[None, :]
    cosine, sine = np.cos(angle), np.sin(angle)
    copies = LANES // head_dim
    table = [cosine, cosine] * copies + [-sine, sine] * copies
    return np.concatenate(table, 1).astype(np.float32)


def body(
    resid_in,
    segment_ids,
    out_grad,
    input_gain,
    ffn_gain,
    query_weight,
    keyvalue_weight,
    attention_output_weight,
    mixer_input_weight,
    state_input_weight,
    step_weight,
    conv_mixer,
    conv_mixer_bias,
    conv_state,
    conv_state_bias,
    step_bias,
    decay_log,
    skip_gain,
    mixer_gain,
    mixer_output_weight,
    gate_up_weight,
    down_weight,
):
    shard_count = lax.axis_size("dp")
    head_dim = keyvalue_weight.shape[2] // 2
    query_width = query_weight.shape[1]
    mixer_local = step_weight.shape[1]
    mixer_width = conv_mixer.shape[1]
    state_width = state_input_weight.shape[1]
    ff = down_weight.shape[0]
    layout = {}
    columns = 0
    for name, size in (
        ("x", mixer_width),
        ("state", state_width),
        ("step", LANES),
        ("kv", 2 * head_dim),
        ("q", query_width),
        ("z", mixer_width),
        ("out", query_width + mixer_width),
        ("gu", 2 * ff),
        ("down", ff),
    ):
        layout[name] = (columns, size)
        columns += size
    layout["in"] = (0, layout["out"][0])
    kv_at, q_at, gu_at = (layout[k][0] for k in ("kv", "q", "gu"))
    config = {
        "devices": shard_count,
        "layout": layout,
        "heads": mixer_local,
        "rows": resid_in.shape,
        "pieces": (
            (0, kv_at, False),
            (kv_at, layout["out"][0] - kv_at, False),
            (*layout["out"], True),
            (*layout["gu"], False),
        ),
        "scatters": (
            (*layout["down"], False),
            (gu_at, ff, False),
            (gu_at + ff, ff, False),
            (*layout["out"], True),
            (q_at, layout["out"][0] - q_at, False),
            (layout["state"][0], q_at - layout["state"][0], False),
            (*layout["x"], False),
        ),
    }

    def lanes(array):
        return jnp.pad(array, (0, LANES - array.shape[0]))

    head_rows = jnp.stack([lanes(step_bias), lanes(decay_log), lanes(skip_gain)])
    rope = jnp.asarray(rope_table(segment_ids.shape[1], head_dim))
    raw = (
        resid_in,
        out_grad,
        input_gain,
        query_weight,
        keyvalue_weight,
        mixer_input_weight,
        state_input_weight,
        step_weight,
        gate_up_weight,
        attention_output_weight,
        mixer_output_weight,
        segment_ids,
        rope,
        conv_mixer,
        conv_mixer_bias,
        conv_state,
        conv_state_bias,
        head_rows,
        mixer_gain,
    )
    if segment_ids.size <= JOINED_TOKENS:
        config["pieces"] = (*config["pieces"], (*layout["down"], False))
        block_out, resid_grad, weight_grads, sums, replicated = joined_layer(
            config, *raw, down_weight, ffn_gain
        )
        return unpack(
            layout, mixer_local, weight_grads, replicated, sums, resid_grad, block_out
        )
    (
        w_all, span_normed_input, span_gradient, branch_low, keys, queries, probs, attention, ext,
        pre, step_pre, entering, state_decay, mixer_y, gate_z, squares, aux, seg_rows,
    ) = mixer(config, *raw)
    block_out, grad_hidden, grad_branch, span_feedforward, activated, grad_gate_up, ffn_gain_part = (
        feed_forward(
            config,
            resid_in,
            branch_low,
            span_gradient,
            out_grad,
            ffn_gain,
            w_all,
            down_weight,
        )
    )
    resid_grad, weight_grads, sums, replicated = backward(
        config,
        resid_in,
        grad_hidden,
        input_gain,
        w_all,
        span_normed_input,
        span_gradient,
        grad_branch,
        branch_low,
        span_feedforward,
        grad_gate_up,
        activated,
        keys,
        queries,
        probs,
        attention,
        ext,
        pre,
        step_pre,
        entering,
        state_decay,
        mixer_y,
        gate_z,
        squares,
        aux,
        seg_rows,
        rope,
        conv_mixer,
        conv_state,
        head_rows,
        mixer_gain,
        ffn_gain_part,
    )
    return unpack(layout, mixer_local, weight_grads, replicated, sums, resid_grad, block_out)


def solution(mesh):
    placed = (
        P(None, ("dp", "tensor"), None),
        P(),
        P(None, ("dp", "tensor"), None),
        P(),
        P(),
        P("dp", "tensor"),
        P("dp", None, None),
        P("tensor", "dp"),
        P("dp", None, "tensor"),
        P("dp", None),
        P("dp", "tensor"),
        P(None, "tensor"),
        P("tensor"),
        P(),
        P(),
        P("tensor"),
        P("tensor"),
        P("tensor"),
        P("tensor"),
        P("tensor", "dp"),
        P("dp", None, "tensor"),
        P("tensor", "dp"),
    )
    return jax.shard_map(
        body,
        mesh=mesh,
        in_specs=placed,
        out_specs=(
            P(None, ("dp", "tensor"), None),
            P(None, ("dp", "tensor"), None),
            P(),
            P(),
            P("dp", "tensor"),
            P("dp", None, None),
            P("tensor", "dp"),
            P("dp", None, "tensor"),
            P("dp", None),
            P("dp", "tensor"),
            P(None, "tensor"),
            P("tensor"),
            P(),
            P(),
            P("tensor"),
            P("tensor"),
            P("tensor"),
            P("tensor"),
            P("tensor", "dp"),
            P("dp", None, "tensor"),
            P("tensor", "dp"),
        ),
        check_vma=False,
    )
```

```python
from functools import partial
import math

import jax
import jax.numpy as jnp
import numpy as np
from jax import lax
from jax.experimental import pallas as pl
from jax.experimental.pallas import tpu as pltpu
from jax.sharding import PartitionSpec as P

KVH = 2
EPSILON = 1e-05
ROTARY_BASE = 100000000000.0
MASKED = -1e30
MATMUL_EXACTNESS = lax.Precision.HIGHEST
LANES = 128
F32 = jnp.float32
BF16 = jnp.bfloat16
VMEM_BYTES = 63 * 2**20
JOINED_TOKENS = 4096


def dot_nn(a, b):
    return lax.dot_general(a, b, (((1,), (0,)), ((), ())), preferred_element_type=F32)


def dot_nt(a, b):
    return lax.dot_general(a, b, (((1,), (1,)), ((), ())), preferred_element_type=F32)


def dot_tn(a, b):
    return lax.dot_general(a, b, (((0,), (0,)), ((), ())), preferred_element_type=F32)


def remote(src, dst, send_sem, recv_sem, where):
    return pltpu.make_async_remote_copy(
        src_ref=src,
        dst_ref=dst,
        send_sem=send_sem,
        recv_sem=recv_sem,
        device_id=where,
        device_id_type=pl.DeviceIdType.MESH,
    )


def add_into(ref, *others):
    total = ref[...].astype(F32)
    for other in others:
        total = total + other[...].astype(F32)
    ref[...] = total.astype(BF16)


class Place:
    def __init__(self, devices):
        self.devices = devices
        self.lines = devices // 2
        self.dp = lax.axis_index("dp")
        self.t = lax.axis_index("tensor")
        self.z = lax.div(self.dp, 2)
        self.p = lax.rem(self.dp, 2)
        self.pair = self.dp + 1 - 2 * self.p
        self.t_near = self.t + 1 - 2 * lax.rem(self.t, 2)
        self.t_far = lax.rem(self.t + 2, 4)
        self.t_both = lax.rem(self.t_near + 2, 4)
        self.first = self.z == 0
        self.last = self.z == self.lines - 1

    def flips(self):
        bit = 1
        while bit < self.devices:
            yield self.dp + bit - 2 * bit * lax.rem(lax.div(self.dp, bit), 2)
            bit *= 2


class LineGather:
    def __init__(self, place, view, recv, right, left, pair, causal=False):
        self.at, self.view = place, view
        self.causal = causal
        self.recv, self.right, self.left, self.side = recv, right, left, pair

    def copy(self, block, sem, where):
        ref = self.view(block)
        return remote(ref, ref, sem, self.recv.at[block], where)

    def send_right(self, zz):
        return self.copy(zz * 2 + self.at.p, self.right.at[zz], {"dp": self.at.dp + 2})

    def send_left(self, zz):
        return self.copy(zz * 2 + self.at.p, self.left.at[zz], {"dp": self.at.dp - 2})

    def send_pair(self, zz):
        return self.copy(zz * 2 + self.at.p, self.side.at[zz], {"dp": self.at.pair})

    def arrived(self, block):
        self.copy(block, self.side.at[0], {"dp": self.at.pair}).wait_recv()

    def start(self):
        at = self.at
        pl.when(jnp.logical_not(at.last))(lambda: self.send_right(at.z).start())
        if not self.causal:
            pl.when(jnp.logical_not(at.first))(lambda: self.send_left(at.z).start())
        self.send_pair(at.z).start()

    def step(self, s):
        at = self.at
        low, high = at.z - 1 - s, at.z + 1 + s

        @pl.when(low >= 0)
        def _():
            self.arrived(low * 2 + at.p)
            pl.when(jnp.logical_not(at.last))(lambda: self.send_right(low).start())
            self.send_pair(low).start()

        if self.causal:
            return

        @pl.when(high < at.lines)
        def _():
            self.arrived(high * 2 + at.p)
            pl.when(jnp.logical_not(at.first))(lambda: self.send_left(high).start())
            self.send_pair(high).start()

    def finish(self):
        at = self.at

        @pl.loop(0, at.z + 1 if self.causal else at.lines)
        def _(zz):
            self.arrived(zz * 2 + 1 - at.p)

    def drain(self):
        at = self.at

        @pl.loop(0, at.z + 1 if self.causal else at.lines)
        def _(zz):
            self.send_pair(zz).wait_send()

            @pl.when(jnp.logical_and(zz <= at.z, jnp.logical_not(at.last)))
            def _():
                self.send_right(zz).wait_send()

            if self.causal:
                return

            @pl.when(jnp.logical_and(zz >= at.z, jnp.logical_not(at.first)))
            def _():
                self.send_left(zz).wait_send()


class CrossGather:
    def __init__(self, place, view, recv, right, left, pair):
        self.at, self.view = place, view
        self.recv, self.right, self.left, self.side = recv, right, left, pair

    def copy(self, block, sem, where):
        ref = self.view(block)
        return remote(ref, ref, sem, self.recv.at[block], where)

    def send_right(self, block):
        return self.copy(block, self.right.at[block], {"dp": self.at.dp + 2})

    def send_left(self, block):
        return self.copy(block, self.left.at[block], {"dp": self.at.dp - 2})

    def send_pair(self):
        return self.copy(self.at.dp, self.side.at[0], {"dp": self.at.pair})

    def arrived(self, block):
        self.copy(block, self.side.at[0], {"dp": self.at.pair}).wait_recv()

    def onward(self, block, right, left):
        at = self.at
        if right:
            pl.when(jnp.logical_not(at.last))(lambda: self.send_right(block).start())
        if left:
            pl.when(jnp.logical_not(at.first))(lambda: self.send_left(block).start())

    def start(self):
        self.send_pair().start()
        self.onward(self.at.dp, True, True)

    def begin(self):
        self.arrived(self.at.pair)
        self.onward(self.at.pair, True, True)

    def step(self, s):
        at = self.at
        low, high = at.z - 1 - s, at.z + 1 + s
        for q in (at.p, 1 - at.p):

            @pl.when(low >= 0)
            def _():
                self.arrived(low * 2 + q)
                self.onward(low * 2 + q, True, False)

            @pl.when(high < at.lines)
            def _():
                self.arrived(high * 2 + q)
                self.onward(high * 2 + q, False, True)

    def finish(self):
        pass

    def drain(self):
        at = self.at
        self.send_pair().wait_send()

        @pl.loop(0, at.devices)
        def _(block):
            zz = lax.div(block, 2)

            @pl.when(jnp.logical_and(zz <= at.z, jnp.logical_not(at.last)))
            def _():
                self.send_right(block).wait_send()

            @pl.when(jnp.logical_and(zz >= at.z, jnp.logical_not(at.first)))
            def _():
                self.send_left(block).wait_send()


class DirectScatter:
    def __init__(self, place, part, got, line, sems, causal=False):
        self.at, self.part, self.got, self.line = place, part, got, line
        self.pair_send, self.pair_recv, self.line_send, self.line_recv = sems
        self.causal = causal

    def pair_copy(self, zz):
        src = self.part(zz * 2 + 1 - self.at.p)
        return remote(
            src, self.got(zz), self.pair_send.at[zz], self.pair_recv.at[zz], {"dp": self.at.pair}
        )

    def line_copy(self, zz):
        target = zz * 2 + self.at.p
        return remote(
            self.part(target),
            self.line(self.at.z),
            self.line_send.at[zz],
            self.line_recv.at[self.at.z],
            {"dp": target},
        )

    def line_arrived(self, zz):
        here = self.part(self.at.dp)
        remote(
            here, self.line(zz), self.line_send.at[zz], self.line_recv.at[zz], {"dp": self.at.pair}
        ).wait_recv()

    def target(self, i):
        return i if self.causal else lax.rem(self.at.z + 1 + i, self.at.lines)

    def start(self):
        @pl.loop(0, self.at.z + 1 if self.causal else self.at.lines)
        def _(i):
            self.pair_copy(self.target(i)).start()

    def send(self):
        @pl.loop(0, self.at.z if self.causal else self.at.lines - 1)
        def _(i):
            zz = self.target(i)
            self.pair_copy(zz).wait_recv()
            add_into(self.part(zz * 2 + self.at.p), self.got(zz))
            self.line_copy(zz).start()

    def finish(self, out):
        at = self.at
        self.pair_copy(at.z).wait_recv()
        out[...] = self.part(at.dp)[...].astype(F32) + self.got(at.z)[...].astype(F32)

        @pl.loop(at.z + 1 if self.causal else 0, at.lines)
        def _(zz):
            @pl.when(zz != at.z)
            def _():
                self.line_arrived(zz)
                out[...] += self.line(zz)[...].astype(F32)

    def drain(self):
        at = self.at

        @pl.loop(0, at.z + 1 if self.causal else at.lines)
        def _(zz):
            self.pair_copy(zz).wait_send()
            pl.when(zz != at.z)(lambda: self.line_copy(zz).wait_send())


class RowGather:
    def __init__(self, place, view, send, recv):
        self.at, self.view, self.send, self.recv = place, view, send, recv

    def copy(self, rank, chunk, sem, near):
        ref = self.view(rank, chunk)
        where = {"tensor": self.at.t_near if near else self.at.t_far}
        return remote(ref, ref, self.send.at[chunk, sem], self.recv.at[chunk, rank], where)

    def start(self, chunk):
        self.copy(self.at.t, chunk, 0, False).start()
        self.copy(self.at.t, chunk, 1, True).start()

    def forward(self, chunk):
        self.copy(self.at.t_far, chunk, 2, False).wait_recv()
        self.copy(self.at.t_far, chunk, 2, True).start()

    def finish(self, chunk):
        self.copy(self.at.t_near, chunk, 1, True).wait_recv()
        self.copy(self.at.t_both, chunk, 2, True).wait_recv()

    def drain(self, chunk):
        self.copy(self.at.t, chunk, 0, False).wait_send()
        self.copy(self.at.t, chunk, 1, True).wait_send()
        self.copy(self.at.t_far, chunk, 2, True).wait_send()


class RowScatter:
    def __init__(self, place, view, near_buf, far_buf, send, recv):
        self.at, self.view = place, view
        self.near_buf, self.far_buf = near_buf, far_buf
        self.send, self.recv = send, recv

    def near_copy(self, chunk, which):
        rank = self.at.t_both if which else self.at.t_near
        return remote(
            self.view(rank, chunk),
            self.near_buf(which, chunk),
            self.send.at[chunk, which],
            self.recv.at[chunk, which],
            {"tensor": self.at.t_near},
        )

    def far_copy(self, chunk):
        return remote(
            self.view(self.at.t_far, chunk),
            self.far_buf(chunk),
            self.send.at[chunk, 2],
            self.recv.at[chunk, 2],
            {"tensor": self.at.t_far},
        )

    def start(self, chunk):
        self.near_copy(chunk, 1).start()
        self.near_copy(chunk, 0).start()

    def middle(self, chunk):
        self.near_copy(chunk, 1).wait_recv()
        ref = self.view(self.at.t_far, chunk)
        ref[...] = (ref[...].astype(F32) + self.near_buf(1, chunk)[...].astype(F32)).astype(BF16)
        self.far_copy(chunk).start()

    def finish(self, chunk):
        self.near_copy(chunk, 0).wait_recv()
        total = self.view(self.at.t, chunk)[...].astype(F32) + self.near_buf(0, chunk)[
            ...
        ].astype(F32)
        self.far_copy(chunk).wait_recv()
        return total + self.far_buf(chunk)[...].astype(F32)

    def drain(self, chunk):
        self.near_copy(chunk, 0).wait_send()
        self.near_copy(chunk, 1).wait_send()
        self.far_copy(chunk).wait_send()


def line_gather_sems(devices):
    dma = pltpu.SemaphoreType.DMA
    return [dma((devices,)), dma((devices // 2,)), dma((devices // 2,)), dma((devices // 2,))]


def scatter_sems(devices):
    return [pltpu.SemaphoreType.DMA((devices // 2,)) for _ in range(4)]


def rms_rows(values, gain):
    return values * lax.rsqrt(jnp.mean(values * values, -1, keepdims=True) + EPSILON) * gain


def rms_rows_grad(values, gain, grad):
    scale = lax.rsqrt(jnp.mean(values * values, -1, keepdims=True) + EPSILON)
    term = grad * gain
    inner = jnp.mean(values * term, -1, keepdims=True)
    return scale * (term - values * (scale * scale * inner)), grad * values * scale


def ffn_kernel(devices, layout, *refs, joined=None):
    (
        x_ref, a_ref, og_ref, ogl_ref, gain_ref, w_any, dn_in,
        out_ref, gh_ref, gb, nf, act, dgu, gain_grad,
        part, part2, near1, far1, near2, far2, near3, far3, hid,
        w_ref, w_dn, w_sem, send, recv, *sems,
    ) = refs
    at = Place(devices)
    seqs, sub, width = x_ref.shape
    span = sub * 4
    half = seqs // 2
    rows = half * span
    first = layout["out"][0] if joined is None else 0
    out_w, gu_w = (pl.ds(layout[k][0] - first, layout[k][1]) for k in ("out", "gu"))
    ff = layout["down"][1]
    if joined is None:
        depth = dn_in.shape[1]
        load = pltpu.make_async_copy(w_any.at[:, pl.ds(first, w_ref.shape[1])], w_ref, w_sem)
        load.start()
        w_dn[pl.ds(pl.multiple_of(at.dp * depth, depth), depth), :] = dn_in[...].T
        Neighbours(at).greet()
    else:
        w_ref = w_any

    def down():
        return w_dn[...] if joined is None else w_ref[:, pl.ds(*layout["down"])]

    def rows_of(buf):
        def view(rank, chunk):
            return buf.at[pl.ds(chunk * half, half), pl.ds(pl.multiple_of(rank * sub, sub), sub), :]

        return view

    def parts_of(buf):
        return lambda which, chunk: buf.at[which, pl.ds(chunk * half, half)]

    def part_of(buf):
        return lambda chunk: buf.at[pl.ds(chunk * half, half)]

    branch = RowScatter(at, rows_of(part), parts_of(near1), part_of(far1), send.at[0], recv.at[0])
    ffn = RowScatter(at, rows_of(part2), parts_of(near2), part_of(far2), send.at[1], recv.at[1])
    back = RowScatter(at, rows_of(part), parts_of(near3), part_of(far3), send.at[2], recv.at[2])
    row_nf = RowGather(at, rows_of(nf), send.at[3], recv.at[3])
    row_gb = RowGather(at, rows_of(gb), send.at[4], recv.at[4])
    mine = pl.ds(pl.multiple_of(at.t * sub, sub), sub)
    gain = gain_ref[...].reshape(1, width)

    def seq_rows(chunk):
        return pl.ds(chunk * half, half)

    def tok_rows(chunk):
        return pl.ds(chunk * rows, rows)

    if joined is None:
        gather = LineGather(
            at, lambda block: w_dn.at[pl.ds(pl.multiple_of(block * depth, depth), depth), :], *sems
        )
        gather.start()
        load.wait()
        gather_step = gather.step
    else:
        joined.step(5, 1)

        def gather_step(s):
            joined.step(6, s)
            if s == 0:
                joined.step(5, 2)
    for c in range(2):
        value = dot_nt(a_ref[tok_rows(c), :], w_ref[:, out_w])
        part[seq_rows(c)] = value.astype(BF16).reshape(half, span, width)
        branch.start(c)
    for c in range(2):
        branch.middle(c)
    gather_step(0)
    for c in range(2):
        hidden = x_ref[seq_rows(c)].astype(F32) + branch.finish(c)
        hid[seq_rows(c)] = hidden
        nf[seq_rows(c), mine, :] = rms_rows(hidden, gain).astype(BF16)
        row_nf.start(c)
    gather_step(1)
    if joined is not None:
        gather_step(2)
        for late in joined.gathers[4:]:
            late.finish()
    for c in range(2):
        row_nf.forward(c)
    if joined is None:
        pl.loop(2, at.lines - 1)(lambda s: gather.step(s))
        gather.finish()
    for c in range(2):
        row_nf.finish(c)
        branch.drain(c)
        flat = nf[seq_rows(c)].reshape(rows, width)
        flat_og = og_ref[seq_rows(c)].reshape(rows, width)
        gate_up = dot_nn(flat, w_ref[:, gu_w])
        gate, up = gate_up[:, :ff], gate_up[:, ff:]
        sigmoid = jax.nn.sigmoid(gate)
        grad_act = dot_nn(flat_og, down())
        act[tok_rows(c), :] = (gate * sigmoid * up).astype(BF16)
        dgu[tok_rows(c), :ff] = (
            grad_act * up * sigmoid * (1.0 + gate * (1.0 - sigmoid))
        ).astype(BF16)
        dgu[tok_rows(c), ff:] = (grad_act * gate * sigmoid).astype(BF16)
        value = dot_nt(dgu[tok_rows(c), :], w_ref[:, gu_w])
        part[seq_rows(c)] = value.astype(BF16).reshape(half, span, width)
        back.start(c)
    for c in range(2):
        value = dot_nt(act[tok_rows(c), :], down())
        part2[seq_rows(c)] = value.astype(BF16).reshape(half, span, width)

    def beside(i):
        if joined is not None:
            joined.beside_feed_forward[i]()

    beside(0)
    for c in range(2):
        back.middle(c)
    beside(1)
    total = jnp.zeros((1, width), F32)
    for c in range(2):
        grad_hidden, terms = rms_rows_grad(hid[seq_rows(c)], gain, back.finish(c))
        total = total + jnp.sum(terms.reshape(half * sub, width), 0, keepdims=True)
        grad_hidden = grad_hidden + ogl_ref[seq_rows(c)].astype(F32)
        gh_ref[seq_rows(c)] = grad_hidden
        gb[seq_rows(c), mine, :] = grad_hidden.astype(BF16)
        row_gb.start(c)
        ffn.start(c)
    gain_grad[...] = total
    beside(2)
    for c in range(2):
        row_gb.forward(c)
        ffn.middle(c)
    for c in range(2):
        row_gb.finish(c)
    for c in range(2):
        out_ref[seq_rows(c)] = (hid[seq_rows(c)] + ffn.finish(c)).astype(BF16)

    def drain():
        for c in range(2):
            row_nf.drain(c)
            row_gb.drain(c)
            back.drain(c)
            ffn.drain(c)

    drain()
    if joined is None:
        gather.drain()


def ffn_specs(cfg):
    layout = cfg["layout"]
    seqs, sub, width = cfg["rows"]
    span = sub * 4
    tokens = seqs * span
    ff = layout["down"][1]
    dma = pltpu.SemaphoreType.DMA
    whole, own = (seqs, span, width), (seqs, sub, width)
    outs = (
        (own, BF16),
        (own, F32),
        (whole, BF16),
        (whole, BF16),
        ((tokens, ff), BF16),
        ((tokens, 2 * ff), BF16),
        ((1, width), F32),
    )
    buffers = [pltpu.VMEM(whole, BF16), pltpu.VMEM(whole, BF16)]
    buffers += [pltpu.VMEM((2,) + own, BF16), pltpu.VMEM(own, BF16)] * 3
    buffers += [pltpu.VMEM(own, F32)]
    weights = [
        pltpu.VMEM((width, layout["down"][0] - layout["out"][0]), BF16),
        pltpu.VMEM((width, ff), BF16),
        dma,
    ]
    sems = [dma((5, 2, 3)), dma((5, 2, 4))]
    return outs, buffers, weights, sems


def feed_forward(cfg, x, a, og, out_grad, gain, w_all, w_down):
    outs, buffers, weights, sems = ffn_specs(cfg)
    vmem = pl.BlockSpec(memory_space=pltpu.VMEM)
    return pl.pallas_call(
        partial(ffn_kernel, cfg["devices"], cfg["layout"]),
        out_shape=tuple(jax.ShapeDtypeStruct(*out) for out in outs),
        in_specs=[vmem] * 5 + [pl.BlockSpec(memory_space=pl.ANY), vmem],
        out_specs=(vmem,) * 7,
        scratch_shapes=buffers + weights + sems + line_gather_sems(cfg["devices"]),
        compiler_params=pltpu.CompilerParams(
            collective_id=1, has_side_effects=True, vmem_limit_bytes=VMEM_BYTES
        ),
        name="feed_forward",
    )(x, a, og, out_grad, gain, w_all, w_down)


def to_row(column):
    size = column.shape[0]
    eye = iota((size, size), 0) == iota((size, size), 1)
    return jnp.sum(jnp.where(eye, column, 0.0), 0, keepdims=True)


def to_column(row):
    size = row.shape[1]
    eye = iota((size, size), 0) == iota((size, size), 1)
    return jnp.sum(jnp.where(eye, row, 0.0), 1, keepdims=True)


def iota(shape, dim):
    return lax.broadcasted_iota(jnp.int32, shape, dim)


def spread(columns, heads, head_dim):
    rows = columns.shape[0]
    lane = iota((rows, LANES), 1)
    blocks = []
    for first in range(0, heads, LANES // head_dim):
        block = jnp.broadcast_to(columns[:, first : first + 1], (rows, LANES))
        for k in range(1, LANES // head_dim):
            block = jnp.where(lane >= k * head_dim, columns[:, first + k : first + k + 1], block)
        blocks.append(block)
    return jnp.concatenate(blocks, 1)


def head_sums(values, heads, head_dim):
    rows = values.shape[0]
    lane = iota((rows, LANES), 1)
    out = jnp.zeros((rows, LANES), F32)
    per = LANES // head_dim
    for h in range(heads):
        block = values[:, h // per * LANES : (h // per + 1) * LANES]
        inside = jnp.logical_and(lane >= h % per * head_dim, lane < (h % per + 1) * head_dim)
        total = jnp.sum(jnp.where(inside, block, 0.0), 1, keepdims=True)
        out = jnp.where(lane == h, total, out)
    return out


def pick_halves(blocks, head_dim):
    lane = iota(blocks[0].shape, 1)
    per = LANES // head_dim
    out = []
    for first in range(0, len(blocks), per):
        block = blocks[first]
        for k in range(1, per):
            block = jnp.where(lane >= k * head_dim, blocks[first + k], block)
        out.append(block)
    return jnp.concatenate(out, 1)


def softplus(value):
    return jnp.maximum(value, 0.0) + jnp.log1p(jnp.exp(-jnp.abs(value)))


def running_sum(values, backward=False):
    rows = values.shape[0]
    row = iota(values.shape, 0)
    step = 1
    while step < rows:
        if backward:
            moved = jnp.where(row < rows - step, pltpu.roll(values, rows - step, 0), 0.0)
        else:
            moved = jnp.where(row >= step, pltpu.roll(values, step, 0), 0.0)
        values = values + moved
        step *= 2
    return values


def turn(values, cosine, sine, half):
    lane = iota(values.shape, 1)
    first = lax.rem(lane, 2 * half) < half
    swapped = jnp.where(
        first, pltpu.roll(values, LANES - half, 1), pltpu.roll(values, half, 1)
    )
    return values * cosine + swapped * sine


def decay_parts(step_pre, decay_log, bias):
    step = softplus(step_pre + bias)
    rate = -jnp.exp(decay_log)
    return step, rate, running_sum(step * rate)


def same_document(aux, row):
    span = aux.shape[0]
    same = aux[:, 5:6] == row
    causal = iota((span, span), 0) >= iota((span, span), 1)
    return jnp.where(jnp.logical_and(same, causal), 0.0, MASKED)


class Neighbours:
    def __init__(self, at):
        self.at = at

    def greet(self, flips=False):
        at = self.at
        barrier = pltpu.get_barrier_semaphore()
        end = at.devices - 1

        def signal(**where):
            pl.semaphore_signal(
                barrier, inc=1, device_id=where, device_id_type=pl.DeviceIdType.MESH
            )

        for other in (at.t_near, at.t_far, at.t_both):
            signal(tensor=other)
        signal(dp=at.pair)
        count = 4
        low, high = at.dp > 0, at.dp < end
        pl.when(low)(lambda: signal(dp=at.dp - 1))
        pl.when(high)(lambda: signal(dp=at.dp + 1))
        count = count + low.astype(jnp.int32) + high.astype(jnp.int32)
        for away in range(2, at.devices, 2):
            signal(dp=lax.rem(at.dp + away, at.devices))
            count = count + 1
        if flips:
            for other in at.flips():
                signal(dp=other)
                count = count + 1
        pl.semaphore_wait(barrier, count)


class TensorTotal:
    def __init__(self, at, own, got, send, recv):
        self.at, self.own, self.got, self.send, self.recv = at, own, got, send, recv

    def copies(self):
        others = (self.at.t_near, self.at.t_far, self.at.t_both)
        return [
            remote(
                self.own, self.got.at[i], self.send.at[i], self.recv.at[i], {"tensor": other}
            )
            for i, other in enumerate(others)
        ]

    def start(self):
        for copy in self.copies():
            copy.start()

    def finish(self):
        for copy in self.copies():
            copy.wait()
        return self.own[...] + self.got[0] + self.got[1] + self.got[2]


class StatePass:
    def __init__(self, at, local, pair_in, chain_in, chain_out, share, result, sems, backward):
        self.at, self.local, self.pair_in = at, local, pair_in
        self.chain_in, self.chain_out, self.share, self.result = chain_in, chain_out, share, result
        self.backward = backward
        self.pair_send, self.pair_recv, self.chain_send, self.chain_recv = sems[:4]
        self.share_send, self.share_recv = sems[4:]
        self.half = local.shape[0] // 2
        self.size = result.shape[1]
        self.head = at.last if backward else at.first
        self.tail = at.first if backward else at.last
        self.onward = at.dp - 2 if backward else at.dp + 2

    def blocks(self):
        return range(self.result.shape[2] // LANES)

    def columns(self, block):
        return pl.ds(block * LANES, LANES)

    def pair_copy(self, block):
        columns = self.columns(block)
        return remote(
            self.local.at[pl.ds((1 - self.at.p) * self.half, self.half), :, columns],
            self.pair_in.at[:, :, columns],
            self.pair_send.at[block],
            self.pair_recv.at[block],
            {"dp": self.at.pair},
        )

    def chain_copy(self, i, block):
        columns = self.columns(block)
        return remote(
            self.chain_out.at[i, :, columns],
            self.chain_in.at[i, :, columns],
            self.chain_send.at[i, block],
            self.chain_recv.at[i, block],
            {"dp": self.onward},
        )

    def share_copy(self, i, block, from_other=False):
        columns = self.columns(block)
        sender = 1 - self.at.p if from_other else self.at.p
        return remote(
            self.share.at[i, :, columns],
            self.result.at[sender * self.half + i, :, columns],
            self.share_send.at[i, block],
            self.share_recv.at[i, block],
            {"dp": self.at.pair},
        )

    def start(self):
        for block in self.blocks():
            self.pair_copy(block).start()

    def run(self):
        for block in self.blocks():
            self.pair_copy(block).wait_recv()
            for i in range(self.half):
                self.pass_on(i, block)

    def pass_on(self, i, block):
        at, size = self.at, self.size
        columns = self.columns(block)
        sooner = at.p == (1 if self.backward else 0)
        mine = self.local[at.p * self.half + i, :, columns].astype(F32)
        other = self.pair_in[i, :, columns].astype(F32)
        one = jnp.where(sooner, mine, other)
        two = jnp.where(sooner, other, mine)
        state1, keep1 = one[:size], one[size : size + 1]
        state2, keep2 = two[:size], two[size : size + 1]

        @pl.when(self.head)
        def _():
            self.chain_in[i, :, columns] = jnp.zeros((size, LANES), BF16)

        @pl.when(jnp.logical_not(self.head))
        def _():
            self.chain_copy(i, block).wait_recv()

        before = self.chain_in[i, :, columns].astype(F32)
        middle = keep1 * before + state1

        @pl.when(jnp.logical_not(self.tail))
        def _():
            self.chain_out[i, :, columns] = (keep2 * middle + state2).astype(BF16)
            self.chain_copy(i, block).start()

        result = jnp.where(sooner, before, middle).astype(BF16)
        self.result[at.p * self.half + i, :, columns] = result
        self.share[i, :, columns] = jnp.where(sooner, middle, before).astype(BF16)
        self.share_copy(i, block).start()

    def finish(self):
        for block in self.blocks():
            for i in range(self.half):
                self.share_copy(i, block, from_other=True).wait_recv()
                self.share_copy(i, block).wait_send()
                pl.when(jnp.logical_not(self.tail))(
                    lambda: self.chain_copy(i, block).wait_send()
                )
            self.pair_copy(block).wait_send()


def state_pass_scratch(half, size, width):
    dma = pltpu.SemaphoreType.DMA
    return [
        pltpu.VMEM((half, size + 16, width), BF16),
        pltpu.VMEM((half, size, width), BF16),
        pltpu.VMEM((half, size, width), BF16),
        pltpu.VMEM((half, size, width), BF16),
        dma((width // LANES,)),
        dma((width // LANES,)),
        dma((half, width // LANES)),
        dma((half, width // LANES)),
        dma((half, width // LANES)),
        dma((half, width // LANES)),
    ]


def packed_columns(layout, name):
    return pl.ds(*layout[name])


def span_row(rows, first, span):
    total = rows.shape[1]
    return pltpu.roll(rows, lax.rem(total - first, total), 1)[:, :span]


def shifted_column(row, before, back):
    span = row.shape[1]
    at, lane = iota((span, span), 0), iota((span, span), 1)
    now = jnp.where(lane == at - back, row, 0.0)
    earlier = jnp.where(lane == at - back + span, before, 0.0)
    return jnp.sum(now + earlier, 1, keepdims=True)


def mixer_kernel(cfg, *refs, joined=None):
    (
        x_ref, og_in, gain_ref, q_in, kv_in, mi_in, st_in, sp_in, gu_in, ao_in, mo_in, seg_ref,
        rope_any, xt_ref, xb_ref, stt_ref, sb_ref, sbias_ref, dlog_ref, skip_ref, mgain_ref,
        w_all, nx, og, low, kv, q2, probs, att, ext, pre, step_buf, entering, carry, y_buf, z_buf,
        squares, aux_ref, seg_rows, head_ref, nxh,
        local, xs_buf, kvh, kvx, kvx_sems, rope_ref, rope_sem, row_send, row_recv, kv_sems, halo_sems, sq_own,
        sq_got, sq_send, sq_recv,
        *rest,
    ) = refs
    devices, layout, pieces, heads = (cfg[k] for k in ("devices", "layout", "pieces", "heads"))
    at = Place(devices)
    seqs, sub, width = x_ref.shape
    span = sub * 4
    tokens = seqs * span
    depth = q_in.shape[0]
    xw = layout["x"][1]
    head_dim = xw // heads
    sw = layout["state"][1]
    size = sw // 2
    mixed = xw + sw
    qw = layout["q"][1]
    at_dim = qw // 2
    count = devices * span
    pass_refs, sems = rest[:10], rest[10:]
    own_rows = pl.ds(pl.multiple_of(at.dp * depth, depth), depth)
    rope_copy = pltpu.make_async_copy(
        rope_any.at[pl.ds(pl.multiple_of(at.dp * span, span), span), :], rope_ref, rope_sem
    )
    rope_copy.start()
    kvh[...] = jnp.zeros(kvh.shape, BF16)

    def own(name, value):
        w_all[own_rows, packed_columns(layout, name)] = value

    even = lax.rem(at.t, 2) == 0
    own("x", mi_in[:, 1, :])
    own("state", st_in[...])
    value = jnp.where(at.t < 2, kv_in[:, 0, :], kv_in[:, 1, :]).astype(F32)
    value = jnp.where(even, value, pltpu.roll(value, at_dim, 1))
    turned = jnp.concatenate(
        [sp_in[...].astype(F32), jnp.zeros((LANES - sp_in.shape[0], depth), F32)], 0
    ).T
    turned = pltpu.roll(turned, at_dim, 1)
    value = jnp.where(iota(value.shape, 1) < at_dim, value, turned)
    own("ks", value.astype(BF16))
    head_ref[...] = jnp.zeros(head_ref.shape, F32)
    for k, ref in enumerate((sbias_ref, dlog_ref, skip_ref)):
        head_ref[k : k + 1, 0:heads] = ref[...].reshape(1, heads)
    Neighbours(at).greet(flips=joined is not None)
    gathers = []
    for i, (first, columns, cross) in enumerate(pieces):

        def view(block, first=first, columns=columns):
            return w_all.at[
                pl.ds(pl.multiple_of(block * depth, depth), depth), pl.ds(first, columns)
            ]

        kind = CrossGather if cross else LineGather
        gathers.append(kind(at, view, *sems[4 * i : 4 * i + 4]))

    def step(i, s):
        if i >= len(gathers):
            return
        if s == 0 and pieces[i][2]:
            gathers[i].begin()
        if s < at.lines - 1:
            gathers[i].step(s)
        if s == 2:
            pl.loop(3, max(at.lines - 1, 3))(lambda k: gathers[i].step(k))

    def begin(i):
        if i < len(gathers):
            gathers[i].start()

    gathers[0].start()
    gathers[1].start()
    gain = gain_ref[...].reshape(1, width)
    mine = pl.ds(pl.multiple_of(at.t * sub, sub), sub)
    half = seqs // 2

    def rows_of(buf):
        def view(rank, chunk):
            return buf.at[pl.ds(chunk * half, half), pl.ds(pl.multiple_of(rank * sub, sub), sub), :]

        return view

    row_nx = RowGather(at, rows_of(nx), row_send.at[0], row_recv.at[0])
    row_og = RowGather(at, rows_of(og), row_send.at[1], row_recv.at[1])
    for chunk in range(2):
        for s in range(chunk * half, chunk * half + half):
            nx[s, mine, :] = rms_rows(x_ref[s].astype(F32), gain).astype(BF16)
        row_nx.start(chunk)
    own("q", q_in[...])
    own("z", mi_in[:, 0, :])
    begin(2)
    before, after = at.dp > 0, at.dp < devices - 1
    seg = seg_ref[...].astype(F32)
    now = span_row(seg, at.dp * span, span)
    old = jnp.where(before, span_row(seg, jnp.maximum(at.dp - 1, 0) * span, span), -1.0)
    seg_rows[...] = jnp.zeros(seg_rows.shape, F32)
    seg_rows[0:seqs, :] = now
    for s in range(seqs):
        row, earlier = now[s : s + 1, :], old[s : s + 1, :]
        column = to_column(row)
        same = [(shifted_column(row, earlier, k) == column).astype(F32) for k in (1, 2, 3)]
        same.append((column == earlier[:, span - 1 :]).astype(F32))
        same.append((column == row[:, span - 1 :]).astype(F32))
        same.append(column)
        lane = iota((span, LANES), 1)
        total = jnp.zeros((span, LANES), F32)
        for k, value in enumerate(same):
            total = jnp.where(lane == k, value, total)
        aux_ref[s] = total
    for chunk in range(2):
        row_nx.forward(chunk)
    for chunk in range(2):
        row_nx.finish(chunk)

    def halo():
        return remote(
            nx.at[:, pl.ds(span - 16, 16), :],
            nxh,
            halo_sems.at[0],
            halo_sems.at[1],
            {"dp": at.dp + 1},
        )

    pl.when(after)(lambda: halo().start())
    step(0, 0)
    step(1, 0)
    for s in range(seqs):
        og[s, mine, :] = og_in[s]
    for chunk in range(2):
        row_og.start(chunk)
    out_at, gu_at = layout["out"][0], layout["gu"][0]
    w_all[own_rows, pl.ds(out_at, qw)] = ao_in[...].T
    w_all[own_rows, pl.ds(out_at + qw, xw)] = mo_in[...].T
    ff = gu_in.shape[2]
    w_all[own_rows, pl.ds(gu_at, ff)] = gu_in[:, 0, :]
    w_all[own_rows, pl.ds(gu_at + ff, ff)] = gu_in[:, 1, :]
    if joined is not None:
        own("down", joined.dn_in[...].T)
    step(0, 1)
    step(1, 1)
    step(0, 2)
    step(1, 2)
    pl.when(before)(lambda: halo().wait_recv())

    @pl.when(jnp.logical_not(before))
    def _():
        nxh[...] = jnp.zeros(nxh.shape, BF16)

    gathers[0].finish()
    rows = nx[...].reshape(tokens, width)
    rows_before = nxh[...].reshape(seqs * 16, width)

    def project(name):
        return dot_nn(rows, w_all[:, packed_columns(layout, name)])

    def project_ext(name, first):
        columns = layout[name][1]
        value = project(name).astype(BF16).astype(F32)
        ext[:, pl.ds(8, span), pl.ds(first, columns)] = value.reshape(seqs, span, columns)
        value = dot_nn(rows_before, w_all[:, packed_columns(layout, name)])
        value = value.astype(BF16).astype(F32).reshape(seqs, 16, columns)
        ext[:, pl.ds(0, 8), pl.ds(first, columns)] = value[:, 8:, :]

    lane = iota((span, LANES), 1)
    key_or_step = project("ks").reshape(seqs, span, LANES)
    for s in range(seqs):
        step_buf[s] = jnp.where(lane < at_dim, pltpu.roll(key_or_step[s], at_dim, 1), 0.0)
    rope_copy.wait()
    cosine, sine = rope_ref[:, :LANES], rope_ref[:, LANES:]
    halves = []
    for s in range(seqs):
        turned = turn(key_or_step[s], cosine, sine, at_dim // 2)
        halves.append(jnp.where(even, turned, key_or_step[s]))
    for s in range(half):
        pair = jnp.where(lane < at_dim, halves[s], pltpu.roll(halves[s + half], at_dim, 1))
        kvh[at.dp, s] = pair.astype(BF16)
    kv_gather = LineGather(
        at,
        lambda block: kvh.at[block],
        kv_sems.at[0],
        kv_sems.at[1],
        kv_sems.at[2],
        kv_sems.at[3],
        causal=True,
    )
    kv_gather.start()
    project_ext("state", xw)
    step(2, 0)
    gathers[1].finish()
    project_ext("x", 0)
    taps = jnp.concatenate([xt_ref[...], stt_ref[...]], 1)
    tap_bias = jnp.concatenate([xb_ref[...].reshape(1, xw), sb_ref[...].reshape(1, sw)], 1)
    step_bias, decay_log, skips = head_ref[0:1, :], head_ref[1:2, :], head_ref[2:3, :]

    def scan_parts(s):
        return decay_parts(step_buf[s], decay_log, step_bias)

    def convolve(s):
        aux = aux_ref[s]
        total = tap_bias + taps[3:4, :] * ext[s, pl.ds(8, span), :]
        for back in (1, 2, 3):
            moved = ext[s, pl.ds(8 - back, span), :] * aux[:, back - 1 : back]
            total = total + taps[3 - back : 4 - back, :] * moved
        pre[s] = total
        active = total * jax.nn.sigmoid(total)
        step, _, running = scan_parts(s)
        scaled = active[:, :xw] * spread(step, heads, head_dim)
        xs_buf[s] = scaled.astype(BF16)
        end = running[span - 1 : span, :]
        tail = spread(jnp.exp(end - running) * aux[:, 4:5], heads, head_dim)
        state_in = active[:, xw : xw + size].astype(BF16)
        local[s, :size, :] = dot_tn(state_in, (scaled * tail).astype(BF16)).astype(BF16)
        keep = jnp.broadcast_to(jnp.exp(end) * aux[span - 1 : span, 3:4], (16, LANES))
        keep = spread(keep, heads, head_dim).astype(BF16)
        local[s, size : size + 16, :] = keep
        carry[s] = keep

    passing = StatePass(
        at, local, pass_refs[0], pass_refs[1], pass_refs[2], pass_refs[3], entering,
        pass_refs[4:], False,
    )
    pl.loop(0, half)(lambda i: convolve((1 - at.p) * half + i))
    passing.start()
    pl.loop(0, half)(lambda i: convolve(at.p * half + i))
    kv_gather.step(0)
    step(2, 1)
    pl.loop(1, at.lines - 1)(lambda s: kv_gather.step(s))
    passing.run()
    begin(3)
    step(2, 2)
    gathers[2].finish()
    scale = 1.0 / math.sqrt(at_dim)
    queries = project("q").reshape(seqs, span, qw)
    for s in range(seqs):
        turned = turn(queries[s], cosine, sine, at_dim // 2) * scale
        q2[s, :span, :] = jnp.where(lane < at_dim, turned, 0.0).astype(BF16)
        turned = pltpu.roll(turned, at_dim, 1)
        q2[s, span:, :] = jnp.where(lane < at_dim, turned, 0.0).astype(BF16)
    z_buf[...] = project("z").astype(BF16).reshape(seqs, span, xw)
    kv_gather.finish()
    kv_swap = remote(kvh, kvx, kvx_sems.at[0], kvx_sems.at[1], {"tensor": at.t_near})
    kv_swap.start()
    step(3, 0)
    begin(4)
    @pl.loop(0, seqs)
    def _(s):
        aux = aux_ref[s]
        active = pre[s] * jax.nn.sigmoid(pre[s])
        _, _, running = scan_parts(s)
        running_rows = running.T
        allowed = same_document(aux, seg_rows[pl.ds(s, 1), :])
        state_in = active[:, xw : xw + size].astype(BF16)
        state_out = active[:, xw + size :].astype(BF16)
        joined_ = dot_nt(state_out, state_in)
        blocks = []
        for h in range(heads):
            gap = running[:, h : h + 1] - running_rows[h : h + 1, :]
            weight = (joined_ * jnp.exp(gap + allowed)).astype(BF16)
            cols = pl.ds(h * head_dim // LANES * LANES, LANES)
            blocks.append(dot_nn(weight, xs_buf[s, :, cols]))
        y_buf[s] = pick_halves(blocks, head_dim) + spread(skips, heads, head_dim) * active[:, :xw]

    step(3, 1)
    step(4, 0)
    kv_swap.wait()
    wide = iota((devices, span, qw), 2) < at_dim
    for s in range(half):
        here, there = kvh[:, s].astype(F32), kvx[:, s].astype(F32)
        keys, values = jnp.where(even, here, there), jnp.where(even, there, here)
        kv[:, s] = jnp.where(wide, keys, pltpu.roll(values, at_dim, 2)).astype(BF16)
        kv[:, s + half] = jnp.where(wide, pltpu.roll(keys, at_dim, 2), values).astype(BF16)
    key_at = iota((span, count), 1)
    query_at = iota((span, count), 0) + at.dp * span
    causal = key_at <= query_at

    @pl.loop(0, seqs)
    def _(s):
        keys = kv[:, s].reshape(count, qw)
        row = seg_ref[pl.ds(s, 1), :].astype(F32)
        allowed = jnp.logical_and(aux_ref[s][:, 5:6] == row, causal)
        bias = jnp.where(allowed, 0.0, MASKED)
        outs = []
        for h in range(2):
            part = pl.ds(h * span, span)
            scores = dot_nt(q2[s, part, :], keys) + bias
            power = jnp.exp(scores - jnp.max(scores, 1, keepdims=True))
            weight = power * (1.0 / jnp.sum(power, 1, keepdims=True))
            weight = weight.astype(BF16)
            probs[s, part, :] = weight
            outs.append(dot_nn(weight, keys))
        att[s] = jnp.where(lane < at_dim, pltpu.roll(outs[0], at_dim, 1), outs[1])

    low[:, pl.ds(0, qw)] = att[...].reshape(tokens, qw).astype(BF16)
    for chunk in range(2):
        row_og.forward(chunk)
    step(3, 2)
    step(4, 1)
    begin(5)
    passing.finish()
    sq_own[...] = jnp.zeros(sq_own.shape, F32)
    for s in range(seqs):
        aux = aux_ref[s]
        state_out = pre[s, :, pl.ds(xw + size, size)]
        state_out = (state_out * jax.nn.sigmoid(state_out)).astype(BF16)
        _, _, running = scan_parts(s)
        factor = spread(jnp.exp(running) * aux[:, 3:4], heads, head_dim)
        y = y_buf[s] + dot_nn(state_out, entering[s]) * factor
        y_buf[s] = y
        gate = z_buf[s].astype(F32)
        gated = y * gate * jax.nn.sigmoid(gate)
        sq_own[s : s + 1, :] = to_row(jnp.sum(gated * gated, 1, keepdims=True))
    total = TensorTotal(at, sq_own, sq_got, sq_send, sq_recv)
    total.start()
    step(4, 2)
    step(5, 0)
    begin(6)
    squares[...] = total.finish()
    for s in range(seqs):
        gate = z_buf[s].astype(F32)
        gated = y_buf[s] * gate * jax.nn.sigmoid(gate)
        norm = lax.rsqrt(to_column(squares[s : s + 1, :]) / (4 * xw) + EPSILON)
        value = gated * norm * mgain_ref[...].reshape(1, xw)
        low[pl.ds(s * span, span), pl.ds(qw, xw)] = value.astype(BF16)
    for chunk in range(2):
        row_og.finish(chunk)
    def drain():
        for gather in [*gathers[:4], kv_gather]:
            gather.drain()
        for row in (row_nx, row_og):
            for chunk in range(2):
                row.drain(chunk)
        pl.when(after)(lambda: halo().wait_send())

    gathers[3].finish()
    if joined is not None:
        joined.step, joined.gathers = step, gathers
        joined.drains.append(drain)
        return
    step(5, 1)
    step(5, 2)
    for gather in gathers[4:]:
        gather.finish()
    for gather in gathers[4:]:
        gather.drain()
    drain()


def gather_sems(devices, pieces):
    dma = pltpu.SemaphoreType.DMA
    out = []
    for _, _, cross in pieces:
        out += [dma((devices,)) for _ in range(4)] if cross else line_gather_sems(devices)
    return out


def mixer_specs(cfg, columns):
    devices, layout, pieces, heads = (cfg[k] for k in ("devices", "layout", "pieces", "heads"))
    seqs, sub, width = cfg["rows"]
    span = sub * 4
    tokens = seqs * span
    xw, sw, qw = (layout[k][1] for k in ("x", "state", "q"))
    size = sw // 2
    count = devices * span
    dma = pltpu.SemaphoreType.DMA
    outs = (
        ((width, columns), BF16),
        ((seqs, span, width), BF16),
        ((seqs, span, width), BF16),
        ((tokens, qw + xw), BF16),
        ((devices, seqs, span, qw), BF16),
        ((seqs, 2 * span, qw), BF16),
        ((seqs, 2 * span, count), BF16),
        ((seqs, span, qw), F32),
        ((seqs, span + 8, xw + sw), F32),
        ((seqs, span, xw + sw), F32),
        ((seqs, span, LANES), F32),
        ((seqs, size, xw), BF16),
        ((seqs, 16, xw), BF16),
        ((seqs, span, xw), F32),
        ((seqs, span, xw), BF16),
        ((8, span), F32),
        ((seqs, span, LANES), F32),
        ((8, span), F32),
        ((8, LANES), F32),
        ((seqs, 16, width), BF16),
    )
    scratch = [
        pltpu.VMEM((seqs, size + 16, xw), BF16),
        pltpu.VMEM((seqs, span, xw), BF16),
        pltpu.VMEM((devices, seqs // 2, span, qw), BF16),
        pltpu.VMEM((devices, seqs // 2, span, qw), BF16),
        dma((2,)),
        pltpu.VMEM((span, 2 * LANES), F32),
        dma,
        dma((2, 2, 3)),
        dma((2, 2, 4)),
        dma((4, devices)),
        dma((2,)),
        pltpu.VMEM((8, span), F32),
        pltpu.VMEM((3, 8, span), F32),
        dma((3,)),
        dma((3,)),
    ]
    scratch += state_pass_scratch(seqs // 2, size, xw) + gather_sems(devices, pieces)
    return outs, scratch


def mixer(cfg, x, *args):
    outs, scratch = mixer_specs(cfg, cfg["layout"]["down"][0])
    vmem = pl.BlockSpec(memory_space=pltpu.VMEM)
    in_specs = [vmem] * (1 + len(args))
    in_specs[12] = pl.BlockSpec(memory_space=pl.ANY)
    return pl.pallas_call(
        partial(mixer_kernel, cfg),
        out_shape=tuple(jax.ShapeDtypeStruct(*out) for out in outs),
        in_specs=in_specs,
        out_specs=(vmem,) * len(outs),
        scratch_shapes=scratch,
        compiler_params=pltpu.CompilerParams(
            collective_id=0, has_side_effects=True, vmem_limit_bytes=VMEM_BYTES
        ),
        name="mixer",
    )(x, *args)


def back_kernel(cfg, *refs, joined=None):
    (
        x_ref, gh_ref, gain_ref, w_any, nx_ref, og_ref, gb_ref, low_ref, nf_any, dgu_any, act_ref,
        kv_any, q2_ref, probs_any, att_ref, ext_ref, pre_ref, step_ref, entering, carry, y_ref,
        z_ref, squares, aux_ref, seg_ref, head_ref, nxh_ref, rope_any, xt_ref, stt_ref, mgain_ref, fgain_ref,
        rg_ref, dw_ref, sums, kvs,
        w_ref, d_in, dlow, dy, dbc, dcum, ext_grad, halo_got, local2, after_state, keys_buf,
        prob_buf, dkv, dkv_other, dkv_swap, dkv_got, dkv_line, dkv_own,
        part, near, far, grads, got, line, small_near, small_far, small_dp, kv_near, kv_far,
        sq_own, sq_got, swap_sems,
        rope_ref, w_sem, early_sems, rope_sem, load_sems, halo_sems, sq_send, sq_recv, send, recv, small_send, small_recv,
        dp_send, dp_recv, kv_send, kv_recv,
        *rest,
    ) = refs
    devices, layout, pieces, heads = (cfg[k] for k in ("devices", "layout", "scatters", "heads"))
    at = Place(devices)
    seqs, sub, width = x_ref.shape
    span = sub * 4
    tokens = seqs * span
    half = seqs // 2
    rows = half * span
    depth = width // devices
    xw, sw, qw = (layout[k][1] for k in ("x", "state", "q"))
    size = sw // 2
    head_dim = xw // heads
    at_dim = qw // 2
    mixed = xw + sw
    count = devices * span
    in_w = layout["in"][1]
    pass_refs, kv_sems, sems = rest[:10], rest[10:14], rest[14:]
    slots = 1 if joined is not None else keys_buf.shape[0]

    def loads(s):
        slot = s % slots
        return (
            pltpu.make_async_copy(kv_any.at[:, s], keys_buf.at[slot], load_sems.at[0, slot]),
            pltpu.make_async_copy(probs_any.at[s], prob_buf.at[slot], load_sems.at[1, slot]),
        )

    if joined is None:
        load = pltpu.make_async_copy(w_any.at[:, pl.ds(0, w_ref.shape[1])], w_ref, w_sem)
        load.start()
        early = (
            pltpu.make_async_copy(nf_any, part, early_sems.at[0]),
            pltpu.make_async_copy(dgu_any, d_in.at[:, pl.ds(0, dgu_any.shape[1])], early_sems.at[1]),
        )
        for copy in early:
            copy.start()
        rope_copy = pltpu.make_async_copy(
            rope_any.at[pl.ds(pl.multiple_of(at.dp * span, span), span), :], rope_ref, rope_sem
        )
        rope_copy.start()
        for copy in loads(0):
            copy.start()
        Neighbours(at).greet(flips=True)
        nf_ref, dgu_ref = part, d_in
    else:
        w_ref, nf_ref, dgu_ref = w_any, nf_any, dgu_any
    taps = jnp.concatenate([xt_ref[...], stt_ref[...]], 1)
    step_bias, decay_log, skips = head_ref[0:1, :], head_ref[1:2, :], head_ref[2:3, :]
    mixer_scale = mgain_ref[...].reshape(1, xw)

    def rows_of(buf):
        def view(rank, chunk):
            return buf.at[pl.ds(chunk * half, half), pl.ds(pl.multiple_of(rank * sub, sub), sub), :]

        return view

    scatters = []
    kept = layout["gu"][0]

    def terms(first):
        return w_any if joined is not None and first >= kept else grads

    for i, (first, columns) in enumerate(pieces):

        def block(buf, k, first=first, columns=columns):
            return buf.at[pl.ds(pl.multiple_of(k * depth, depth), depth), pl.ds(first, columns)]

        scatters.append(
            DirectScatter(
                at,
                partial(block, terms(first)),
                partial(block, got),
                partial(block, line),
                sems[4 * i : 4 * i + 4],
            )
        )

    def finish(i):
        first, columns = pieces[i]
        scatters[i].finish(dw_ref.at[:, pl.ds(first, columns)])

    def product(lhs, rhs_ref, first, columns, into):
        tile = 2 * LANES if columns % (2 * LANES) == 0 else LANES

        @pl.loop(0, columns // tile)
        def _(j):
            src = pl.ds(pl.multiple_of(first + j * tile, LANES), tile)
            dst = pl.ds(pl.multiple_of(into + j * tile, LANES), tile)
            terms(into)[:, dst] = dot_tn(lhs, rhs_ref[:, src]).astype(BF16)

    def weights(i, lhs_ref, rhs_ref, first):
        into, columns = pieces[i]
        product(lhs_ref[...].reshape(tokens, width), rhs_ref, first, columns, into)

    ff = layout["down"][1]

    def gradients(i, *args):
        weights(i, *args)
        scatters[i].start()

    def first():
        if joined is not None:
            for late in joined.gathers[4:]:
                late.drain()
        gradients(0, og_ref, act_ref, 0)

    def second():
        gradients(1, nf_ref, dgu_ref, 0)

    def third():
        gradients(2, nf_ref, dgu_ref, ff)
        scatters[0].send()

    if joined is not None:
        joined.beside_feed_forward = (first, second, third)
        yield
    else:
        first()
        load.wait()
    dlow[...] = dot_nn(
        gb_ref[...].reshape(tokens, width), w_ref[:, pl.ds(*layout["out"])]
    )
    mixer_gain = jnp.zeros((1, xw), F32)
    sq_own[...] = jnp.zeros(sq_own.shape, F32)
    for s in range(seqs):
        gate = z_ref[s].astype(F32)
        gated = y_ref[s] * gate * jax.nn.sigmoid(gate)
        norm = lax.rsqrt(to_column(squares[s : s + 1, :]) / (4 * xw) + EPSILON)
        grad = dlow[pl.ds(s * span, span), pl.ds(qw, xw)]
        mixer_gain = mixer_gain + jnp.sum(grad * gated * norm, 0, keepdims=True)
        inner = jnp.sum(gated * grad * mixer_scale, 1, keepdims=True)
        sq_own[s : s + 1, :] = to_row(inner)
    total = TensorTotal(at, sq_own, sq_got, sq_send, sq_recv)
    total.start()
    if joined is None:
        for copy in early:
            copy.wait()
        second()
        third()
    weights(3, gb_ref, low_ref, 0)
    scatters[1].send()
    inner_rows = total.finish()
    for s in range(seqs):
        gate = z_ref[s].astype(F32)
        sigmoid = jax.nn.sigmoid(gate)
        gated = y_ref[s] * gate * sigmoid
        norm = lax.rsqrt(to_column(squares[s : s + 1, :]) / (4 * xw) + EPSILON)
        inner = to_column(inner_rows[s : s + 1, :])
        term = dlow[pl.ds(s * span, span), pl.ds(qw, xw)] * mixer_scale
        grad = norm * (term - gated * (norm * norm * inner / (4 * xw)))
        dy[s] = grad * gate * sigmoid
        grad = grad * y_ref[s] * sigmoid * (1.0 + gate * (1.0 - sigmoid))
        d_in[pl.ds(s * span, span), pl.ds(*layout["z"])] = grad.astype(BF16)

    def parts(s):
        active = pre_ref[s] * jax.nn.sigmoid(pre_ref[s])
        step, rate, running = decay_parts(step_ref[s], decay_log, step_bias)
        state_in = active[:, xw : xw + size].astype(BF16)
        state_out = active[:, xw + size :].astype(BF16)
        return active[:, :xw], state_in, state_out, step, rate, running

    @pl.loop(0, seqs)
    def _(s):
        _, _, state_out, _, _, running = parts(s)
        factor = spread(jnp.exp(running) * aux_ref[s][:, 3:4], heads, head_dim)
        low = (dy[s] * factor).astype(BF16)
        local2[s, :size, :] = dot_tn(state_out, low).astype(BF16)
        local2[s, size:, :] = carry[s]

    passing = StatePass(
        at, local2, pass_refs[0], pass_refs[1], pass_refs[2], pass_refs[3], after_state,
        pass_refs[4:], True,
    )
    passing.start()
    scatters[3].start()
    @pl.loop(0, seqs)
    def _(s):
        x, state_in, state_out, step, _, running = parts(s)
        running_rows = running.T
        allowed = same_document(aux_ref[s], seg_ref[pl.ds(s, 1), :])
        xs = (x * spread(step, heads, head_dim)).astype(BF16)
        joined = dot_nt(state_out, state_in)
        lane = iota((span, LANES), 1)
        d_joined = jnp.zeros((span, span), F32)
        d_running = jnp.zeros((span, LANES), F32)
        blocks = []
        for h in range(heads):
            cols = slice(h * head_dim // LANES * LANES, h * head_dim // LANES * LANES + LANES)
            begin = h * head_dim % LANES
            inside = jnp.logical_and(lane >= begin, lane < begin + head_dim)
            grad = dy[s, :, pl.ds(cols.start, LANES)]
            decay = jnp.exp(running[:, h : h + 1] - running_rows[h : h + 1, :] + allowed)
            weight = joined * decay
            d_weight = dot_nt(jnp.where(inside, grad, 0.0).astype(BF16), xs[:, cols])
            d_joined = d_joined + d_weight * decay
            product_ = (d_weight * weight).astype(BF16)
            one = (lane == h).astype(BF16)
            d_running = d_running + dot_nn(product_, one) - dot_tn(product_, one)
            blocks.append(dot_tn(weight.astype(BF16), grad.astype(BF16)))
        dlow[pl.ds(pl.multiple_of(s * span, span), span), pl.ds(qw, xw)] = pick_halves(blocks, head_dim)
        d_joined = d_joined.astype(BF16)
        factor = spread(jnp.exp(running) * aux_ref[s][:, 3:4], heads, head_dim)
        crossed = dot_nn(state_out, entering[s]) * factor
        dcum[s] = d_running + head_sums(dy[s] * crossed, heads, head_dim)
        low = (dy[s] * factor).astype(BF16)
        dbc[s, :, :size] = dot_tn(d_joined, state_out)
        dbc[s, :, size:] = dot_nn(d_joined, state_in) + dot_nt(low, entering[s])

    scatters[2].send()
    passing.run()
    lane = iota((span, LANES), 1)
    upper = lane >= at_dim
    even = lax.rem(at.t, 2) == 0
    if joined is None:
        rope_copy.wait()
    cosine, sine = rope_ref[:, :LANES], rope_ref[:, LANES:]
    scale = 1.0 / math.sqrt(at_dim)
    for s in range(seqs):
        slot = s % slots
        if joined is None:
            for copy in loads(s):
                copy.wait()
            if slots > 1 and s + 1 < seqs:
                for copy in loads(s + 1):
                    copy.start()
            keys, weights_ref = keys_buf[slot].reshape(count, qw), prob_buf.at[slot]
        else:
            keys, weights_ref = kv_any[:, s].reshape(count, qw), probs_any.at[s]
        grad = dlow[pl.ds(s * span, span), pl.ds(0, qw)].astype(BF16).astype(F32)
        inner = grad * att_ref[s]
        d_keys = jnp.zeros((count, qw), F32)
        d_query = []
        for h in range(2):
            mine = upper if h else jnp.logical_not(upper)
            delta = jnp.sum(jnp.where(mine, inner, 0.0), 1, keepdims=True)
            moved = grad if h else pltpu.roll(grad, at_dim, 1)
            moved = jnp.where(upper, moved, 0.0).astype(BF16)
            weight = weights_ref[pl.ds(h * span, span), :]
            d_weight = dot_nt(moved, keys)
            d_score = (weight.astype(F32) * (d_weight - delta)).astype(BF16)
            query = q2_ref[s, pl.ds(h * span, span), :]
            d_keys = d_keys + dot_tn(d_score, query) + dot_tn(weight, moved)
            d_query.append(dot_nn(d_score, keys))
        d_keys = jnp.where(even, d_keys, pltpu.roll(d_keys, at_dim, 1))
        turned = pltpu.roll(d_keys, at_dim, 1).reshape(devices, span, qw)
        d_keys = d_keys.reshape(devices, span, qw)
        if s < half:
            dkv[:, s] = d_keys.astype(BF16)
            dkv_other[:, s] = turned.astype(BF16)
        else:
            wide = iota((devices, span, qw), 2) < at_dim
            kept_half = dkv[:, s - half].astype(F32)
            dkv[:, s - half] = jnp.where(wide, kept_half, turned).astype(BF16)
            kept_half = dkv_other[:, s - half].astype(F32)
            dkv_other[:, s - half] = jnp.where(wide, kept_half, d_keys).astype(BF16)
        d_query = jnp.where(upper, pltpu.roll(d_query[1], at_dim, 1), d_query[0]) * scale
        d_in[pl.ds(s * span, span), pl.ds(*layout["q"])] = turn(
            d_query, cosine, -sine, at_dim // 2
        ).astype(BF16)
    kv_scatter = DirectScatter(
        at,
        lambda k: dkv.at[k],
        lambda zz: dkv_got.at[zz],
        lambda zz: dkv_line.at[zz],
        kv_sems,
        causal=True,
    )
    kv_swap = remote(
        dkv_other, dkv_swap, swap_sems.at[0], swap_sems.at[1], {"tensor": at.t_near}
    )
    kv_swap.start()
    gradients(4, nx_ref, d_in, pieces[4][0])
    kv_swap.wait()
    dkv[...] = (dkv[...].astype(F32) + dkv_swap[...].astype(F32)).astype(BF16)
    kv_scatter.start()
    scatters[3].send()
    finish(0)
    kv_scatter.send()
    passing.finish()
    tap_grads = [jnp.zeros((1, mixed), F32) for _ in range(4)]
    bias_grad = jnp.zeros((1, mixed), F32)
    step_grad = jnp.zeros((1, LANES), F32)
    decay_grad = jnp.zeros((1, LANES), F32)
    skip_grad = jnp.zeros((1, xw), F32)
    ext_grad[:, pl.ds(0, 8), :] = jnp.zeros((seqs, 8, mixed), F32)
    for s in range(seqs):
        aux = aux_ref[s]
        x, state_in, state_out, step, rate, running = parts(s)
        step_wide = spread(step, heads, head_dim)
        xs = x * step_wide
        end = running[span - 1 : span, :]
        tail = spread(jnp.exp(end - running) * aux[:, 4:5], heads, head_dim)
        later = after_state[s]
        found = dot_nn(state_in, later)
        weighted = xs * tail
        d_xs = dlow[pl.ds(s * span, span), pl.ds(qw, xw)] + found * tail
        d_in_state = dbc[s, :, :size] + dot_nt(weighted.astype(BF16), later)
        moved = head_sums(found * weighted, heads, head_dim)
        carried = jnp.sum(later.astype(F32) * entering[s].astype(F32), 0, keepdims=True)
        carried = head_sums(carried, heads, head_dim) * jnp.exp(end) * aux[span - 1 : span, 3:4]
        final = jnp.sum(moved, 0, keepdims=True) + carried
        d_running = dcum[s] - moved
        d_running = d_running + jnp.where(iota((span, LANES), 0) == span - 1, final, 0.0)
        d_decay = running_sum(d_running, backward=True)
        d_step = head_sums(d_xs * x, heads, head_dim) + d_decay * rate
        d_step = d_step * jax.nn.sigmoid(step_ref[s] + step_bias)
        d_in[pl.ds(s * span, span), pl.ds(*layout["ks"])] = pltpu.roll(d_step, at_dim, 1).astype(BF16)
        step_grad = step_grad + jnp.sum(d_step, 0, keepdims=True)
        decay_grad = decay_grad + jnp.sum(d_decay * step, 0, keepdims=True) * rate
        skip_grad = skip_grad + jnp.sum(dy[s] * x, 0, keepdims=True)
        d_x = d_xs * step_wide + spread(skips, heads, head_dim) * dy[s]
        value = pre_ref[s]
        sigmoid = jax.nn.sigmoid(value)
        slope = sigmoid * (1.0 + value * (1.0 - sigmoid))
        outer = jnp.concatenate([d_x, d_in_state, dbc[s, :, size:]], 1) * slope
        bias_grad = bias_grad + jnp.sum(outer, 0, keepdims=True)
        ext_grad[s, pl.ds(8, span), :] = taps[3:4, :] * outer
        tap_grads[3] = tap_grads[3] + jnp.sum(
            outer * ext_ref[s, pl.ds(8, span), :], 0, keepdims=True
        )
        for back in (1, 2, 3):
            valid = outer * aux[:, back - 1 : back]
            tap_grads[3 - back] = tap_grads[3 - back] + jnp.sum(
                valid * ext_ref[s, pl.ds(8 - back, span), :], 0, keepdims=True
            )
            ext_grad[s, pl.ds(8 - back, span), :] += taps[3 - back : 4 - back, :] * valid
    before, after = at.dp > 0, at.dp < devices - 1

    def halo():
        return remote(
            ext_grad.at[:, pl.ds(0, 8), :],
            halo_got,
            halo_sems.at[0],
            halo_sems.at[1],
            {"dp": at.dp - 1},
        )

    pl.when(before)(lambda: halo().start())
    sums[...] = jnp.zeros(sums.shape, F32)
    sums[1:2, :] = fgain_ref[...]
    for k in range(4):
        sums[2 + k : 3 + k, pl.ds(0, sw)] = tap_grads[k][:, xw:]
        sums[8 + k : 9 + k, pl.ds(0, xw)] = tap_grads[k][:, :xw]
    sums[6:7, pl.ds(0, sw)] = bias_grad[:, xw:]
    sums[12:13, pl.ds(0, xw)] = bias_grad[:, :xw]
    sums[13:14, pl.ds(0, xw)] = mixer_gain
    sums[14:15, pl.ds(0, LANES)] = step_grad
    sums[14:15, pl.ds(LANES, LANES)] = decay_grad
    sums[14:15, pl.ds(2 * LANES, LANES)] = head_sums(
        jnp.broadcast_to(skip_grad, (8, xw)), heads, head_dim
    )[:1]
    finish(1)
    kv_scatter.finish(dkv_own)
    for s in range(seqs):
        value = dkv_own[s % half]
        value = value if s < half else pltpu.roll(value, at_dim, 1)
        value = jnp.where(even, turn(value, cosine, -sine, at_dim // 2), value)
        where = (pl.ds(s * span, span), pl.ds(*layout["ks"]))
        d_in[where] = jnp.where(upper, d_in[where].astype(F32), value).astype(BF16)
    value = ext_grad[:, pl.ds(8, span), :].reshape(tokens, mixed).astype(BF16)
    d_in[:, pl.ds(*layout["x"])] = value[:, :xw]
    d_in[:, pl.ds(*layout["state"])] = value[:, xw:]
    halo_rows = jnp.concatenate([jnp.zeros((seqs, 8, mixed), F32), ext_grad[:, pl.ds(0, 8), :]], 1)
    halo_rows = halo_rows.reshape(seqs * 16, mixed).astype(BF16)
    rows_before = nxh_ref[...].reshape(seqs * 16, width)
    halo_x, halo_state = halo_rows[:, :xw], halo_rows[:, xw:]
    weights(5, nx_ref, d_in, pieces[5][0])
    into = pl.ds(*layout["state"])
    grads[:, into] = (grads[:, into].astype(F32) + dot_tn(rows_before, halo_state)).astype(BF16)
    scatters[5].start()
    weights(6, nx_ref, d_in, pieces[6][0])
    into = pl.ds(*layout["x"])
    grads[:, into] = (grads[:, into].astype(F32) + dot_tn(rows_before, halo_x)).astype(BF16)
    scatters[6].start()
    pl.when(after)(lambda: halo().wait_recv())

    @pl.when(after)
    def _():
        ext_grad[:, pl.ds(span, 8), :] += halo_got[...]

    for s in range(seqs):
        value = ext_grad[s, pl.ds(span - 8, 16), :].astype(BF16)
        ends = pl.ds(s * span + span - 16, 16)
        d_in[ends, pl.ds(*layout["x"])] = value[:, :xw]
        d_in[ends, pl.ds(*layout["state"])] = value[:, xw:]
    back = RowScatter(
        at,
        rows_of(part),
        lambda which, chunk: near.at[which, pl.ds(chunk * half, half)],
        lambda chunk: far.at[pl.ds(chunk * half, half)],
        send,
        recv,
    )
    for c in range(2):
        value = dot_nt(d_in[pl.ds(c * rows, rows), :], w_ref[:, pl.ds(0, in_w)])
        part[pl.ds(c * half, half)] = value.astype(BF16).reshape(half, span, width)
        back.start(c)
    for c in range(2):
        back.middle(c)
    scatters[4].send()
    finish(2)
    total = jnp.zeros((1, width), F32)
    gain = gain_ref[...].reshape(1, width)
    for c in range(2):
        seq = pl.ds(c * half, half)
        grad, terms = rms_rows_grad(x_ref[seq].astype(F32), gain, back.finish(c))
        rg_ref[seq] = gh_ref[seq] + grad
        total = total + jnp.sum(terms.reshape(half * sub, width), 0, keepdims=True)
    sums[0:1, :] = total
    exchanges = [
        (sums.at[pl.ds(0, 8)], small_near, small_send.at[0], small_recv.at[0], {"tensor": at.t_near}),
        (sums.at[pl.ds(0, 8)], small_far, small_send.at[1], small_recv.at[1], {"tensor": at.t_far}),
    ] + [
        (sums, small_dp.at[i], dp_send.at[i], dp_recv.at[i], {"dp": other})
        for i, other in enumerate(at.flips())
    ]

    def begin(i):
        remote(*exchanges[i]).start()

    def end(i):
        remote(*exchanges[i]).wait()
        into, other = exchanges[i][:2]
        into[...] += other[...]

    begin(0)
    finish(3)
    end(0)
    begin(1)
    scatters[5].send()
    end(1)
    begin(2)
    scatters[6].send()
    end(2)
    begin(3)
    finish(4)
    end(3)
    finish(5)
    kvw = layout["ks"][1]
    kv_near[0, :, pl.ds(0, kvw)] = dw_ref[:, pl.ds(*layout["ks"])].astype(BF16)
    kv_near[0, :, pl.ds(kvw, sw)] = dw_ref[:, pl.ds(*layout["state"])].astype(BF16)
    copy = remote(kv_near.at[0], kv_near.at[1], kv_send.at[0], kv_recv.at[0], {"tensor": at.t_near})
    copy.start()
    begin(4)
    copy.wait()
    here, there = kv_near[0].astype(F32), kv_near[1].astype(F32)
    keys = jnp.where(even, here[:, :kvw], there[:, :kvw])
    values = jnp.where(even, there[:, :kvw], here[:, :kvw])
    low_lanes = iota(keys.shape, 1) < at_dim
    keys = jnp.where(low_lanes, keys, pltpu.roll(values, at_dim, 1))
    kv_far[0, :, :kvw] = keys.astype(BF16)
    kv_far[0, :, kvw:] = (here[:, kvw:] + there[:, kvw:]).astype(BF16)
    copy = remote(kv_far.at[0], kv_far.at[1], kv_send.at[1], kv_recv.at[1], {"tensor": at.t_far})
    copy.start()
    end(4)
    for i in range(5, len(exchanges)):
        begin(i)
        end(i)
    finish(6)
    copy.wait()
    own_first = at.t < 2
    for k in range(2):
        mine_first = own_first if k == 0 else jnp.logical_not(own_first)
        kvs[:, pl.ds(k * kvw, kvw)] = jnp.where(
            mine_first, kv_far[0, :, :kvw], kv_far[1, :, :kvw]
        ).astype(F32)
    kvs[:, pl.ds(2 * kvw, sw)] = kv_far[0, :, kvw:].astype(F32) + kv_far[1, :, kvw:].astype(F32)
    for scatter in [*scatters, kv_scatter]:
        scatter.drain()
    for c in range(2):
        back.drain(c)
    pl.when(before)(lambda: halo().wait_send())
    yield


def back_specs(cfg, joined=False):
    devices, layout, pieces = (cfg[k] for k in ("devices", "layout", "scatters"))
    seqs, sub, width = cfg["rows"]
    span = sub * 4
    tokens = seqs * span
    half = seqs // 2
    depth = width // devices
    lines = devices // 2
    columns = layout["down"][0] + layout["down"][1]
    xw, sw, qw, kvw = (layout[k][1] for k in ("x", "state", "q", "ks"))
    size = sw // 2
    mixed = xw + sw
    in_w = layout["in"][1]
    own = (seqs, sub, width)
    rounds = devices.bit_length() - 1
    slots = 2 if devices * span <= 2048 else 1
    dma = pltpu.SemaphoreType.DMA
    outs = (
        (own, F32),
        ((depth, columns), F32),
        ((16, width), F32),
        ((depth, 2 * kvw + sw), F32),
    )
    scratch = {
        "w": pltpu.VMEM((width, in_w + qw + xw), BF16),
        "d_in": pltpu.VMEM((tokens, in_w), BF16),
        "dlow": pltpu.VMEM((tokens, qw + xw), F32),
        "dy": pltpu.VMEM((seqs, span, xw), F32),
        "dbc": pltpu.VMEM((seqs, span, sw), F32),
        "dcum": pltpu.VMEM((seqs, span, LANES), F32),
        "ext_grad": pltpu.VMEM((seqs, span + 8, mixed), F32),
        "halo_got": pltpu.VMEM((seqs, 8, mixed), F32),
        "local2": pltpu.VMEM((seqs, size + 16, xw), BF16),
        "after_state": pltpu.VMEM((seqs, size, xw), BF16),
        "keys_buf": pltpu.VMEM((slots, devices, span, qw), BF16),
        "prob_buf": pltpu.VMEM((slots, 2 * span, devices * span), BF16),
        "dkv": pltpu.VMEM((devices, half, span, qw), BF16),
        "dkv_other": pltpu.VMEM((devices, half, span, qw), BF16),
        "dkv_swap": pltpu.VMEM((devices, half, span, qw), BF16),
        "dkv_got": pltpu.VMEM((lines, half, span, qw), BF16),
        "dkv_line": pltpu.VMEM((lines, half, span, qw), BF16),
        "dkv_own": pltpu.VMEM((half, span, qw), F32),
        "part": pltpu.VMEM((seqs, span, width), BF16),
        "near": pltpu.VMEM((2,) + own, BF16),
        "far": pltpu.VMEM(own, BF16),
        "grads": pltpu.VMEM((width, layout["gu"][0] if joined else columns), BF16),
        "got": pltpu.VMEM((lines * depth, columns), BF16),
        "line": pltpu.VMEM((lines * depth, columns), BF16),
        "small_near": pltpu.VMEM((8, width), F32),
        "small_far": pltpu.VMEM((8, width), F32),
        "small_dp": pltpu.VMEM((rounds, 16, width), F32),
        "kv_near": pltpu.VMEM((2, depth, kvw + sw), BF16),
        "kv_far": pltpu.VMEM((2, depth, kvw + sw), BF16),
        "sq_own": pltpu.VMEM((8, span), F32),
        "sq_got": pltpu.VMEM((3, 8, span), F32),
        "swap_sems": dma((2,)),
        "rope": pltpu.VMEM((span, 2 * LANES), F32),
        "w_sem": dma,
        "early_sems": dma((2,)),
        "rope_sem": dma,
        "load_sems": dma((2, 2)),
        "halo_sems": dma((2,)),
        "sq_send": dma((3,)),
        "sq_recv": dma((3,)),
        "send": dma((2, 3)),
        "recv": dma((2, 4)),
        "small_send": dma((2,)),
        "small_recv": dma((2,)),
        "dp_send": dma((rounds,)),
        "dp_recv": dma((rounds,)),
        "kv_send": dma((2,)),
        "kv_recv": dma((2,)),
    }
    rest = (
        state_pass_scratch(half, size, xw)
        + scatter_sems(devices) * (1 + len(pieces))
    )
    return outs, scratch, rest


APART = (
    "w", "keys_buf", "prob_buf", "part", "rope", "w_sem", "early_sems", "rope_sem", "load_sems",
)


def run_back(cfg, *refs):
    for _ in back_kernel(cfg, *refs):
        pass


def backward(cfg, x, *args):
    outs, scratch, rest = back_specs(cfg)
    vmem = pl.BlockSpec(memory_space=pltpu.VMEM)
    in_specs = [vmem] * (1 + len(args))
    for i in (3, 8, 9, 11, 13, 27):
        in_specs[i] = pl.BlockSpec(memory_space=pl.ANY)
    return pl.pallas_call(
        partial(run_back, cfg),
        out_shape=tuple(jax.ShapeDtypeStruct(*out) for out in outs),
        in_specs=in_specs,
        out_specs=(vmem,) * len(outs),
        scratch_shapes=list(scratch.values()) + rest,
        compiler_params=pltpu.CompilerParams(
            collective_id=2, has_side_effects=True, vmem_limit_bytes=VMEM_BYTES
        ),
        name="backward",
    )(x, *args)


class Joined:
    def __init__(self, dn_in):
        self.dn_in = dn_in
        self.drains = []


def joined_kernel(cfg, *refs):
    devices, layout = cfg["devices"], cfg["layout"]
    inputs, refs = refs[:23], refs[23:]
    dn_in, fgain_ref = inputs[21:]
    x_ref, og_in, gain_ref = inputs[:3]
    rope_any, xt_ref, _, stt_ref = inputs[12:16]
    mgain_ref = inputs[20]
    inputs = inputs[:21]
    block_out, rg, dw, sums, kvs = refs[:5]
    refs = refs[5:]

    def take(count):
        nonlocal refs
        taken, refs = refs[:count], refs[count:]
        return taken

    mix_outs, mix_scratch = mixer_specs(cfg, layout["down"][0] + layout["down"][1])
    mixed = take(len(mix_outs))
    mixed_scratch = take(len(mix_scratch))
    ffn_outs, buffers, _, sems = ffn_specs(cfg)
    fed = (block_out, *take(len(ffn_outs) - 1))
    fed_scratch = (*take(len(buffers)), None, None, None, *take(len(sems)))
    _, scratch, rest = back_specs(cfg, True)
    names = [name for name in scratch if name not in APART]
    mine = dict(zip(names, take(len(names))))
    mine["part"] = fed_scratch[0]
    mine["rope"] = mixed_scratch[5]
    back_scratch = [mine.get(name) for name in scratch] + list(take(len(rest)))
    (
        w_all, nx, og, low, kv, q2, probs, att, ext, pre, step_buf, entering, carry, y_buf, z_buf,
        squares, aux_ref, seg_rows, head_ref, nxh,
    ) = mixed
    _, gh, gb, nf, act, dgu, gain_part = fed
    joined = Joined(dn_in)
    later = back_kernel(
        cfg, x_ref, gh, gain_ref, w_all, nx, og, gb, low, nf, dgu, act, kv, q2, probs, att, ext, pre,
        step_buf, entering, carry, y_buf, z_buf, squares, aux_ref, seg_rows, head_ref, nxh, rope_any, xt_ref,
        stt_ref, mgain_ref, gain_part, rg, dw, sums, kvs, *back_scratch, joined=joined,
    )
    mixer_kernel(cfg, *inputs, *mixed, *mixed_scratch, joined=joined)
    next(later)
    ffn_kernel(
        devices, layout, x_ref, low, og, og_in, fgain_ref, w_all, None, *fed, *fed_scratch,
        joined=joined,
    )
    next(later)
    for drain in joined.drains:
        drain()


def joined_layer(cfg, *args):
    layout = cfg["layout"]
    mix_outs, mix_scratch = mixer_specs(cfg, layout["down"][0] + layout["down"][1])
    ffn_outs, buffers, _, sems = ffn_specs(cfg)
    outs, scratch, rest = back_specs(cfg, True)
    vmem = pl.BlockSpec(memory_space=pltpu.VMEM)
    in_specs = [vmem] * len(args)
    in_specs[12] = pl.BlockSpec(memory_space=pl.ANY)
    return pl.pallas_call(
        partial(joined_kernel, cfg),
        out_shape=tuple(jax.ShapeDtypeStruct(*out) for out in (ffn_outs[0], *outs)),
        in_specs=in_specs,
        out_specs=(vmem,) * 5,
        scratch_shapes=[pltpu.VMEM(*out) for out in mix_outs]
        + mix_scratch
        + [pltpu.VMEM(*out) for out in ffn_outs[1:]]
        + buffers
        + sems
        + [ref for name, ref in scratch.items() if name not in APART]
        + rest,
        compiler_params=pltpu.CompilerParams(
            collective_id=0, has_side_effects=True, vmem_limit_bytes=VMEM_BYTES
        ),
        name="layer",
    )(*args)


def unpack_kernel(layout, local, *refs):
    (
        dw, kvs, sums, rg, block,
        block_out, rg_out, gain1, gain2, wq, wkv, wao, wmi, wst, wsp, cw, cb, csw, csb, sbias,
        dlog, skip, mgain, wmo, wgu, wdn,
    ) = refs
    block_out[...] = block[...]
    rg_out[...] = rg[...]
    width = sums.shape[1]
    xw, sw = layout["x"][1], layout["state"][1]
    qw = layout["q"][1]
    ff = layout["down"][1]
    kvw = layout["ks"][1]

    def part(name):
        return dw[:, pl.ds(*layout[name])]

    gain1[...] = sums[0:1, :].reshape(width)
    gain2[...] = sums[1:2, :].reshape(width)
    wq[...] = part("q")
    wkv[:, 0, :] = kvs[:, :kvw]
    wkv[:, 1, :] = kvs[:, kvw : 2 * kvw]
    out = part("out")
    wao[...] = out[:, :qw].T
    wmo[...] = out[:, qw:].T
    wdn[...] = part("down").T
    wmi[:, 0, :] = part("z")
    wmi[:, 1, :] = part("x")
    wst[...] = kvs[:, 2 * kvw :]
    wsp[...] = part("ks").T[kvw // 2 : kvw // 2 + local, :]
    gate_up = part("gu")
    wgu[:, 0, :] = gate_up[:, :ff]
    wgu[:, 1, :] = gate_up[:, ff:]
    cw[...] = sums[8:12, :xw]
    cb[...] = sums[12:13, :xw].reshape(xw)
    csw[...] = sums[2:6, :sw]
    csb[...] = sums[6:7, :sw].reshape(sw)
    sbias[...] = sums[14:15, :local].reshape(local)
    dlog[...] = sums[14:15, LANES : LANES + local].reshape(local)
    skip[...] = sums[14:15, 2 * LANES : 2 * LANES + local].reshape(local)
    mgain[...] = sums[13:14, :xw].reshape(xw)


def unpack(layout, local, dw, kvs, sums, rg, block):
    depth = dw.shape[0]
    width = sums.shape[1]
    xw, sw, qw, ff, kvw = (layout[k][1] for k in ("x", "state", "q", "down", "ks"))

    def shape(*dims):
        return jax.ShapeDtypeStruct(dims, F32)

    outs = (
        jax.ShapeDtypeStruct(block.shape, BF16),
        shape(*rg.shape),
        shape(width),
        shape(width),
        shape(depth, qw),
        shape(depth, 2, kvw),
        shape(qw, depth),
        shape(depth, 2, xw),
        shape(depth, sw),
        shape(local, depth),
        shape(4, xw),
        shape(xw),
        shape(4, sw),
        shape(sw),
        shape(local),
        shape(local),
        shape(local),
        shape(xw),
        shape(xw, depth),
        shape(depth, 2, ff),
        shape(ff, depth),
    )
    vmem = pl.BlockSpec(memory_space=pltpu.VMEM)
    return pl.pallas_call(
        partial(unpack_kernel, layout, local),
        out_shape=outs,
        in_specs=[vmem] * 5,
        out_specs=(vmem,) * len(outs),
        name="unpack",
    )(dw, kvs, sums, rg, block)


def rope_table(length, head_dim):
    half = head_dim // 2
    frequency = np.exp(-math.log(ROTARY_BASE) * 2.0 * np.arange(half) / head_dim)
    angle = np.arange(length)[:, None] * frequency[None, :]
    cosine, sine = np.cos(angle), np.sin(angle)
    copies = LANES // head_dim
    table = [cosine, cosine] * copies + [-sine, sine] * copies
    return np.concatenate(table, 1).astype(np.float32)


def body(
    resid_in,
    segment_ids,
    out_grad,
    input_gain,
    ffn_gain,
    query_weight,
    keyvalue_weight,
    attention_output_weight,
    mixer_input_weight,
    state_input_weight,
    step_weight,
    conv_mixer,
    conv_mixer_bias,
    conv_state,
    conv_state_bias,
    step_bias,
    decay_log,
    skip_gain,
    mixer_gain,
    mixer_output_weight,
    gate_up_weight,
    down_weight,
):
    shard_count = lax.axis_size("dp")
    head_dim = keyvalue_weight.shape[2] // 2
    query_width = query_weight.shape[1]
    mixer_local = step_weight.shape[1]
    mixer_width = conv_mixer.shape[1]
    state_width = state_input_weight.shape[1]
    ff = down_weight.shape[0]
    layout = {}
    columns = 0
    for name, size in (
        ("state", state_width),
        ("ks", 2 * head_dim),
        ("x", mixer_width),
        ("q", query_width),
        ("z", mixer_width),
        ("out", query_width + mixer_width),
        ("gu", 2 * ff),
        ("down", ff),
    ):
        layout[name] = (columns, size)
        columns += size
    layout["in"] = (0, layout["out"][0])
    q_at, gu_at = (layout[k][0] for k in ("q", "gu"))
    config = {
        "devices": shard_count,
        "layout": layout,
        "heads": mixer_local,
        "rows": resid_in.shape,
        "pieces": (
            (0, layout["x"][0], False),
            (*layout["x"], False),
            (q_at, layout["out"][0] - q_at, False),
            (*layout["out"], False),
            (gu_at, ff, False),
            (gu_at + ff, ff, False),
        ),
        "scatters": (
            layout["down"],
            (gu_at, ff),
            (gu_at + ff, ff),
            layout["out"],
            (q_at, layout["out"][0] - q_at),
            (0, layout["x"][0]),
            layout["x"],
        ),
    }

    rope = jnp.asarray(rope_table(segment_ids.shape[1], head_dim))
    def results(outs):
        return (*outs[:9], outs[9].T, *outs[10:])

    raw = (
        resid_in,
        out_grad,
        input_gain,
        query_weight,
        keyvalue_weight,
        mixer_input_weight,
        state_input_weight,
        step_weight.T,
        gate_up_weight,
        attention_output_weight,
        mixer_output_weight,
        segment_ids,
        rope,
        conv_mixer,
        conv_mixer_bias,
        conv_state,
        conv_state_bias,
        step_bias,
        decay_log,
        skip_gain,
        mixer_gain,
    )
    if segment_ids.size <= JOINED_TOKENS:
        config["pieces"] = (*config["pieces"], (*layout["down"], False))
        block_out, resid_grad, weight_grads, sums, replicated = joined_layer(
            config, *raw, down_weight, ffn_gain
        )
        return results(
            unpack(layout, mixer_local, weight_grads, replicated, sums, resid_grad, block_out)
        )
    (
        w_all, span_normed_input, span_gradient, branch_low, keys, queries, probs, attention, ext,
        pre, step_pre, entering, state_decay, mixer_y, gate_z, squares, aux, seg_rows, head_rows,
        rows_before,
    ) = mixer(config, *raw)
    block_out, grad_hidden, grad_branch, span_feedforward, activated, grad_gate_up, ffn_gain_part = (
        feed_forward(
            config,
            resid_in,
            branch_low,
            span_gradient,
            out_grad,
            ffn_gain,
            w_all,
            down_weight,
        )
    )
    resid_grad, weight_grads, sums, replicated = backward(
        config,
        resid_in,
        grad_hidden,
        input_gain,
        w_all,
        span_normed_input,
        span_gradient,
        grad_branch,
        branch_low,
        span_feedforward,
        grad_gate_up,
        activated,
        keys,
        queries,
        probs,
        attention,
        ext,
        pre,
        step_pre,
        entering,
        state_decay,
        mixer_y,
        gate_z,
        squares,
        aux,
        seg_rows,
        head_rows,
        rows_before,
        rope,
        conv_mixer,
        conv_state,
        mixer_gain,
        ffn_gain_part,
    )
    return results(
        unpack(layout, mixer_local, weight_grads, replicated, sums, resid_grad, block_out)
    )


def solution(mesh):
    placed = (
        P(None, ("dp", "tensor"), None),
        P(),
        P(None, ("dp", "tensor"), None),
        P(),
        P(),
        P("dp", "tensor"),
        P("dp", None, None),
        P("tensor", "dp"),
        P("dp", None, "tensor"),
        P("dp", None),
        P("dp", "tensor"),
        P(None, "tensor"),
        P("tensor"),
        P(),
        P(),
        P("tensor"),
        P("tensor"),
        P("tensor"),
        P("tensor"),
        P("tensor", "dp"),
        P("dp", None, "tensor"),
        P("tensor", "dp"),
    )
    return jax.shard_map(
        body,
        mesh=mesh,
        in_specs=placed,
        out_specs=(
            P(None, ("dp", "tensor"), None),
            P(None, ("dp", "tensor"), None),
            P(),
            P(),
            P("dp", "tensor"),
            P("dp", None, None),
            P("tensor", "dp"),
            P("dp", None, "tensor"),
            P("dp", None),
            P("dp", "tensor"),
            P(None, "tensor"),
            P("tensor"),
            P(),
            P(),
            P("tensor"),
            P("tensor"),
            P("tensor"),
            P("tensor"),
            P("tensor", "dp"),
            P("dp", None, "tensor"),
            P("tensor", "dp"),
        ),
        check_vma=False,
    )
```

```python
from functools import partial
import math

import jax
import jax.numpy as jnp
import numpy as np
from jax import lax
from jax.experimental import pallas as pl
from jax.experimental.pallas import tpu as pltpu
from jax.sharding import PartitionSpec as P

KVH = 2
EPSILON = 1e-05
ROTARY_BASE = 100000000000.0
MASKED = -1e30
MATMUL_EXACTNESS = lax.Precision.HIGHEST
LANES = 128
F32 = jnp.float32
BF16 = jnp.bfloat16
VMEM_BYTES = 63 * 2**20
JOINED_TOKENS = 4096


def dot_nn(a, b):
    return lax.dot_general(a, b, (((1,), (0,)), ((), ())), preferred_element_type=F32)


def dot_nt(a, b):
    return lax.dot_general(a, b, (((1,), (1,)), ((), ())), preferred_element_type=F32)


def dot_tn(a, b):
    return lax.dot_general(a, b, (((0,), (0,)), ((), ())), preferred_element_type=F32)


def remote(src, dst, send_sem, recv_sem, where):
    return pltpu.make_async_remote_copy(
        src_ref=src,
        dst_ref=dst,
        send_sem=send_sem,
        recv_sem=recv_sem,
        device_id=where,
        device_id_type=pl.DeviceIdType.MESH,
    )


def add_into(ref, *others):
    total = ref[...].astype(F32)
    for other in others:
        total = total + other[...].astype(F32)
    ref[...] = total.astype(BF16)


class Place:
    def __init__(self, devices):
        self.devices = devices
        self.lines = devices // 2
        self.dp = lax.axis_index("dp")
        self.t = lax.axis_index("tensor")
        self.z = lax.div(self.dp, 2)
        self.p = lax.rem(self.dp, 2)
        self.pair = self.dp + 1 - 2 * self.p
        self.t_near = self.t + 1 - 2 * lax.rem(self.t, 2)
        self.t_far = lax.rem(self.t + 2, 4)
        self.t_both = lax.rem(self.t_near + 2, 4)
        self.first = self.z == 0
        self.last = self.z == self.lines - 1

    def flips(self):
        bit = 1
        while bit < self.devices:
            yield self.dp + bit - 2 * bit * lax.rem(lax.div(self.dp, bit), 2)
            bit *= 2


class LineGather:
    def __init__(self, place, view, recv, right, left, pair, causal=False):
        self.at, self.view = place, view
        self.causal = causal
        self.recv, self.right, self.left, self.side = recv, right, left, pair

    def copy(self, block, sem, where):
        ref = self.view(block)
        return remote(ref, ref, sem, self.recv.at[block], where)

    def send_right(self, zz):
        return self.copy(zz * 2 + self.at.p, self.right.at[zz], {"dp": self.at.dp + 2})

    def send_left(self, zz):
        return self.copy(zz * 2 + self.at.p, self.left.at[zz], {"dp": self.at.dp - 2})

    def send_pair(self, zz):
        return self.copy(zz * 2 + self.at.p, self.side.at[zz], {"dp": self.at.pair})

    def arrived(self, block):
        self.copy(block, self.side.at[0], {"dp": self.at.pair}).wait_recv()

    def start(self):
        at = self.at
        pl.when(jnp.logical_not(at.last))(lambda: self.send_right(at.z).start())
        if not self.causal:
            pl.when(jnp.logical_not(at.first))(lambda: self.send_left(at.z).start())
        self.send_pair(at.z).start()

    def step(self, s):
        at = self.at
        low, high = at.z - 1 - s, at.z + 1 + s

        @pl.when(low >= 0)
        def _():
            self.arrived(low * 2 + at.p)
            pl.when(jnp.logical_not(at.last))(lambda: self.send_right(low).start())
            self.send_pair(low).start()

        if self.causal:
            return

        @pl.when(high < at.lines)
        def _():
            self.arrived(high * 2 + at.p)
            pl.when(jnp.logical_not(at.first))(lambda: self.send_left(high).start())
            self.send_pair(high).start()

    def finish(self):
        at = self.at

        @pl.loop(0, at.z + 1 if self.causal else at.lines)
        def _(zz):
            self.arrived(zz * 2 + 1 - at.p)

    def drain(self):
        at = self.at

        @pl.loop(0, at.z + 1 if self.causal else at.lines)
        def _(zz):
            self.send_pair(zz).wait_send()

            @pl.when(jnp.logical_and(zz <= at.z, jnp.logical_not(at.last)))
            def _():
                self.send_right(zz).wait_send()

            if self.causal:
                return

            @pl.when(jnp.logical_and(zz >= at.z, jnp.logical_not(at.first)))
            def _():
                self.send_left(zz).wait_send()


class CrossGather:
    def __init__(self, place, view, recv, right, left, pair):
        self.at, self.view = place, view
        self.recv, self.right, self.left, self.side = recv, right, left, pair

    def copy(self, block, sem, where):
        ref = self.view(block)
        return remote(ref, ref, sem, self.recv.at[block], where)

    def send_right(self, block):
        return self.copy(block, self.right.at[block], {"dp": self.at.dp + 2})

    def send_left(self, block):
        return self.copy(block, self.left.at[block], {"dp": self.at.dp - 2})

    def send_pair(self):
        return self.copy(self.at.dp, self.side.at[0], {"dp": self.at.pair})

    def arrived(self, block):
        self.copy(block, self.side.at[0], {"dp": self.at.pair}).wait_recv()

    def onward(self, block, right, left):
        at = self.at
        if right:
            pl.when(jnp.logical_not(at.last))(lambda: self.send_right(block).start())
        if left:
            pl.when(jnp.logical_not(at.first))(lambda: self.send_left(block).start())

    def start(self):
        self.send_pair().start()
        self.onward(self.at.dp, True, True)

    def begin(self):
        self.arrived(self.at.pair)
        self.onward(self.at.pair, True, True)

    def step(self, s):
        at = self.at
        low, high = at.z - 1 - s, at.z + 1 + s
        for q in (at.p, 1 - at.p):

            @pl.when(low >= 0)
            def _():
                self.arrived(low * 2 + q)
                self.onward(low * 2 + q, True, False)

            @pl.when(high < at.lines)
            def _():
                self.arrived(high * 2 + q)
                self.onward(high * 2 + q, False, True)

    def finish(self):
        pass

    def drain(self):
        at = self.at
        self.send_pair().wait_send()

        @pl.loop(0, at.devices)
        def _(block):
            zz = lax.div(block, 2)

            @pl.when(jnp.logical_and(zz <= at.z, jnp.logical_not(at.last)))
            def _():
                self.send_right(block).wait_send()

            @pl.when(jnp.logical_and(zz >= at.z, jnp.logical_not(at.first)))
            def _():
                self.send_left(block).wait_send()


class DirectScatter:
    def __init__(self, place, part, got, line, sems, causal=False):
        self.at, self.part, self.got, self.line = place, part, got, line
        self.pair_send, self.pair_recv, self.line_send, self.line_recv = sems
        self.causal = causal

    def pair_copy(self, zz):
        src = self.part(zz * 2 + 1 - self.at.p)
        return remote(
            src, self.got(zz), self.pair_send.at[zz], self.pair_recv.at[zz], {"dp": self.at.pair}
        )

    def line_copy(self, zz):
        target = zz * 2 + self.at.p
        return remote(
            self.part(target),
            self.line(self.at.z),
            self.line_send.at[zz],
            self.line_recv.at[self.at.z],
            {"dp": target},
        )

    def line_arrived(self, zz):
        here = self.part(self.at.dp)
        remote(
            here, self.line(zz), self.line_send.at[zz], self.line_recv.at[zz], {"dp": self.at.pair}
        ).wait_recv()

    def target(self, i):
        return i if self.causal else lax.rem(self.at.z + 1 + i, self.at.lines)

    def start(self):
        @pl.loop(0, self.at.z + 1 if self.causal else self.at.lines)
        def _(i):
            self.pair_copy(self.target(i)).start()

    def send(self):
        @pl.loop(0, self.at.z if self.causal else self.at.lines - 1)
        def _(i):
            zz = self.target(i)
            self.pair_copy(zz).wait_recv()
            add_into(self.part(zz * 2 + self.at.p), self.got(zz))
            self.line_copy(zz).start()

    def pass_on(self):
        pass

    def finish(self, out):
        at = self.at
        self.pair_copy(at.z).wait_recv()
        out[...] = self.part(at.dp)[...].astype(F32) + self.got(at.z)[...].astype(F32)

        @pl.loop(at.z + 1 if self.causal else 0, at.lines)
        def _(zz):
            @pl.when(zz != at.z)
            def _():
                self.line_arrived(zz)
                out[...] += self.line(zz)[...].astype(F32)

    def drain(self):
        at = self.at

        @pl.loop(0, at.z + 1 if self.causal else at.lines)
        def _(zz):
            self.pair_copy(zz).wait_send()
            pl.when(zz != at.z)(lambda: self.line_copy(zz).wait_send())


class RelayScatter(DirectScatter):
    def __init__(self, *args):
        super().__init__(*args)
        self.side = lax.div(self.at.z, 2)
        self.place = self.mirror(self.at.z)

    def mirror(self, zz):
        return zz + self.side * (3 - 2 * zz)

    def hop(self, target, to, slot):
        target, to, slot = (self.mirror(k) for k in (target, to, slot))
        return remote(
            self.part(target * 2 + self.at.p),
            self.line(slot),
            self.line_send.at[target],
            self.line_recv.at[slot],
            {"dp": to * 2 + self.at.p},
        )

    def joined_pair(self, target, also=None):
        zz = self.mirror(target)
        self.pair_copy(zz).wait_recv()
        ref = self.part(zz * 2 + self.at.p)
        if also is None:
            add_into(ref, self.got(zz))
        else:
            slot = self.mirror(also)
            self.line_arrived(slot)
            add_into(ref, self.got(zz), self.line(slot))

    def start(self):
        @pl.when(self.place == 0)
        def _():
            for target in (2, 3, 1, 0):
                self.pair_copy(self.mirror(target)).start()

        @pl.when(self.place == 1)
        def _():
            for target in (0, 2, 3, 1):
                self.pair_copy(self.mirror(target)).start()

    def send(self):
        @pl.when(self.place == 0)
        def _():
            for target, slot in ((2, 1), (3, 3), (1, 0)):
                self.joined_pair(target)
                self.hop(target, 1, slot).start()

        @pl.when(self.place == 1)
        def _():
            self.joined_pair(0)
            self.hop(0, 0, 1).start()

    def pass_on(self):
        @pl.when(self.place == 1)
        def _():
            for target, also in ((2, 1), (3, 3)):
                self.joined_pair(target, also)
                self.hop(target, target, 1).start()

    def finish(self, out):
        at = self.at
        self.pair_copy(at.z).wait_recv()
        out[...] = self.part(at.dp)[...].astype(F32) + self.got(at.z)[...].astype(F32)

        def add(place):
            zz = self.mirror(place)
            self.line_arrived(zz)
            out[...] += self.line(zz)[...].astype(F32)

        pl.when(self.place == 0)(lambda: add(1))
        pl.when(self.place == 1)(lambda: add(0))
        add(2)


class RowGather:
    def __init__(self, place, view, send, recv):
        self.at, self.view, self.send, self.recv = place, view, send, recv

    def copy(self, rank, chunk, sem, near):
        ref = self.view(rank, chunk)
        where = {"tensor": self.at.t_near if near else self.at.t_far}
        return remote(ref, ref, self.send.at[chunk, sem], self.recv.at[chunk, rank], where)

    def start(self, chunk):
        self.copy(self.at.t, chunk, 0, False).start()
        self.copy(self.at.t, chunk, 1, True).start()

    def forward(self, chunk):
        self.copy(self.at.t_far, chunk, 2, False).wait_recv()
        self.copy(self.at.t_far, chunk, 2, True).start()

    def finish(self, chunk):
        self.copy(self.at.t_near, chunk, 1, True).wait_recv()
        self.copy(self.at.t_both, chunk, 2, True).wait_recv()

    def drain(self, chunk):
        self.copy(self.at.t, chunk, 0, False).wait_send()
        self.copy(self.at.t, chunk, 1, True).wait_send()
        self.copy(self.at.t_far, chunk, 2, True).wait_send()


class RowScatter:
    def __init__(self, place, view, near_buf, far_buf, send, recv):
        self.at, self.view = place, view
        self.near_buf, self.far_buf = near_buf, far_buf
        self.send, self.recv = send, recv

    def near_copy(self, chunk, which):
        rank = self.at.t_both if which else self.at.t_near
        return remote(
            self.view(rank, chunk),
            self.near_buf(which, chunk),
            self.send.at[chunk, which],
            self.recv.at[chunk, which],
            {"tensor": self.at.t_near},
        )

    def far_copy(self, chunk):
        return remote(
            self.view(self.at.t_far, chunk),
            self.far_buf(chunk),
            self.send.at[chunk, 2],
            self.recv.at[chunk, 2],
            {"tensor": self.at.t_far},
        )

    def start(self, chunk):
        self.near_copy(chunk, 1).start()
        self.near_copy(chunk, 0).start()

    def middle(self, chunk):
        self.near_copy(chunk, 1).wait_recv()
        ref = self.view(self.at.t_far, chunk)
        ref[...] = (ref[...].astype(F32) + self.near_buf(1, chunk)[...].astype(F32)).astype(BF16)
        self.far_copy(chunk).start()

    def finish(self, chunk):
        self.near_copy(chunk, 0).wait_recv()
        total = self.view(self.at.t, chunk)[...].astype(F32) + self.near_buf(0, chunk)[
            ...
        ].astype(F32)
        self.far_copy(chunk).wait_recv()
        return total + self.far_buf(chunk)[...].astype(F32)

    def drain(self, chunk):
        self.near_copy(chunk, 0).wait_send()
        self.near_copy(chunk, 1).wait_send()
        self.far_copy(chunk).wait_send()


def line_gather_sems(devices):
    dma = pltpu.SemaphoreType.DMA
    return [dma((devices,)), dma((devices // 2,)), dma((devices // 2,)), dma((devices // 2,))]


def scatter_sems(devices):
    return [pltpu.SemaphoreType.DMA((devices // 2,)) for _ in range(4)]


def rms_rows(values, gain):
    return values * lax.rsqrt(jnp.mean(values * values, -1, keepdims=True) + EPSILON) * gain


def rms_rows_grad(values, gain, grad):
    scale = lax.rsqrt(jnp.mean(values * values, -1, keepdims=True) + EPSILON)
    term = grad * gain
    inner = jnp.mean(values * term, -1, keepdims=True)
    return scale * (term - values * (scale * scale * inner)), grad * values * scale


def ffn_kernel(devices, layout, *refs, joined=None):
    (
        x_ref, a_ref, og_ref, ogl_ref, gain_ref, w_any, dn_in,
        out_ref, gh_ref, gb, nf, act, dgu, gain_grad,
        part, part2, near1, far1, near2, far2, near3, far3, hid,
        w_ref, w_dn, w_sem, send, recv, *sems,
    ) = refs
    at = Place(devices)
    seqs, sub, width = x_ref.shape
    span = sub * 4
    half = seqs // 2
    rows = half * span
    first = layout["out"][0] if joined is None else 0
    out_w, gu_w = (pl.ds(layout[k][0] - first, layout[k][1]) for k in ("out", "gu"))
    ff = layout["down"][1]
    if joined is None:
        depth = dn_in.shape[1]
        load = pltpu.make_async_copy(w_any.at[:, pl.ds(first, w_ref.shape[1])], w_ref, w_sem)
        load.start()
        w_dn[pl.ds(pl.multiple_of(at.dp * depth, depth), depth), :] = dn_in[...].T
        Neighbours(at).greet()
    else:
        w_ref = w_any

    def down():
        return w_dn[...] if joined is None else w_ref[:, pl.ds(*layout["down"])]

    def rows_of(buf):
        def view(rank, chunk):
            return buf.at[pl.ds(chunk * half, half), pl.ds(pl.multiple_of(rank * sub, sub), sub), :]

        return view

    def parts_of(buf):
        return lambda which, chunk: buf.at[which, pl.ds(chunk * half, half)]

    def part_of(buf):
        return lambda chunk: buf.at[pl.ds(chunk * half, half)]

    branch = RowScatter(at, rows_of(part), parts_of(near1), part_of(far1), send.at[0], recv.at[0])
    ffn = RowScatter(at, rows_of(part2), parts_of(near2), part_of(far2), send.at[1], recv.at[1])
    back = RowScatter(at, rows_of(part), parts_of(near3), part_of(far3), send.at[2], recv.at[2])
    row_nf = RowGather(at, rows_of(nf), send.at[3], recv.at[3])
    row_gb = RowGather(at, rows_of(gb), send.at[4], recv.at[4])
    mine = pl.ds(pl.multiple_of(at.t * sub, sub), sub)
    gain = gain_ref[...].reshape(1, width)

    def seq_rows(chunk):
        return pl.ds(chunk * half, half)

    def tok_rows(chunk):
        return pl.ds(chunk * rows, rows)

    if joined is None:
        gather = LineGather(
            at, lambda block: w_dn.at[pl.ds(pl.multiple_of(block * depth, depth), depth), :], *sems
        )
        gather.start()
        load.wait()
        gather_step = gather.step
    else:

        def gather_step(s):
            if s == 0:
                joined.step(6, 2)

    for c in range(2):
        value = dot_nt(a_ref[tok_rows(c), :], w_ref[:, out_w])
        part[seq_rows(c)] = value.astype(BF16).reshape(half, span, width)
        branch.start(c)
    if joined is not None:
        joined.step(5, 2)
        joined.step(6, 1)
    for c in range(2):
        branch.middle(c)
    gather_step(0)
    for c in range(2):
        hidden = x_ref[seq_rows(c)].astype(F32) + branch.finish(c)
        hid[seq_rows(c)] = hidden
        nf[seq_rows(c), mine, :] = rms_rows(hidden, gain).astype(BF16)
        row_nf.start(c)
    gather_step(1)
    if joined is not None:
        gather_step(2)
    for c in range(2):
        row_nf.forward(c)
    if joined is not None:
        for late in joined.gathers[4:6]:
            late.finish()
    if joined is None:
        pl.loop(2, at.lines - 1)(lambda s: gather.step(s))
        gather.finish()
    for c in range(2):
        row_nf.finish(c)
        branch.drain(c)
        flat = nf[seq_rows(c)].reshape(rows, width)
        flat_og = og_ref[seq_rows(c)].reshape(rows, width)
        gate_up = dot_nn(flat, w_ref[:, gu_w])
        gate, up = gate_up[:, :ff], gate_up[:, ff:]
        sigmoid = jax.nn.sigmoid(gate)
        if joined is not None and c == 0:
            joined.gathers[6].finish()
        grad_act = dot_nn(flat_og, down())
        act[tok_rows(c), :] = (gate * sigmoid * up).astype(BF16)
        dgu[tok_rows(c), :ff] = (
            grad_act * up * sigmoid * (1.0 + gate * (1.0 - sigmoid))
        ).astype(BF16)
        dgu[tok_rows(c), ff:] = (grad_act * gate * sigmoid).astype(BF16)
        value = dot_nt(dgu[tok_rows(c), :], w_ref[:, gu_w])
        part[seq_rows(c)] = value.astype(BF16).reshape(half, span, width)
        back.start(c)
    for c in range(2):
        value = dot_nt(act[tok_rows(c), :], down())
        part2[seq_rows(c)] = value.astype(BF16).reshape(half, span, width)

    def beside(i):
        if joined is not None:
            joined.beside_feed_forward[i]()

    beside(0)
    for c in range(2):
        back.middle(c)
    beside(1)
    total = jnp.zeros((1, width), F32)
    for c in range(2):
        grad_hidden, terms = rms_rows_grad(hid[seq_rows(c)], gain, back.finish(c))
        total = total + jnp.sum(terms.reshape(half * sub, width), 0, keepdims=True)
        grad_hidden = grad_hidden + ogl_ref[seq_rows(c)].astype(F32)
        gh_ref[seq_rows(c)] = grad_hidden
        gb[seq_rows(c), mine, :] = grad_hidden.astype(BF16)
        row_gb.start(c)
        ffn.start(c)
    gain_grad[...] = total
    beside(2)
    for c in range(2):
        row_gb.forward(c)
        ffn.middle(c)
    for c in range(2):
        row_gb.finish(c)
    beside(3)
    for c in range(2):
        out_ref[seq_rows(c)] = (hid[seq_rows(c)] + ffn.finish(c)).astype(BF16)

    def drain():
        for c in range(2):
            row_nf.drain(c)
            row_gb.drain(c)
            back.drain(c)
            ffn.drain(c)

    drain()
    if joined is None:
        gather.drain()


def ffn_specs(cfg):
    layout = cfg["layout"]
    seqs, sub, width = cfg["rows"]
    span = sub * 4
    tokens = seqs * span
    ff = layout["down"][1]
    dma = pltpu.SemaphoreType.DMA
    whole, own = (seqs, span, width), (seqs, sub, width)
    outs = (
        (own, BF16),
        (own, F32),
        (whole, BF16),
        (whole, BF16),
        ((tokens, ff), BF16),
        ((tokens, 2 * ff), BF16),
        ((1, width), F32),
    )
    buffers = [pltpu.VMEM(whole, BF16), pltpu.VMEM(whole, BF16)]
    buffers += [pltpu.VMEM((2,) + own, BF16), pltpu.VMEM(own, BF16)] * 3
    buffers += [pltpu.VMEM(own, F32)]
    weights = [
        pltpu.VMEM((width, layout["down"][0] - layout["out"][0]), BF16),
        pltpu.VMEM((width, ff), BF16),
        dma,
    ]
    sems = [dma((5, 2, 3)), dma((5, 2, 4))]
    return outs, buffers, weights, sems


def feed_forward(cfg, x, a, og, out_grad, gain, w_all, w_down):
    outs, buffers, weights, sems = ffn_specs(cfg)
    vmem = pl.BlockSpec(memory_space=pltpu.VMEM)
    return pl.pallas_call(
        partial(ffn_kernel, cfg["devices"], cfg["layout"]),
        out_shape=tuple(jax.ShapeDtypeStruct(*out) for out in outs),
        in_specs=[vmem] * 5 + [pl.BlockSpec(memory_space=pl.ANY), vmem],
        out_specs=(vmem,) * 7,
        scratch_shapes=buffers + weights + sems + line_gather_sems(cfg["devices"]),
        compiler_params=pltpu.CompilerParams(
            collective_id=1, has_side_effects=True, vmem_limit_bytes=VMEM_BYTES
        ),
        name="feed_forward",
    )(x, a, og, out_grad, gain, w_all, w_down)


def to_row(column):
    size = column.shape[0]
    eye = iota((size, size), 0) == iota((size, size), 1)
    return jnp.sum(jnp.where(eye, column, 0.0), 0, keepdims=True)


def to_column(row):
    size = row.shape[1]
    eye = iota((size, size), 0) == iota((size, size), 1)
    return jnp.sum(jnp.where(eye, row, 0.0), 1, keepdims=True)


def iota(shape, dim):
    return lax.broadcasted_iota(jnp.int32, shape, dim)


def spread(columns, heads, head_dim):
    rows = columns.shape[0]
    lane = iota((rows, LANES), 1)
    blocks = []
    for first in range(0, heads, LANES // head_dim):
        block = jnp.broadcast_to(columns[:, first : first + 1], (rows, LANES))
        for k in range(1, LANES // head_dim):
            block = jnp.where(lane >= k * head_dim, columns[:, first + k : first + k + 1], block)
        blocks.append(block)
    return jnp.concatenate(blocks, 1)


def head_sums(values, heads, head_dim):
    rows = values.shape[0]
    lane = iota((rows, LANES), 1)
    out = jnp.zeros((rows, LANES), F32)
    per = LANES // head_dim
    for h in range(heads):
        block = values[:, h // per * LANES : (h // per + 1) * LANES]
        inside = jnp.logical_and(lane >= h % per * head_dim, lane < (h % per + 1) * head_dim)
        total = jnp.sum(jnp.where(inside, block, 0.0), 1, keepdims=True)
        out = jnp.where(lane == h, total, out)
    return out


def pick_halves(blocks, head_dim):
    lane = iota(blocks[0].shape, 1)
    per = LANES // head_dim
    out = []
    for first in range(0, len(blocks), per):
        block = blocks[first]
        for k in range(1, per):
            block = jnp.where(lane >= k * head_dim, blocks[first + k], block)
        out.append(block)
    return jnp.concatenate(out, 1)


def softplus(value):
    return jnp.maximum(value, 0.0) + jnp.log1p(jnp.exp(-jnp.abs(value)))


def running_sum(values, backward=False):
    rows = values.shape[0]
    row = iota(values.shape, 0)
    step = 1
    while step < rows:
        if backward:
            moved = jnp.where(row < rows - step, pltpu.roll(values, rows - step, 0), 0.0)
        else:
            moved = jnp.where(row >= step, pltpu.roll(values, step, 0), 0.0)
        values = values + moved
        step *= 2
    return values


def turn(values, cosine, sine, half):
    lane = iota(values.shape, 1)
    first = lax.rem(lane, 2 * half) < half
    swapped = jnp.where(
        first, pltpu.roll(values, LANES - half, 1), pltpu.roll(values, half, 1)
    )
    return values * cosine + swapped * sine


def decay_parts(step_pre, decay_log, bias):
    step = softplus(step_pre + bias)
    rate = -jnp.exp(decay_log)
    return step, rate, running_sum(step * rate)


def same_document(aux, row):
    span = aux.shape[0]
    same = aux[:, 5:6] == row
    causal = iota((span, span), 0) >= iota((span, span), 1)
    return jnp.where(jnp.logical_and(same, causal), 0.0, MASKED)


class Neighbours:
    def __init__(self, at):
        self.at = at

    def greet(self, flips=False):
        at = self.at
        barrier = pltpu.get_barrier_semaphore()
        end = at.devices - 1

        def signal(**where):
            pl.semaphore_signal(
                barrier, inc=1, device_id=where, device_id_type=pl.DeviceIdType.MESH
            )

        for other in (at.t_near, at.t_far, at.t_both):
            signal(tensor=other)
        signal(dp=at.pair)
        count = 4
        low, high = at.dp > 0, at.dp < end
        pl.when(low)(lambda: signal(dp=at.dp - 1))
        pl.when(high)(lambda: signal(dp=at.dp + 1))
        count = count + low.astype(jnp.int32) + high.astype(jnp.int32)
        for away in range(2, at.devices, 2):
            signal(dp=lax.rem(at.dp + away, at.devices))
            count = count + 1
        if flips:
            for other in at.flips():
                signal(dp=other)
                count = count + 1
        pl.semaphore_wait(barrier, count)


class TensorTotal:
    def __init__(self, at, own, got, send, recv):
        self.at, self.own, self.got, self.send, self.recv = at, own, got, send, recv

    def copies(self):
        others = (self.at.t_near, self.at.t_far, self.at.t_both)
        return [
            remote(
                self.own, self.got.at[i], self.send.at[i], self.recv.at[i], {"tensor": other}
            )
            for i, other in enumerate(others)
        ]

    def start(self):
        for copy in self.copies():
            copy.start()

    def finish(self):
        for copy in self.copies():
            copy.wait()
        return self.own[...] + self.got[0] + self.got[1] + self.got[2]


class StatePass:
    def __init__(self, at, local, pair_in, chain_in, chain_out, share, result, sems, backward):
        self.at, self.local, self.pair_in = at, local, pair_in
        self.chain_in, self.chain_out, self.share, self.result = chain_in, chain_out, share, result
        self.backward = backward
        self.pair_send, self.pair_recv, self.chain_send, self.chain_recv = sems[:4]
        self.share_send, self.share_recv = sems[4:]
        self.half = local.shape[0] // 2
        self.size = result.shape[1]
        self.head = at.last if backward else at.first
        self.tail = at.first if backward else at.last
        self.onward = at.dp - 2 if backward else at.dp + 2

    def blocks(self):
        return range(self.result.shape[2] // LANES)

    def columns(self, block):
        return pl.ds(block * LANES, LANES)

    def pair_copy(self, block):
        columns = self.columns(block)
        return remote(
            self.local.at[pl.ds((1 - self.at.p) * self.half, self.half), :, columns],
            self.pair_in.at[:, :, columns],
            self.pair_send.at[block],
            self.pair_recv.at[block],
            {"dp": self.at.pair},
        )

    def chain_copy(self, i, block):
        columns = self.columns(block)
        return remote(
            self.chain_out.at[i, :, columns],
            self.chain_in.at[i, :, columns],
            self.chain_send.at[i, block],
            self.chain_recv.at[i, block],
            {"dp": self.onward},
        )

    def share_copy(self, i, block, from_other=False):
        columns = self.columns(block)
        sender = 1 - self.at.p if from_other else self.at.p
        return remote(
            self.share.at[i, :, columns],
            self.result.at[sender * self.half + i, :, columns],
            self.share_send.at[i, block],
            self.share_recv.at[i, block],
            {"dp": self.at.pair},
        )

    def start(self):
        for block in self.blocks():
            self.pair_copy(block).start()

    def run(self):
        for block in self.blocks():
            self.pair_copy(block).wait_recv()
            for i in range(self.half):
                self.pass_on(i, block)

    def pass_on(self, i, block):
        at, size = self.at, self.size
        columns = self.columns(block)
        sooner = at.p == (1 if self.backward else 0)
        mine = self.local[at.p * self.half + i, :, columns].astype(F32)
        other = self.pair_in[i, :, columns].astype(F32)
        one = jnp.where(sooner, mine, other)
        two = jnp.where(sooner, other, mine)
        state1, keep1 = one[:size], one[size : size + 1]
        state2, keep2 = two[:size], two[size : size + 1]

        @pl.when(self.head)
        def _():
            self.chain_in[i, :, columns] = jnp.zeros((size, LANES), BF16)

        @pl.when(jnp.logical_not(self.head))
        def _():
            self.chain_copy(i, block).wait_recv()

        before = self.chain_in[i, :, columns].astype(F32)
        middle = keep1 * before + state1

        @pl.when(jnp.logical_not(self.tail))
        def _():
            self.chain_out[i, :, columns] = (keep2 * middle + state2).astype(BF16)
            self.chain_copy(i, block).start()

        result = jnp.where(sooner, before, middle).astype(BF16)
        self.result[at.p * self.half + i, :, columns] = result
        self.share[i, :, columns] = jnp.where(sooner, middle, before).astype(BF16)
        self.share_copy(i, block).start()

    def finish(self):
        for block in self.blocks():
            for i in range(self.half):
                self.share_copy(i, block, from_other=True).wait_recv()
                self.share_copy(i, block).wait_send()
                pl.when(jnp.logical_not(self.tail))(
                    lambda: self.chain_copy(i, block).wait_send()
                )
            self.pair_copy(block).wait_send()


def state_pass_scratch(half, size, width):
    dma = pltpu.SemaphoreType.DMA
    return [
        pltpu.VMEM((half, size + 16, width), BF16),
        pltpu.VMEM((half, size, width), BF16),
        pltpu.VMEM((half, size, width), BF16),
        pltpu.VMEM((half, size, width), BF16),
        dma((width // LANES,)),
        dma((width // LANES,)),
        dma((half, width // LANES)),
        dma((half, width // LANES)),
        dma((half, width // LANES)),
        dma((half, width // LANES)),
    ]


def packed_columns(layout, name):
    return pl.ds(*layout[name])


def span_row(rows, first, span):
    total = rows.shape[1]
    return pltpu.roll(rows, lax.rem(total - first, total), 1)[:, :span]


def shifted_column(row, before, back):
    span = row.shape[1]
    at, lane = iota((span, span), 0), iota((span, span), 1)
    now = jnp.where(lane == at - back, row, 0.0)
    earlier = jnp.where(lane == at - back + span, before, 0.0)
    return jnp.sum(now + earlier, 1, keepdims=True)


def mixer_kernel(cfg, *refs, joined=None):
    (
        x_ref, og_in, gain_ref, q_in, kv_in, mi_in, st_in, sp_in, gu_in, ao_in, mo_in, seg_ref,
        rope_any, xt_ref, xb_ref, stt_ref, sb_ref, sbias_ref, dlog_ref, skip_ref, mgain_ref,
        w_all, nx, og, low, kv, q2, probs, att, ext, pre, step_buf, entering, carry, y_buf, z_buf,
        squares, aux_ref, seg_rows, head_ref, nxh,
        local, xs_buf, kvh, kvx, kvx_sems, rope_ref, rope_sem, row_send, row_recv, kv_sems, halo_sems, sq_own,
        sq_got, sq_send, sq_recv,
        *rest,
    ) = refs
    devices, layout, pieces, heads = (cfg[k] for k in ("devices", "layout", "pieces", "heads"))
    at = Place(devices)
    seqs, sub, width = x_ref.shape
    span = sub * 4
    tokens = seqs * span
    depth = q_in.shape[0]
    xw = layout["x"][1]
    head_dim = xw // heads
    sw = layout["state"][1]
    size = sw // 2
    mixed = xw + sw
    qw = layout["q"][1]
    at_dim = qw // 2
    count = devices * span
    pass_refs, sems = rest[:10], rest[10:]
    own_rows = pl.ds(pl.multiple_of(at.dp * depth, depth), depth)
    rope_copy = pltpu.make_async_copy(
        rope_any.at[pl.ds(pl.multiple_of(at.dp * span, span), span), :], rope_ref, rope_sem
    )
    rope_copy.start()
    kvh[...] = jnp.zeros(kvh.shape, BF16)

    def own(name, value):
        w_all[own_rows, packed_columns(layout, name)] = value

    even = lax.rem(at.t, 2) == 0
    own("x", mi_in[:, 1, :])
    own("state", st_in[...])
    value = jnp.where(at.t < 2, kv_in[:, 0, :], kv_in[:, 1, :]).astype(F32)
    value = jnp.where(even, value, pltpu.roll(value, at_dim, 1))
    turned = jnp.concatenate(
        [sp_in[...].astype(F32), jnp.zeros((LANES - sp_in.shape[0], depth), F32)], 0
    ).T
    turned = pltpu.roll(turned, at_dim, 1)
    value = jnp.where(iota(value.shape, 1) < at_dim, value, turned)
    own("ks", value.astype(BF16))
    head_ref[...] = jnp.zeros(head_ref.shape, F32)
    for k, ref in enumerate((sbias_ref, dlog_ref, skip_ref)):
        head_ref[k : k + 1, 0:heads] = ref[...].reshape(1, heads)
    Neighbours(at).greet(flips=joined is not None)
    gathers = []
    for i, (first, columns, cross) in enumerate(pieces):

        def view(block, first=first, columns=columns):
            return w_all.at[
                pl.ds(pl.multiple_of(block * depth, depth), depth), pl.ds(first, columns)
            ]

        kind = CrossGather if cross else LineGather
        gathers.append(kind(at, view, *sems[4 * i : 4 * i + 4]))

    def step(i, s):
        if i >= len(gathers):
            return
        if s == 0 and pieces[i][2]:
            gathers[i].begin()
        if s < at.lines - 1:
            gathers[i].step(s)
        if s == 2:
            pl.loop(3, max(at.lines - 1, 3))(lambda k: gathers[i].step(k))

    def begin(i):
        if i < len(gathers):
            gathers[i].start()

    gathers[0].start()
    gathers[1].start()
    gain = gain_ref[...].reshape(1, width)
    mine = pl.ds(pl.multiple_of(at.t * sub, sub), sub)
    half = seqs // 2

    def rows_of(buf):
        def view(rank, chunk):
            return buf.at[pl.ds(chunk * half, half), pl.ds(pl.multiple_of(rank * sub, sub), sub), :]

        return view

    row_nx = RowGather(at, rows_of(nx), row_send.at[0], row_recv.at[0])
    row_og = RowGather(at, rows_of(og), row_send.at[1], row_recv.at[1])
    for chunk in range(2):
        for s in range(chunk * half, chunk * half + half):
            nx[s, mine, :] = rms_rows(x_ref[s].astype(F32), gain).astype(BF16)
        row_nx.start(chunk)
    own("q", q_in[...])
    own("z", mi_in[:, 0, :])
    begin(2)
    before, after = at.dp > 0, at.dp < devices - 1
    seg = seg_ref[...].astype(F32)
    now = span_row(seg, at.dp * span, span)
    old = jnp.where(before, span_row(seg, jnp.maximum(at.dp - 1, 0) * span, span), -1.0)
    seg_rows[...] = jnp.zeros(seg_rows.shape, F32)
    seg_rows[0:seqs, :] = now
    for s in range(seqs):
        row, earlier = now[s : s + 1, :], old[s : s + 1, :]
        column = to_column(row)
        same = [(shifted_column(row, earlier, k) == column).astype(F32) for k in (1, 2, 3)]
        same.append((column == earlier[:, span - 1 :]).astype(F32))
        same.append((column == row[:, span - 1 :]).astype(F32))
        same.append(column)
        lane = iota((span, LANES), 1)
        total = jnp.zeros((span, LANES), F32)
        for k, value in enumerate(same):
            total = jnp.where(lane == k, value, total)
        aux_ref[s] = total
    for chunk in range(2):
        row_nx.forward(chunk)
    for chunk in range(2):
        row_nx.finish(chunk)

    def halo():
        return remote(
            nx.at[:, pl.ds(span - 16, 16), :],
            nxh,
            halo_sems.at[0],
            halo_sems.at[1],
            {"dp": at.dp + 1},
        )

    pl.when(after)(lambda: halo().start())
    step(0, 0)
    step(1, 0)
    for s in range(seqs):
        og[s, mine, :] = og_in[s]
    for chunk in range(2):
        row_og.start(chunk)
    out_at, gu_at = layout["out"][0], layout["gu"][0]
    w_all[own_rows, pl.ds(out_at, qw)] = ao_in[...].T
    w_all[own_rows, pl.ds(out_at + qw, xw)] = mo_in[...].T
    ff = gu_in.shape[2]
    w_all[own_rows, pl.ds(gu_at, ff)] = gu_in[:, 0, :]
    w_all[own_rows, pl.ds(gu_at + ff, ff)] = gu_in[:, 1, :]
    if joined is not None:
        own("down", joined.dn_in[...].T)
    step(0, 1)
    step(1, 1)
    step(0, 2)
    step(1, 2)
    pl.when(before)(lambda: halo().wait_recv())

    @pl.when(jnp.logical_not(before))
    def _():
        nxh[...] = jnp.zeros(nxh.shape, BF16)

    gathers[0].finish()
    rows = nx[...].reshape(tokens, width)
    rows_before = nxh[...].reshape(seqs * 16, width)

    def project(name):
        return dot_nn(rows, w_all[:, packed_columns(layout, name)])

    def project_ext(name, first):
        columns = layout[name][1]
        value = project(name).astype(BF16).astype(F32)
        ext[:, pl.ds(8, span), pl.ds(first, columns)] = value.reshape(seqs, span, columns)
        value = dot_nn(rows_before, w_all[:, packed_columns(layout, name)])
        value = value.astype(BF16).astype(F32).reshape(seqs, 16, columns)
        ext[:, pl.ds(0, 8), pl.ds(first, columns)] = value[:, 8:, :]

    lane = iota((span, LANES), 1)
    key_or_step = project("ks").reshape(seqs, span, LANES)
    for s in range(seqs):
        step_buf[s] = jnp.where(lane < at_dim, pltpu.roll(key_or_step[s], at_dim, 1), 0.0)
    rope_copy.wait()
    cosine, sine = rope_ref[:, :LANES], rope_ref[:, LANES:]
    halves = []
    for s in range(seqs):
        turned = turn(key_or_step[s], cosine, sine, at_dim // 2)
        halves.append(jnp.where(even, turned, key_or_step[s]))
    for s in range(half):
        pair = jnp.where(lane < at_dim, halves[s], pltpu.roll(halves[s + half], at_dim, 1))
        kvh[at.dp, s] = pair.astype(BF16)
    kv_gather = LineGather(
        at,
        lambda block: kvh.at[block],
        kv_sems.at[0],
        kv_sems.at[1],
        kv_sems.at[2],
        kv_sems.at[3],
        causal=True,
    )
    kv_gather.start()
    begin(3)
    project_ext("state", xw)
    step(2, 0)
    gathers[1].finish()
    project_ext("x", 0)
    taps = jnp.concatenate([xt_ref[...], stt_ref[...]], 1)
    tap_bias = jnp.concatenate([xb_ref[...].reshape(1, xw), sb_ref[...].reshape(1, sw)], 1)
    step_bias, decay_log, skips = head_ref[0:1, :], head_ref[1:2, :], head_ref[2:3, :]

    def scan_parts(s):
        return decay_parts(step_buf[s], decay_log, step_bias)

    def convolve(s):
        aux = aux_ref[s]
        total = tap_bias + taps[3:4, :] * ext[s, pl.ds(8, span), :]
        for back in (1, 2, 3):
            moved = ext[s, pl.ds(8 - back, span), :] * aux[:, back - 1 : back]
            total = total + taps[3 - back : 4 - back, :] * moved
        pre[s] = total
        active = total * jax.nn.sigmoid(total)
        step, _, running = scan_parts(s)
        scaled = active[:, :xw] * spread(step, heads, head_dim)
        xs_buf[s] = scaled.astype(BF16)
        end = running[span - 1 : span, :]
        tail = spread(jnp.exp(end - running) * aux[:, 4:5], heads, head_dim)
        state_in = active[:, xw : xw + size].astype(BF16)
        local[s, :size, :] = dot_tn(state_in, (scaled * tail).astype(BF16)).astype(BF16)
        keep = jnp.broadcast_to(jnp.exp(end) * aux[span - 1 : span, 3:4], (16, LANES))
        keep = spread(keep, heads, head_dim).astype(BF16)
        local[s, size : size + 16, :] = keep
        carry[s] = keep

    passing = StatePass(
        at, local, pass_refs[0], pass_refs[1], pass_refs[2], pass_refs[3], entering,
        pass_refs[4:], False,
    )
    pl.loop(0, half)(lambda i: convolve((1 - at.p) * half + i))
    passing.start()
    begin(4)
    begin(5)
    pl.loop(0, half)(lambda i: convolve(at.p * half + i))
    kv_gather.step(0)
    step(2, 1)
    pl.loop(1, at.lines - 1)(lambda s: kv_gather.step(s))
    step(3, 0)
    passing.run()
    begin(6)
    step(2, 2)
    gathers[2].finish()
    scale = 1.0 / math.sqrt(at_dim)
    queries = project("q").reshape(seqs, span, qw)
    for s in range(seqs):
        turned = turn(queries[s], cosine, sine, at_dim // 2) * scale
        q2[s, :span, :] = jnp.where(lane < at_dim, turned, 0.0).astype(BF16)
        turned = pltpu.roll(turned, at_dim, 1)
        q2[s, span:, :] = jnp.where(lane < at_dim, turned, 0.0).astype(BF16)
    z_buf[...] = project("z").astype(BF16).reshape(seqs, span, xw)
    kv_gather.finish()
    kv_swap = remote(kvh, kvx, kvx_sems.at[0], kvx_sems.at[1], {"tensor": at.t_near})
    kv_swap.start()
    step(4, 0)
    @pl.loop(0, seqs)
    def _(s):
        aux = aux_ref[s]
        active = pre[s] * jax.nn.sigmoid(pre[s])
        _, _, running = scan_parts(s)
        running_rows = running.T
        allowed = same_document(aux, seg_rows[pl.ds(s, 1), :])
        state_in = active[:, xw : xw + size].astype(BF16)
        state_out = active[:, xw + size :].astype(BF16)
        joined_ = dot_nt(state_out, state_in)
        blocks = []
        for h in range(heads):
            gap = running[:, h : h + 1] - running_rows[h : h + 1, :]
            weight = (joined_ * jnp.exp(gap + allowed)).astype(BF16)
            cols = pl.ds(h * head_dim // LANES * LANES, LANES)
            blocks.append(dot_nn(weight, xs_buf[s, :, cols]))
        y_buf[s] = pick_halves(blocks, head_dim) + spread(skips, heads, head_dim) * active[:, :xw]

    step(3, 1)
    step(5, 0)
    step(4, 1)
    kv_swap.wait()
    wide = iota((devices, span, qw), 2) < at_dim
    for s in range(half):
        here, there = kvh[:, s].astype(F32), kvx[:, s].astype(F32)
        keys, values = jnp.where(even, here, there), jnp.where(even, there, here)
        kv[:, s] = jnp.where(wide, keys, pltpu.roll(values, at_dim, 2)).astype(BF16)
        kv[:, s + half] = jnp.where(wide, pltpu.roll(keys, at_dim, 2), values).astype(BF16)
    step(3, 2)
    step(6, 0)
    key_at = iota((span, count), 1)
    query_at = iota((span, count), 0) + at.dp * span
    causal = key_at <= query_at

    @pl.loop(0, seqs)
    def _(s):
        keys = kv[:, s].reshape(count, qw)
        row = seg_ref[pl.ds(s, 1), :].astype(F32)
        allowed = jnp.logical_and(aux_ref[s][:, 5:6] == row, causal)
        bias = jnp.where(allowed, 0.0, MASKED)
        outs = []
        for h in range(2):
            part = pl.ds(h * span, span)
            scores = dot_nt(q2[s, part, :], keys) + bias
            power = jnp.exp(scores - jnp.max(scores, 1, keepdims=True))
            weight = power * (1.0 / jnp.sum(power, 1, keepdims=True))
            weight = weight.astype(BF16)
            probs[s, part, :] = weight
            outs.append(dot_nn(weight, keys))
        att[s] = jnp.where(lane < at_dim, pltpu.roll(outs[0], at_dim, 1), outs[1])

    low[:, pl.ds(0, qw)] = att[...].reshape(tokens, qw).astype(BF16)
    for chunk in range(2):
        row_og.forward(chunk)
    step(5, 1)
    step(4, 2)
    passing.finish()
    sq_own[...] = jnp.zeros(sq_own.shape, F32)
    for s in range(seqs):
        aux = aux_ref[s]
        state_out = pre[s, :, pl.ds(xw + size, size)]
        state_out = (state_out * jax.nn.sigmoid(state_out)).astype(BF16)
        _, _, running = scan_parts(s)
        factor = spread(jnp.exp(running) * aux[:, 3:4], heads, head_dim)
        y = y_buf[s] + dot_nn(state_out, entering[s]) * factor
        y_buf[s] = y
        gate = z_buf[s].astype(F32)
        gated = y * gate * jax.nn.sigmoid(gate)
        sq_own[s : s + 1, :] = to_row(jnp.sum(gated * gated, 1, keepdims=True))
    total = TensorTotal(at, sq_own, sq_got, sq_send, sq_recv)
    total.start()
    squares[...] = total.finish()
    for s in range(seqs):
        gate = z_buf[s].astype(F32)
        gated = y_buf[s] * gate * jax.nn.sigmoid(gate)
        norm = lax.rsqrt(to_column(squares[s : s + 1, :]) / (4 * xw) + EPSILON)
        value = gated * norm * mgain_ref[...].reshape(1, xw)
        low[pl.ds(s * span, span), pl.ds(qw, xw)] = value.astype(BF16)
    for chunk in range(2):
        row_og.finish(chunk)
    def drain():
        for gather in [*gathers[:4], kv_gather]:
            gather.drain()
        for row in (row_nx, row_og):
            for chunk in range(2):
                row.drain(chunk)
        pl.when(after)(lambda: halo().wait_send())

    gathers[3].finish()
    if joined is not None:
        joined.step, joined.gathers = step, gathers
        joined.drains.append(drain)
        return
    step(5, 2)
    for gather in gathers[4:]:
        gather.finish()
    for gather in gathers[4:]:
        gather.drain()
    drain()


def gather_sems(devices, pieces):
    dma = pltpu.SemaphoreType.DMA
    out = []
    for _, _, cross in pieces:
        out += [dma((devices,)) for _ in range(4)] if cross else line_gather_sems(devices)
    return out


def mixer_specs(cfg, columns):
    devices, layout, pieces, heads = (cfg[k] for k in ("devices", "layout", "pieces", "heads"))
    seqs, sub, width = cfg["rows"]
    span = sub * 4
    tokens = seqs * span
    xw, sw, qw = (layout[k][1] for k in ("x", "state", "q"))
    size = sw // 2
    count = devices * span
    dma = pltpu.SemaphoreType.DMA
    outs = (
        ((width, columns), BF16),
        ((seqs, span, width), BF16),
        ((seqs, span, width), BF16),
        ((tokens, qw + xw), BF16),
        ((devices, seqs, span, qw), BF16),
        ((seqs, 2 * span, qw), BF16),
        ((seqs, 2 * span, count), BF16),
        ((seqs, span, qw), F32),
        ((seqs, span + 8, xw + sw), F32),
        ((seqs, span, xw + sw), F32),
        ((seqs, span, LANES), F32),
        ((seqs, size, xw), BF16),
        ((seqs, 16, xw), BF16),
        ((seqs, span, xw), F32),
        ((seqs, span, xw), BF16),
        ((8, span), F32),
        ((seqs, span, LANES), F32),
        ((8, span), F32),
        ((8, LANES), F32),
        ((seqs, 16, width), BF16),
    )
    scratch = [
        pltpu.VMEM((seqs, size + 16, xw), BF16),
        pltpu.VMEM((seqs, span, xw), BF16),
        pltpu.VMEM((devices, seqs // 2, span, qw), BF16),
        pltpu.VMEM((devices, seqs // 2, span, qw), BF16),
        dma((2,)),
        pltpu.VMEM((span, 2 * LANES), F32),
        dma,
        dma((2, 2, 3)),
        dma((2, 2, 4)),
        dma((4, devices)),
        dma((2,)),
        pltpu.VMEM((8, span), F32),
        pltpu.VMEM((3, 8, span), F32),
        dma((3,)),
        dma((3,)),
    ]
    scratch += state_pass_scratch(seqs // 2, size, xw) + gather_sems(devices, pieces)
    return outs, scratch


def mixer(cfg, x, *args):
    outs, scratch = mixer_specs(cfg, cfg["layout"]["down"][0])
    vmem = pl.BlockSpec(memory_space=pltpu.VMEM)
    in_specs = [vmem] * (1 + len(args))
    in_specs[12] = pl.BlockSpec(memory_space=pl.ANY)
    return pl.pallas_call(
        partial(mixer_kernel, cfg),
        out_shape=tuple(jax.ShapeDtypeStruct(*out) for out in outs),
        in_specs=in_specs,
        out_specs=(vmem,) * len(outs),
        scratch_shapes=scratch,
        compiler_params=pltpu.CompilerParams(
            collective_id=0, has_side_effects=True, vmem_limit_bytes=VMEM_BYTES
        ),
        name="mixer",
    )(x, *args)


def back_kernel(cfg, *refs, joined=None):
    (
        x_ref, gh_ref, gain_ref, w_any, nx_ref, og_ref, gb_ref, low_ref, nf_any, dgu_any, act_ref,
        kv_any, q2_ref, probs_any, att_ref, ext_ref, pre_ref, step_ref, entering, carry, y_ref,
        z_ref, squares, aux_ref, seg_ref, head_ref, nxh_ref, rope_any, xt_ref, stt_ref, mgain_ref, fgain_ref,
        rg_ref, dw_ref, sums, kvs,
        w_ref, d_in, dlow, dy, dbc, dcum, ext_grad, halo_got, local2, after_state, keys_buf,
        prob_buf, dkv, dkv_other, dkv_swap, dkv_got, dkv_line, dkv_own,
        part, near, far, grads, got, line, small_near, small_far, small_dp, kv_near, kv_far,
        sq_own, sq_got, swap_sems,
        rope_ref, w_sem, early_sems, rope_sem, load_sems, halo_sems, sq_send, sq_recv, send, recv, small_send, small_recv,
        dp_send, dp_recv, kv_send, kv_recv,
        *rest,
    ) = refs
    devices, layout, pieces, heads = (cfg[k] for k in ("devices", "layout", "scatters", "heads"))
    at = Place(devices)
    seqs, sub, width = x_ref.shape
    span = sub * 4
    tokens = seqs * span
    half = seqs // 2
    rows = half * span
    depth = width // devices
    xw, sw, qw = (layout[k][1] for k in ("x", "state", "q"))
    size = sw // 2
    head_dim = xw // heads
    at_dim = qw // 2
    mixed = xw + sw
    count = devices * span
    in_w = layout["in"][1]
    pass_refs, kv_sems, sems = rest[:10], rest[10:14], rest[14:]
    slots = 1 if joined is not None else keys_buf.shape[0]

    def loads(s):
        slot = s % slots
        return (
            pltpu.make_async_copy(kv_any.at[:, s], keys_buf.at[slot], load_sems.at[0, slot]),
            pltpu.make_async_copy(probs_any.at[s], prob_buf.at[slot], load_sems.at[1, slot]),
        )

    if joined is None:
        load = pltpu.make_async_copy(w_any.at[:, pl.ds(0, w_ref.shape[1])], w_ref, w_sem)
        load.start()
        early = (
            pltpu.make_async_copy(nf_any, part, early_sems.at[0]),
            pltpu.make_async_copy(dgu_any, d_in.at[:, pl.ds(0, dgu_any.shape[1])], early_sems.at[1]),
        )
        for copy in early:
            copy.start()
        rope_copy = pltpu.make_async_copy(
            rope_any.at[pl.ds(pl.multiple_of(at.dp * span, span), span), :], rope_ref, rope_sem
        )
        rope_copy.start()
        for copy in loads(0):
            copy.start()
        Neighbours(at).greet(flips=True)
        nf_ref, dgu_ref = part, d_in
    else:
        w_ref, nf_ref, dgu_ref = w_any, nf_any, dgu_any
    taps = jnp.concatenate([xt_ref[...], stt_ref[...]], 1)
    step_bias, decay_log, skips = head_ref[0:1, :], head_ref[1:2, :], head_ref[2:3, :]
    mixer_scale = mgain_ref[...].reshape(1, xw)

    def rows_of(buf):
        def view(rank, chunk):
            return buf.at[pl.ds(chunk * half, half), pl.ds(pl.multiple_of(rank * sub, sub), sub), :]

        return view

    scatters = []
    kept = layout["gu"][0]

    def terms(first):
        return w_any if joined is not None and first >= kept else grads

    kind = RelayScatter if at.lines == 4 else DirectScatter
    for i, (first, columns) in enumerate(pieces):

        def block(buf, k, first=first, columns=columns):
            return buf.at[pl.ds(pl.multiple_of(k * depth, depth), depth), pl.ds(first, columns)]

        scatters.append(
            kind(
                at,
                partial(block, terms(first)),
                partial(block, got),
                partial(block, line),
                sems[4 * i : 4 * i + 4],
            )
        )

    def finish(i):
        first, columns = pieces[i]
        scatters[i].finish(dw_ref.at[:, pl.ds(first, columns)])

    def product(lhs, rhs_ref, first, columns, into):
        tile = 2 * LANES if columns % (2 * LANES) == 0 else LANES

        @pl.loop(0, columns // tile)
        def _(j):
            src = pl.ds(pl.multiple_of(first + j * tile, LANES), tile)
            dst = pl.ds(pl.multiple_of(into + j * tile, LANES), tile)
            terms(into)[:, dst] = dot_tn(lhs, rhs_ref[:, src]).astype(BF16)

    def weights(i, lhs_ref, rhs_ref, first):
        into, columns = pieces[i]
        product(lhs_ref[...].reshape(tokens, width), rhs_ref, first, columns, into)

    ff = layout["down"][1]

    def gradients(i, *args):
        weights(i, *args)
        scatters[i].start()

    def first():
        if joined is not None:
            for late in joined.gathers[4:]:
                late.drain()
        gradients(0, og_ref, act_ref, 0)

    def second():
        gradients(1, nf_ref, dgu_ref, 0)

    def third():
        gradients(2, nf_ref, dgu_ref, ff)

    def fourth():
        scatters[0].send()

    if joined is not None:
        joined.beside_feed_forward = (first, second, third, fourth)
        yield
    else:
        first()
        load.wait()
    dlow[...] = dot_nn(
        gb_ref[...].reshape(tokens, width), w_ref[:, pl.ds(*layout["out"])]
    )
    mixer_gain = jnp.zeros((1, xw), F32)
    sq_own[...] = jnp.zeros(sq_own.shape, F32)
    for s in range(seqs):
        gate = z_ref[s].astype(F32)
        gated = y_ref[s] * gate * jax.nn.sigmoid(gate)
        norm = lax.rsqrt(to_column(squares[s : s + 1, :]) / (4 * xw) + EPSILON)
        grad = dlow[pl.ds(s * span, span), pl.ds(qw, xw)]
        mixer_gain = mixer_gain + jnp.sum(grad * gated * norm, 0, keepdims=True)
        inner = jnp.sum(gated * grad * mixer_scale, 1, keepdims=True)
        sq_own[s : s + 1, :] = to_row(inner)
    total = TensorTotal(at, sq_own, sq_got, sq_send, sq_recv)
    total.start()
    if joined is None:
        for copy in early:
            copy.wait()
        second()
        third()
        fourth()
    weights(3, gb_ref, low_ref, 0)
    scatters[1].send()
    scatters[0].pass_on()
    inner_rows = total.finish()
    for s in range(seqs):
        gate = z_ref[s].astype(F32)
        sigmoid = jax.nn.sigmoid(gate)
        gated = y_ref[s] * gate * sigmoid
        norm = lax.rsqrt(to_column(squares[s : s + 1, :]) / (4 * xw) + EPSILON)
        inner = to_column(inner_rows[s : s + 1, :])
        term = dlow[pl.ds(s * span, span), pl.ds(qw, xw)] * mixer_scale
        grad = norm * (term - gated * (norm * norm * inner / (4 * xw)))
        dy[s] = grad * gate * sigmoid
        grad = grad * y_ref[s] * sigmoid * (1.0 + gate * (1.0 - sigmoid))
        d_in[pl.ds(s * span, span), pl.ds(*layout["z"])] = grad.astype(BF16)

    def parts(s):
        active = pre_ref[s] * jax.nn.sigmoid(pre_ref[s])
        step, rate, running = decay_parts(step_ref[s], decay_log, step_bias)
        state_in = active[:, xw : xw + size].astype(BF16)
        state_out = active[:, xw + size :].astype(BF16)
        return active[:, :xw], state_in, state_out, step, rate, running

    @pl.loop(0, seqs)
    def _(s):
        _, _, state_out, _, _, running = parts(s)
        factor = spread(jnp.exp(running) * aux_ref[s][:, 3:4], heads, head_dim)
        low = (dy[s] * factor).astype(BF16)
        local2[s, :size, :] = dot_tn(state_out, low).astype(BF16)
        local2[s, size:, :] = carry[s]

    passing = StatePass(
        at, local2, pass_refs[0], pass_refs[1], pass_refs[2], pass_refs[3], after_state,
        pass_refs[4:], True,
    )
    passing.start()
    scatters[3].start()
    @pl.loop(0, seqs)
    def _(s):
        x, state_in, state_out, step, _, running = parts(s)
        running_rows = running.T
        allowed = same_document(aux_ref[s], seg_ref[pl.ds(s, 1), :])
        xs = (x * spread(step, heads, head_dim)).astype(BF16)
        joined = dot_nt(state_out, state_in)
        lane = iota((span, LANES), 1)
        d_joined = jnp.zeros((span, span), F32)
        d_running = jnp.zeros((span, LANES), F32)
        blocks = []
        for h in range(heads):
            cols = slice(h * head_dim // LANES * LANES, h * head_dim // LANES * LANES + LANES)
            begin = h * head_dim % LANES
            inside = jnp.logical_and(lane >= begin, lane < begin + head_dim)
            grad = dy[s, :, pl.ds(cols.start, LANES)]
            decay = jnp.exp(running[:, h : h + 1] - running_rows[h : h + 1, :] + allowed)
            weight = joined * decay
            d_weight = dot_nt(jnp.where(inside, grad, 0.0).astype(BF16), xs[:, cols])
            d_joined = d_joined + d_weight * decay
            product_ = (d_weight * weight).astype(BF16)
            one = (lane == h).astype(BF16)
            d_running = d_running + dot_nn(product_, one) - dot_tn(product_, one)
            blocks.append(dot_tn(weight.astype(BF16), grad.astype(BF16)))
        dlow[pl.ds(pl.multiple_of(s * span, span), span), pl.ds(qw, xw)] = pick_halves(blocks, head_dim)
        d_joined = d_joined.astype(BF16)
        factor = spread(jnp.exp(running) * aux_ref[s][:, 3:4], heads, head_dim)
        crossed = dot_nn(state_out, entering[s]) * factor
        dcum[s] = d_running + head_sums(dy[s] * crossed, heads, head_dim)
        low = (dy[s] * factor).astype(BF16)
        dbc[s, :, :size] = dot_tn(d_joined, state_out)
        dbc[s, :, size:] = dot_nn(d_joined, state_in) + dot_nt(low, entering[s])

    passing.run()
    scatters[2].send()
    scatters[1].pass_on()
    lane = iota((span, LANES), 1)
    upper = lane >= at_dim
    even = lax.rem(at.t, 2) == 0
    if joined is None:
        rope_copy.wait()
    cosine, sine = rope_ref[:, :LANES], rope_ref[:, LANES:]
    scale = 1.0 / math.sqrt(at_dim)
    for s in range(seqs):
        slot = s % slots
        if joined is None:
            for copy in loads(s):
                copy.wait()
            if slots > 1 and s + 1 < seqs:
                for copy in loads(s + 1):
                    copy.start()
            keys, weights_ref = keys_buf[slot].reshape(count, qw), prob_buf.at[slot]
        else:
            keys, weights_ref = kv_any[:, s].reshape(count, qw), probs_any.at[s]
        grad = dlow[pl.ds(s * span, span), pl.ds(0, qw)].astype(BF16).astype(F32)
        inner = grad * att_ref[s]
        d_keys = jnp.zeros((count, qw), F32)
        d_query = []
        for h in range(2):
            mine = upper if h else jnp.logical_not(upper)
            delta = jnp.sum(jnp.where(mine, inner, 0.0), 1, keepdims=True)
            moved = grad if h else pltpu.roll(grad, at_dim, 1)
            moved = jnp.where(upper, moved, 0.0).astype(BF16)
            weight = weights_ref[pl.ds(h * span, span), :]
            d_weight = dot_nt(moved, keys)
            d_score = (weight.astype(F32) * (d_weight - delta)).astype(BF16)
            query = q2_ref[s, pl.ds(h * span, span), :]
            d_keys = d_keys + dot_tn(d_score, query) + dot_tn(weight, moved)
            d_query.append(dot_nn(d_score, keys))
        d_keys = jnp.where(even, d_keys, pltpu.roll(d_keys, at_dim, 1))
        turned = pltpu.roll(d_keys, at_dim, 1).reshape(devices, span, qw)
        d_keys = d_keys.reshape(devices, span, qw)
        if s < half:
            dkv[:, s] = d_keys.astype(BF16)
            dkv_other[:, s] = turned.astype(BF16)
        else:
            wide = iota((devices, span, qw), 2) < at_dim
            kept_half = dkv[:, s - half].astype(F32)
            dkv[:, s - half] = jnp.where(wide, kept_half, turned).astype(BF16)
            kept_half = dkv_other[:, s - half].astype(F32)
            dkv_other[:, s - half] = jnp.where(wide, kept_half, d_keys).astype(BF16)
        d_query = jnp.where(upper, pltpu.roll(d_query[1], at_dim, 1), d_query[0]) * scale
        d_in[pl.ds(s * span, span), pl.ds(*layout["q"])] = turn(
            d_query, cosine, -sine, at_dim // 2
        ).astype(BF16)
    kv_scatter = DirectScatter(
        at,
        lambda k: dkv.at[k],
        lambda zz: dkv_got.at[zz],
        lambda zz: dkv_line.at[zz],
        kv_sems,
        causal=True,
    )
    kv_swap = remote(
        dkv_other, dkv_swap, swap_sems.at[0], swap_sems.at[1], {"tensor": at.t_near}
    )
    kv_swap.start()
    gradients(4, nx_ref, d_in, pieces[4][0])
    kv_swap.wait()
    dkv[...] = (dkv[...].astype(F32) + dkv_swap[...].astype(F32)).astype(BF16)
    kv_scatter.start()
    scatters[2].pass_on()
    scatters[3].send()
    finish(0)
    kv_scatter.send()
    scatters[3].pass_on()
    passing.finish()
    tap_grads = [jnp.zeros((1, mixed), F32) for _ in range(4)]
    bias_grad = jnp.zeros((1, mixed), F32)
    step_grad = jnp.zeros((1, LANES), F32)
    decay_grad = jnp.zeros((1, LANES), F32)
    skip_grad = jnp.zeros((1, xw), F32)
    ext_grad[:, pl.ds(0, 8), :] = jnp.zeros((seqs, 8, mixed), F32)
    for s in range(seqs):
        aux = aux_ref[s]
        x, state_in, state_out, step, rate, running = parts(s)
        step_wide = spread(step, heads, head_dim)
        xs = x * step_wide
        end = running[span - 1 : span, :]
        tail = spread(jnp.exp(end - running) * aux[:, 4:5], heads, head_dim)
        later = after_state[s]
        found = dot_nn(state_in, later)
        weighted = xs * tail
        d_xs = dlow[pl.ds(s * span, span), pl.ds(qw, xw)] + found * tail
        d_in_state = dbc[s, :, :size] + dot_nt(weighted.astype(BF16), later)
        moved = head_sums(found * weighted, heads, head_dim)
        carried = jnp.sum(later.astype(F32) * entering[s].astype(F32), 0, keepdims=True)
        carried = head_sums(carried, heads, head_dim) * jnp.exp(end) * aux[span - 1 : span, 3:4]
        final = jnp.sum(moved, 0, keepdims=True) + carried
        d_running = dcum[s] - moved
        d_running = d_running + jnp.where(iota((span, LANES), 0) == span - 1, final, 0.0)
        d_decay = running_sum(d_running, backward=True)
        d_step = head_sums(d_xs * x, heads, head_dim) + d_decay * rate
        d_step = d_step * jax.nn.sigmoid(step_ref[s] + step_bias)
        d_in[pl.ds(s * span, span), pl.ds(*layout["ks"])] = pltpu.roll(d_step, at_dim, 1).astype(BF16)
        step_grad = step_grad + jnp.sum(d_step, 0, keepdims=True)
        decay_grad = decay_grad + jnp.sum(d_decay * step, 0, keepdims=True) * rate
        skip_grad = skip_grad + jnp.sum(dy[s] * x, 0, keepdims=True)
        d_x = d_xs * step_wide + spread(skips, heads, head_dim) * dy[s]
        value = pre_ref[s]
        sigmoid = jax.nn.sigmoid(value)
        slope = sigmoid * (1.0 + value * (1.0 - sigmoid))
        outer = jnp.concatenate([d_x, d_in_state, dbc[s, :, size:]], 1) * slope
        bias_grad = bias_grad + jnp.sum(outer, 0, keepdims=True)
        ext_grad[s, pl.ds(8, span), :] = taps[3:4, :] * outer
        tap_grads[3] = tap_grads[3] + jnp.sum(
            outer * ext_ref[s, pl.ds(8, span), :], 0, keepdims=True
        )
        for back in (1, 2, 3):
            valid = outer * aux[:, back - 1 : back]
            tap_grads[3 - back] = tap_grads[3 - back] + jnp.sum(
                valid * ext_ref[s, pl.ds(8 - back, span), :], 0, keepdims=True
            )
            ext_grad[s, pl.ds(8 - back, span), :] += taps[3 - back : 4 - back, :] * valid
    before, after = at.dp > 0, at.dp < devices - 1

    def halo():
        return remote(
            ext_grad.at[:, pl.ds(0, 8), :],
            halo_got,
            halo_sems.at[0],
            halo_sems.at[1],
            {"dp": at.dp - 1},
        )

    pl.when(before)(lambda: halo().start())
    sums[...] = jnp.zeros(sums.shape, F32)
    sums[1:2, :] = fgain_ref[...]
    for k in range(4):
        sums[2 + k : 3 + k, pl.ds(0, sw)] = tap_grads[k][:, xw:]
        sums[8 + k : 9 + k, pl.ds(0, xw)] = tap_grads[k][:, :xw]
    sums[6:7, pl.ds(0, sw)] = bias_grad[:, xw:]
    sums[12:13, pl.ds(0, xw)] = bias_grad[:, :xw]
    sums[13:14, pl.ds(0, xw)] = mixer_gain
    sums[14:15, pl.ds(0, LANES)] = step_grad
    sums[14:15, pl.ds(LANES, LANES)] = decay_grad
    sums[14:15, pl.ds(2 * LANES, LANES)] = head_sums(
        jnp.broadcast_to(skip_grad, (8, xw)), heads, head_dim
    )[:1]
    finish(1)
    kv_scatter.finish(dkv_own)
    for s in range(seqs):
        value = dkv_own[s % half]
        value = value if s < half else pltpu.roll(value, at_dim, 1)
        value = jnp.where(even, turn(value, cosine, -sine, at_dim // 2), value)
        where = (pl.ds(s * span, span), pl.ds(*layout["ks"]))
        d_in[where] = jnp.where(upper, d_in[where].astype(F32), value).astype(BF16)
    value = ext_grad[:, pl.ds(8, span), :].reshape(tokens, mixed).astype(BF16)
    d_in[:, pl.ds(*layout["x"])] = value[:, :xw]
    d_in[:, pl.ds(*layout["state"])] = value[:, xw:]
    halo_rows = jnp.concatenate([jnp.zeros((seqs, 8, mixed), F32), ext_grad[:, pl.ds(0, 8), :]], 1)
    halo_rows = halo_rows.reshape(seqs * 16, mixed).astype(BF16)
    rows_before = nxh_ref[...].reshape(seqs * 16, width)
    halo_x, halo_state = halo_rows[:, :xw], halo_rows[:, xw:]
    weights(5, nx_ref, d_in, pieces[5][0])
    into = pl.ds(*layout["state"])
    grads[:, into] = (grads[:, into].astype(F32) + dot_tn(rows_before, halo_state)).astype(BF16)
    scatters[5].start()
    weights(6, nx_ref, d_in, pieces[6][0])
    into = pl.ds(*layout["x"])
    grads[:, into] = (grads[:, into].astype(F32) + dot_tn(rows_before, halo_x)).astype(BF16)
    scatters[6].start()
    scatters[4].send()
    pl.when(after)(lambda: halo().wait_recv())

    @pl.when(after)
    def _():
        ext_grad[:, pl.ds(span, 8), :] += halo_got[...]

    for s in range(seqs):
        value = ext_grad[s, pl.ds(span - 8, 16), :].astype(BF16)
        ends = pl.ds(s * span + span - 16, 16)
        d_in[ends, pl.ds(*layout["x"])] = value[:, :xw]
        d_in[ends, pl.ds(*layout["state"])] = value[:, xw:]
    back = RowScatter(
        at,
        rows_of(part),
        lambda which, chunk: near.at[which, pl.ds(chunk * half, half)],
        lambda chunk: far.at[pl.ds(chunk * half, half)],
        send,
        recv,
    )
    for c in range(2):
        value = dot_nt(d_in[pl.ds(c * rows, rows), :], w_ref[:, pl.ds(0, in_w)])
        part[pl.ds(c * half, half)] = value.astype(BF16).reshape(half, span, width)
        back.start(c)
    scatters[4].pass_on()
    for c in range(2):
        back.middle(c)
    scatters[5].send()
    finish(2)
    total = jnp.zeros((1, width), F32)
    gain = gain_ref[...].reshape(1, width)
    for c in range(2):
        seq = pl.ds(c * half, half)
        grad, terms = rms_rows_grad(x_ref[seq].astype(F32), gain, back.finish(c))
        rg_ref[seq] = gh_ref[seq] + grad
        total = total + jnp.sum(terms.reshape(half * sub, width), 0, keepdims=True)
    sums[0:1, :] = total
    exchanges = [
        (sums.at[pl.ds(0, 8)], small_near, small_send.at[0], small_recv.at[0], {"tensor": at.t_near}),
        (sums.at[pl.ds(0, 8)], small_far, small_send.at[1], small_recv.at[1], {"tensor": at.t_far}),
    ] + [
        (sums, small_dp.at[i], dp_send.at[i], dp_recv.at[i], {"dp": other})
        for i, other in enumerate(at.flips())
    ]

    def begin(i):
        remote(*exchanges[i]).start()

    def end(i):
        remote(*exchanges[i]).wait()
        into, other = exchanges[i][:2]
        into[...] += other[...]

    begin(0)
    scatters[6].send()
    scatters[5].pass_on()
    end(0)
    begin(1)
    finish(3)
    end(1)
    begin(2)
    scatters[6].pass_on()
    end(2)
    begin(3)
    finish(4)
    end(3)
    finish(5)
    kvw = layout["ks"][1]
    kv_near[0, :, pl.ds(0, kvw)] = dw_ref[:, pl.ds(*layout["ks"])].astype(BF16)
    kv_near[0, :, pl.ds(kvw, sw)] = dw_ref[:, pl.ds(*layout["state"])].astype(BF16)
    copy = remote(kv_near.at[0], kv_near.at[1], kv_send.at[0], kv_recv.at[0], {"tensor": at.t_near})
    copy.start()
    begin(4)
    copy.wait()
    here, there = kv_near[0].astype(F32), kv_near[1].astype(F32)
    keys = jnp.where(even, here[:, :kvw], there[:, :kvw])
    values = jnp.where(even, there[:, :kvw], here[:, :kvw])
    low_lanes = iota(keys.shape, 1) < at_dim
    keys = jnp.where(low_lanes, keys, pltpu.roll(values, at_dim, 1))
    kv_far[0, :, :kvw] = keys.astype(BF16)
    kv_far[0, :, kvw:] = (here[:, kvw:] + there[:, kvw:]).astype(BF16)
    copy = remote(kv_far.at[0], kv_far.at[1], kv_send.at[1], kv_recv.at[1], {"tensor": at.t_far})
    copy.start()
    end(4)
    for i in range(5, len(exchanges)):
        begin(i)
        end(i)
    finish(6)
    copy.wait()
    own_first = at.t < 2
    for k in range(2):
        mine_first = own_first if k == 0 else jnp.logical_not(own_first)
        kvs[:, pl.ds(k * kvw, kvw)] = jnp.where(
            mine_first, kv_far[0, :, :kvw], kv_far[1, :, :kvw]
        ).astype(F32)
    kvs[:, pl.ds(2 * kvw, sw)] = kv_far[0, :, kvw:].astype(F32) + kv_far[1, :, kvw:].astype(F32)
    for scatter in [*scatters, kv_scatter]:
        scatter.drain()
    for c in range(2):
        back.drain(c)
    pl.when(before)(lambda: halo().wait_send())
    yield


def back_specs(cfg, joined=False):
    devices, layout, pieces = (cfg[k] for k in ("devices", "layout", "scatters"))
    seqs, sub, width = cfg["rows"]
    span = sub * 4
    tokens = seqs * span
    half = seqs // 2
    depth = width // devices
    lines = devices // 2
    columns = layout["down"][0] + layout["down"][1]
    xw, sw, qw, kvw = (layout[k][1] for k in ("x", "state", "q", "ks"))
    size = sw // 2
    mixed = xw + sw
    in_w = layout["in"][1]
    own = (seqs, sub, width)
    rounds = devices.bit_length() - 1
    slots = 2 if devices * span <= 2048 else 1
    dma = pltpu.SemaphoreType.DMA
    outs = (
        (own, F32),
        ((depth, columns), F32),
        ((16, width), F32),
        ((depth, 2 * kvw + sw), F32),
    )
    scratch = {
        "w": pltpu.VMEM((width, in_w + qw + xw), BF16),
        "d_in": pltpu.VMEM((tokens, in_w), BF16),
        "dlow": pltpu.VMEM((tokens, qw + xw), F32),
        "dy": pltpu.VMEM((seqs, span, xw), F32),
        "dbc": pltpu.VMEM((seqs, span, sw), F32),
        "dcum": pltpu.VMEM((seqs, span, LANES), F32),
        "ext_grad": pltpu.VMEM((seqs, span + 8, mixed), F32),
        "halo_got": pltpu.VMEM((seqs, 8, mixed), F32),
        "local2": pltpu.VMEM((seqs, size + 16, xw), BF16),
        "after_state": pltpu.VMEM((seqs, size, xw), BF16),
        "keys_buf": pltpu.VMEM((slots, devices, span, qw), BF16),
        "prob_buf": pltpu.VMEM((slots, 2 * span, devices * span), BF16),
        "dkv": pltpu.VMEM((devices, half, span, qw), BF16),
        "dkv_other": pltpu.VMEM((devices, half, span, qw), BF16),
        "dkv_swap": pltpu.VMEM((devices, half, span, qw), BF16),
        "dkv_got": pltpu.VMEM((lines, half, span, qw), BF16),
        "dkv_line": pltpu.VMEM((lines, half, span, qw), BF16),
        "dkv_own": pltpu.VMEM((half, span, qw), F32),
        "part": pltpu.VMEM((seqs, span, width), BF16),
        "near": pltpu.VMEM((2,) + own, BF16),
        "far": pltpu.VMEM(own, BF16),
        "grads": pltpu.VMEM((width, layout["gu"][0] if joined else columns), BF16),
        "got": pltpu.VMEM((lines * depth, columns), BF16),
        "line": pltpu.VMEM((lines * depth, columns), BF16),
        "small_near": pltpu.VMEM((8, width), F32),
        "small_far": pltpu.VMEM((8, width), F32),
        "small_dp": pltpu.VMEM((rounds, 16, width), F32),
        "kv_near": pltpu.VMEM((2, depth, kvw + sw), BF16),
        "kv_far": pltpu.VMEM((2, depth, kvw + sw), BF16),
        "sq_own": pltpu.VMEM((8, span), F32),
        "sq_got": pltpu.VMEM((3, 8, span), F32),
        "swap_sems": dma((2,)),
        "rope": pltpu.VMEM((span, 2 * LANES), F32),
        "w_sem": dma,
        "early_sems": dma((2,)),
        "rope_sem": dma,
        "load_sems": dma((2, 2)),
        "halo_sems": dma((2,)),
        "sq_send": dma((3,)),
        "sq_recv": dma((3,)),
        "send": dma((2, 3)),
        "recv": dma((2, 4)),
        "small_send": dma((2,)),
        "small_recv": dma((2,)),
        "dp_send": dma((rounds,)),
        "dp_recv": dma((rounds,)),
        "kv_send": dma((2,)),
        "kv_recv": dma((2,)),
    }
    rest = (
        state_pass_scratch(half, size, xw)
        + scatter_sems(devices) * (1 + len(pieces))
    )
    return outs, scratch, rest


APART = (
    "w", "keys_buf", "prob_buf", "part", "rope", "w_sem", "early_sems", "rope_sem", "load_sems",
)


def run_back(cfg, *refs):
    for _ in back_kernel(cfg, *refs):
        pass


def backward(cfg, x, *args):
    outs, scratch, rest = back_specs(cfg)
    vmem = pl.BlockSpec(memory_space=pltpu.VMEM)
    in_specs = [vmem] * (1 + len(args))
    for i in (3, 8, 9, 11, 13, 27):
        in_specs[i] = pl.BlockSpec(memory_space=pl.ANY)
    return pl.pallas_call(
        partial(run_back, cfg),
        out_shape=tuple(jax.ShapeDtypeStruct(*out) for out in outs),
        in_specs=in_specs,
        out_specs=(vmem,) * len(outs),
        scratch_shapes=list(scratch.values()) + rest,
        compiler_params=pltpu.CompilerParams(
            collective_id=2, has_side_effects=True, vmem_limit_bytes=VMEM_BYTES
        ),
        name="backward",
    )(x, *args)


class Joined:
    def __init__(self, dn_in):
        self.dn_in = dn_in
        self.drains = []


def joined_kernel(cfg, *refs):
    devices, layout = cfg["devices"], cfg["layout"]
    inputs, refs = refs[:23], refs[23:]
    dn_in, fgain_ref = inputs[21:]
    x_ref, og_in, gain_ref = inputs[:3]
    rope_any, xt_ref, _, stt_ref = inputs[12:16]
    mgain_ref = inputs[20]
    inputs = inputs[:21]
    block_out, rg, dw, sums, kvs = refs[:5]
    refs = refs[5:]

    def take(count):
        nonlocal refs
        taken, refs = refs[:count], refs[count:]
        return taken

    mix_outs, mix_scratch = mixer_specs(cfg, layout["down"][0] + layout["down"][1])
    mixed = take(len(mix_outs))
    mixed_scratch = take(len(mix_scratch))
    ffn_outs, buffers, _, sems = ffn_specs(cfg)
    fed = (block_out, *take(len(ffn_outs) - 1))
    fed_scratch = (*take(len(buffers)), None, None, None, *take(len(sems)))
    _, scratch, rest = back_specs(cfg, True)
    names = [name for name in scratch if name not in APART]
    mine = dict(zip(names, take(len(names))))
    mine["part"] = fed_scratch[0]
    mine["rope"] = mixed_scratch[5]
    back_scratch = [mine.get(name) for name in scratch] + list(take(len(rest)))
    (
        w_all, nx, og, low, kv, q2, probs, att, ext, pre, step_buf, entering, carry, y_buf, z_buf,
        squares, aux_ref, seg_rows, head_ref, nxh,
    ) = mixed
    _, gh, gb, nf, act, dgu, gain_part = fed
    joined = Joined(dn_in)
    later = back_kernel(
        cfg, x_ref, gh, gain_ref, w_all, nx, og, gb, low, nf, dgu, act, kv, q2, probs, att, ext, pre,
        step_buf, entering, carry, y_buf, z_buf, squares, aux_ref, seg_rows, head_ref, nxh, rope_any, xt_ref,
        stt_ref, mgain_ref, gain_part, rg, dw, sums, kvs, *back_scratch, joined=joined,
    )
    mixer_kernel(cfg, *inputs, *mixed, *mixed_scratch, joined=joined)
    next(later)
    ffn_kernel(
        devices, layout, x_ref, low, og, og_in, fgain_ref, w_all, None, *fed, *fed_scratch,
        joined=joined,
    )
    next(later)
    for drain in joined.drains:
        drain()


def joined_layer(cfg, *args):
    layout = cfg["layout"]
    mix_outs, mix_scratch = mixer_specs(cfg, layout["down"][0] + layout["down"][1])
    ffn_outs, buffers, _, sems = ffn_specs(cfg)
    outs, scratch, rest = back_specs(cfg, True)
    vmem = pl.BlockSpec(memory_space=pltpu.VMEM)
    in_specs = [vmem] * len(args)
    in_specs[12] = pl.BlockSpec(memory_space=pl.ANY)
    return pl.pallas_call(
        partial(joined_kernel, cfg),
        out_shape=tuple(jax.ShapeDtypeStruct(*out) for out in (ffn_outs[0], *outs)),
        in_specs=in_specs,
        out_specs=(vmem,) * 5,
        scratch_shapes=[pltpu.VMEM(*out) for out in mix_outs]
        + mix_scratch
        + [pltpu.VMEM(*out) for out in ffn_outs[1:]]
        + buffers
        + sems
        + [ref for name, ref in scratch.items() if name not in APART]
        + rest,
        compiler_params=pltpu.CompilerParams(
            collective_id=0, has_side_effects=True, vmem_limit_bytes=VMEM_BYTES
        ),
        name="layer",
    )(*args)


def unpack_kernel(layout, local, *refs):
    (
        dw, kvs, sums, rg, block,
        block_out, rg_out, gain1, gain2, wq, wkv, wao, wmi, wst, wsp, cw, cb, csw, csb, sbias,
        dlog, skip, mgain, wmo, wgu, wdn,
    ) = refs
    block_out[...] = block[...]
    rg_out[...] = rg[...]
    width = sums.shape[1]
    xw, sw = layout["x"][1], layout["state"][1]
    qw = layout["q"][1]
    ff = layout["down"][1]
    kvw = layout["ks"][1]

    def part(name):
        return dw[:, pl.ds(*layout[name])]

    gain1[...] = sums[0:1, :].reshape(width)
    gain2[...] = sums[1:2, :].reshape(width)
    wq[...] = part("q")
    wkv[:, 0, :] = kvs[:, :kvw]
    wkv[:, 1, :] = kvs[:, kvw : 2 * kvw]
    out = part("out")
    wao[...] = out[:, :qw].T
    wmo[...] = out[:, qw:].T
    wdn[...] = part("down").T
    wmi[:, 0, :] = part("z")
    wmi[:, 1, :] = part("x")
    wst[...] = kvs[:, 2 * kvw :]
    wsp[...] = part("ks").T[kvw // 2 : kvw // 2 + local, :]
    gate_up = part("gu")
    wgu[:, 0, :] = gate_up[:, :ff]
    wgu[:, 1, :] = gate_up[:, ff:]
    cw[...] = sums[8:12, :xw]
    cb[...] = sums[12:13, :xw].reshape(xw)
    csw[...] = sums[2:6, :sw]
    csb[...] = sums[6:7, :sw].reshape(sw)
    sbias[...] = sums[14:15, :local].reshape(local)
    dlog[...] = sums[14:15, LANES : LANES + local].reshape(local)
    skip[...] = sums[14:15, 2 * LANES : 2 * LANES + local].reshape(local)
    mgain[...] = sums[13:14, :xw].reshape(xw)


def unpack(layout, local, dw, kvs, sums, rg, block):
    depth = dw.shape[0]
    width = sums.shape[1]
    xw, sw, qw, ff, kvw = (layout[k][1] for k in ("x", "state", "q", "down", "ks"))

    def shape(*dims):
        return jax.ShapeDtypeStruct(dims, F32)

    outs = (
        jax.ShapeDtypeStruct(block.shape, BF16),
        shape(*rg.shape),
        shape(width),
        shape(width),
        shape(depth, qw),
        shape(depth, 2, kvw),
        shape(qw, depth),
        shape(depth, 2, xw),
        shape(depth, sw),
        shape(local, depth),
        shape(4, xw),
        shape(xw),
        shape(4, sw),
        shape(sw),
        shape(local),
        shape(local),
        shape(local),
        shape(xw),
        shape(xw, depth),
        shape(depth, 2, ff),
        shape(ff, depth),
    )
    vmem = pl.BlockSpec(memory_space=pltpu.VMEM)
    return pl.pallas_call(
        partial(unpack_kernel, layout, local),
        out_shape=outs,
        in_specs=[vmem] * 5,
        out_specs=(vmem,) * len(outs),
        name="unpack",
    )(dw, kvs, sums, rg, block)


def rope_table(length, head_dim):
    half = head_dim // 2
    frequency = np.exp(-math.log(ROTARY_BASE) * 2.0 * np.arange(half) / head_dim)
    angle = np.arange(length)[:, None] * frequency[None, :]
    cosine, sine = np.cos(angle), np.sin(angle)
    copies = LANES // head_dim
    table = [cosine, cosine] * copies + [-sine, sine] * copies
    return np.concatenate(table, 1).astype(np.float32)


def body(
    resid_in,
    segment_ids,
    out_grad,
    input_gain,
    ffn_gain,
    query_weight,
    keyvalue_weight,
    attention_output_weight,
    mixer_input_weight,
    state_input_weight,
    step_weight,
    conv_mixer,
    conv_mixer_bias,
    conv_state,
    conv_state_bias,
    step_bias,
    decay_log,
    skip_gain,
    mixer_gain,
    mixer_output_weight,
    gate_up_weight,
    down_weight,
):
    shard_count = lax.axis_size("dp")
    head_dim = keyvalue_weight.shape[2] // 2
    query_width = query_weight.shape[1]
    mixer_local = step_weight.shape[1]
    mixer_width = conv_mixer.shape[1]
    state_width = state_input_weight.shape[1]
    ff = down_weight.shape[0]
    layout = {}
    columns = 0
    for name, size in (
        ("state", state_width),
        ("ks", 2 * head_dim),
        ("x", mixer_width),
        ("q", query_width),
        ("z", mixer_width),
        ("out", query_width + mixer_width),
        ("gu", 2 * ff),
        ("down", ff),
    ):
        layout[name] = (columns, size)
        columns += size
    layout["in"] = (0, layout["out"][0])
    q_at, gu_at = (layout[k][0] for k in ("q", "gu"))
    config = {
        "devices": shard_count,
        "layout": layout,
        "heads": mixer_local,
        "rows": resid_in.shape,
        "pieces": (
            (0, layout["x"][0], False),
            (*layout["x"], False),
            (q_at, layout["out"][0] - q_at, False),
            (*layout["out"], False),
            (gu_at, ff, False),
            (gu_at + ff, ff, False),
        ),
        "scatters": (
            layout["down"],
            (gu_at, ff),
            (gu_at + ff, ff),
            layout["out"],
            (q_at, layout["out"][0] - q_at),
            (0, layout["x"][0]),
            layout["x"],
        ),
    }

    rope = jnp.asarray(rope_table(segment_ids.shape[1], head_dim))
    def results(outs):
        return (*outs[:9], outs[9].T, *outs[10:])

    raw = (
        resid_in,
        out_grad,
        input_gain,
        query_weight,
        keyvalue_weight,
        mixer_input_weight,
        state_input_weight,
        step_weight.T,
        gate_up_weight,
        attention_output_weight,
        mixer_output_weight,
        segment_ids,
        rope,
        conv_mixer,
        conv_mixer_bias,
        conv_state,
        conv_state_bias,
        step_bias,
        decay_log,
        skip_gain,
        mixer_gain,
    )
    if segment_ids.size <= JOINED_TOKENS:
        config["pieces"] = (*config["pieces"], (*layout["down"], False))
        block_out, resid_grad, weight_grads, sums, replicated = joined_layer(
            config, *raw, down_weight, ffn_gain
        )
        return results(
            unpack(layout, mixer_local, weight_grads, replicated, sums, resid_grad, block_out)
        )
    (
        w_all, span_normed_input, span_gradient, branch_low, keys, queries, probs, attention, ext,
        pre, step_pre, entering, state_decay, mixer_y, gate_z, squares, aux, seg_rows, head_rows,
        rows_before,
    ) = mixer(config, *raw)
    block_out, grad_hidden, grad_branch, span_feedforward, activated, grad_gate_up, ffn_gain_part = (
        feed_forward(
            config,
            resid_in,
            branch_low,
            span_gradient,
            out_grad,
            ffn_gain,
            w_all,
            down_weight,
        )
    )
    resid_grad, weight_grads, sums, replicated = backward(
        config,
        resid_in,
        grad_hidden,
        input_gain,
        w_all,
        span_normed_input,
        span_gradient,
        grad_branch,
        branch_low,
        span_feedforward,
        grad_gate_up,
        activated,
        keys,
        queries,
        probs,
        attention,
        ext,
        pre,
        step_pre,
        entering,
        state_decay,
        mixer_y,
        gate_z,
        squares,
        aux,
        seg_rows,
        head_rows,
        rows_before,
        rope,
        conv_mixer,
        conv_state,
        mixer_gain,
        ffn_gain_part,
    )
    return results(
        unpack(layout, mixer_local, weight_grads, replicated, sums, resid_grad, block_out)
    )


def solution(mesh):
    placed = (
        P(None, ("dp", "tensor"), None),
        P(),
        P(None, ("dp", "tensor"), None),
        P(),
        P(),
        P("dp", "tensor"),
        P("dp", None, None),
        P("tensor", "dp"),
        P("dp", None, "tensor"),
        P("dp", None),
        P("dp", "tensor"),
        P(None, "tensor"),
        P("tensor"),
        P(),
        P(),
        P("tensor"),
        P("tensor"),
        P("tensor"),
        P("tensor"),
        P("tensor", "dp"),
        P("dp", None, "tensor"),
        P("tensor", "dp"),
    )
    return jax.shard_map(
        body,
        mesh=mesh,
        in_specs=placed,
        out_specs=(
            P(None, ("dp", "tensor"), None),
            P(None, ("dp", "tensor"), None),
            P(),
            P(),
            P("dp", "tensor"),
            P("dp", None, None),
            P("tensor", "dp"),
            P("dp", None, "tensor"),
            P("dp", None),
            P("dp", "tensor"),
            P(None, "tensor"),
            P("tensor"),
            P(),
            P(),
            P("tensor"),
            P("tensor"),
            P("tensor"),
            P("tensor"),
            P("tensor", "dp"),
            P("dp", None, "tensor"),
            P("tensor", "dp"),
        ),
        check_vma=False,
    )
```
